32 devices in a mesh: ctx: 16 (over z, y, core), tp: 2 (over x).
Axes of the slice: x: 2, y: 2, z: 4, core: 2. Of those that a mesh axis runs over, the one named last changes fastest.
Arguments:
- hidden: bfloat16 [4096, 1024], P('ctx'), may hold values from -6 to 6
- pair_of: int32 [16], replicated, may hold values from 0 to 15, each once
- ln1_gain: bfloat16 [1024], replicated, may hold values from 0.099609375 to 1.8984375
- ln1_bias: bfloat16 [1024], replicated, may hold values from -3 to 3
- ln2_gain: bfloat16 [1024], replicated, may hold values from 0.099609375 to 1.8984375
- ln2_bias: bfloat16 [1024], replicated, may hold values from -3 to 3
- w_qkv: bfloat16 [3, 1024, 1024], P(None, None, 'tp'), may hold values from -0.25 to 0.25
- b_qkv: bfloat16 [3, 1024], P(None, 'tp'), may hold values from -0.5 to 0.5
- w_out: bfloat16 [1024, 1024], P('tp'), may hold values from -1.5 to 1.5
- b_out: bfloat16 [1024], replicated, may hold values from -3 to 3
- w_up: bfloat16 [1024, 4096], P(None, 'tp'), may hold values from -0.1875 to 0.1875
- b_up: bfloat16 [4096], P('tp'), may hold values from -4 to 4
- w_down: bfloat16 [4096, 1024], P('tp'), may hold values from -0.09375 to 0.09375
- b_down: bfloat16 [1024], replicated, may hold values from -3 to 3
- cotangent: bfloat16 [4096, 1024], P('ctx'), may hold values from -6 to 6
Outputs:
- output: bfloat16 [4096, 1024], P('ctx')
- d_hidden: float32 [4096, 1024], P('ctx')
- d_ln1_gain: float32 [1024], replicated
- d_ln1_bias: float32 [1024], replicated
- d_ln2_gain: float32 [1024], replicated
- d_ln2_bias: float32 [1024], replicated
- d_w_qkv: float32 [3, 1024, 1024], P(None, None, 'tp')
- d_b_qkv: float32 [3, 1024], P(None, 'tp')
- d_w_out: float32 [1024, 1024], P('tp')
- d_b_out: float32 [1024], replicated
- d_w_up: float32 [1024, 4096], P(None, 'tp')
- d_b_up: float32 [4096], P('tp')
- d_w_down: float32 [4096, 1024], P('tp')
- d_b_down: float32 [1024], replicated
The draws below stay inside these ranges and needn't reach their ends.
Inputs may be any that keep to these rules, and one draw needn't show every extreme that they name: Index c of ctx holds the blocks pair_of[c] and 31 - pair_of[c] of 128 tokens each, in that order; every value appears once.
All inputs are finite; a program needn't handle non-finite values.
Results may differ from the reference program's by a relative error of at most 0.012.
The reference program's roundings to bfloat16 on the way count: a program that leaves them out, or rounds other values in their place, can miss the bound.
Values may be sent and summed in bfloat16 or wider, within the bound.
No kernel may reach another device: no remote copies, remote signals or barrier semaphores. Data moves between devices by JAX's collectives and lax.ppermute only.
A program may use at most 384 MiB of HBM per device.

```python
import jax
import jax.numpy as jnp
from jax import lax

D = 1024
HEADS = 16
HEAD_DIM = 64
FF = 4096
ROT = 16
BLK = 128
PAIRS = 16
SEQ_LEN = 4096


def block_scale(rng, extent, split, low, top_value):
    factor_of = 1.0
    for position, shards_of in split:
        draws = jax.random.uniform(jax.random.fold_in(jax.random.fold_in(rng, 6), position), (shards_of,), jnp.float32, low / len(split), top_value / len(split))
        factor_of = factor_of * jnp.repeat(jnp.exp(draws), extent[position] // shards_of).reshape((-1,) + (1,) * (len(extent) - 1 - position))
    return factor_of


def normal_values(key, shape, scale, bound, split=(), kind=jnp.bfloat16):
    gain = block_scale(key, shape, split, -0.22, 0.18) if split else 1.0
    array = jax.random.normal(key, shape, jnp.float32) * scale * gain
    return jnp.minimum(jnp.maximum(array, -bound), bound).astype(kind)


def setup_inputs(seed: int = 0) -> dict:
    key_of = jax.random.split(jax.random.key(seed), 16)
    hidden = normal_values(key_of[0], (SEQ_LEN, D), 1.0, 6.0, ((0, 16),))
    pair_of = jax.random.permutation(key_of[1], PAIRS).astype(jnp.int32)
    ln1_gain = jnp.clip(1.0 + 0.18 * jax.random.normal(key_of[2], (D,), jnp.float32), 0.099609375, 1.8984375).astype(jnp.bfloat16)
    ln1_bias = normal_values(key_of[3], (D,), 0.3, 3.0)
    ln2_gain = jnp.clip(1.0 + 0.18 * jax.random.normal(key_of[4], (D,), jnp.float32), 0.099609375, 1.8984375).astype(jnp.bfloat16)
    ln2_bias = normal_values(key_of[5], (D,), 0.3, 3.0)
    w_qkv = normal_values(key_of[6], (3, D, D), (D // 2) ** -0.5, 0.25, ((2, 2),))
    b_qkv = normal_values(key_of[7], (3, D), 0.05, 0.5, ((1, 2),))
    w_out = normal_values(key_of[8], (D, D), (max(D // 64, 4)) ** -0.5, 1.5, ((0, 2),))
    b_out = normal_values(key_of[9], (D,), 0.3, 3.0)
    w_up = normal_values(key_of[10], (D, FF), D ** -0.5, 0.1875, ((1, 2),))
    b_up = normal_values(key_of[11], (FF,), 0.5, 4.0, ((0, 2),))
    w_down = normal_values(key_of[12], (FF, D), FF ** -0.5, 0.09375, ((0, 2),))
    b_down = normal_values(key_of[13], (D,), 0.3, 3.0)
    cotangent = normal_values(key_of[14], (SEQ_LEN, D), 1.0, 6.0, ((0, 16),))
    return dict(hidden=hidden, pair_of=pair_of, ln1_gain=ln1_gain, ln1_bias=ln1_bias, ln2_gain=ln2_gain, ln2_bias=ln2_bias, w_qkv=w_qkv, b_qkv=b_qkv, w_out=w_out, b_out=b_out, w_up=w_up, b_up=b_up, w_down=w_down, b_down=b_down, cotangent=cotangent)


@jax.custom_vjp
def low(v):
    return lax.optimization_barrier(v.astype(jnp.bfloat16)).astype(jnp.float32)

@jax.custom_vjp
def low_back(v):
    return v

def low_keep(v):
    return (low(v), None)

def low_pass(kept, grad):
    return (grad,)

def back_keep(v):
    return (v, None)

def back_low(kept, grad):
    return (low(grad),)
low.defvjp(low_keep, low_pass)
low_back.defvjp(back_keep, back_low)
norm_eps = 1e-05
masked_score = -1e+30
highest = lax.Precision.HIGHEST

def layer_norm(values, gains, shifts):
    average = lax.optimization_barrier(jnp.mean(values, axis=-1, keepdims=True))
    centred = values - average
    spread = lax.optimization_barrier(jnp.mean(centred * centred, axis=-1, keepdims=True))
    return centred * lax.rsqrt(spread + norm_eps) * gains + shifts

def rotate(tensor, cos_table, sine_table):
    half_rot = ROT // 2
    moving = tensor[..., :ROT]
    turned = jnp.concatenate([-moving[..., half_rot:], moving[..., :half_rot]], axis=-1)
    rotated = moving * cos_table[:, None, :] + turned * sine_table[:, None, :]
    return jnp.concatenate([rotated, tensor[..., ROT:]], axis=-1)

def token_positions(pair_of):
    within = jnp.arange(2 * BLK, dtype=jnp.int32)[None, :]
    first_pos = pair_of[:, None] * BLK + within
    second = (2 * PAIRS - 1 - pair_of[:, None]) * BLK + within - BLK
    return jnp.where(within < BLK, first_pos, second).reshape(-1).astype(jnp.int32)

def rotary_tables(positions):
    exponent = jnp.arange(0, ROT, 2, dtype=jnp.float32) / ROT
    inverse = 10000.0 ** (-exponent)
    angles = positions.astype(jnp.float32)[:, None] * inverse[None, :]
    angles = jnp.concatenate([angles, angles], axis=-1)
    return (jnp.cos(angles), jnp.sin(angles))

def attend_block(queries, key_rows, value_rows, query_pos, key_pos):
    scores = low_back(jnp.dot(queries, key_rows.T, precision=highest) * HEAD_DIM ** (-0.5))
    visible = key_pos[None, :] <= query_pos[:, None]
    scores = jnp.where(visible, scores, masked_score)
    peaks = lax.optimization_barrier(jnp.max(scores, axis=-1, keepdims=True))
    weights = jnp.exp(scores - peaks)
    weights = weights / lax.optimization_barrier(jnp.sum(weights, axis=-1, keepdims=True))
    return jnp.dot(low(weights), value_rows, precision=highest)

def attention(queries, key_rows, value_rows, positions):
    query_block = min(2048, SEQ_LEN)
    block_count = SEQ_LEN // query_block
    heads_q = queries.transpose(1, 0, 2).reshape(HEADS, block_count, query_block, HEAD_DIM)
    heads_k = key_rows.transpose(1, 0, 2)
    heads_v = value_rows.transpose(1, 0, 2)
    pos_blocks = positions.reshape(block_count, query_block)
    kernel = jax.checkpoint(attend_block)

    def one_head(packed):
        head_q, head_k, head_v = packed
        return lax.map(lambda pair_args: kernel(pair_args[0], head_k, head_v, pair_args[1], positions), (head_q, pos_blocks))
    result = lax.map(one_head, (heads_q, heads_k, heads_v))
    return result.reshape(HEADS, SEQ_LEN, HEAD_DIM).transpose(1, 0, 2)

def forward(hidden, ln1_gain, ln1_bias, ln2_gain, ln2_bias, w_qkv, b_qkv, w_out, b_out, w_up, b_up, w_down, b_down, cos_table, sine_table, positions):
    normed_attn = low(layer_norm(hidden, ln1_gain, ln1_bias))
    normed_mlp = low(layer_norm(hidden, ln2_gain, ln2_bias))
    project = jnp.einsum('td,sde->ste', normed_attn, w_qkv, precision=highest) + b_qkv[:, None, :]
    project = low_back(project)
    shaped = project.reshape(3, SEQ_LEN, HEADS, HEAD_DIM)
    queries = low(rotate(shaped[0], cos_table, sine_table))
    key_rows = low(rotate(shaped[1], cos_table, sine_table))
    value_rows = low(shaped[2])
    attended = low_back(low(attention(queries, key_rows, value_rows, positions))).reshape(SEQ_LEN, D)
    pre_act = low_back(jnp.dot(normed_mlp, w_up, precision=highest) + b_up)
    active = low(jax.nn.gelu(pre_act, approximate=False))
    branch_attn = jnp.dot(attended, w_out, precision=highest)
    branch_mlp = jnp.dot(active, w_down, precision=highest)
    return hidden + branch_attn + b_out + branch_mlp + b_down

def reference(hidden, pair_of, ln1_gain, ln1_bias, ln2_gain, ln2_bias, w_qkv, b_qkv, w_out, b_out, w_up, b_up, w_down, b_down, cotangent):
    positions = token_positions(pair_of)
    cos_table, sine_table = rotary_tables(positions)
    floats = tuple((tensor.astype(jnp.float32) for tensor in (hidden, ln1_gain, ln1_bias, ln2_gain, ln2_bias, w_qkv, b_qkv, w_out, b_out, w_up, b_up, w_down, b_down)))

    def layer_fn(*params):
        return forward(*params, cos_table, sine_table, positions)
    output, pullback = jax.vjp(layer_fn, *floats)
    gradients = pullback(cotangent.astype(jnp.float32))
    d_hidden, d_ln1_gain, d_ln1_bias, d_ln2_gain, d_ln2_bias, d_w_qkv, d_b_qkv, d_w_out, d_b_out, d_w_up, d_b_up, d_w_down, d_b_down = gradients
    return (output.astype(jnp.bfloat16), d_hidden, d_ln1_gain, d_ln1_bias, d_ln2_gain, d_ln2_bias, d_w_qkv, d_b_qkv, d_w_out, d_b_out, d_w_up, d_b_up, d_w_down, d_b_down)
```

```python
import functools

import jax
import jax.numpy as jnp
import numpy as np
from jax import lax
from jax.experimental import pallas as pl
from jax.experimental.pallas import tpu as pltpu
from jax.sharding import PartitionSpec as P

HEAD_DIM = 64
ROT = 16
HALF = ROT // 2
BLOCK = 128
LANES = 128
KEYS = 512
SUB = 128
MIB = 1 << 20

norm_eps = 1e-05
masked_score = -1e30
score_scale = HEAD_DIM ** (-0.5)
low = jnp.bfloat16
full = jnp.float32


def mm(left, right):
    return lax.dot_general(left, right, (((1,), (0,)), ((), ())), preferred_element_type=full)


def mm_nt(left, right):
    return lax.dot_general(left, right, (((1,), (1,)), ((), ())), preferred_element_type=full)


def turn(tensor):
    return tensor.astype(full).T.astype(low)


def lane_ids(shape):
    return lax.broadcasted_iota(jnp.int32, shape, len(shape) - 1)


def row_ids(shape):
    return lax.broadcasted_iota(jnp.int32, shape, len(shape) - 2)


def rotary_partner(tensor):
    lanes = lane_ids(tensor.shape)
    ahead = pltpu.roll(tensor, LANES - HALF, 1)
    behind = pltpu.roll(tensor, HALF, 1)
    return jnp.where(lanes % ROT < HALF, ahead, behind)


def spec_vmem():
    return pl.BlockSpec(memory_space=pltpu.VMEM)


def spec_smem():
    return pl.BlockSpec(memory_space=pltpu.SMEM)


def params(mib):
    return pltpu.CompilerParams(vmem_limit_bytes=mib * MIB)


def shape_of(shape, kind):
    return jax.ShapeDtypeStruct(shape, kind)


def project_kernel(
    heads, group, pair_ref, hidden_ref, cot_ref, norm_ref, inv_ref, w_qkv_ref, b_qkv_ref, w_out_ref, *rest
):
    h1_ref, h2_ref, xhat_ref, std_ref, d_bias_ref = rest[:5]
    send_refs = rest[5 : 5 + heads]
    packed = rest[5 + heads]
    rows = hidden_ref.shape[0]
    me = lax.axis_index("ctx")
    pair = pair_ref[me]
    total_blocks = 2 * pair_ref.shape[0]

    x = hidden_ref[...].astype(full)
    centred = x - jnp.mean(x, axis=-1, keepdims=True)
    spread = jnp.mean(centred * centred, axis=-1, keepdims=True)
    inv_std = lax.rsqrt(spread + norm_eps)
    xhat = centred * inv_std
    xhat_ref[...] = xhat
    std_ref[...] = jnp.broadcast_to(inv_std, std_ref.shape)
    gains = norm_ref[...].astype(full)
    h1 = (xhat * gains[0:1] + gains[1:2]).astype(low)
    h1_ref[...] = h1
    h2_ref[...] = (xhat * gains[2:3] + gains[3:4]).astype(low)
    d_bias_ref[...] = jnp.sum(cot_ref[...].astype(full), axis=0, keepdims=True)

    row = row_ids((rows, LANES))
    lane = lane_ids((rows, LANES))
    start = jnp.where(row < BLOCK, pair * BLOCK, (total_blocks - 2 - pair) * BLOCK)
    angle = (start + row).astype(full) * inv_ref[...]
    in_head = lane % HEAD_DIM
    cosine = jnp.where(in_head < ROT, jnp.cos(angle), 1.0)
    sine = jnp.sin(angle)
    sine = jnp.where(in_head < HALF, -sine, jnp.where(in_head < ROT, sine, 0.0))

    def projected(s):
        return mm(h1, w_qkv_ref[s]) + b_qkv_ref[s : s + 1].astype(full)

    def turned(tile):
        return tile * cosine + rotary_partner(tile) * sine

    queries, keys, values = projected(0), projected(1), projected(2)
    grads = mm_nt(cot_ref[...], w_out_ref[...])
    left = lane < HEAD_DIM
    for i in range(heads // 2):
        cut = slice(i * LANES, (i + 1) * LANES)
        q = turned(queries[:, cut]).astype(low).astype(full) * score_scale
        k = turned(keys[:, cut])
        v = values[:, cut]
        g = grads[:, cut]
        packed[2 * i, :, :LANES] = jnp.where(left, g, pltpu.roll(q, HEAD_DIM, 1)).astype(low)
        packed[2 * i, :, LANES:] = jnp.where(left, v, pltpu.roll(k, HEAD_DIM, 1)).astype(low)
        packed[2 * i + 1, :, :LANES] = jnp.where(left, pltpu.roll(g, HEAD_DIM, 1), q).astype(low)
        packed[2 * i + 1, :, LANES:] = jnp.where(left, pltpu.roll(v, HEAD_DIM, 1), k).astype(low)
    own = me // group
    for r in range(heads):
        send_refs[r][...] = packed[lax.rem(own + r, heads)]


def project(heads, group, pair_of, hidden, cot, norms, inverse, w_qkv, b_qkv, w_out):
    rows, width = hidden.shape
    outs = [
        shape_of((rows, width), low),
        shape_of((rows, width), low),
        shape_of((rows, width), full),
        shape_of((rows, LANES), full),
        shape_of((1, width), full),
    ] + [shape_of((rows, 2 * LANES), low)] * heads
    return pl.pallas_call(
        functools.partial(project_kernel, heads, group),
        out_shape=outs,
        in_specs=[spec_smem()] + [spec_vmem()] * 7,
        out_specs=[spec_vmem()] * len(outs),
        scratch_shapes=[pltpu.VMEM((heads, rows, 2 * LANES), low)],
        compiler_params=params(40),
        cost_estimate=pl.CostEstimate(
            flops=2 * rows * width * 4 * w_out.shape[0], bytes_accessed=8 * MIB, transcendentals=0
        ),
        name="project",
    )(pair_of, hidden, cot, norms, inverse, w_qkv, b_qkv, w_out)


def mlp_kernel(
    h2_ref, cot_ref, xhat_ref, w_up_ref, b_up_ref, w_down_ref, part_ref, back_ref, sums_ref, d_b_up_ref, grad_ref, h2_turned, part_acc, back_acc
):
    step = pl.program_id(0)

    @pl.when(step == 0)
    def _():
        h2_turned[...] = turn(h2_ref[...])
        part_acc[...] = jnp.zeros_like(part_acc)
        back_acc[...] = jnp.zeros_like(back_acc)

    cot = cot_ref[...]
    w_up = w_up_ref[...]
    w_down = w_down_ref[...]
    u = mm(h2_ref[...], w_up) + b_up_ref[...].astype(full)
    cdf = 0.5 * (1.0 + lax.erf(u * np.float32(np.sqrt(0.5))))
    active = u * cdf
    active_low = active.astype(low)
    slope = cdf + u * jnp.exp(-0.5 * u * u) * np.float32(1.0 / np.sqrt(2.0 * np.pi))
    du = (mm_nt(cot, w_down) * slope).astype(low)
    part_acc[...] += mm(active_low, w_down)
    back_acc[...] += mm_nt(du, w_up)
    d_b_up_ref[...] = jnp.sum(du.astype(full), axis=0, keepdims=True)
    up = mm(h2_turned[...], du).astype(low)
    down = mm(active.T.astype(low), cot).astype(low)
    depth = up.shape[0]
    for b in range(grad_ref.shape[0]):
        grad_ref[b, :depth] = up[:, b * LANES : (b + 1) * LANES]
        for t in range(down.shape[1] // LANES):
            grad_ref[b, depth + t * LANES : depth + (t + 1) * LANES] = down[
                b * LANES : (b + 1) * LANES, t * LANES : (t + 1) * LANES
            ]

    @pl.when(step == pl.num_programs(0) - 1)
    def _():
        part_ref[...] = part_acc[...]
        back = back_acc[...]
        back_ref[...] = back.astype(low)
        sums_ref[0:1] = jnp.sum(back * xhat_ref[...], axis=0, keepdims=True)
        sums_ref[1:2] = jnp.sum(back, axis=0, keepdims=True)


def mlp(h2, cot, xhat, w_up, b_up, w_down):
    rows, width = h2.shape
    hidden_units = w_up.shape[1]
    tile = 2 * LANES
    steps = hidden_units // tile
    whole = lambda shape: pl.BlockSpec(shape, lambda f: (0,) * len(shape))
    outs = [
        shape_of((rows, width), full),
        shape_of((rows, width), low),
        shape_of((2, width), full),
        shape_of((1, hidden_units), full),
        shape_of((hidden_units // LANES, 2 * width, LANES), low),
    ]
    return pl.pallas_call(
        mlp_kernel,
        grid=(steps,),
        out_shape=outs,
        in_specs=[
            whole((rows, width)),
            whole((rows, width)),
            whole((rows, width)),
            pl.BlockSpec((width, tile), lambda f: (0, f)),
            pl.BlockSpec((1, tile), lambda f: (0, f)),
            pl.BlockSpec((tile, width), lambda f: (f, 0)),
        ],
        out_specs=[
            whole((rows, width)),
            whole((rows, width)),
            whole((2, width)),
            pl.BlockSpec((1, tile), lambda f: (0, f)),
            pl.BlockSpec((2, 2 * width, LANES), lambda f: (f, 0, 0)),
        ],
        scratch_shapes=[
            pltpu.VMEM((width, rows), low),
            pltpu.VMEM((rows, width), full),
            pltpu.VMEM((rows, width), full),
        ],
        compiler_params=params(40),
        cost_estimate=pl.CostEstimate(
            flops=12 * rows * width * hidden_units, bytes_accessed=20 * MIB, transcendentals=0
        ),
        name="feed_forward",
    )(h2, cot, xhat, w_up, b_up, w_down)


def attention_kernel(heads, group, pair_ref, cos_ref, sin_ref, *rest):
    got_refs = rest[:heads]
    rest = rest[heads:]
    if group > 1:
        other_ref, rest = rest[0], rest[1:]
    out_refs = rest[:heads]
    rest = rest[heads:]
    d_own_ref, rest = rest[0], rest[1:]
    if group > 1:
        d_other_ref, rest = rest[0], rest[1:]
    queries, values_keys, turned_keys, weights_in, weights_out, stored, sums, finals, results = rest

    rows = got_refs[0].shape[0]
    owners = pair_ref.shape[0]
    total_blocks = 2 * owners
    per_chunk = KEYS // BLOCK
    tasks = (total_blocks + 1 + per_chunk - 1) // per_chunk
    me = lax.axis_index("ctx")
    own_head = me // group
    own_sub = lax.rem(me, group)

    def blocks_of(r, d):
        owner = lax.rem(own_head - r + heads, heads) * group + lax.rem(own_sub + d, group)
        pair = pair_ref[owner]
        return pair, total_blocks - 1 - pair

    def place(tile, block):
        at = pl.multiple_of(block * BLOCK, BLOCK)
        values_keys[pl.ds(at, BLOCK), :] = tile
        turned_keys[:, pl.ds(at, BLOCK)] = turn(tile)

    for r in range(heads):
        queries[r] = got_refs[r][:, :LANES]
        for half, block in enumerate(blocks_of(r, 0)):
            place(got_refs[r][half * BLOCK : (half + 1) * BLOCK, LANES:], block)
        for d in range(1, group):
            for half, block in enumerate(blocks_of(r, d)):
                at = r * rows + half * BLOCK
                place(other_ref[d - 1, at : at + BLOCK, :], block)
    sums[...] = jnp.zeros_like(sums)

    lane = lane_ids((BLOCK, LANES))
    left = lane < HEAD_DIM
    offset = row_ids((SUB, BLOCK)) - lane_ids((SUB, BLOCK))

    def one_pair(r, carry):
        blocks = blocks_of(r, 0)
        first = blocks[0] // per_chunk + 1
        for half in range(2):
            both = queries[r, half * BLOCK : (half + 1) * BLOCK, :]
            both_turned = turn(both)
            upper = row_ids((LANES, BLOCK)) < HEAD_DIM
            zero = jnp.zeros_like(both_turned)
            weights_in[half, :, :BLOCK] = jnp.where(upper, both_turned, zero)
            weights_in[half, :, BLOCK:] = jnp.where(upper, zero, both_turned)
            weights_out[half, :BLOCK, :] = jnp.where(left, both, zero)
            weights_out[half, BLOCK:, :] = jnp.where(left, zero, both)
        finals[...] = jnp.zeros_like(finals)

        def task(t):
            is_first = t < first
            chunk = jnp.where(is_first, first - 1 - t, t - first)
            return is_first, chunk

        stats = []
        for t in range(tasks):
            is_first, chunk = task(t)
            half = jnp.where(is_first, 0, 1)
            weights = weights_in[half]
            for u in range(KEYS // SUB):
                at = pl.multiple_of(chunk * KEYS + u * SUB, SUB)
                both = mm(values_keys[pl.ds(at, SUB), :], weights)
                grads = both[:, :BLOCK]
                scores = both[:, BLOCK:]
                if t == 0:
                    scores = jnp.where(offset <= blocks[0] * BLOCK - at, scores, masked_score)
                if t == tasks - 1:
                    scores = jnp.where(offset <= blocks[1] * BLOCK - at, scores, masked_score)
                peak = jnp.max(scores, axis=0, keepdims=True)
                raised = jnp.exp(scores - peak)
                total = jnp.sum(raised, axis=0, keepdims=True)
                weighted = jnp.sum(raised * grads, axis=0, keepdims=True)
                stored[t, u * SUB : (u + 1) * SUB, :BLOCK] = raised
                stored[t, u * SUB : (u + 1) * SUB, BLOCK:] = grads
                stats.append((is_first, peak, total, weighted))

        def finish(wanted):
            top = jnp.full((1, BLOCK), masked_score, full)
            for is_first, peak, total, weighted in stats:
                top = jnp.maximum(top, jnp.where(is_first == wanted, peak, masked_score))
            all_total = jnp.zeros((1, BLOCK), full)
            all_weighted = jnp.zeros((1, BLOCK), full)
            for is_first, peak, total, weighted in stats:
                factor = jnp.where(is_first == wanted, jnp.exp(peak - top), 0.0)
                all_total = all_total + total * factor
                all_weighted = all_weighted + weighted * factor
            return top, 1.0 / all_total, all_weighted / all_total

        ends = (finish(True), finish(False))

        for t in range(tasks):
            is_first, chunk = task(t)
            half = jnp.where(is_first, 0, 1)
            weights = weights_out[half]
            top, inverse, delta = (jnp.where(is_first, a, b) for a, b in zip(*ends))
            parts = []
            for u in range(KEYS // SUB):
                peak = stats[t * (KEYS // SUB) + u][1]
                factor = jnp.exp(peak - top) * inverse
                probs = stored[t, u * SUB : (u + 1) * SUB, :BLOCK] * factor
                grads = stored[t, u * SUB : (u + 1) * SUB, BLOCK:]
                d_scores = probs * (grads - delta)
                both = jnp.concatenate([probs, d_scores], axis=1).astype(low)
                at = pl.multiple_of(chunk * KEYS + u * SUB, SUB)
                sums[pl.ds(at, SUB), :] += mm(both, weights)
                parts.append(both)
            at = pl.multiple_of(chunk * KEYS, KEYS)
            finals[half] += mm(turned_keys[:, pl.ds(at, KEYS)], jnp.concatenate(parts, axis=0))

        for half in range(2):
            both = jnp.concatenate(
                [finals[half, :HEAD_DIM, :BLOCK], finals[half, HEAD_DIM:, BLOCK:] * score_scale], axis=0
            ).T
            at = pl.multiple_of(r * rows + half * BLOCK, BLOCK)
            both = both * cos_ref[pl.ds(at, BLOCK), :] + rotary_partner(both) * sin_ref[pl.ds(at, BLOCK), :]
            results[r, half * BLOCK : (half + 1) * BLOCK, :] = both.astype(low)
        return carry

    lax.fori_loop(0, heads, one_pair, 0)

    for r in range(heads):
        out_refs[r][...] = results[r]
        for d in range(group):
            for half, block in enumerate(blocks_of(r, d)):
                at = r * rows + half * BLOCK
                tile = sums[pl.ds(pl.multiple_of(block * BLOCK, BLOCK), BLOCK), :]
                if d == 0:
                    d_own_ref[at : at + BLOCK, :] = tile
                else:
                    d_other_ref[d - 1, at : at + BLOCK, :] = tile


def attention(heads, group, pair_of, cosine, sine, got, other):
    rows = got[0].shape[0]
    owners = pair_of.shape[0]
    total_keys = owners * rows
    tasks = (2 * owners + KEYS // BLOCK) // (KEYS // BLOCK)
    outs = [shape_of((rows, LANES), low)] * heads + [shape_of((heads * rows, LANES), full)]
    operands = [pair_of, cosine, sine, *got]
    if group > 1:
        outs.append(shape_of((group - 1, heads * rows, LANES), full))
        operands.append(other)
    found = pl.pallas_call(
        functools.partial(attention_kernel, heads, group),
        out_shape=outs,
        in_specs=[spec_smem()] + [spec_vmem()] * (len(operands) - 1),
        out_specs=[spec_vmem()] * len(outs),
        scratch_shapes=[
            pltpu.VMEM((heads, rows, LANES), low),
            pltpu.VMEM((total_keys, LANES), low),
            pltpu.VMEM((LANES, total_keys), low),
            pltpu.VMEM((2, LANES, 2 * BLOCK), low),
            pltpu.VMEM((2, 2 * BLOCK, LANES), low),
            pltpu.VMEM((tasks, KEYS, 2 * BLOCK), full),
            pltpu.VMEM((total_keys, LANES), full),
            pltpu.VMEM((2, LANES, 2 * BLOCK), full),
            pltpu.VMEM((heads, rows, LANES), low),
        ],
        compiler_params=params(56),
        cost_estimate=pl.CostEstimate(
            flops=20_000_000_000, bytes_accessed=8 * MIB, transcendentals=0
        ),
        name="attention",
    )(*operands)
    return found[:heads], found[heads], (found[heads + 1] if group > 1 else None)


def combine_kernel(heads, terms, cos_ref, sin_ref, *refs):
    rows = cos_ref.shape[0] // heads
    for r in range(heads):
        cut = slice(r * rows, (r + 1) * rows)
        total = refs[0][cut, :]
        for term in refs[1:terms]:
            total = total + term[cut, :]
        total = total * cos_ref[cut, :] + rotary_partner(total) * sin_ref[cut, :]
        refs[terms + r][...] = total.astype(low)


def combine(heads, cosine, sine, terms):
    rows = cosine.shape[0] // heads
    return pl.pallas_call(
        functools.partial(combine_kernel, heads, len(terms)),
        out_shape=[shape_of((rows, LANES), low)] * heads,
        in_specs=[spec_vmem()] * (2 + len(terms)),
        out_specs=[spec_vmem()] * heads,
        compiler_params=params(40),
        cost_estimate=pl.CostEstimate(flops=10**7, bytes_accessed=5 * MIB, transcendentals=0),
        name="combine",
    )(cosine, sine, *terms)


def return_kernel(heads, group, h1_ref, xhat_ref, cot_ref, part_ref, w_qkv_ref, w_out_ref, *rest):
    first_refs, second_refs = rest[:heads], rest[heads : 2 * heads]
    part_low_ref, back_ref, sums_ref, d_b_ref, grad_ref, first, second, attended, d_proj = rest[2 * heads :]
    own = lax.axis_index("ctx") // group
    for r in range(heads):
        head = lax.rem(own + r, heads)
        first[head] = first_refs[r][...]
        second[head] = second_refs[r][...]
    rows = h1_ref.shape[0]
    left = lane_ids((rows, LANES)) < HEAD_DIM
    for i in range(heads // 2):
        cut = slice(i * LANES, (i + 1) * LANES)
        a, b = first[2 * i].astype(full), first[2 * i + 1].astype(full)
        attended[:, cut] = jnp.where(left, a, pltpu.roll(b, HEAD_DIM, 1)).astype(low)
        d_proj[0, :, cut] = jnp.where(left, pltpu.roll(a, HEAD_DIM, 1), b).astype(low)
        a, b = second[2 * i].astype(full), second[2 * i + 1].astype(full)
        d_proj[2, :, cut] = jnp.where(left, a, pltpu.roll(b, HEAD_DIM, 1)).astype(low)
        d_proj[1, :, cut] = jnp.where(left, pltpu.roll(a, HEAD_DIM, 1), b).astype(low)
    part_low_ref[...] = (part_ref[...] + mm(attended[...], w_out_ref[...])).astype(low)
    back = mm_nt(d_proj[0], w_qkv_ref[0]) + mm_nt(d_proj[1], w_qkv_ref[1]) + mm_nt(d_proj[2], w_qkv_ref[2])
    back_ref[...] = back.astype(low)
    sums_ref[0:1] = jnp.sum(back * xhat_ref[...], axis=0, keepdims=True)
    sums_ref[1:2] = jnp.sum(back, axis=0, keepdims=True)
    h1_turned = turn(h1_ref[...])
    depth, tiles = h1_turned.shape[0], heads // 2
    for s in range(3):
        d_b_ref[s : s + 1] = jnp.sum(d_proj[s].astype(full), axis=0, keepdims=True)
        grad = mm(h1_turned, d_proj[s]).astype(low)
        for t in range(tiles):
            at = (s * tiles + t) * depth
            grad_ref[at : at + depth] = grad[:, t * LANES : (t + 1) * LANES]
    grad = mm(turn(attended[...]), cot_ref[...]).astype(low)
    height = grad.shape[0]
    for t in range(depth // LANES):
        at = 3 * tiles * depth + t * height
        grad_ref[at : at + height] = grad[:, t * LANES : (t + 1) * LANES]


def back_projections(heads, group, h1, xhat, cot, part, w_qkv, w_out, first, second):
    rows, width = h1.shape
    local_width = w_out.shape[0]
    outs = [
        shape_of((rows, width), low),
        shape_of((rows, width), low),
        shape_of((2, width), full),
        shape_of((3, local_width), full),
        shape_of((4 * width * local_width // LANES, LANES), low),
    ]
    return pl.pallas_call(
        functools.partial(return_kernel, heads, group),
        out_shape=outs,
        in_specs=[spec_vmem()] * (6 + 2 * heads),
        out_specs=[spec_vmem()] * len(outs),
        scratch_shapes=[
            pltpu.VMEM((heads, rows, LANES), low),
            pltpu.VMEM((heads, rows, LANES), low),
            pltpu.VMEM((rows, local_width), low),
            pltpu.VMEM((3, rows, local_width), low),
        ],
        compiler_params=params(56),
        cost_estimate=pl.CostEstimate(
            flops=16 * rows * width * local_width, bytes_accessed=14 * MIB, transcendentals=0
        ),
        name="back_projections",
    )(h1, xhat, cot, part, w_qkv, w_out, *first, *second)


def finish_kernel(hidden_ref, cot_ref, xhat_ref, std_ref, norm_ref, bias_ref, part_refs, back_refs, next_refs, out_ref, grad_ref):
    gains = norm_ref[...].astype(full)
    biases = bias_ref[...].astype(full)
    summed = part_refs[0][...].astype(full) + part_refs[1][...].astype(full)
    out_ref[...] = (hidden_ref[...].astype(full) + summed + biases[0:1] + biases[1:2]).astype(low)
    e1 = back_refs[0][...].astype(full) + back_refs[1][...].astype(full)
    e2 = next_refs[0][...].astype(full) + next_refs[1][...].astype(full)
    f = e1 * gains[0:1] + e2 * gains[2:3]
    xhat = xhat_ref[...]
    inv_std = std_ref[:, 0:1]
    grad_ref[...] = cot_ref[...].astype(full) + inv_std * (
        f - jnp.mean(f, axis=-1, keepdims=True) - xhat * jnp.mean(f * xhat, axis=-1, keepdims=True)
    )


def finish(hidden, cot, xhat, inv_std, norms, biases, parts, backs, nexts):
    rows, width = hidden.shape

    def body(*refs):
        finish_kernel(*refs[:6], refs[6:8], refs[8:10], refs[10:12], *refs[12:])

    return pl.pallas_call(
        body,
        out_shape=[shape_of((rows, width), low), shape_of((rows, width), full)],
        in_specs=[spec_vmem()] * 12,
        out_specs=[spec_vmem()] * 2,
        compiler_params=params(40),
        cost_estimate=pl.CostEstimate(flops=10**7, bytes_accessed=8 * MIB, transcendentals=0),
        name="finish",
    )(hidden, cot, xhat, inv_std, norms, biases, *parts, *backs, *nexts)


def unpack_mlp(packed, width, hidden_units):
    blocks = hidden_units // LANES

    def body(in_ref, up_ref, down_ref):
        up_ref[...] = in_ref[:width].astype(full)
        for t in range(width // LANES):
            at = width + t * LANES
            down_ref[:, t * LANES : (t + 1) * LANES] = in_ref[at : at + LANES].astype(full)

    return pl.pallas_call(
        body,
        grid=(blocks,),
        out_shape=[shape_of((width, hidden_units), full), shape_of((hidden_units, width), full)],
        in_specs=[pl.BlockSpec((2 * width, LANES), lambda f: (f, 0))],
        out_specs=[pl.BlockSpec((width, LANES), lambda f: (0, f)), pl.BlockSpec((LANES, width), lambda f: (f, 0))],
        compiler_params=params(40),
        name="unpack_feed_forward",
    )(packed)


def unpack_attention(packed, width, local_width):
    tiles = local_width // LANES
    first = 3 * tiles
    per_step = width // local_width
    last = width // LANES // per_step

    def body(in_ref, qkv_ref, out_ref):
        step = pl.program_id(0)

        @pl.when(step < first)
        def _():
            qkv_ref[0] = in_ref[...].astype(full)

        @pl.when(step >= first)
        def _():
            for t in range(per_step):
                out_ref[:, t * LANES : (t + 1) * LANES] = in_ref[t * local_width : (t + 1) * local_width].astype(full)

    def qkv_at(f):
        g = jnp.minimum(f, first - 1)
        return (g // tiles, 0, g % tiles)

    return pl.pallas_call(
        body,
        grid=(first + last,),
        out_shape=[shape_of((3, width, local_width), full), shape_of((local_width, width), full)],
        in_specs=[pl.BlockSpec((width, LANES), lambda f: (f, 0))],
        out_specs=[
            pl.BlockSpec((1, width, LANES), qkv_at),
            pl.BlockSpec((local_width, per_step * LANES), lambda f: (0, jnp.maximum(f - first, 0))),
        ],
        compiler_params=params(40),
        name="unpack_attention",
    )(packed)


def rotary_rows(pair_of, heads, group, rows):
    owners = pair_of.shape[0]
    me = lax.axis_index("ctx")
    sources = lax.rem(me // group - jnp.arange(heads) + heads, heads) * group + lax.rem(me, group)
    pairs = jnp.sum(jnp.where(sources[:, None] == jnp.arange(owners)[None, :], pair_of[None, :], 0), axis=1)
    row = lax.broadcasted_iota(jnp.int32, (heads, rows, LANES), 1)
    lane = lax.broadcasted_iota(jnp.int32, (heads, rows, LANES), 2) - HEAD_DIM
    start = jnp.where(row < BLOCK, pairs[:, None, None], 2 * owners - 2 - pairs[:, None, None]) * BLOCK
    return start + row, lane


def local(
    hidden,
    pair_of,
    ln1_gain,
    ln1_bias,
    ln2_gain,
    ln2_bias,
    w_qkv,
    b_qkv,
    w_out,
    b_out,
    w_up,
    b_up,
    w_down,
    b_down,
    cotangent,
):
    owners = lax.axis_size("ctx")
    sides = lax.axis_size("tp")
    rows, width = hidden.shape
    local_width = w_qkv.shape[2]
    hidden_units = w_up.shape[1]
    heads = local_width // HEAD_DIM
    group = owners // heads

    exponent = np.arange(0, ROT, 2, dtype=np.float32) / np.float32(ROT)
    inverse = jnp.asarray(np.tile(np.float32(10000.0) ** (-exponent), LANES // HALF)[None, :], full)
    norms = jnp.stack([ln1_gain, ln1_bias, ln2_gain, ln2_bias])
    biases = jnp.stack([b_out, b_down])

    h1, h2, xhat, inv_std, d_bias, *sends = project(
        heads, group, pair_of, hidden, cotangent, norms, inverse, w_qkv, b_qkv, w_out
    )

    def head_shift(array, r, back=False):
        step = -r if back else r
        pairs = [(c, ((c // group + step) % heads) * group + c % group) for c in range(owners)]
        return lax.ppermute(array, "ctx", pairs)

    def group_shift(array, d):
        pairs = [(c, c // group * group + (c % group + d) % group) for c in range(owners)]
        return lax.ppermute(array, "ctx", pairs)

    got = [sends[0]] + [head_shift(sends[r], r) for r in range(1, heads)]

    part, back2, sums2, d_b_up, grad_mlp = mlp(h2, cotangent, xhat, w_up, b_up[None, :], w_down)
    grad_mlp = grad_mlp.reshape(-1, LANES)

    def reduced(grad):
        own = lax.psum_scatter(grad, "ctx", scatter_dimension=0, tiled=True)
        return lax.all_gather(own, "ctx", axis=0, tiled=True)

    total_mlp = reduced(grad_mlp)

    position, lane = rotary_rows(pair_of, heads, group, rows)
    angle = position.astype(full) * inverse[0][None, None, :]
    turning = (lane >= 0) & (lane < ROT)
    cosine = jnp.where(turning, jnp.cos(angle), 1.0).reshape(heads * rows, LANES)
    sine = jnp.sin(angle)
    sine = jnp.where(turning, jnp.where(lane < HALF, sine, -sine), 0.0).reshape(heads * rows, LANES)

    other = None
    if group > 1:
        mine = jnp.concatenate([array[:, LANES:] for array in got], axis=0)
        other = jnp.stack([group_shift(mine, group - d) for d in range(1, group)])

    firsts, d_own, d_other = attention(heads, group, pair_of, cosine, sine, got, other)
    firsts = [firsts[0]] + [head_shift(firsts[r], r, True) for r in range(1, heads)]
    terms = [d_own] + [group_shift(d_other[d - 1], d) for d in range(1, group)]
    seconds = combine(heads, cosine, sine, terms)
    seconds = [seconds[0]] + [head_shift(seconds[r], r, True) for r in range(1, heads)]

    part_low, back1, sums1, d_b_qkv, grad_att = back_projections(
        heads, group, h1, xhat, cotangent, part, w_qkv, w_out, firsts, seconds
    )
    total_att = reduced(grad_att)

    def across(array):
        return lax.ppermute(array, "tp", [(t, (t + 1) % sides) for t in range(sides)])

    output, d_hidden = finish(
        hidden,
        cotangent,
        xhat,
        inv_std,
        norms,
        biases,
        (part_low, across(part_low)),
        (back1, across(back1)),
        (back2, across(back2)),
    )

    small = jnp.concatenate(
        [sums1.reshape(1, -1), sums2.reshape(1, -1), d_bias, d_b_up, d_b_qkv.reshape(1, -1)], axis=1
    )
    step = 1
    while step < owners:
        small = small + lax.ppermute(small, "ctx", [(c, c ^ step) for c in range(owners)])
        step *= 2
    norm_sums = small[:, : 4 * width]
    norm_sums = (norm_sums + across(norm_sums)).reshape(4, width)
    at = 4 * width
    d_bias = small[0, at : at + width]
    d_b_up = small[0, at + width : at + width + hidden_units]
    d_b_qkv = small[0, at + width + hidden_units :].reshape(3, local_width)

    d_w_up, d_w_down = unpack_mlp(total_mlp, width, hidden_units)
    d_w_qkv, d_w_out = unpack_attention(total_att, width, local_width)
    return (
        output,
        d_hidden,
        norm_sums[0],
        norm_sums[1],
        norm_sums[2],
        norm_sums[3],
        d_w_qkv,
        d_b_qkv,
        d_w_out,
        d_bias,
        d_w_up,
        d_b_up,
        d_w_down,
        d_bias,
    )


def solution(mesh):
    placed = (
        P("ctx", None),
        P(),
        P(),
        P(),
        P(),
        P(),
        P(None, None, "tp"),
        P(None, "tp"),
        P("tp", None),
        P(),
        P(None, "tp"),
        P("tp"),
        P("tp", None),
        P(),
        P("ctx", None),
    )
    return jax.shard_map(
        local,
        mesh=mesh,
        in_specs=placed,
        out_specs=(
            P("ctx", None),
            P("ctx", None),
            P(),
            P(),
            P(),
            P(),
            P(None, None, "tp"),
            P(None, "tp"),
            P("tp", None),
            P(),
            P(None, "tp"),
            P("tp"),
            P("tp", None),
            P(),
        ),
        check_vma=False,
    )
```

```python
import functools

import jax
import jax.numpy as jnp
import numpy as np
from jax import lax
from jax.experimental import pallas as pl
from jax.experimental.pallas import tpu as pltpu
from jax.sharding import PartitionSpec as P

HEAD_DIM = 64
ROT = 16
HALF = ROT // 2
BLOCK = 128
LANES = 128
KEYS = 512
SUB = 128
MIB = 1 << 20

norm_eps = 1e-05
masked_score = -1e30
score_scale = HEAD_DIM ** (-0.5)
low = jnp.bfloat16
full = jnp.float32


def mm(left, right):
    return lax.dot_general(left, right, (((1,), (0,)), ((), ())), preferred_element_type=full)


def mm_nt(left, right):
    return lax.dot_general(left, right, (((1,), (1,)), ((), ())), preferred_element_type=full)


def turn(tensor):
    return tensor.astype(full).T.astype(low)


def lane_ids(shape):
    return lax.broadcasted_iota(jnp.int32, shape, len(shape) - 1)


def row_ids(shape):
    return lax.broadcasted_iota(jnp.int32, shape, len(shape) - 2)


def rotary_partner(tensor):
    lanes = lane_ids(tensor.shape)
    ahead = pltpu.roll(tensor, LANES - HALF, 1)
    behind = pltpu.roll(tensor, HALF, 1)
    return jnp.where(lanes % ROT < HALF, ahead, behind)


def spec_vmem():
    return pl.BlockSpec(memory_space=pltpu.VMEM)


def spec_smem():
    return pl.BlockSpec(memory_space=pltpu.SMEM)


def params(mib):
    return pltpu.CompilerParams(vmem_limit_bytes=mib * MIB)


def shape_of(shape, kind):
    return jax.ShapeDtypeStruct(shape, kind)


def block_tables(inverse, blocks):
    row = row_ids((BLOCK, LANES)).astype(full)
    start = blocks.astype(full) * float(BLOCK)
    return jnp.cos(row * inverse), jnp.sin(row * inverse), jnp.cos(start * inverse), jnp.sin(start * inverse)


def project_kernel(heads, group, pair_ref, inv_ref, *rest):
    given, rest = rest[:12], rest[12:]
    h1_ref, h2_ref, xhat_ref, std_ref, d_bias_ref, gains_ref, bias_ref, b_up_out_ref = rest[:8]
    send_refs = rest[8 : 8 + heads]
    packed, held, sems = rest[8 + heads], rest[9 + heads : -1], rest[-1]
    copies = [pltpu.make_async_copy(src, dst, sems.at[i]) for i, (src, dst) in enumerate(zip(given, held))]
    for copy in copies:
        copy.start()
    (
        hidden_ref,
        g1_ref,
        c1_ref,
        g2_ref,
        c2_ref,
        cot_ref,
        w_out_ref,
        w_qkv_ref,
        b_qkv_ref,
        b_up_ref,
        b_out_ref,
        b_down_ref,
    ) = held
    rows = hidden_ref.shape[0]
    me = lax.axis_index("ctx")
    pair = pair_ref[me]
    total_blocks = 2 * pair_ref.shape[0]

    first = jnp.where(row_ids((8, LANES)) == 0, pair, total_blocks - 1 - pair)
    inverse = inv_ref[...]
    cos_row, sin_row, cos_block, sin_block = block_tables(inverse, first)
    in_head = lane_ids((BLOCK, LANES)) % HEAD_DIM
    tables = []
    for half in range(2):
        cos_at, sin_at = cos_block[half : half + 1], sin_block[half : half + 1]
        cosine = cos_row * cos_at - sin_row * sin_at
        sine = sin_row * cos_at + cos_row * sin_at
        cosine = jnp.where(in_head < ROT, cosine, 1.0)
        sine = jnp.where(in_head < HALF, -sine, jnp.where(in_head < ROT, sine, 0.0))
        tables.append((cosine, sine))
    cosine = jnp.concatenate([tables[0][0], tables[1][0]], axis=0)
    sine = jnp.concatenate([tables[0][1], tables[1][1]], axis=0)

    for copy in copies[:5]:
        copy.wait()
    x = hidden_ref[...].astype(full)
    centred = x - jnp.mean(x, axis=-1, keepdims=True)
    spread = jnp.mean(centred * centred, axis=-1, keepdims=True)
    inv_std = lax.rsqrt(spread + norm_eps)
    xhat = centred * inv_std
    xhat_ref[...] = xhat
    std_ref[...] = jnp.broadcast_to(inv_std, std_ref.shape)

    def as_row(ref):
        return ref[...].astype(full)[None, :]

    gain1, gain2 = as_row(g1_ref), as_row(g2_ref)
    h1 = (xhat * gain1 + as_row(c1_ref)).astype(low)
    h1_ref[...] = h1
    h2_ref[...] = (xhat * gain2 + as_row(c2_ref)).astype(low)
    gains_ref[0:1] = gain1
    gains_ref[1:2] = gain2
    for copy in copies[5:]:
        copy.wait()
    b_up_out_ref[...] = as_row(b_up_ref)
    bias_ref[0:1] = as_row(b_out_ref)
    bias_ref[1:2] = as_row(b_down_ref)
    d_bias_ref[...] = jnp.sum(cot_ref[...].astype(full), axis=0, keepdims=True)

    lane = lane_ids((rows, LANES))

    def projected(s):
        return mm(h1, w_qkv_ref[s]) + b_qkv_ref[s : s + 1].astype(full)

    def turned(tile):
        return tile * cosine + rotary_partner(tile) * sine

    queries, keys, values = projected(0), projected(1), projected(2)
    grads = mm_nt(cot_ref[...], w_out_ref[...])
    left = lane < HEAD_DIM
    for i in range(heads // 2):
        cut = slice(i * LANES, (i + 1) * LANES)
        q = turned(queries[:, cut]).astype(low).astype(full) * score_scale
        k = turned(keys[:, cut])
        v = values[:, cut]
        g = grads[:, cut]
        packed[2 * i, :, :LANES] = jnp.where(left, g, pltpu.roll(q, HEAD_DIM, 1)).astype(low)
        packed[2 * i, :, LANES:] = jnp.where(left, v, pltpu.roll(k, HEAD_DIM, 1)).astype(low)
        packed[2 * i + 1, :, :LANES] = jnp.where(left, pltpu.roll(g, HEAD_DIM, 1), q).astype(low)
        packed[2 * i + 1, :, LANES:] = jnp.where(left, pltpu.roll(v, HEAD_DIM, 1), k).astype(low)
    own = me // group
    for r in range(heads):
        send_refs[r][...] = packed[lax.rem(own + r, heads)]


def project(heads, group, pair_of, inverse, given):
    hidden, w_out, b_up = given[0], given[6], given[9]
    rows, width = hidden.shape
    outs = [
        shape_of((rows, width), low),
        shape_of((rows, width), low),
        shape_of((rows, width), full),
        shape_of((rows, LANES), full),
        shape_of((1, width), full),
        shape_of((2, width), full),
        shape_of((2, width), full),
        shape_of((1, b_up.shape[0]), full),
    ] + [shape_of((rows, 2 * LANES), low)] * heads
    found = pl.pallas_call(
        functools.partial(project_kernel, heads, group),
        out_shape=outs,
        in_specs=[spec_smem(), spec_vmem()] + [pl.BlockSpec(memory_space=pl.ANY)] * len(given),
        out_specs=[spec_vmem()] * len(outs),
        scratch_shapes=[pltpu.VMEM((heads, rows, 2 * LANES), low)]
        + [pltpu.VMEM(array.shape, array.dtype) for array in given]
        + [pltpu.SemaphoreType.DMA((len(given),))],
        compiler_params=params(32),
        cost_estimate=pl.CostEstimate(
            flops=2 * rows * width * 4 * w_out.shape[0], bytes_accessed=8 * MIB, transcendentals=0
        ),
        name="project",
    )(pair_of, inverse, *given)
    return found[:8], found[8:]


def mlp_kernel(
    h2_ref, cot_ref, xhat_ref, w_up_ref, b_up_ref, w_down_ref, part_ref, back_ref, sums_ref, d_b_up_ref, grad_ref, h2_turned, part_acc, back_acc
):
    step = pl.program_id(0)

    @pl.when(step == 0)
    def _():
        h2_turned[...] = turn(h2_ref[...])
        part_acc[...] = jnp.zeros_like(part_acc)
        back_acc[...] = jnp.zeros_like(back_acc)

    cot = cot_ref[...]
    w_up = w_up_ref[...]
    w_down = w_down_ref[...]
    u = mm(h2_ref[...], w_up) + b_up_ref[...].astype(full)
    cdf = 0.5 * (1.0 + lax.erf(u * np.float32(np.sqrt(0.5))))
    active = u * cdf
    active_low = active.astype(low)
    slope = cdf + u * jnp.exp(-0.5 * u * u) * np.float32(1.0 / np.sqrt(2.0 * np.pi))
    du = (mm_nt(cot, w_down) * slope).astype(low)
    part_acc[...] += mm(active_low, w_down)
    back_acc[...] += mm_nt(du, w_up)
    d_b_up_ref[...] = jnp.sum(du.astype(full), axis=0, keepdims=True)
    up = mm(h2_turned[...], du).astype(low)
    down = mm(active.T.astype(low), cot).astype(low)
    depth = up.shape[0]
    for b in range(grad_ref.shape[0]):
        grad_ref[b, :depth] = up[:, b * LANES : (b + 1) * LANES]
        for t in range(down.shape[1] // LANES):
            grad_ref[b, depth + t * LANES : depth + (t + 1) * LANES] = down[
                b * LANES : (b + 1) * LANES, t * LANES : (t + 1) * LANES
            ]

    @pl.when(step == pl.num_programs(0) - 1)
    def _():
        part_ref[...] = part_acc[...]
        back = back_acc[...]
        back_ref[...] = back.astype(low)
        sums_ref[0:1] = jnp.sum(back * xhat_ref[...], axis=0, keepdims=True)
        sums_ref[1:2] = jnp.sum(back, axis=0, keepdims=True)


def mlp(h2, cot, xhat, w_up, b_up, w_down):
    rows, width = h2.shape
    hidden_units = w_up.shape[1]
    tile = 2 * LANES
    steps = hidden_units // tile
    whole = lambda shape: pl.BlockSpec(shape, lambda f: (0,) * len(shape))
    outs = [
        shape_of((rows, width), full),
        shape_of((rows, width), low),
        shape_of((2, width), full),
        shape_of((1, hidden_units), full),
        shape_of((hidden_units // LANES, 2 * width, LANES), low),
    ]
    return pl.pallas_call(
        mlp_kernel,
        grid=(steps,),
        out_shape=outs,
        in_specs=[
            whole((rows, width)),
            whole((rows, width)),
            whole((rows, width)),
            pl.BlockSpec((width, tile), lambda f: (0, f)),
            pl.BlockSpec((1, tile), lambda f: (0, f)),
            pl.BlockSpec((tile, width), lambda f: (f, 0)),
        ],
        out_specs=[
            whole((rows, width)),
            whole((rows, width)),
            whole((2, width)),
            pl.BlockSpec((1, tile), lambda f: (0, f)),
            pl.BlockSpec((2, 2 * width, LANES), lambda f: (f, 0, 0)),
        ],
        scratch_shapes=[
            pltpu.VMEM((width, rows), low),
            pltpu.VMEM((rows, width), full),
            pltpu.VMEM((rows, width), full),
        ],
        compiler_params=params(40),
        cost_estimate=pl.CostEstimate(
            flops=12 * rows * width * hidden_units, bytes_accessed=20 * MIB, transcendentals=0
        ),
        name="feed_forward",
    )(h2, cot, xhat, w_up, b_up, w_down)


def attention_kernel(heads, group, pair_ref, inv_ref, after_ref, *rest):
    del after_ref
    got_refs = rest[:heads]
    rest = rest[heads:]
    if group > 1:
        other_ref, rest = rest[0], rest[1:]
    out_refs = rest[:heads]
    rest = rest[heads:]
    d_own_ref, rest = rest[0], rest[1:]
    if group > 1:
        d_other_ref, rest = rest[0], rest[1:]
    queries, values_keys, turned_keys, weights_in, weights_out, stored, sums, finals, results, block_cos, block_sin = rest

    rows = got_refs[0].shape[0]
    owners = pair_ref.shape[0]
    total_blocks = 2 * owners
    per_chunk = KEYS // BLOCK
    tasks = (total_blocks + 1 + per_chunk - 1) // per_chunk
    me = lax.axis_index("ctx")
    own_head = me // group
    own_sub = lax.rem(me, group)

    def blocks_of(r, d):
        owner = lax.rem(own_head - r + heads, heads) * group + lax.rem(own_sub + d, group)
        pair = pair_ref[owner]
        return pair, total_blocks - 1 - pair

    def place(tile, block):
        at = pl.multiple_of(block * BLOCK, BLOCK)
        values_keys[pl.ds(at, BLOCK), :] = tile
        turned_keys[:, pl.ds(at, BLOCK)] = turn(tile)

    for r in range(heads):
        queries[r] = got_refs[r][:, :LANES]
        for half, block in enumerate(blocks_of(r, 0)):
            place(got_refs[r][half * BLOCK : (half + 1) * BLOCK, LANES:], block)
        for d in range(1, group):
            for half, block in enumerate(blocks_of(r, d)):
                at = r * rows + half * BLOCK
                place(other_ref[d - 1, at : at + BLOCK, :], block)
    sums[...] = jnp.zeros_like(sums)

    lane = lane_ids((BLOCK, LANES))
    left = lane < HEAD_DIM
    in_key = lane - HEAD_DIM
    moving = (in_key >= 0) & (in_key < ROT)
    forward = (in_key >= 0) & (in_key < HALF)
    cos_row, sin_row, block_cos[...], block_sin[...] = block_tables(inv_ref[...], row_ids(block_cos.shape))

    def rotated_back(tile, block):
        cos_at, sin_at = block_cos[pl.ds(block, 1), :], block_sin[pl.ds(block, 1), :]
        cosine = jnp.where(moving, cos_row * cos_at - sin_row * sin_at, 1.0)
        sine = sin_row * cos_at + cos_row * sin_at
        sine = jnp.where(moving, jnp.where(forward, sine, -sine), 0.0)
        return tile * cosine + rotary_partner(tile) * sine

    offset = row_ids((SUB, BLOCK)) - lane_ids((SUB, BLOCK))

    def one_pair(r, carry):
        blocks = blocks_of(r, 0)
        first = blocks[0] // per_chunk + 1
        for half in range(2):
            both = queries[r, half * BLOCK : (half + 1) * BLOCK, :]
            both_turned = turn(both)
            upper = row_ids((LANES, BLOCK)) < HEAD_DIM
            zero = jnp.zeros_like(both_turned)
            weights_in[half, :, :BLOCK] = jnp.where(upper, both_turned, zero)
            weights_in[half, :, BLOCK:] = jnp.where(upper, zero, both_turned)
            weights_out[half, :BLOCK, :] = jnp.where(left, both, zero)
            weights_out[half, BLOCK:, :] = jnp.where(left, zero, both)
        finals[...] = jnp.zeros_like(finals)

        def task(t):
            is_first = t < first
            chunk = jnp.where(is_first, first - 1 - t, t - first)
            return is_first, chunk

        stats = []
        for t in range(tasks):
            is_first, chunk = task(t)
            half = jnp.where(is_first, 0, 1)
            weights = weights_in[half]
            for u in range(KEYS // SUB):
                at = pl.multiple_of(chunk * KEYS + u * SUB, SUB)
                both = mm(values_keys[pl.ds(at, SUB), :], weights)
                grads = both[:, :BLOCK]
                scores = both[:, BLOCK:]
                if t == 0:
                    scores = jnp.where(offset <= blocks[0] * BLOCK - at, scores, masked_score)
                if t == tasks - 1:
                    scores = jnp.where(offset <= blocks[1] * BLOCK - at, scores, masked_score)
                peak = jnp.max(scores, axis=0, keepdims=True)
                raised = jnp.exp(scores - peak)
                total = jnp.sum(raised, axis=0, keepdims=True)
                weighted = jnp.sum(raised * grads, axis=0, keepdims=True)
                stored[t, u * SUB : (u + 1) * SUB, :BLOCK] = raised
                stored[t, u * SUB : (u + 1) * SUB, BLOCK:] = grads
                stats.append((is_first, peak, total, weighted))

        def finish(wanted):
            top = jnp.full((1, BLOCK), masked_score, full)
            for is_first, peak, total, weighted in stats:
                top = jnp.maximum(top, jnp.where(is_first == wanted, peak, masked_score))
            all_total = jnp.zeros((1, BLOCK), full)
            all_weighted = jnp.zeros((1, BLOCK), full)
            for is_first, peak, total, weighted in stats:
                factor = jnp.where(is_first == wanted, jnp.exp(peak - top), 0.0)
                all_total = all_total + total * factor
                all_weighted = all_weighted + weighted * factor
            return top, 1.0 / all_total, all_weighted / all_total

        ends = (finish(True), finish(False))

        for t in range(tasks):
            is_first, chunk = task(t)
            half = jnp.where(is_first, 0, 1)
            weights = weights_out[half]
            top, inverse, delta = (jnp.where(is_first, a, b) for a, b in zip(*ends))
            parts = []
            for u in range(KEYS // SUB):
                peak = stats[t * (KEYS // SUB) + u][1]
                factor = jnp.exp(peak - top) * inverse
                probs = stored[t, u * SUB : (u + 1) * SUB, :BLOCK] * factor
                grads = stored[t, u * SUB : (u + 1) * SUB, BLOCK:]
                d_scores = probs * (grads - delta)
                both = jnp.concatenate([probs, d_scores], axis=1).astype(low)
                at = pl.multiple_of(chunk * KEYS + u * SUB, SUB)
                sums[pl.ds(at, SUB), :] += mm(both, weights)
                parts.append(both)
            at = pl.multiple_of(chunk * KEYS, KEYS)
            finals[half] += mm(turned_keys[:, pl.ds(at, KEYS)], jnp.concatenate(parts, axis=0))

        for half in range(2):
            both = jnp.concatenate(
                [finals[half, :HEAD_DIM, :BLOCK], finals[half, HEAD_DIM:, BLOCK:] * score_scale], axis=0
            ).T
            results[r, half * BLOCK : (half + 1) * BLOCK, :] = rotated_back(both, blocks[half]).astype(low)
        return carry

    lax.fori_loop(0, heads, one_pair, 0)

    for r in range(heads):
        out_refs[r][...] = results[r]
        for d in range(group):
            for half, block in enumerate(blocks_of(r, d)):
                at = r * rows + half * BLOCK
                tile = rotated_back(sums[pl.ds(pl.multiple_of(block * BLOCK, BLOCK), BLOCK), :], block)
                if d == 0:
                    d_own_ref[at : at + BLOCK, :] = tile
                else:
                    d_other_ref[d - 1, at : at + BLOCK, :] = tile


def attention(heads, group, pair_of, inverse, after, got, other):
    rows = got[0].shape[0]
    owners = pair_of.shape[0]
    total_keys = owners * rows
    tasks = (2 * owners + KEYS // BLOCK) // (KEYS // BLOCK)
    outs = [shape_of((rows, LANES), low)] * heads + [shape_of((heads * rows, LANES), full)]
    operands = [pair_of, inverse, after, *got]
    if group > 1:
        outs.append(shape_of((group - 1, heads * rows, LANES), full))
        operands.append(other)
    found = pl.pallas_call(
        functools.partial(attention_kernel, heads, group),
        out_shape=outs,
        in_specs=[spec_smem(), spec_vmem(), pl.BlockSpec(memory_space=pl.ANY)] + [spec_vmem()] * (len(operands) - 3),
        out_specs=[spec_vmem()] * len(outs),
        scratch_shapes=[
            pltpu.VMEM((heads, rows, LANES), low),
            pltpu.VMEM((total_keys, LANES), low),
            pltpu.VMEM((LANES, total_keys), low),
            pltpu.VMEM((2, LANES, 2 * BLOCK), low),
            pltpu.VMEM((2, 2 * BLOCK, LANES), low),
            pltpu.VMEM((tasks, KEYS, 2 * BLOCK), full),
            pltpu.VMEM((total_keys, LANES), full),
            pltpu.VMEM((2, LANES, 2 * BLOCK), full),
            pltpu.VMEM((heads, rows, LANES), low),
            pltpu.VMEM((2 * owners, LANES), full),
            pltpu.VMEM((2 * owners, LANES), full),
        ],
        compiler_params=params(16 + total_keys * 3 * KEYS // MIB),
        cost_estimate=pl.CostEstimate(
            flops=20_000_000_000, bytes_accessed=8 * MIB, transcendentals=0
        ),
        name="attention",
    )(*operands)
    return found[:heads], found[heads], (found[heads + 1] if group > 1 else None)


def combine_kernel(heads, terms, *refs):
    rows = refs[0].shape[0] // heads
    for r in range(heads):
        cut = slice(r * rows, (r + 1) * rows)
        total = refs[0][cut, :]
        for term in refs[1:terms]:
            total = total + term[cut, :]
        refs[terms + heads + r][:, :LANES] = refs[terms + r][...]
        refs[terms + heads + r][:, LANES:] = total.astype(low)


def combine(heads, terms, firsts):
    rows = firsts[0].shape[0]
    return pl.pallas_call(
        functools.partial(combine_kernel, heads, len(terms)),
        out_shape=[shape_of((rows, 2 * LANES), low)] * heads,
        in_specs=[spec_vmem()] * (heads + len(terms)),
        out_specs=[spec_vmem()] * heads,
        compiler_params=params(24),
        cost_estimate=pl.CostEstimate(flops=10**7, bytes_accessed=3 * MIB, transcendentals=0),
        name="combine",
    )(*terms, *firsts)


def return_kernel(heads, group, order, h1_ref, xhat_ref, cot_ref, part_ref, w_qkv_ref, w_out_ref, *rest):
    got_refs = rest[:heads]
    part_low_ref, back_ref, sums_ref, d_b_ref, keep_ref, send_ref, first, second, attended, d_proj, grads = rest[heads:]
    own = lax.axis_index("ctx") // group
    for r in range(heads):
        head = lax.rem(own + r, heads)
        first[head] = got_refs[r][:, :LANES]
        second[head] = got_refs[r][:, LANES:]
    chunk_rows = grads.shape[1]

    def put(at, tile):
        step = min(chunk_rows, tile.shape[0])
        for off in range(0, tile.shape[0], step):
            chunk, inside = divmod(at + off, chunk_rows)
            grads[chunk, inside : inside + step] = tile[off : off + step]

    rows = h1_ref.shape[0]
    left = lane_ids((rows, LANES)) < HEAD_DIM
    for i in range(heads // 2):
        cut = slice(i * LANES, (i + 1) * LANES)
        a, b = first[2 * i].astype(full), first[2 * i + 1].astype(full)
        attended[:, cut] = jnp.where(left, a, pltpu.roll(b, HEAD_DIM, 1)).astype(low)
        d_proj[0, :, cut] = jnp.where(left, pltpu.roll(a, HEAD_DIM, 1), b).astype(low)
        a, b = second[2 * i].astype(full), second[2 * i + 1].astype(full)
        d_proj[2, :, cut] = jnp.where(left, a, pltpu.roll(b, HEAD_DIM, 1)).astype(low)
        d_proj[1, :, cut] = jnp.where(left, pltpu.roll(a, HEAD_DIM, 1), b).astype(low)
    part_low_ref[...] = (part_ref[...] + mm(attended[...], w_out_ref[...])).astype(low)
    back = mm_nt(d_proj[0], w_qkv_ref[0]) + mm_nt(d_proj[1], w_qkv_ref[1]) + mm_nt(d_proj[2], w_qkv_ref[2])
    back_ref[...] = back.astype(low)
    sums_ref[0:1] = jnp.sum(back * xhat_ref[...], axis=0, keepdims=True)
    sums_ref[1:2] = jnp.sum(back, axis=0, keepdims=True)
    h1_turned = turn(h1_ref[...])
    depth, tiles = h1_turned.shape[0], heads // 2
    for s in range(3):
        d_b_ref[s : s + 1] = jnp.sum(d_proj[s].astype(full), axis=0, keepdims=True)
        grad = mm(h1_turned, d_proj[s]).astype(low)
        for t in range(tiles):
            at = (s * tiles + t) * depth
            put(at, grad[:, t * LANES : (t + 1) * LANES])
    grad = mm(turn(attended[...]), cot_ref[...]).astype(low)
    height = grad.shape[0]
    for t in range(depth // LANES):
        at = 3 * tiles * depth + t * height
        put(at, grad[:, t * LANES : (t + 1) * LANES])
    core, place, way = ring_place(order)
    chips = len(order)
    for t in range(chips):
        keep_ref[t] = grads[core * chips + lax.rem(place + way * (t + 1) + 2 * chips * chips, chips)]
        send_ref[t] = grads[(1 - core) * chips + lax.rem(place - way * (t + 1) + 2 * chips * chips, chips)]


def ring_place(order):
    me = lax.axis_index("ctx")
    chip, core = me // 2, lax.rem(me, 2)
    place = sum(jnp.where(chip == c, i, 0) for i, c in enumerate(order))
    return core, place, 2 * core - 1


def back_projections(heads, group, order, h1, xhat, cot, part, w_qkv, w_out, got):
    rows, width = h1.shape
    local_width = w_out.shape[0]
    chips = len(order)
    chunk_rows = 4 * width * local_width // LANES // (2 * chips)
    outs = [
        shape_of((rows, width), low),
        shape_of((rows, width), low),
        shape_of((2, width), full),
        shape_of((3, local_width), full),
        shape_of((chips, chunk_rows, LANES), low),
        shape_of((chips, chunk_rows, LANES), low),
    ]
    return pl.pallas_call(
        functools.partial(return_kernel, heads, group, order),
        out_shape=outs,
        in_specs=[spec_vmem()] * (6 + heads),
        out_specs=[spec_vmem()] * len(outs),
        scratch_shapes=[
            pltpu.VMEM((heads, rows, LANES), low),
            pltpu.VMEM((heads, rows, LANES), low),
            pltpu.VMEM((rows, local_width), low),
            pltpu.VMEM((3, rows, local_width), low),
            pltpu.VMEM((2 * chips, chunk_rows, LANES), low),
        ],
        compiler_params=params(40),
        cost_estimate=pl.CostEstimate(
            flops=16 * rows * width * local_width, bytes_accessed=14 * MIB, transcendentals=0
        ),
        name="back_projections",
    )(h1, xhat, cot, part, w_qkv, w_out, *got)


def finish_kernel(hidden_ref, cot_ref, xhat_ref, std_ref, gains_ref, bias_ref, part_refs, back_refs, next_refs, out_ref, grad_ref):
    gains = gains_ref[...]
    biases = bias_ref[...]
    summed = part_refs[0][...].astype(full) + part_refs[1][...].astype(full)
    out_ref[...] = (hidden_ref[...].astype(full) + summed + biases[0:1] + biases[1:2]).astype(low)
    e1 = back_refs[0][...].astype(full) + back_refs[1][...].astype(full)
    e2 = next_refs[0][...].astype(full) + next_refs[1][...].astype(full)
    f = e1 * gains[0:1] + e2 * gains[1:2]
    xhat = xhat_ref[...]
    inv_std = std_ref[:, 0:1]
    grad_ref[...] = cot_ref[...].astype(full) + inv_std * (
        f - jnp.mean(f, axis=-1, keepdims=True) - xhat * jnp.mean(f * xhat, axis=-1, keepdims=True)
    )


def finish(hidden, cot, xhat, inv_std, gains, biases, parts, backs, nexts):
    rows, width = hidden.shape

    def body(*refs):
        finish_kernel(*refs[:6], refs[6:8], refs[8:10], refs[10:12], *refs[12:])

    return pl.pallas_call(
        body,
        out_shape=[shape_of((rows, width), low), shape_of((rows, width), full)],
        in_specs=[spec_vmem()] * 12,
        out_specs=[spec_vmem()] * 2,
        compiler_params=params(40),
        cost_estimate=pl.CostEstimate(flops=10**7, bytes_accessed=8 * MIB, transcendentals=0),
        name="finish",
    )(hidden, cot, xhat, inv_std, gains, biases, *parts, *backs, *nexts)


def unpack_mlp(packed, width, hidden_units):
    blocks = hidden_units // LANES

    def body(in_ref, up_ref, down_ref):
        up_ref[...] = in_ref[:width].astype(full)
        for t in range(width // LANES):
            at = width + t * LANES
            down_ref[:, t * LANES : (t + 1) * LANES] = in_ref[at : at + LANES].astype(full)

    return pl.pallas_call(
        body,
        grid=(blocks,),
        out_shape=[shape_of((width, hidden_units), full), shape_of((hidden_units, width), full)],
        in_specs=[pl.BlockSpec((2 * width, LANES), lambda f: (f, 0))],
        out_specs=[pl.BlockSpec((width, LANES), lambda f: (0, f)), pl.BlockSpec((LANES, width), lambda f: (f, 0))],
        compiler_params=params(40),
        name="unpack_feed_forward",
    )(packed)


def unpack_attention_kernel(order, width, local_width, *rest):
    chips = len(order)
    own_refs, other_refs = rest[:chips], rest[chips : 2 * chips]
    qkv_ref, out_ref, held, sems = rest[2 * chips :]
    core, place, way = ring_place(order)
    chunk_rows = own_refs[0].shape[0]
    unit = min(chunk_rows, local_width)
    tiles = local_width // LANES
    split = 3 * tiles * width
    waits = []
    for t in range(chips):
        for side, refs in enumerate((own_refs, other_refs)):
            turn_way = way if side == 0 else -way
            half = core if side == 0 else 1 - core
            chunk = half * chips + lax.rem(place + turn_way * t + chips * chips, chips)
            slot = 2 * t + side
            held[slot] = refs[t][...].astype(full)
            for j in range(chunk_rows // unit):
                base = chunk * chunk_rows + j * unit
                source = held.at[slot, pl.ds(j * unit, unit), :]
                sem = sems.at[slot * (chunk_rows // unit) + j]
                in_qkv = base < split
                tile = base // width
                row = pl.multiple_of(lax.rem(base, width), unit)
                s = jnp.minimum(tile // tiles, 2)
                column = pl.multiple_of(lax.rem(tile, tiles) * LANES, LANES)
                to_qkv = pltpu.make_async_copy(source, qkv_ref.at[s, pl.ds(row, unit), pl.ds(column, LANES)], sem)
                after = jnp.maximum(base - split, 0)
                row = pl.multiple_of(lax.rem(after, local_width), unit)
                column = pl.multiple_of(after // local_width * LANES, LANES)
                to_out = pltpu.make_async_copy(source, out_ref.at[pl.ds(row, unit), pl.ds(column, LANES)], sem)

                @pl.when(in_qkv)
                def _():
                    to_qkv.start()

                @pl.when(jnp.logical_not(in_qkv))
                def _():
                    to_out.start()

                waits.append(to_qkv)
    for copy in waits:
        copy.wait()


def unpack_attention(order, width, local_width, own, other):
    chips = len(order)
    chunk_rows = own[0].shape[0]
    return pl.pallas_call(
        functools.partial(unpack_attention_kernel, order, width, local_width),
        out_shape=[shape_of((3, width, local_width), full), shape_of((local_width, width), full)],
        in_specs=[spec_vmem()] * (2 * chips),
        out_specs=[pl.BlockSpec(memory_space=pl.ANY)] * 2,
        scratch_shapes=[
            pltpu.VMEM((2 * chips, chunk_rows, LANES), full),
            pltpu.SemaphoreType.DMA((2 * chips * (chunk_rows // min(chunk_rows, local_width)),)),
        ],
        compiler_params=params(32),
        cost_estimate=pl.CostEstimate(flops=10**6, bytes_accessed=12 * MIB, transcendentals=0),
        name="unpack_attention",
    )(*own, *other)


def local(
    hidden,
    pair_of,
    ln1_gain,
    ln1_bias,
    ln2_gain,
    ln2_bias,
    w_qkv,
    b_qkv,
    w_out,
    b_out,
    w_up,
    b_up,
    w_down,
    b_down,
    cotangent,
):
    owners = lax.axis_size("ctx")
    sides = lax.axis_size("tp")
    rows, width = hidden.shape
    local_width = w_qkv.shape[2]
    hidden_units = w_up.shape[1]
    heads = local_width // HEAD_DIM
    group = owners // heads

    exponent = np.arange(0, ROT, 2, dtype=np.float32) / np.float32(ROT)
    inverse = jnp.asarray(np.tile(np.float32(10000.0) ** (-exponent), LANES // HALF)[None, :], full)
    order = (0, 2, 4, 6, 7, 5, 3, 1) if owners == 16 else tuple(range(owners // 2))
    chips = len(order)

    (h1, h2, xhat, inv_std, d_bias, gains, biases, b_up_row), sends = project(
        heads,
        group,
        pair_of,
        inverse,
        (hidden, ln1_gain, ln1_bias, ln2_gain, ln2_bias, cotangent, w_out, w_qkv, b_qkv, b_up, b_out, b_down),
    )

    def head_shift(array, r, back=False):
        step = -r if back else r
        pairs = [(c, ((c // group + step) % heads) * group + c % group) for c in range(owners)]
        return lax.ppermute(array, "ctx", pairs)

    def group_shift(array, d):
        pairs = [(c, c // group * group + (c % group + d) % group) for c in range(owners)]
        return lax.ppermute(array, "ctx", pairs)

    got = [sends[0]] + [head_shift(sends[r], r) for r in range(1, heads)]

    part, back2, sums2, d_b_up, grad_mlp = mlp(h2, cotangent, xhat, w_up, b_up_row, w_down)
    grad_mlp = grad_mlp.reshape(-1, LANES)

    def reduced(grad):
        own = lax.psum_scatter(grad, "ctx", scatter_dimension=0, tiled=True)
        return lax.all_gather(own, "ctx", axis=0, tiled=True)

    total_mlp = reduced(grad_mlp)

    other = None
    if group > 1:
        mine = jnp.concatenate([array[:, LANES:] for array in got], axis=0)
        other = jnp.stack([group_shift(mine, group - d) for d in range(1, group)])

    firsts, d_own, d_other = attention(heads, group, pair_of, inverse, sums2, got, other)
    terms = [d_own] + [group_shift(d_other[d - 1], d) for d in range(1, group)]
    backs = combine(heads, terms, firsts)
    backs = [backs[0]] + [head_shift(backs[r], r, True) for r in range(1, heads)]

    part_low, back1, sums1, d_b_qkv, keep, send = back_projections(
        heads, group, order, h1, xhat, cotangent, part, w_qkv, w_out, backs
    )

    def ring(array):
        pairs = []
        for i, chip in enumerate(order):
            pairs.append((2 * chip, 2 * order[(i + 1) % chips]))
            pairs.append((2 * chip + 1, 2 * order[(i - 1) % chips] + 1))
        return lax.ppermute(array, "ctx", pairs)

    def other_core(array):
        return lax.ppermute(array, "ctx", [(c, c ^ 1) for c in range(owners)])

    came = other_core(send)
    total = keep[0].astype(full) + came[0].astype(full)
    for t in range(1, chips):
        moved = ring(total.astype(low))
        total = moved.astype(full) + (keep[t].astype(full) + came[t].astype(full))
    own_parts = [total.astype(low)]
    other_parts = []
    for t in range(chips):
        other_parts.append(other_core(own_parts[t]))
        if t < chips - 1:
            own_parts.append(ring(own_parts[t]))

    def across(array):
        return lax.ppermute(array, "tp", [(t, (t + 1) % sides) for t in range(sides)])

    output, d_hidden = finish(
        hidden,
        cotangent,
        xhat,
        inv_std,
        gains,
        biases,
        (part_low, across(part_low)),
        (back1, across(back1)),
        (back2, across(back2)),
    )

    small = jnp.concatenate(
        [sums1.reshape(1, -1), sums2.reshape(1, -1), d_bias, d_b_up, d_b_qkv.reshape(1, -1)], axis=1
    )
    step = 1
    while step < owners:
        small = small + lax.ppermute(small, "ctx", [(c, c ^ step) for c in range(owners)])
        step *= 2
    norm_sums = small[:, : 4 * width]
    norm_sums = (norm_sums + across(norm_sums)).reshape(4, width)
    at = 4 * width
    d_bias = small[0, at : at + width]
    d_b_up = small[0, at + width : at + width + hidden_units]
    d_b_qkv = small[0, at + width + hidden_units :].reshape(3, local_width)

    d_w_up, d_w_down = unpack_mlp(total_mlp, width, hidden_units)
    d_w_qkv, d_w_out = unpack_attention(order, width, local_width, own_parts, other_parts)
    return (
        output,
        d_hidden,
        norm_sums[0],
        norm_sums[1],
        norm_sums[2],
        norm_sums[3],
        d_w_qkv,
        d_b_qkv,
        d_w_out,
        d_bias,
        d_w_up,
        d_b_up,
        d_w_down,
        d_bias,
    )


def solution(mesh):
    placed = (
        P("ctx", None),
        P(),
        P(),
        P(),
        P(),
        P(),
        P(None, None, "tp"),
        P(None, "tp"),
        P("tp", None),
        P(),
        P(None, "tp"),
        P("tp"),
        P("tp", None),
        P(),
        P("ctx", None),
    )
    return jax.shard_map(
        local,
        mesh=mesh,
        in_specs=placed,
        out_specs=(
            P("ctx", None),
            P("ctx", None),
            P(),
            P(),
            P(),
            P(),
            P(None, None, "tp"),
            P(None, "tp"),
            P("tp", None),
            P(),
            P(None, "tp"),
            P("tp"),
            P("tp", None),
            P(),
        ),
        check_vma=False,
    )
```

```python
import functools

import jax
import jax.numpy as jnp
import numpy as np
from jax import lax
from jax.experimental import pallas as pl
from jax.experimental.pallas import tpu as pltpu
from jax.sharding import PartitionSpec as P

HEAD_DIM = 64
ROT = 16
HALF = ROT // 2
BLOCK = 128
LANES = 128
KEYS = 512
SUB = 128
MIB = 1 << 20

norm_eps = 1e-05
masked_score = -1e30
score_scale = HEAD_DIM ** (-0.5)
low = jnp.bfloat16
full = jnp.float32


def mm(left, right):
    return lax.dot_general(left, right, (((1,), (0,)), ((), ())), preferred_element_type=full)


def mm_nt(left, right):
    return lax.dot_general(left, right, (((1,), (1,)), ((), ())), preferred_element_type=full)


def turn(tensor):
    return tensor.astype(full).T.astype(low)


def lane_ids(shape):
    return lax.broadcasted_iota(jnp.int32, shape, len(shape) - 1)


def row_ids(shape):
    return lax.broadcasted_iota(jnp.int32, shape, len(shape) - 2)


def rotary_partner(tensor):
    lanes = lane_ids(tensor.shape)
    ahead = pltpu.roll(tensor, LANES - HALF, 1)
    behind = pltpu.roll(tensor, HALF, 1)
    return jnp.where(lanes % ROT < HALF, ahead, behind)


def spec_vmem():
    return pl.BlockSpec(memory_space=pltpu.VMEM)


def spec_smem():
    return pl.BlockSpec(memory_space=pltpu.SMEM)


def spec_hbm():
    return pl.BlockSpec(memory_space=pltpu.HBM)


def params(mib):
    return pltpu.CompilerParams(vmem_limit_bytes=mib * MIB)


def shape_of(shape, kind):
    return jax.ShapeDtypeStruct(shape, kind)


def block_tables(inverse, blocks):
    row = row_ids((BLOCK, LANES)).astype(full)
    start = blocks.astype(full) * float(BLOCK)
    return jnp.cos(row * inverse), jnp.sin(row * inverse), jnp.cos(start * inverse), jnp.sin(start * inverse)


def project_kernel(heads, group, pair_ref, inv_ref, *rest):
    given, rest = rest[:12], rest[12:]
    h1_ref, h2_ref, xhat_ref, std_ref, d_bias_ref, gains_ref, bias_ref, b_up_out_ref = rest[:8]
    send_refs = rest[8 : 8 + heads]
    packed, held, sems = rest[8 + heads], rest[9 + heads : -1], rest[-1]
    copies = [pltpu.make_async_copy(src, dst, sems.at[i]) for i, (src, dst) in enumerate(zip(given, held))]
    for copy in copies:
        copy.start()
    (
        hidden_ref,
        g1_ref,
        c1_ref,
        g2_ref,
        c2_ref,
        cot_ref,
        w_out_ref,
        w_qkv_ref,
        b_qkv_ref,
        b_up_ref,
        b_out_ref,
        b_down_ref,
    ) = held
    rows = hidden_ref.shape[0]
    me = lax.axis_index("ctx")
    pair = pair_ref[me]
    total_blocks = 2 * pair_ref.shape[0]

    first = jnp.where(row_ids((8, LANES)) == 0, pair, total_blocks - 1 - pair)
    inverse = inv_ref[...]
    cos_row, sin_row, cos_block, sin_block = block_tables(inverse, first)
    in_head = lane_ids((BLOCK, LANES)) % HEAD_DIM
    tables = []
    for half in range(2):
        cos_at, sin_at = cos_block[half : half + 1], sin_block[half : half + 1]
        cosine = cos_row * cos_at - sin_row * sin_at
        sine = sin_row * cos_at + cos_row * sin_at
        cosine = jnp.where(in_head < ROT, cosine, 1.0)
        sine = jnp.where(in_head < HALF, -sine, jnp.where(in_head < ROT, sine, 0.0))
        tables.append((cosine, sine))
    cosine = jnp.concatenate([tables[0][0], tables[1][0]], axis=0)
    sine = jnp.concatenate([tables[0][1], tables[1][1]], axis=0)

    for copy in copies[:5]:
        copy.wait()
    x = hidden_ref[...].astype(full)
    centred = x - jnp.mean(x, axis=-1, keepdims=True)
    spread = jnp.mean(centred * centred, axis=-1, keepdims=True)
    inv_std = lax.rsqrt(spread + norm_eps)
    xhat = centred * inv_std
    xhat_ref[...] = xhat
    std_ref[...] = jnp.broadcast_to(inv_std, std_ref.shape)

    def as_row(ref):
        return ref[...].astype(full)[None, :]

    gain1, gain2 = as_row(g1_ref), as_row(g2_ref)
    h1 = (xhat * gain1 + as_row(c1_ref)).astype(low)
    h1_ref[...] = h1
    h2_ref[...] = (xhat * gain2 + as_row(c2_ref)).astype(low)
    gains_ref[0:1] = gain1
    gains_ref[1:2] = gain2
    for copy in copies[5:]:
        copy.wait()
    b_up_out_ref[...] = as_row(b_up_ref)
    bias_ref[0:1] = as_row(b_out_ref)
    bias_ref[1:2] = as_row(b_down_ref)
    d_bias_ref[...] = jnp.sum(cot_ref[...].astype(full), axis=0, keepdims=True)

    lane = lane_ids((rows, LANES))

    def projected(s):
        return mm(h1, w_qkv_ref[s]) + b_qkv_ref[s : s + 1].astype(full)

    def turned(tile):
        return tile * cosine + rotary_partner(tile) * sine

    queries, keys, values = projected(0), projected(1), projected(2)
    grads = mm_nt(cot_ref[...], w_out_ref[...])
    left = lane < HEAD_DIM
    for i in range(heads // 2):
        cut = slice(i * LANES, (i + 1) * LANES)
        q = turned(queries[:, cut]).astype(low).astype(full) * score_scale
        k = turned(keys[:, cut])
        v = values[:, cut]
        g = grads[:, cut]
        packed[2 * i, :, :LANES] = jnp.where(left, g, pltpu.roll(q, HEAD_DIM, 1)).astype(low)
        packed[2 * i, :, LANES:] = jnp.where(left, v, pltpu.roll(k, HEAD_DIM, 1)).astype(low)
        packed[2 * i + 1, :, :LANES] = jnp.where(left, pltpu.roll(g, HEAD_DIM, 1), q).astype(low)
        packed[2 * i + 1, :, LANES:] = jnp.where(left, pltpu.roll(v, HEAD_DIM, 1), k).astype(low)
    own = me // group
    for r in range(heads):
        send_refs[r][...] = packed[lax.rem(own + r, heads)]


def project(heads, group, pair_of, inverse, given):
    hidden, w_out, b_up = given[0], given[6], given[9]
    rows, width = hidden.shape
    outs = [
        shape_of((rows, width), low),
        shape_of((rows, width), low),
        shape_of((rows, width), full),
        shape_of((rows, LANES), full),
        shape_of((1, width), full),
        shape_of((2, width), full),
        shape_of((2, width), full),
        shape_of((1, b_up.shape[0]), full),
    ] + [shape_of((rows, 2 * LANES), low)] * heads
    found = pl.pallas_call(
        functools.partial(project_kernel, heads, group),
        out_shape=outs,
        in_specs=[spec_smem(), spec_vmem()] + [spec_hbm()] * len(given),
        out_specs=[spec_vmem()] * len(outs),
        scratch_shapes=[pltpu.VMEM((heads, rows, 2 * LANES), low)]
        + [pltpu.VMEM(array.shape, array.dtype) for array in given]
        + [pltpu.SemaphoreType.DMA((len(given),))],
        compiler_params=params(60),
        cost_estimate=pl.CostEstimate(
            flops=2 * rows * width * 4 * w_out.shape[0], bytes_accessed=8 * MIB, transcendentals=0
        ),
        name="project",
    )(pair_of, inverse, *given)
    return found[:8], found[8:]


def mlp_kernel(
    core_ref,
    h2_ref,
    cot_ref,
    xhat_ref,
    up_keep_ref,
    up_send_ref,
    b_keep_ref,
    b_send_ref,
    down_keep_ref,
    down_send_ref,
    part_ref,
    back_ref,
    sums_ref,
    d_b_up_ref,
    keep_ref,
    send_ref,
    h2_turned,
    part_acc,
    back_acc,
):
    step = pl.program_id(0)
    steps = pl.num_programs(0)

    @pl.when(step == 0)
    def _():
        h2_turned[...] = turn(h2_ref[...])
        part_acc[...] = jnp.zeros_like(part_acc)
        back_acc[...] = jnp.zeros_like(back_acc)

    cot = cot_ref[...]
    w_up = jnp.concatenate([up_keep_ref[...], up_send_ref[...]], axis=1)
    w_down = jnp.concatenate([down_keep_ref[...], down_send_ref[...]], axis=0)
    u = mm(h2_ref[...], w_up) + jnp.concatenate([b_keep_ref[...], b_send_ref[...]], axis=1)
    cdf = 0.5 * (1.0 + lax.erf(u * np.float32(np.sqrt(0.5))))
    active = u * cdf
    active_low = active.astype(low)
    slope = cdf + u * jnp.exp(-0.5 * u * u) * np.float32(1.0 / np.sqrt(2.0 * np.pi))
    du = (mm_nt(cot, w_down) * slope).astype(low)
    part_acc[...] += mm(active_low, w_down)
    back_acc[...] += mm_nt(du, w_up)
    d_b_up = jnp.sum(du.astype(full), axis=0, keepdims=True)
    up = mm(h2_turned[...], du).astype(low)
    down = mm(active.T.astype(low), cot).astype(low)
    depth = up.shape[0]
    core = core_ref[0]
    for b, (half, grad_ref) in enumerate(((core, keep_ref), (1 - core, send_ref))):
        at = pl.multiple_of((half * steps + step) * LANES, LANES)
        d_b_up_ref[:, pl.ds(at, LANES)] = d_b_up[:, b * LANES : (b + 1) * LANES]
        grad_ref[:depth] = up[:, b * LANES : (b + 1) * LANES]
        for t in range(down.shape[1] // LANES):
            grad_ref[depth + t * LANES : depth + (t + 1) * LANES] = down[
                b * LANES : (b + 1) * LANES, t * LANES : (t + 1) * LANES
            ]

    @pl.when(step == steps - 1)
    def _():
        part_ref[...] = part_acc[...]
        back = back_acc[...]
        back_ref[...] = back.astype(low)
        sums_ref[0:1] = jnp.sum(back * xhat_ref[...], axis=0, keepdims=True)
        sums_ref[1:2] = jnp.sum(back, axis=0, keepdims=True)


def mlp(core, h2, cot, xhat, w_up, b_up, w_down):
    rows, width = h2.shape
    hidden_units = w_up.shape[1]
    steps = hidden_units // LANES // 2
    whole = lambda shape: pl.BlockSpec(shape, lambda f, c: (0,) * len(shape))
    kept = lambda f, c: c[0] * steps + f
    sent = lambda f, c: (1 - c[0]) * steps + f
    columns = lambda height, at: pl.BlockSpec((height, LANES), lambda f, c: (0, at(f, c)))
    flat = lambda at: pl.BlockSpec((LANES, width), lambda f, c: (at(f, c), 0))
    grads = pl.BlockSpec((2 * width, LANES), lambda f, c: (f, 0))
    outs = [
        shape_of((rows, width), full),
        shape_of((rows, width), low),
        shape_of((2, width), full),
        shape_of((1, hidden_units), full),
        shape_of((steps * 2 * width, LANES), low),
        shape_of((steps * 2 * width, LANES), low),
    ]
    return pl.pallas_call(
        mlp_kernel,
        grid_spec=pltpu.PrefetchScalarGridSpec(
            num_scalar_prefetch=1,
            grid=(steps,),
            in_specs=[
                whole((rows, width)),
                whole((rows, width)),
                whole((rows, width)),
                columns(width, kept),
                columns(width, sent),
                columns(1, kept),
                columns(1, sent),
                flat(kept),
                flat(sent),
            ],
            out_specs=[
                whole((rows, width)),
                whole((rows, width)),
                whole((2, width)),
                whole((1, hidden_units)),
                grads,
                grads,
            ],
            scratch_shapes=[
                pltpu.VMEM((width, rows), low),
                pltpu.VMEM((rows, width), full),
                pltpu.VMEM((rows, width), full),
            ],
        ),
        out_shape=outs,
        compiler_params=params(24),
        cost_estimate=pl.CostEstimate(
            flops=12 * rows * width * hidden_units, bytes_accessed=20 * MIB, transcendentals=0
        ),
        name="feed_forward",
    )(core, h2, cot, xhat, w_up, w_up, b_up, b_up, w_down, w_down)


def attention_kernel(heads, group, places, is_first, is_last, pair_ref, inv_ref, token_ref, *rest):
    del token_ref
    count = heads if is_first else len(places)
    got_refs, rest = rest[:count], rest[count:]
    if is_first:
        if group > 1:
            other_ref, rest = rest[0], rest[1:]
    else:
        rest = rest[3:]
    out_refs, rest = rest[: len(places)], rest[len(places) :]
    if is_last:
        d_own_ref, rest = rest[0], rest[1:]
        if group > 1:
            d_other_ref, rest = rest[0], rest[1:]
    (values_keys, turned_keys, sums), rest = rest[:3], rest[3:]
    queries, weights_in, weights_out, stored, finals, results, block_cos, block_sin = rest

    rows = got_refs[0].shape[0]
    owners = pair_ref.shape[0]
    total_blocks = 2 * owners
    per_chunk = KEYS // BLOCK
    tasks = (total_blocks + 1 + per_chunk - 1) // per_chunk
    me = lax.axis_index("ctx")
    own_head = me // group
    own_sub = lax.rem(me, group)

    def blocks_of(r, d):
        owner = lax.rem(own_head - r + heads, heads) * group + lax.rem(own_sub + d, group)
        pair = pair_ref[owner]
        return pair, total_blocks - 1 - pair

    def place(tile, block):
        at = pl.multiple_of(block * BLOCK, BLOCK)
        values_keys[pl.ds(at, BLOCK), :] = tile
        turned_keys[:, pl.ds(at, BLOCK)] = turn(tile)

    if is_first:
        for r in range(heads):
            for half, block in enumerate(blocks_of(r, 0)):
                place(got_refs[r][half * BLOCK : (half + 1) * BLOCK, LANES:], block)
            for d in range(1, group):
                for half, block in enumerate(blocks_of(r, d)):
                    at = r * rows + half * BLOCK
                    place(other_ref[d - 1, at : at + BLOCK, :], block)
        sums[...] = jnp.zeros_like(sums)
    for i, r in enumerate(places):
        queries[i] = got_refs[r if is_first else i][:, :LANES]

    lane = lane_ids((BLOCK, LANES))
    left = lane < HEAD_DIM
    in_key = lane - HEAD_DIM
    moving = (in_key >= 0) & (in_key < ROT)
    forward = (in_key >= 0) & (in_key < HALF)
    cos_row, sin_row, block_cos[...], block_sin[...] = block_tables(inv_ref[...], row_ids(block_cos.shape))

    def rotated_back(tile, block):
        cos_at, sin_at = block_cos[pl.ds(block, 1), :], block_sin[pl.ds(block, 1), :]
        cosine = jnp.where(moving, cos_row * cos_at - sin_row * sin_at, 1.0)
        sine = sin_row * cos_at + cos_row * sin_at
        sine = jnp.where(moving, jnp.where(forward, sine, -sine), 0.0)
        return tile * cosine + rotary_partner(tile) * sine

    offset = row_ids((SUB, BLOCK)) - lane_ids((SUB, BLOCK))

    def one_pair(i, carry):
        blocks = blocks_of(places[0] + i, 0)
        first = blocks[0] // per_chunk + 1
        for half in range(2):
            both = queries[i, half * BLOCK : (half + 1) * BLOCK, :]
            both_turned = turn(both)
            upper = row_ids((LANES, BLOCK)) < HEAD_DIM
            zero = jnp.zeros_like(both_turned)
            weights_in[half, :, :BLOCK] = jnp.where(upper, both_turned, zero)
            weights_in[half, :, BLOCK:] = jnp.where(upper, zero, both_turned)
            weights_out[half, :BLOCK, :] = jnp.where(left, both, zero)
            weights_out[half, BLOCK:, :] = jnp.where(left, zero, both)
        finals[...] = jnp.zeros_like(finals)

        def task(t):
            is_low = t < first
            chunk = jnp.where(is_low, first - 1 - t, t - first)
            return is_low, chunk

        stats = []
        for t in range(tasks):
            is_low, chunk = task(t)
            half = jnp.where(is_low, 0, 1)
            weights = weights_in[half]
            for u in range(KEYS // SUB):
                at = pl.multiple_of(chunk * KEYS + u * SUB, SUB)
                both = mm(values_keys[pl.ds(at, SUB), :], weights)
                grads = both[:, :BLOCK]
                scores = both[:, BLOCK:]
                if t == 0:
                    scores = jnp.where(offset <= blocks[0] * BLOCK - at, scores, masked_score)
                if t == tasks - 1:
                    scores = jnp.where(offset <= blocks[1] * BLOCK - at, scores, masked_score)
                peak = jnp.max(scores, axis=0, keepdims=True)
                raised = jnp.exp(scores - peak)
                total = jnp.sum(raised, axis=0, keepdims=True)
                weighted = jnp.sum(raised * grads, axis=0, keepdims=True)
                stored[t, u * SUB : (u + 1) * SUB, :BLOCK] = raised
                stored[t, u * SUB : (u + 1) * SUB, BLOCK:] = grads
                stats.append((is_low, peak, total, weighted))

        def finish(wanted):
            top = jnp.full((1, BLOCK), masked_score, full)
            for is_low, peak, total, weighted in stats:
                top = jnp.maximum(top, jnp.where(is_low == wanted, peak, masked_score))
            all_total = jnp.zeros((1, BLOCK), full)
            all_weighted = jnp.zeros((1, BLOCK), full)
            for is_low, peak, total, weighted in stats:
                factor = jnp.where(is_low == wanted, jnp.exp(peak - top), 0.0)
                all_total = all_total + total * factor
                all_weighted = all_weighted + weighted * factor
            return top, 1.0 / all_total, all_weighted / all_total

        ends = (finish(True), finish(False))

        for t in range(tasks):
            is_low, chunk = task(t)
            half = jnp.where(is_low, 0, 1)
            weights = weights_out[half]
            top, inverse, delta = (jnp.where(is_low, a, b) for a, b in zip(*ends))
            parts = []
            for u in range(KEYS // SUB):
                peak = stats[t * (KEYS // SUB) + u][1]
                factor = jnp.exp(peak - top) * inverse
                probs = stored[t, u * SUB : (u + 1) * SUB, :BLOCK] * factor
                grads = stored[t, u * SUB : (u + 1) * SUB, BLOCK:]
                d_scores = probs * (grads - delta)
                both = jnp.concatenate([probs, d_scores], axis=1).astype(low)
                at = pl.multiple_of(chunk * KEYS + u * SUB, SUB)
                sums[pl.ds(at, SUB), :] += mm(both, weights)
                parts.append(both)
            at = pl.multiple_of(chunk * KEYS, KEYS)
            finals[half] += mm(turned_keys[:, pl.ds(at, KEYS)], jnp.concatenate(parts, axis=0))

        for half in range(2):
            both = jnp.concatenate(
                [finals[half, :HEAD_DIM, :BLOCK], finals[half, HEAD_DIM:, BLOCK:] * score_scale], axis=0
            ).T
            results[i, half * BLOCK : (half + 1) * BLOCK, :] = rotated_back(both, blocks[half]).astype(low)
        return carry

    lax.fori_loop(0, len(places), one_pair, 0)

    for i in range(len(places)):
        out_refs[i][...] = results[i]
    if is_last:
        for r in range(heads):
            for d in range(group):
                for half, block in enumerate(blocks_of(r, d)):
                    at = r * rows + half * BLOCK
                    tile = rotated_back(sums[pl.ds(pl.multiple_of(block * BLOCK, BLOCK), BLOCK), :], block)
                    if d == 0:
                        d_own_ref[at : at + BLOCK, :] = tile
                    else:
                        d_other_ref[d - 1, at : at + BLOCK, :] = tile


def attention(heads, group, places, pair_of, inverse, token, got, other, state):
    is_first, is_last = state is None, places[-1] == heads - 1
    rows = got[0].shape[0]
    owners = pair_of.shape[0]
    total_keys = owners * rows
    tasks = (2 * owners + KEYS // BLOCK) // (KEYS // BLOCK)
    operands = [pair_of, inverse, token, *(got if is_first else [got[r] for r in places])]
    outs = [shape_of((rows, LANES), low)] * len(places)
    if is_first:
        operands += [] if other is None else [other]
    else:
        operands += list(state)
    if is_last:
        outs.append(shape_of((heads * rows, LANES), full))
        if group > 1:
            outs.append(shape_of((group - 1, heads * rows, LANES), full))
    kept = [
        shape_of((total_keys, LANES), low),
        shape_of((LANES, total_keys), low),
        shape_of((total_keys, LANES), full),
    ]
    aliases = {} if is_first else {len(operands) - 3 + i: len(outs) + i for i in range(3)}
    found = pl.pallas_call(
        functools.partial(attention_kernel, heads, group, places, is_first, is_last),
        out_shape=outs + kept,
        in_specs=[spec_smem()] + [spec_vmem()] * (len(operands) - 1),
        out_specs=[spec_vmem()] * (len(outs) + 3),
        input_output_aliases=aliases,
        scratch_shapes=[
            pltpu.VMEM((len(places), rows, LANES), low),
            pltpu.VMEM((2, LANES, 2 * BLOCK), low),
            pltpu.VMEM((2, 2 * BLOCK, LANES), low),
            pltpu.VMEM((tasks, KEYS, 2 * BLOCK), full),
            pltpu.VMEM((2, LANES, 2 * BLOCK), full),
            pltpu.VMEM((len(places), rows, LANES), low),
            pltpu.VMEM((2 * owners, LANES), full),
            pltpu.VMEM((2 * owners, LANES), full),
        ],
        compiler_params=params(8 + total_keys * 2 * KEYS // MIB),
        cost_estimate=pl.CostEstimate(
            flops=3_000_000_000 * len(places), bytes_accessed=2 * MIB, transcendentals=0
        ),
        name="attention",
    )(*operands)
    return found[: len(places)], found[len(places) : len(outs)], found[len(outs) :]


def combine_kernel(heads, terms, *refs):
    rows = refs[0].shape[0] // heads
    for r in range(heads):
        cut = slice(r * rows, (r + 1) * rows)
        total = refs[0][cut, :]
        for term in refs[1:terms]:
            total = total + term[cut, :]
        refs[terms + heads + r][:, :LANES] = refs[terms + r][...]
        refs[terms + heads + r][:, LANES:] = total.astype(low)


def combine(heads, terms, firsts):
    rows = firsts[0].shape[0]
    return pl.pallas_call(
        functools.partial(combine_kernel, heads, len(terms)),
        out_shape=[shape_of((rows, 2 * LANES), low)] * heads,
        in_specs=[spec_vmem()] * (heads + len(terms)),
        out_specs=[spec_vmem()] * heads,
        compiler_params=params(24),
        cost_estimate=pl.CostEstimate(flops=10**7, bytes_accessed=3 * MIB, transcendentals=0),
        name="combine",
    )(*terms, *firsts)


def return_kernel(heads, group, chips, h1_ref, xhat_ref, cot_ref, part_ref, w_qkv_ref, w_out_ref, *rest):
    got_refs = rest[:heads]
    part_low_ref, back_ref, sums_ref, d_b_ref, keep_ref, send_ref, first, second, attended, d_proj, grads = rest[heads:]
    own = lax.axis_index("ctx") // group
    for r in range(heads):
        head = lax.rem(own + r, heads)
        first[head] = got_refs[r][:, :LANES]
        second[head] = got_refs[r][:, LANES:]
    chunk_rows = grads.shape[1]

    def put(at, tile):
        step = min(chunk_rows, tile.shape[0])
        for off in range(0, tile.shape[0], step):
            chunk, inside = divmod(at + off, chunk_rows)
            grads[chunk, inside : inside + step] = tile[off : off + step]

    rows = h1_ref.shape[0]
    left = lane_ids((rows, LANES)) < HEAD_DIM
    for i in range(heads // 2):
        cut = slice(i * LANES, (i + 1) * LANES)
        a, b = first[2 * i].astype(full), first[2 * i + 1].astype(full)
        attended[:, cut] = jnp.where(left, a, pltpu.roll(b, HEAD_DIM, 1)).astype(low)
        d_proj[0, :, cut] = jnp.where(left, pltpu.roll(a, HEAD_DIM, 1), b).astype(low)
        a, b = second[2 * i].astype(full), second[2 * i + 1].astype(full)
        d_proj[2, :, cut] = jnp.where(left, a, pltpu.roll(b, HEAD_DIM, 1)).astype(low)
        d_proj[1, :, cut] = jnp.where(left, pltpu.roll(a, HEAD_DIM, 1), b).astype(low)
    part_low_ref[...] = (part_ref[...] + mm(attended[...], w_out_ref[...])).astype(low)
    back = mm_nt(d_proj[0], w_qkv_ref[0]) + mm_nt(d_proj[1], w_qkv_ref[1]) + mm_nt(d_proj[2], w_qkv_ref[2])
    back_ref[...] = back.astype(low)
    sums_ref[0:1] = jnp.sum(back * xhat_ref[...], axis=0, keepdims=True)
    sums_ref[1:2] = jnp.sum(back, axis=0, keepdims=True)
    h1_turned = turn(h1_ref[...])
    depth, tiles = h1_turned.shape[0], heads // 2
    for s in range(3):
        d_b_ref[s : s + 1] = jnp.sum(d_proj[s].astype(full), axis=0, keepdims=True)
        grad = mm(h1_turned, d_proj[s]).astype(low)
        for t in range(tiles):
            at = (s * tiles + t) * depth
            put(at, grad[:, t * LANES : (t + 1) * LANES])
    grad = mm(turn(attended[...]), cot_ref[...]).astype(low)
    height = grad.shape[0]
    for t in range(depth // LANES):
        at = 3 * tiles * depth + t * height
        put(at, grad[:, t * LANES : (t + 1) * LANES])
    core = lax.rem(lax.axis_index("ctx"), 2)
    keep_ref[...] = grads[pl.ds(core * chips, chips)]
    send_ref[...] = grads[pl.ds((1 - core) * chips, chips)]


def back_projections(heads, group, chips, h1, xhat, cot, part, w_qkv, w_out, got):
    rows, width = h1.shape
    local_width = w_out.shape[0]
    chunk_rows = 4 * width * local_width // LANES // (2 * chips)
    outs = [
        shape_of((rows, width), low),
        shape_of((rows, width), low),
        shape_of((2, width), full),
        shape_of((3, local_width), full),
        shape_of((chips, chunk_rows, LANES), low),
        shape_of((chips, chunk_rows, LANES), low),
    ]
    return pl.pallas_call(
        functools.partial(return_kernel, heads, group, chips),
        out_shape=outs,
        in_specs=[spec_vmem()] * (6 + heads),
        out_specs=[spec_vmem()] * len(outs),
        scratch_shapes=[
            pltpu.VMEM((heads, rows, LANES), low),
            pltpu.VMEM((heads, rows, LANES), low),
            pltpu.VMEM((rows, local_width), low),
            pltpu.VMEM((3, rows, local_width), low),
            pltpu.VMEM((2 * chips, chunk_rows, LANES), low),
        ],
        compiler_params=params(40),
        cost_estimate=pl.CostEstimate(
            flops=16 * rows * width * local_width, bytes_accessed=14 * MIB, transcendentals=0
        ),
        name="back_projections",
    )(h1, xhat, cot, part, w_qkv, w_out, *got)


def finish_kernel(hidden_ref, cot_ref, xhat_ref, std_ref, gains_ref, bias_ref, part_refs, back_refs, next_refs, out_ref, grad_ref):
    gains = gains_ref[...]
    biases = bias_ref[...]
    summed = part_refs[0][...].astype(full) + part_refs[1][...].astype(full)
    out_ref[...] = (hidden_ref[...].astype(full) + summed + biases[0:1] + biases[1:2]).astype(low)
    e1 = back_refs[0][...].astype(full) + back_refs[1][...].astype(full)
    e2 = next_refs[0][...].astype(full) + next_refs[1][...].astype(full)
    f = e1 * gains[0:1] + e2 * gains[1:2]
    xhat = xhat_ref[...]
    inv_std = std_ref[:, 0:1]
    grad_ref[...] = cot_ref[...].astype(full) + inv_std * (
        f - jnp.mean(f, axis=-1, keepdims=True) - xhat * jnp.mean(f * xhat, axis=-1, keepdims=True)
    )


def finish(hidden, cot, xhat, inv_std, gains, biases, parts, backs, nexts):
    rows, width = hidden.shape

    def body(*refs):
        finish_kernel(*refs[:6], refs[6:8], refs[8:10], refs[10:12], *refs[12:])

    return pl.pallas_call(
        body,
        out_shape=[shape_of((rows, width), low), shape_of((rows, width), full)],
        in_specs=[spec_vmem()] * 12,
        out_specs=[spec_vmem()] * 2,
        compiler_params=params(40),
        cost_estimate=pl.CostEstimate(flops=10**7, bytes_accessed=8 * MIB, transcendentals=0),
        name="finish",
    )(hidden, cot, xhat, inv_std, gains, biases, *parts, *backs, *nexts)


def to_attention(width, local_width, source, refs, base, unit):
    qkv_ref, out_ref = refs
    tiles = local_width // LANES
    split = 3 * tiles * width
    tile = base // width
    row = pl.multiple_of(lax.rem(base, width), unit)
    column = pl.multiple_of(lax.rem(tile, tiles) * LANES, LANES)
    yield base < split, source, qkv_ref.at[jnp.minimum(tile // tiles, 2), pl.ds(row, unit), pl.ds(column, LANES)]
    after = jnp.maximum(base - split, 0)
    row = pl.multiple_of(lax.rem(after, local_width), unit)
    column = pl.multiple_of(after // local_width * LANES, LANES)
    yield base >= split, source, out_ref.at[pl.ds(row, unit), pl.ds(column, LANES)]


def to_mlp(width, source, refs, base, unit):
    up_ref, down_ref = refs
    block, inside = base // (2 * width), lax.rem(base, 2 * width)
    block_at = pl.multiple_of(block * LANES, LANES)
    row = pl.multiple_of(jnp.minimum(inside, width - unit), unit)
    yield inside < width, source, up_ref.at[pl.ds(row, unit), pl.ds(block_at, LANES)]
    for t in range(unit // LANES):
        column = pl.multiple_of(jnp.maximum(inside - width, 0) + t * LANES, LANES)
        cut = source.at[pl.ds(t * LANES, LANES), :]
        yield inside >= width, cut, down_ref.at[pl.ds(block_at, LANES), pl.ds(column, LANES)]


def unpack_kernel(route, count, unit, has_old, ids_ref, *rest):
    parts, rest = rest[:count], rest[count:]
    rest = rest[2:] if has_old else rest
    targets, (held, sems) = rest[:2], rest[2:]
    chunk_rows = parts[0].shape[0]
    units = chunk_rows // unit
    per_unit = sems.shape[0] // (count * units)

    def moves():
        for i in range(count):
            for j in range(units):
                source = held.at[i, pl.ds(j * unit, unit), :]
                base = ids_ref[i] * chunk_rows + j * unit
                for n, (applies, piece, target) in enumerate(route(source, targets, base, unit)):
                    sem = sems.at[(i * units + j) * per_unit + n]
                    yield i, applies, pltpu.make_async_copy(piece, target, sem)

    done = -1
    for i, applies, copy in moves():
        if i != done:
            held[i] = parts[i][...].astype(full)
            done = i
        pl.when(applies)(copy.start)
    for i, applies, copy in moves():
        pl.when(applies)(copy.wait)


def unpack(name, route, cases, unit, shapes, ids, parts, old):
    count = len(parts)
    chunk_rows = parts[0].shape[0]
    operands = [ids, *parts, *(old or ())]
    return pl.pallas_call(
        functools.partial(unpack_kernel, route, count, unit, old is not None),
        out_shape=[shape_of(shape, full) for shape in shapes],
        in_specs=[spec_smem()] + [spec_vmem()] * count + [spec_hbm()] * (len(operands) - 1 - count),
        out_specs=[spec_hbm()] * 2,
        input_output_aliases={} if old is None else {1 + count: 0, 2 + count: 1},
        scratch_shapes=[
            pltpu.VMEM((count, chunk_rows, LANES), full),
            pltpu.SemaphoreType.DMA((count * (chunk_rows // unit) * cases,)),
        ],
        compiler_params=params(8 + count * chunk_rows * 3 * LANES * 2 // MIB),
        cost_estimate=pl.CostEstimate(
            flops=10**6, bytes_accessed=count * chunk_rows * LANES * 6, transcendentals=0
        ),
        name=name,
    )(*operands)


def local(
    hidden,
    pair_of,
    ln1_gain,
    ln1_bias,
    ln2_gain,
    ln2_bias,
    w_qkv,
    b_qkv,
    w_out,
    b_out,
    w_up,
    b_up,
    w_down,
    b_down,
    cotangent,
):
    owners = lax.axis_size("ctx")
    sides = lax.axis_size("tp")
    rows, width = hidden.shape
    local_width = w_qkv.shape[2]
    hidden_units = w_up.shape[1]
    heads = local_width // HEAD_DIM
    group = owners // heads

    exponent = np.arange(0, ROT, 2, dtype=np.float32) / np.float32(ROT)
    inverse = jnp.asarray(np.tile(np.float32(10000.0) ** (-exponent), LANES // HALF)[None, :], full)
    order = (0, 2, 4, 6, 7, 5, 3, 1) if owners == 16 else tuple(range(owners // 2))
    chips = len(order)

    (h1, h2, xhat, inv_std, d_bias, gains, biases, b_up_row), sends = project(
        heads,
        group,
        pair_of,
        inverse,
        (hidden, ln1_gain, ln1_bias, ln2_gain, ln2_bias, cotangent, w_out, w_qkv, b_qkv, b_up, b_out, b_down),
    )

    def head_shift(array, r, back=False):
        step = -r if back else r
        pairs = [(c, ((c // group + step) % heads) * group + c % group) for c in range(owners)]
        return lax.ppermute(array, "ctx", pairs)

    def group_shift(array, d):
        pairs = [(c, c // group * group + (c % group + d) % group) for c in range(owners)]
        return lax.ppermute(array, "ctx", pairs)

    got = [sends[0]] + [head_shift(sends[r], r) for r in range(1, heads)]

    me = lax.axis_index("ctx")
    chip, core = me // 2, lax.rem(me, 2)
    place = sum(jnp.where(chip == c, i, 0) for i, c in enumerate(order))
    way = 1 - 2 * core
    far, near = chips // 2, chips - 1 - chips // 2

    def ring(array, forward):
        pairs = []
        for i, c in enumerate(order):
            for k in range(2):
                step = 1 if (k == 0) == forward else -1
                pairs.append((2 * c + k, 2 * order[(i + step) % chips] + k))
        return lax.ppermute(array, "ctx", pairs)

    def other_core(array):
        return lax.ppermute(array, "ctx", [(c, c ^ 1) for c in range(owners)])

    def target(distance):
        return lax.rem(place + way * distance + chips, chips)

    long_way = [far - t for t in range(far)]
    short_way = [t - near for t in range(near)]

    def terms_of(keep, send):
        found = {}
        for distance in sorted(long_way + short_way, key=lambda d: (-(d - 0.5) ** 2, d)) + [0]:
            there = lax.rem(place - way * distance + chips, chips)
            came = other_core(lax.dynamic_index_in_dim(send, there, 0, keepdims=False)).astype(full)
            found[distance] = came + lax.dynamic_index_in_dim(keep, target(distance), 0, keepdims=False).astype(full)
        return found

    def scatter_start(terms, token=None):
        after = 0.0 if token is None else token
        return (terms[far] + after).astype(low), (terms[-near] + after).astype(low)

    def scatter_step(terms, t, sends, token=None):
        long_send, short_send = sends
        long_got = ring(long_send, True).astype(full)
        if token is not None:
            long_got = long_got + token
        last = t == far - 1
        long_next = long_got if last else (long_got + terms[far - 1 - t]).astype(low)
        short_next = short_send
        if t < near:
            short_got = ring(short_send, False).astype(full)
            if token is not None:
                short_got = short_got + token
            short_next = short_got if t == near - 1 else (short_got + terms[t + 1 - near]).astype(low)
        if last:
            return (terms[0] + long_next + short_next).astype(low)
        return long_next, short_next

    def gather(own):
        base, other_base = core * chips, (1 - core) * chips
        found = [(own, base + place), (other_core(own), other_base + place)]
        long_part = short_part = own
        for t in range(far):
            long_part = ring(long_part, True)
            found.append((long_part, base + target(-t - 1)))
            found.append((other_core(long_part), other_base + target(t + 1)))
            if t < near:
                short_part = ring(short_part, False)
                found.append((short_part, base + target(t + 1)))
                found.append((other_core(short_part), other_base + target(-t - 1)))
        return found

    part, back2, sums2, d_b_up, keep_mlp, send_mlp = mlp(
        core[None], h2, cotangent, xhat, w_up, b_up_row, w_down
    )
    terms_mlp = terms_of(keep_mlp.reshape(chips, -1, LANES), send_mlp.reshape(chips, -1, LANES))

    other = None
    if group > 1:
        mine = jnp.concatenate([array[:, LANES:] for array in got], axis=0)
        other = jnp.stack([group_shift(mine, group - d) for d in range(1, group)])

    cuts = (0, 1, 4, heads)
    firsts, state, token = [], None, sums2
    for t in range(3):
        found, ends, state = attention(
            heads, group, tuple(range(cuts[t], cuts[t + 1])), pair_of, inverse, token, got, other, state
        )
        firsts += found
        after = found[0][0, 0].astype(full) * 0.0
        if t == 0:
            sends_mlp = scatter_start(terms_mlp, after)
        elif t == 1:
            sends_mlp = scatter_step(terms_mlp, 0, sends_mlp, after)
        token = sends_mlp[0][:16] + sends_mlp[1][:16]
    d_own, d_other = ends[0], (ends[1] if group > 1 else None)
    terms = [d_own] + [group_shift(d_other[d - 1], d) for d in range(1, group)]
    backs = combine(heads, terms, firsts)
    backs = [backs[0]] + [head_shift(backs[r], r, True) for r in range(1, heads)]
    for t in range(1, far - 1):
        sends_mlp = scatter_step(terms_mlp, t, sends_mlp)
    own_mlp = scatter_step(terms_mlp, far - 1, sends_mlp)
    parts_mlp = gather(own_mlp)

    part_low, back1, sums1, d_b_qkv, keep, send = back_projections(
        heads, group, chips, h1, xhat, cotangent, part, w_qkv, w_out, backs
    )

    def across(array):
        return lax.ppermute(array, "tp", [(t, (t + 1) % sides) for t in range(sides)])

    output, d_hidden = finish(
        hidden,
        cotangent,
        xhat,
        inv_std,
        gains,
        biases,
        (part_low, across(part_low)),
        (back1, across(back1)),
        (back2, across(back2)),
    )

    terms_att = terms_of(keep, send)
    sends_att = scatter_start(terms_att)
    for t in range(far - 1):
        sends_att = scatter_step(terms_att, t, sends_att)
    own_att = scatter_step(terms_att, far - 1, sends_att, output[0, 0].astype(full) * 0.0)
    parts_att = gather(own_att)

    small = jnp.concatenate(
        [sums1.reshape(1, -1), sums2.reshape(1, -1), d_bias, d_b_up, d_b_qkv.reshape(1, -1)], axis=1
    )
    small = small + own_att[0, 0].astype(full) * 0.0
    step = 1
    while step < owners:
        small = small + lax.ppermute(small, "ctx", [(c, c ^ step) for c in range(owners)])
        step *= 2
    norm_sums = small[:, : 4 * width]
    norm_sums = (norm_sums + across(norm_sums)).reshape(4, width)
    at = 4 * width
    d_bias = small[0, at : at + width]
    d_b_up = small[0, at + width : at + width + hidden_units]
    d_b_qkv = small[0, at + width + hidden_units :].reshape(3, local_width)

    def unpacked(name, route, cases, unit, shapes, found, pieces):
        old = None
        per_piece = -(-len(found) // pieces)
        for i in range(0, len(found), per_piece):
            parts, ids = zip(*found[i : i + per_piece])
            old = unpack(name, route, cases, unit, shapes, jnp.stack(ids), parts, old)
        return old

    unit = min(parts_mlp[0][0].shape[0], local_width)
    d_w_up, d_w_down = unpacked(
        "unpack_feed_forward",
        functools.partial(to_mlp, width),
        1 + unit // LANES,
        unit,
        ((width, hidden_units), (hidden_units, width)),
        parts_mlp,
        4,
    )
    unit = min(parts_att[0][0].shape[0], local_width)
    d_w_qkv, d_w_out = unpacked(
        "unpack_attention",
        functools.partial(to_attention, width, local_width),
        2,
        unit,
        ((3, width, local_width), (local_width, width)),
        parts_att,
        2,
    )
    return (
        output,
        d_hidden,
        norm_sums[0],
        norm_sums[1],
        norm_sums[2],
        norm_sums[3],
        d_w_qkv,
        d_b_qkv,
        d_w_out,
        d_bias,
        d_w_up,
        d_b_up,
        d_w_down,
        d_bias,
    )


def solution(mesh):
    placed = (
        P("ctx", None),
        P(),
        P(),
        P(),
        P(),
        P(),
        P(None, None, "tp"),
        P(None, "tp"),
        P("tp", None),
        P(),
        P(None, "tp"),
        P("tp"),
        P("tp", None),
        P(),
        P("ctx", None),
    )
    return jax.shard_map(
        local,
        mesh=mesh,
        in_specs=placed,
        out_specs=(
            P("ctx", None),
            P("ctx", None),
            P(),
            P(),
            P(),
            P(),
            P(None, None, "tp"),
            P(None, "tp"),
            P("tp", None),
            P(),
            P(None, "tp"),
            P("tp"),
            P("tp", None),
            P(),
        ),
        check_vma=False,
    )
```

```python
import functools

import jax
import jax.numpy as jnp
import numpy as np
from jax import lax
from jax.experimental import pallas as pl
from jax.experimental.pallas import tpu as pltpu
from jax.sharding import PartitionSpec as P

HEAD_DIM = 64
ROT = 16
HALF = ROT // 2
BLOCK = 128
LANES = 128
KEYS = 512
MIB = 1 << 20

norm_eps = 1e-05
masked_score = -1e30
score_scale = HEAD_DIM ** (-0.5)
low = jnp.bfloat16
full = jnp.float32


def mm(left, right):
    return lax.dot_general(left, right, (((1,), (0,)), ((), ())), preferred_element_type=full)


def mm_nt(left, right):
    return lax.dot_general(left, right, (((1,), (1,)), ((), ())), preferred_element_type=full)


def turn(tensor):
    return tensor.astype(full).T.astype(low)


def lane_ids(shape):
    return lax.broadcasted_iota(jnp.int32, shape, len(shape) - 1)


def row_ids(shape):
    return lax.broadcasted_iota(jnp.int32, shape, len(shape) - 2)


def rotary_partner(tensor):
    lanes = lane_ids(tensor.shape)
    ahead = pltpu.roll(tensor, LANES - HALF, 1)
    behind = pltpu.roll(tensor, HALF, 1)
    return jnp.where(lanes % ROT < HALF, ahead, behind)


def spec_vmem():
    return pl.BlockSpec(memory_space=pltpu.VMEM)


def spec_smem():
    return pl.BlockSpec(memory_space=pltpu.SMEM)


def spec_hbm():
    return pl.BlockSpec(memory_space=pltpu.HBM)


def params(mib):
    return pltpu.CompilerParams(vmem_limit_bytes=mib * MIB)


def shape_of(shape, kind):
    return jax.ShapeDtypeStruct(shape, kind)


def block_tables(inverse, blocks):
    row = row_ids((BLOCK, LANES)).astype(full)
    start = blocks.astype(full) * float(BLOCK)
    return jnp.cos(row * inverse), jnp.sin(row * inverse), jnp.cos(start * inverse), jnp.sin(start * inverse)


def project_kernel(heads, group, pair_ref, inv_ref, *rest):
    given, rest = rest[:12], rest[12:]
    h1_ref, h2_ref, xhat_ref, std_ref, d_bias_ref, gains_ref, bias_ref, b_up_out_ref = rest[:8]
    send_refs = rest[8 : 8 + heads]
    packed, held, sems = rest[8 + heads], rest[9 + heads : -1], rest[-1]
    copies = [pltpu.make_async_copy(src, dst, sems.at[i]) for i, (src, dst) in enumerate(zip(given, held))]
    for copy in copies:
        copy.start()
    (
        hidden_ref,
        g1_ref,
        c1_ref,
        g2_ref,
        c2_ref,
        cot_ref,
        w_out_ref,
        w_qkv_ref,
        b_qkv_ref,
        b_up_ref,
        b_out_ref,
        b_down_ref,
    ) = held
    rows = hidden_ref.shape[0]
    me = lax.axis_index("ctx")
    pair = pair_ref[me]
    total_blocks = 2 * pair_ref.shape[0]

    first = jnp.where(row_ids((8, LANES)) == 0, pair, total_blocks - 1 - pair)
    inverse = inv_ref[...]
    cos_row, sin_row, cos_block, sin_block = block_tables(inverse, first)
    in_head = lane_ids((BLOCK, LANES)) % HEAD_DIM
    tables = []
    for half in range(2):
        cos_at, sin_at = cos_block[half : half + 1], sin_block[half : half + 1]
        cosine = cos_row * cos_at - sin_row * sin_at
        sine = sin_row * cos_at + cos_row * sin_at
        cosine = jnp.where(in_head < ROT, cosine, 1.0)
        sine = jnp.where(in_head < HALF, -sine, jnp.where(in_head < ROT, sine, 0.0))
        tables.append((cosine, sine))
    cosine = jnp.concatenate([tables[0][0], tables[1][0]], axis=0)
    sine = jnp.concatenate([tables[0][1], tables[1][1]], axis=0)

    for copy in copies[:5]:
        copy.wait()
    x = hidden_ref[...].astype(full)
    centred = x - jnp.mean(x, axis=-1, keepdims=True)
    spread = jnp.mean(centred * centred, axis=-1, keepdims=True)
    inv_std = lax.rsqrt(spread + norm_eps)
    xhat = centred * inv_std
    xhat_ref[...] = xhat
    std_ref[...] = jnp.broadcast_to(inv_std, std_ref.shape)

    def as_row(ref):
        return ref[...].astype(full)[None, :]

    gain1, gain2 = as_row(g1_ref), as_row(g2_ref)
    h1 = (xhat * gain1 + as_row(c1_ref)).astype(low)
    h1_ref[...] = h1
    h2_ref[...] = (xhat * gain2 + as_row(c2_ref)).astype(low)
    gains_ref[0:1] = gain1
    gains_ref[1:2] = gain2
    for copy in copies[5:]:
        copy.wait()
    b_up_out_ref[...] = as_row(b_up_ref)
    bias_ref[0:1] = as_row(b_out_ref)
    bias_ref[1:2] = as_row(b_down_ref)
    d_bias_ref[...] = jnp.sum(cot_ref[...].astype(full), axis=0, keepdims=True)

    lane = lane_ids((rows, LANES))

    def projected(s):
        return mm(h1, w_qkv_ref[s]) + b_qkv_ref[s : s + 1].astype(full)

    def turned(tile):
        return tile * cosine + rotary_partner(tile) * sine

    queries, keys, values = projected(0), projected(1), projected(2)
    grads = mm_nt(cot_ref[...], w_out_ref[...])
    left = lane < HEAD_DIM
    for i in range(heads // 2):
        cut = slice(i * LANES, (i + 1) * LANES)
        q = turned(queries[:, cut]).astype(low).astype(full) * score_scale
        k = turned(keys[:, cut])
        v = values[:, cut]
        g = grads[:, cut]
        packed[2 * i, :, :LANES] = jnp.where(left, g, pltpu.roll(q, HEAD_DIM, 1)).astype(low)
        packed[2 * i, :, LANES:] = jnp.where(left, v, pltpu.roll(k, HEAD_DIM, 1)).astype(low)
        packed[2 * i + 1, :, :LANES] = jnp.where(left, pltpu.roll(g, HEAD_DIM, 1), q).astype(low)
        packed[2 * i + 1, :, LANES:] = jnp.where(left, pltpu.roll(v, HEAD_DIM, 1), k).astype(low)
    own = me // group
    for r in range(heads):
        send_refs[r][...] = packed[lax.rem(own + r, heads)]


def project(heads, group, pair_of, inverse, given):
    hidden, w_out, b_up = given[0], given[6], given[9]
    rows, width = hidden.shape
    outs = [
        shape_of((rows, width), low),
        shape_of((rows, width), low),
        shape_of((rows, width), full),
        shape_of((rows, LANES), full),
        shape_of((1, width), full),
        shape_of((2, width), full),
        shape_of((2, width), full),
        shape_of((1, b_up.shape[0]), full),
    ] + [shape_of((rows, 2 * LANES), low)] * heads
    found = pl.pallas_call(
        functools.partial(project_kernel, heads, group),
        out_shape=outs,
        in_specs=[spec_smem(), spec_vmem()] + [spec_hbm()] * len(given),
        out_specs=[spec_vmem()] * len(outs),
        scratch_shapes=[pltpu.VMEM((heads, rows, 2 * LANES), low)]
        + [pltpu.VMEM(array.shape, array.dtype) for array in given]
        + [pltpu.SemaphoreType.DMA((len(given),))],
        compiler_params=params(60),
        cost_estimate=pl.CostEstimate(
            flops=2 * rows * width * 4 * w_out.shape[0], bytes_accessed=8 * MIB, transcendentals=0
        ),
        name="project",
    )(pair_of, inverse, *given)
    return found[:8], found[8:]


def mlp_kernel(
    early,
    ids_ref,
    h2_ref,
    cot_ref,
    xhat_ref,
    up_keep_ref,
    up_send_ref,
    b_keep_ref,
    b_send_ref,
    down_keep_ref,
    down_send_ref,
    part_ref,
    back_ref,
    sums_ref,
    d_b_up_ref,
    keep_ref,
    early_ref,
    send_ref,
    h2_turned,
    part_acc,
    back_acc,
):
    step = pl.program_id(0)
    steps = pl.num_programs(0)

    @pl.when(step == 0)
    def _():
        h2_turned[...] = turn(h2_ref[...])
        part_acc[...] = jnp.zeros_like(part_acc)
        back_acc[...] = jnp.zeros_like(back_acc)

    cot = cot_ref[...]
    w_up = jnp.concatenate([up_keep_ref[...], up_send_ref[...]], axis=1)
    w_down = jnp.concatenate([down_keep_ref[...], down_send_ref[...]], axis=0)
    u = mm(h2_ref[...], w_up) + jnp.concatenate([b_keep_ref[...], b_send_ref[...]], axis=1)
    cdf = 0.5 * (1.0 + lax.erf(u * np.float32(np.sqrt(0.5))))
    active = u * cdf
    active_low = active.astype(low)
    slope = cdf + u * jnp.exp(-0.5 * u * u) * np.float32(1.0 / np.sqrt(2.0 * np.pi))
    du = (mm_nt(cot, w_down) * slope).astype(low)
    part_acc[...] += mm(active_low, w_down)
    back_acc[...] += mm_nt(du, w_up)
    d_b_up = jnp.sum(du.astype(full), axis=0, keepdims=True)
    up = mm(h2_turned[...], du).astype(low)
    down = mm(active.T.astype(low), cot).astype(low)
    depth = up.shape[0]

    def put(b, grad_ref):
        grad_ref[:depth] = up[:, b * LANES : (b + 1) * LANES]
        for t in range(down.shape[1] // LANES):
            grad_ref[depth + t * LANES : depth + (t + 1) * LANES] = down[
                b * LANES : (b + 1) * LANES, t * LANES : (t + 1) * LANES
            ]

    for b in range(2):
        at = pl.multiple_of(ids_ref[b * steps + step] * LANES, LANES)
        d_b_up_ref[:, pl.ds(at, LANES)] = d_b_up[:, b * LANES : (b + 1) * LANES]
    put(0, keep_ref)

    @pl.when(step < early)
    def _():
        put(1, early_ref)

    @pl.when(step >= early)
    def _():
        put(1, send_ref)

    @pl.when(step == steps - 1)
    def _():
        part_ref[...] = part_acc[...]
        back = back_acc[...]
        back_ref[...] = back.astype(low)
        sums_ref[0:1] = jnp.sum(back * xhat_ref[...], axis=0, keepdims=True)
        sums_ref[1:2] = jnp.sum(back, axis=0, keepdims=True)


def mlp(ids, early, h2, cot, xhat, w_up, b_up, w_down):
    rows, width = h2.shape
    hidden_units = w_up.shape[1]
    steps = hidden_units // LANES // 2
    whole = lambda shape: pl.BlockSpec(shape, lambda f, c: (0,) * len(shape))
    kept = lambda f, c: c[f]
    sent = lambda f, c: c[steps + f]
    columns = lambda height, at: pl.BlockSpec((height, LANES), lambda f, c: (0, at(f, c)))
    flat = lambda at: pl.BlockSpec((LANES, width), lambda f, c: (at(f, c), 0))
    grads = lambda at: pl.BlockSpec((2 * width, LANES), lambda f, c: (at(f), 0))
    outs = [
        shape_of((rows, width), full),
        shape_of((rows, width), low),
        shape_of((2, width), full),
        shape_of((1, hidden_units), full),
        shape_of((steps * 2 * width, LANES), low),
        shape_of((early * 2 * width, LANES), low),
        shape_of(((steps - early) * 2 * width, LANES), low),
    ]
    return pl.pallas_call(
        functools.partial(mlp_kernel, early),
        grid_spec=pltpu.PrefetchScalarGridSpec(
            num_scalar_prefetch=1,
            grid=(steps,),
            in_specs=[
                whole((rows, width)),
                whole((rows, width)),
                whole((rows, width)),
                columns(width, kept),
                columns(width, sent),
                columns(1, kept),
                columns(1, sent),
                flat(kept),
                flat(sent),
            ],
            out_specs=[
                whole((rows, width)),
                whole((rows, width)),
                whole((2, width)),
                whole((1, hidden_units)),
                grads(lambda f: f),
                grads(lambda f: jnp.minimum(f, early - 1)),
                grads(lambda f: jnp.maximum(f - early, 0)),
            ],
            scratch_shapes=[
                pltpu.VMEM((width, rows), low),
                pltpu.VMEM((rows, width), full),
                pltpu.VMEM((rows, width), full),
            ],
        ),
        out_shape=outs,
        compiler_params=params(60),
        cost_estimate=pl.CostEstimate(
            flops=12 * rows * width * hidden_units, bytes_accessed=20 * MIB, transcendentals=0
        ),
        name="feed_forward",
    )(ids, h2, cot, xhat, w_up, w_up, b_up, b_up, w_down, w_down)


def attention_kernel(heads, group, places, is_first, is_last, pair_ref, inv_ref, token_ref, *rest):
    del token_ref
    if is_first:
        got_refs, rest = rest[:heads], rest[heads:]
        if group > 1:
            other_ref, rest = rest[0], rest[1:]
    else:
        rest = rest[4:]
    out_refs, rest = rest[: len(places)], rest[len(places) :]
    if is_last:
        d_own_ref, rest = rest[0], rest[1:]
        if group > 1:
            d_other_ref, rest = rest[0], rest[1:]
    (values_keys, turned_keys, sums, queries), rest = rest[:4], rest[4:]
    token_out, rest = rest[0], rest[1:]
    weights_in, weights_out, stored, packed, finals, results, block_cos, block_sin = rest
    token_out[...] = jnp.zeros_like(token_out)

    rows = queries.shape[1]
    owners = pair_ref.shape[0]
    total_blocks = 2 * owners
    per_chunk = KEYS // BLOCK
    tasks = (total_blocks + 1 + per_chunk - 1) // per_chunk
    me = lax.axis_index("ctx")
    own_head = me // group
    own_sub = lax.rem(me, group)

    def blocks_of(r, d):
        owner = lax.rem(own_head - r + heads, heads) * group + lax.rem(own_sub + d, group)
        pair = pair_ref[owner]
        return pair, total_blocks - 1 - pair

    def place(tile, block):
        at = pl.multiple_of(block * BLOCK, BLOCK)
        values_keys[pl.ds(at, BLOCK), :] = tile
        turned_keys[:, pl.ds(at, BLOCK)] = turn(tile)

    if is_first:
        for r in range(heads):
            queries[r] = got_refs[r][:, :LANES]
            for half, block in enumerate(blocks_of(r, 0)):
                place(got_refs[r][half * BLOCK : (half + 1) * BLOCK, LANES:], block)
            for d in range(1, group):
                for half, block in enumerate(blocks_of(r, d)):
                    at = r * rows + half * BLOCK
                    place(other_ref[d - 1, at : at + BLOCK, :], block)
        sums[...] = jnp.zeros_like(sums)

    lane = lane_ids((BLOCK, LANES))
    left = lane < HEAD_DIM
    in_key = lane - HEAD_DIM
    moving = (in_key >= 0) & (in_key < ROT)
    forward = (in_key >= 0) & (in_key < HALF)
    cos_row, sin_row, block_cos[...], block_sin[...] = block_tables(inv_ref[...], row_ids(block_cos.shape))

    def rotated_back(tile, block):
        cos_at, sin_at = block_cos[pl.ds(block, 1), :], block_sin[pl.ds(block, 1), :]
        cosine = jnp.where(moving, cos_row * cos_at - sin_row * sin_at, 1.0)
        sine = sin_row * cos_at + cos_row * sin_at
        sine = jnp.where(moving, jnp.where(forward, sine, -sine), 0.0)
        return tile * cosine + rotary_partner(tile) * sine

    offset = row_ids((BLOCK, BLOCK)) - lane_ids((BLOCK, BLOCK))

    def one_pair(i, carry):
        blocks = blocks_of(places[0] + i, 0)
        first = blocks[0] // per_chunk + 1
        for half in range(2):
            both = queries[places[0] + i, half * BLOCK : (half + 1) * BLOCK, :]
            both_turned = turn(both)
            upper = row_ids((LANES, BLOCK)) < HEAD_DIM
            zero = jnp.zeros_like(both_turned)
            weights_in[half, :, :BLOCK] = jnp.where(upper, both_turned, zero)
            weights_in[half, :, BLOCK:] = jnp.where(upper, zero, both_turned)
            weights_out[half, :BLOCK, :] = jnp.where(left, both, zero)
            weights_out[half, BLOCK:, :] = jnp.where(left, zero, both)
        finals[...] = jnp.zeros_like(finals)

        def task(t):
            is_low = t < first
            chunk = jnp.where(is_low, first - 1 - t, t - first)
            return is_low, chunk

        subs = [slice(u * BLOCK, (u + 1) * BLOCK) for u in range(per_chunk)]
        stats = []
        for t in range(tasks):
            is_low, chunk = task(t)
            at = pl.multiple_of(chunk * KEYS, KEYS)
            stored[t] = mm(values_keys[pl.ds(at, KEYS), :], weights_in[jnp.where(is_low, 0, 1)])
            top = jnp.full((8, BLOCK), masked_score, full)
            for u, sub in enumerate(subs):
                scores = stored[t, sub, BLOCK:]
                if t in (0, tasks - 1):
                    query_at = blocks[0 if t == 0 else 1] * BLOCK
                    scores = jnp.where(offset <= query_at - at - u * BLOCK, scores, masked_score)
                    stored[t, sub, BLOCK:] = scores
                for v in range(BLOCK // 8):
                    top = jnp.maximum(top, scores[v * 8 : v * 8 + 8])
            peak = jnp.max(top, axis=0, keepdims=True)
            total = jnp.zeros((8, BLOCK), full)
            weighted = jnp.zeros((8, BLOCK), full)
            for sub in subs:
                raised = jnp.exp(stored[t, sub, BLOCK:] - peak)
                stored[t, sub, BLOCK:] = raised
                product = raised * stored[t, sub, :BLOCK]
                for v in range(BLOCK // 8):
                    total = total + raised[v * 8 : v * 8 + 8]
                    weighted = weighted + product[v * 8 : v * 8 + 8]
            stats.append((is_low, peak, jnp.sum(total, axis=0, keepdims=True), jnp.sum(weighted, axis=0, keepdims=True)))

        def finish(wanted):
            top = jnp.full((1, BLOCK), masked_score, full)
            for is_low, peak, total, weighted in stats:
                top = jnp.maximum(top, jnp.where(is_low == wanted, peak, masked_score))
            all_total = jnp.zeros((1, BLOCK), full)
            all_weighted = jnp.zeros((1, BLOCK), full)
            for is_low, peak, total, weighted in stats:
                factor = jnp.where(is_low == wanted, jnp.exp(peak - top), 0.0)
                all_total = all_total + total * factor
                all_weighted = all_weighted + weighted * factor
            return top, 1.0 / all_total, all_weighted / all_total

        ends = (finish(True), finish(False))

        for t in range(tasks):
            is_low, chunk = task(t)
            half = jnp.where(is_low, 0, 1)
            top, inverse, delta = (jnp.where(is_low, a, b) for a, b in zip(*ends))
            factor = jnp.exp(stats[t][1] - top) * inverse
            slot = t % packed.shape[0]
            for sub in subs:
                probs = stored[t, sub, BLOCK:] * factor
                d_scores = probs * (stored[t, sub, :BLOCK] - delta)
                packed[slot, sub, :BLOCK] = probs.astype(low)
                packed[slot, sub, BLOCK:] = d_scores.astype(low)
            at = pl.multiple_of(chunk * KEYS, KEYS)
            sums[pl.ds(at, KEYS), :] += mm(packed[slot], weights_out[half])
            finals[half] += mm(turned_keys[:, pl.ds(at, KEYS)], packed[slot])

        for half in range(2):
            both = jnp.concatenate(
                [finals[half, :HEAD_DIM, :BLOCK], finals[half, HEAD_DIM:, BLOCK:] * score_scale], axis=0
            ).T
            results[i, half * BLOCK : (half + 1) * BLOCK, :] = rotated_back(both, blocks[half]).astype(low)
        return carry

    lax.fori_loop(0, len(places), one_pair, 0)

    for i in range(len(places)):
        out_refs[i][...] = results[i]
    if is_last:
        for r in range(heads):
            for d in range(group):
                for half, block in enumerate(blocks_of(r, d)):
                    at = r * rows + half * BLOCK
                    tile = rotated_back(sums[pl.ds(pl.multiple_of(block * BLOCK, BLOCK), BLOCK), :], block)
                    if d == 0:
                        d_own_ref[at : at + BLOCK, :] = tile
                    else:
                        d_other_ref[d - 1, at : at + BLOCK, :] = tile


def attention(heads, group, places, pair_of, inverse, token, got, other, state):
    is_first, is_last = state is None, places[-1] == heads - 1
    rows = got[0].shape[0]
    owners = pair_of.shape[0]
    total_keys = owners * rows
    tasks = (2 * owners + KEYS // BLOCK) // (KEYS // BLOCK)
    operands = [pair_of, inverse, token]
    outs = [shape_of((rows, LANES), low)] * len(places)
    if is_first:
        operands += [*got] if other is None else [*got, other]
    else:
        operands += list(state)
    if is_last:
        outs.append(shape_of((heads * rows, LANES), full))
        if group > 1:
            outs.append(shape_of((group - 1, heads * rows, LANES), full))
    kept = [
        shape_of((total_keys, LANES), low),
        shape_of((LANES, total_keys), low),
        shape_of((total_keys, LANES), full),
        shape_of((heads, rows, LANES), low),
    ]
    aliases = {} if is_first else {len(operands) - 4 + i: len(outs) + i for i in range(4)}
    found = pl.pallas_call(
        functools.partial(attention_kernel, heads, group, places, is_first, is_last),
        out_shape=outs + kept + [shape_of((1, LANES), full)],
        in_specs=[spec_smem()] + [spec_vmem()] * (len(operands) - 1),
        out_specs=[spec_vmem()] * (len(outs) + 5),
        input_output_aliases=aliases,
        scratch_shapes=[
            pltpu.VMEM((2, LANES, 2 * BLOCK), low),
            pltpu.VMEM((2, 2 * BLOCK, LANES), low),
            pltpu.VMEM((tasks, KEYS, 2 * BLOCK), full),
            pltpu.VMEM((3, KEYS, 2 * BLOCK), low),
            pltpu.VMEM((2, LANES, 2 * BLOCK), full),
            pltpu.VMEM((len(places), rows, LANES), low),
            pltpu.VMEM((2 * owners, LANES), full),
            pltpu.VMEM((2 * owners, LANES), full),
        ],
        compiler_params=params(8 + total_keys * 2 * KEYS // MIB),
        cost_estimate=pl.CostEstimate(
            flops=2_500_000_000 * len(places), bytes_accessed=2 * MIB, transcendentals=0
        ),
        name="attention",
    )(*operands)
    n = len(places)
    return found[:n], found[n : len(outs)], found[len(outs) : len(outs) + 4], found[-1]


def combine_kernel(heads, terms, *refs):
    rows = refs[0].shape[0] // heads
    for r in range(heads):
        cut = slice(r * rows, (r + 1) * rows)
        total = refs[0][cut, :]
        for term in refs[1:terms]:
            total = total + term[cut, :]
        refs[terms + heads + r][:, :LANES] = refs[terms + r][...]
        refs[terms + heads + r][:, LANES:] = total.astype(low)


def combine(heads, terms, firsts):
    rows = firsts[0].shape[0]
    return pl.pallas_call(
        functools.partial(combine_kernel, heads, len(terms)),
        out_shape=[shape_of((rows, 2 * LANES), low)] * heads,
        in_specs=[spec_vmem()] * (heads + len(terms)),
        out_specs=[spec_vmem()] * heads,
        compiler_params=params(24),
        cost_estimate=pl.CostEstimate(flops=10**7, bytes_accessed=3 * MIB, transcendentals=0),
        name="combine",
    )(*terms, *firsts)


def return_kernel(heads, group, early, ids_ref, *rest):
    given, rest = rest[: 6 + heads], rest[6 + heads :]
    both_ref, sums_ref, d_b_ref, keep_ref, early_ref, send_ref = rest[:6]
    first, second, attended, d_proj, grads = rest[6:11]
    held, sems = rest[11:-1], rest[-1]
    copies = [pltpu.make_async_copy(src, dst, sems.at[i]) for i, (src, dst) in enumerate(zip(given, held))]
    for copy in copies[6:] + copies[:6]:
        copy.start()
    w_out_ref, w_qkv_ref, part_ref, h1_ref, xhat_ref, cot_ref, *got_refs = held
    own = lax.axis_index("ctx") // group
    for r in range(heads):
        head = lax.rem(own + r, heads)
        copies[6 + r].wait()
        first[head] = got_refs[r][:, :LANES]
        second[head] = got_refs[r][:, LANES:]
    chunk_rows = grads.shape[1]
    chips = keep_ref.shape[0]

    def put(at, tile):
        step = min(chunk_rows, tile.shape[0])
        for off in range(0, tile.shape[0], step):
            chunk, inside = divmod(at + off, chunk_rows)
            grads[chunk, inside : inside + step] = tile[off : off + step]

    rows = h1_ref.shape[0]
    left = lane_ids((rows, LANES)) < HEAD_DIM
    for i in range(heads // 2):
        cut = slice(i * LANES, (i + 1) * LANES)
        a, b = first[2 * i].astype(full), first[2 * i + 1].astype(full)
        attended[:, cut] = jnp.where(left, a, pltpu.roll(b, HEAD_DIM, 1)).astype(low)
        d_proj[0, :, cut] = jnp.where(left, pltpu.roll(a, HEAD_DIM, 1), b).astype(low)
        a, b = second[2 * i].astype(full), second[2 * i + 1].astype(full)
        d_proj[2, :, cut] = jnp.where(left, a, pltpu.roll(b, HEAD_DIM, 1)).astype(low)
        d_proj[1, :, cut] = jnp.where(left, pltpu.roll(a, HEAD_DIM, 1), b).astype(low)
    for copy in copies[:6]:
        copy.wait()
    both_ref[:rows] = (part_ref[...] + mm(attended[...], w_out_ref[...])).astype(low)
    back = mm_nt(d_proj[0], w_qkv_ref[0]) + mm_nt(d_proj[1], w_qkv_ref[1]) + mm_nt(d_proj[2], w_qkv_ref[2])
    both_ref[rows:] = back.astype(low)
    sums_ref[0:1] = jnp.sum(back * xhat_ref[...], axis=0, keepdims=True)
    sums_ref[1:2] = jnp.sum(back, axis=0, keepdims=True)
    h1_turned = turn(h1_ref[...])
    depth, tiles = h1_turned.shape[0], heads // 2
    for s in range(3):
        d_b_ref[s : s + 1] = jnp.sum(d_proj[s].astype(full), axis=0, keepdims=True)
        grad = mm(h1_turned, d_proj[s]).astype(low)
        for t in range(tiles):
            put((s * tiles + t) * depth, grad[:, t * LANES : (t + 1) * LANES])
    grad = mm(turn(attended[...]), cot_ref[...]).astype(low)
    height = grad.shape[0]
    for t in range(depth // LANES):
        put(3 * tiles * depth + t * height, grad[:, t * LANES : (t + 1) * LANES])
    for t in range(chips):
        keep_ref[t] = grads[ids_ref[t]]
        target = early_ref.at[t] if t < early else send_ref.at[t - early]
        target[...] = grads[ids_ref[chips + t]]


def back_projections(heads, group, early, ids, w_out, w_qkv, part, h1, xhat, cot, got):
    rows, width = h1.shape
    local_width = w_out.shape[0]
    chips = ids.shape[0] // 2
    chunk_rows = 4 * width * local_width // LANES // (2 * chips)
    given = (w_out, w_qkv, part, h1, xhat, cot, *got)
    outs = [
        shape_of((2 * rows, width), low),
        shape_of((2, width), full),
        shape_of((3, local_width), full),
        shape_of((chips, chunk_rows, LANES), low),
        shape_of((early, chunk_rows, LANES), low),
        shape_of((chips - early, chunk_rows, LANES), low),
    ]
    return pl.pallas_call(
        functools.partial(return_kernel, heads, group, early),
        out_shape=outs,
        in_specs=[spec_smem()] + [spec_hbm()] * len(given),
        out_specs=[spec_vmem()] * len(outs),
        scratch_shapes=[
            pltpu.VMEM((heads, rows, LANES), low),
            pltpu.VMEM((heads, rows, LANES), low),
            pltpu.VMEM((rows, local_width), low),
            pltpu.VMEM((3, rows, local_width), low),
            pltpu.VMEM((2 * chips, chunk_rows, LANES), low),
        ]
        + [pltpu.VMEM(array.shape, array.dtype) for array in given]
        + [pltpu.SemaphoreType.DMA((len(given),))],
        compiler_params=params(60),
        cost_estimate=pl.CostEstimate(
            flops=16 * rows * width * local_width, bytes_accessed=14 * MIB, transcendentals=0
        ),
        name="back_projections",
    )(ids, *given)


def finish_kernel(
    hidden_ref, cot_ref, xhat_ref, std_ref, gains_ref, bias_ref, ours_ref, theirs_ref, e2_ours_ref, e2_theirs_ref, out_ref, grad_ref, token_ref
):
    rows = hidden_ref.shape[0]
    gains = gains_ref[...]
    biases = bias_ref[...]
    summed = ours_ref[:rows].astype(full) + theirs_ref[:rows].astype(full)
    out_ref[...] = (hidden_ref[...].astype(full) + summed + biases[0:1] + biases[1:2]).astype(low)
    e1 = ours_ref[rows:].astype(full) + theirs_ref[rows:].astype(full)
    e2 = e2_ours_ref[...].astype(full) + e2_theirs_ref[...].astype(full)
    f = e1 * gains[0:1] + e2 * gains[1:2]
    xhat = xhat_ref[...]
    inv_std = std_ref[:, 0:1]
    grad_ref[...] = cot_ref[...].astype(full) + inv_std * (
        f - jnp.mean(f, axis=-1, keepdims=True) - xhat * jnp.mean(f * xhat, axis=-1, keepdims=True)
    )
    token_ref[...] = jnp.zeros_like(token_ref)


def finish(*operands):
    rows, width = operands[0].shape
    return pl.pallas_call(
        finish_kernel,
        out_shape=[shape_of((rows, width), low), shape_of((rows, width), full), shape_of((1, LANES), full)],
        in_specs=[spec_vmem()] * len(operands),
        out_specs=[spec_vmem()] * 3,
        compiler_params=params(24),
        cost_estimate=pl.CostEstimate(flops=10**7, bytes_accessed=8 * MIB, transcendentals=0),
        name="finish",
    )(*operands)


def to_attention(width, local_width, source, refs, base, unit):
    qkv_ref, out_ref = refs
    tiles = local_width // LANES
    split = 3 * tiles * width
    tile = base // width
    row = pl.multiple_of(lax.rem(base, width), unit)
    column = pl.multiple_of(lax.rem(tile, tiles) * LANES, LANES)
    yield base < split, source, qkv_ref.at[jnp.minimum(tile // tiles, 2), pl.ds(row, unit), pl.ds(column, LANES)]
    after = jnp.maximum(base - split, 0)
    row = pl.multiple_of(lax.rem(after, local_width), unit)
    column = pl.multiple_of(after // local_width * LANES, LANES)
    yield base >= split, source, out_ref.at[pl.ds(row, unit), pl.ds(column, LANES)]


def to_mlp(width, source, refs, base, unit):
    up_ref, down_ref = refs
    block, inside = base // (2 * width), lax.rem(base, 2 * width)
    block_at = pl.multiple_of(block * LANES, LANES)
    row = pl.multiple_of(jnp.minimum(inside, width - unit), unit)
    yield inside < width, source, up_ref.at[pl.ds(row, unit), pl.ds(block_at, LANES)]
    for t in range(unit // LANES):
        column = pl.multiple_of(jnp.maximum(inside - width, 0) + t * LANES, LANES)
        cut = source.at[pl.ds(t * LANES, LANES), :]
        yield inside >= width, cut, down_ref.at[pl.ds(block_at, LANES), pl.ds(column, LANES)]


def unpack_kernel(route, count, unit, has_old, ids_ref, *rest):
    parts, rest = rest[:count], rest[count:]
    rest = rest[2:] if has_old else rest
    targets, (token_ref, held, sems) = rest[:2], rest[2:]
    token_ref[...] = jnp.zeros_like(token_ref)
    chunk_rows = parts[0].shape[0]
    units = chunk_rows // unit
    per_unit = sems.shape[0] // (count * units)

    def moves():
        for i in range(count):
            for j in range(units):
                source = held.at[i, pl.ds(j * unit, unit), :]
                base = ids_ref[i] * chunk_rows + j * unit
                for n, (applies, piece, target) in enumerate(route(source, targets, base, unit)):
                    sem = sems.at[(i * units + j) * per_unit + n]
                    yield i, applies, pltpu.make_async_copy(piece, target, sem)

    done = -1
    for i, applies, copy in moves():
        if i != done:
            held[i] = parts[i][...].astype(full)
            done = i
        pl.when(applies)(copy.start)
    for i, applies, copy in moves():
        pl.when(applies)(copy.wait)


def unpack(name, route, cases, unit, shapes, ids, parts, old):
    count = len(parts)
    chunk_rows = parts[0].shape[0]
    operands = [ids, *parts, *(old or ())]
    return pl.pallas_call(
        functools.partial(unpack_kernel, route, count, unit, old is not None),
        out_shape=[shape_of(shape, full) for shape in shapes] + [shape_of((1, LANES), full)],
        in_specs=[spec_smem()] + [spec_vmem()] * count + [spec_hbm()] * (len(operands) - 1 - count),
        out_specs=[spec_hbm()] * 2 + [spec_vmem()],
        input_output_aliases={} if old is None else {1 + count: 0, 2 + count: 1},
        scratch_shapes=[
            pltpu.VMEM((count, chunk_rows, LANES), full),
            pltpu.SemaphoreType.DMA((count * (chunk_rows // unit) * cases,)),
        ],
        compiler_params=params(8 + count * chunk_rows * 3 * LANES * 2 // MIB),
        cost_estimate=pl.CostEstimate(
            flops=10**6, bytes_accessed=count * chunk_rows * LANES * 6, transcendentals=0
        ),
        name=name,
    )(*operands)


def local(
    hidden,
    pair_of,
    ln1_gain,
    ln1_bias,
    ln2_gain,
    ln2_bias,
    w_qkv,
    b_qkv,
    w_out,
    b_out,
    w_up,
    b_up,
    w_down,
    b_down,
    cotangent,
):
    owners = lax.axis_size("ctx")
    sides = lax.axis_size("tp")
    rows, width = hidden.shape
    local_width = w_qkv.shape[2]
    hidden_units = w_up.shape[1]
    heads = local_width // HEAD_DIM
    group = owners // heads

    exponent = np.arange(0, ROT, 2, dtype=np.float32) / np.float32(ROT)
    inverse = jnp.asarray(np.tile(np.float32(10000.0) ** (-exponent), LANES // HALF)[None, :], full)
    order = (0, 2, 4, 6, 7, 5, 3, 1) if owners == 16 else tuple(range(owners // 2))
    chips = len(order)

    (h1, h2, xhat, inv_std, d_bias, gains, biases, b_up_row), sends = project(
        heads,
        group,
        pair_of,
        inverse,
        (hidden, ln1_gain, ln1_bias, ln2_gain, ln2_bias, cotangent, w_out, w_qkv, b_qkv, b_up, b_out, b_down),
    )

    def head_shift(array, r, back=False):
        step = -r if back else r
        pairs = [(c, ((c // group + step) % heads) * group + c % group) for c in range(owners)]
        return lax.ppermute(array, "ctx", pairs)

    def group_shift(array, d):
        pairs = [(c, c // group * group + (c % group + d) % group) for c in range(owners)]
        return lax.ppermute(array, "ctx", pairs)

    got = [sends[0]] + [head_shift(sends[r], r) for r in range(1, heads)]

    me = lax.axis_index("ctx")
    chip, core = me // 2, lax.rem(me, 2)
    place = sum(jnp.where(chip == c, i, 0) for i, c in enumerate(order))
    way = 1 - 2 * core
    far, near = chips // 2, chips - 1 - chips // 2

    def ring(array, forward):
        pairs = []
        for i, c in enumerate(order):
            for k in range(2):
                step = 1 if (k == 0) == forward else -1
                pairs.append((2 * c + k, 2 * order[(i + step) % chips] + k))
        return lax.ppermute(array, "ctx", pairs)

    def other_core(array):
        return lax.ppermute(array, "ctx", [(c, c ^ 1) for c in range(owners)])

    def across(array):
        return lax.ppermute(array, "tp", [(t, (t + 1) % sides) for t in range(sides)])

    def target(distance):
        return lax.rem(place + way * distance + chips, chips)

    def zero(array):
        return array[:1].astype(full) * 0.0

    slots = [far, -near]
    for t in range(1, far):
        slots += [far - t] if t >= near else [far - t, t - near]
    slots.append(0)
    early = 2
    slot_ids = jnp.stack(
        [core * chips + target(d) for d in slots] + [(1 - core) * chips + target(-d) for d in slots]
    )

    def terms_of(keep, came):
        def term(i):
            return keep[i].astype(full) + came[i].astype(full)

        return {d: term(i) for i, d in enumerate(slots)}

    def scatter_start(terms, token):
        return (terms[far] + token).astype(low), (terms[-near] + token).astype(low)

    def scatter_step(terms, t, sends, token):
        long_send, short_send = sends
        long_got = ring(long_send, True).astype(full) + token
        last = t == far - 1
        long_next = long_got if last else (long_got + terms[far - 1 - t]).astype(low)
        short_next = short_send
        if t < near:
            short_got = ring(short_send, False).astype(full) + token
            short_next = short_got if t == near - 1 else (short_got + terms[t + 1 - near]).astype(low)
        if last:
            return (terms[0] + long_next + short_next).astype(low)
        return long_next, short_next

    base, other_base = core * chips, (1 - core) * chips

    def gather_start(own):
        return [(own, base + place), (other_core(own), other_base + place)]

    def gather_step(t, sends, token):
        long_send, short_send = sends
        if token is not None:
            long_send = (long_send.astype(full) + token).astype(low)
        long_got = ring(long_send, True)
        found = [(long_got, base + target(-t - 1)), (other_core(long_got), other_base + target(t + 1))]
        short_got = short_send
        if t < near:
            if token is not None:
                short_send = (short_send.astype(full) + token).astype(low)
            short_got = ring(short_send, False)
            found += [(short_got, base + target(t + 1)), (other_core(short_got), other_base + target(-t - 1))]
        return (long_got, short_got), found

    blocks = hidden_units // LANES // 2
    in_slots = blocks == chips
    mlp_ids = slot_ids if in_slots else jnp.concatenate(
        [core * blocks + jnp.arange(blocks), (1 - core) * blocks + jnp.arange(blocks)]
    )
    part, back2, sums2, d_b_up, keep_mlp, early_mlp, send_mlp = mlp(
        mlp_ids.astype(jnp.int32), early, h2, cotangent, xhat, w_up, b_up_row, w_down
    )
    chunk = keep_mlp.shape[0] // chips
    came_mlp = jnp.concatenate([other_core(early_mlp), other_core(send_mlp)]) if not in_slots else None
    if in_slots:
        halves = [other_core(array).reshape(-1, chunk, LANES) for array in (early_mlp, send_mlp)]
        came_mlp = [half[i] for half in halves for i in range(half.shape[0])]
        terms_mlp = terms_of(keep_mlp.reshape(chips, chunk, LANES), came_mlp)
    else:
        summed = (keep_mlp.astype(full) + came_mlp.astype(full)).reshape(chips, chunk, LANES)
        terms_mlp = {d: lax.dynamic_index_in_dim(summed, target(d), 0, keepdims=False) for d in slots}
    theirs2 = across(back2)

    other = None
    if group > 1:
        mine = jnp.concatenate([array[:, LANES:] for array in got], axis=0)
        other = jnp.stack([group_shift(mine, group - d) for d in range(1, group)])

    middle = heads // 4
    firsts, _, state, token = attention(
        heads, group, tuple(range(middle)), pair_of, inverse, sums2, got, other, None
    )
    sends_mlp = scatter_start(terms_mlp, token)
    token = zero(sends_mlp[0]) + zero(sends_mlp[1]) + zero(theirs2)[:, :LANES]
    found, ends, state, token = attention(
        heads, group, tuple(range(middle, heads)), pair_of, inverse, token, got, other, state
    )
    firsts = firsts + found
    d_own, d_other = ends[0], (ends[1] if group > 1 else None)
    terms = [d_own] + [group_shift(d_other[d - 1], d) for d in range(1, group)]
    backs = combine(heads, terms, firsts)
    backs = [backs[0]] + [head_shift(backs[r], r, True) for r in range(1, heads)]
    sends_mlp = scatter_step(terms_mlp, 0, sends_mlp, token)

    both, sums1, d_b_qkv, keep, early_att, send_att = back_projections(
        heads, group, early, slot_ids.astype(jnp.int32), w_out, w_qkv, part, h1, xhat, cotangent, backs
    )
    theirs = across(both)
    output, d_hidden, finish_token = finish(
        hidden, cotangent, xhat, inv_std, gains, biases, both, theirs, back2, theirs2
    )
    halves = [other_core(array) for array in (early_att, send_att)]
    terms_att = terms_of(keep, [half[i] for half in halves for i in range(half.shape[0])])

    small = jnp.concatenate(
        [sums1.reshape(1, -1), sums2.reshape(1, -1), d_bias, d_b_up, d_b_qkv.reshape(1, -1)], axis=1
    )

    def unpack_some(name, route, cases, unit, shapes, found, old):
        parts, ids = zip(*found)
        *old, token = unpack(name, route, cases, unit, shapes, jnp.stack(ids), parts, old)
        return old, token

    unit_mlp = min(chunk, local_width)
    unit_att = min(keep.shape[1], local_width)
    unpack_mlp = functools.partial(
        unpack_some,
        "unpack_feed_forward",
        functools.partial(to_mlp, width),
        1 + unit_mlp // LANES,
        unit_mlp,
        ((width, hidden_units), (hidden_units, width)),
    )
    unpack_att = functools.partial(
        unpack_some,
        "unpack_attention",
        functools.partial(to_attention, width, local_width),
        2,
        unit_att,
        ((3, width, local_width), (local_width, width)),
    )

    nothing = jnp.zeros((1, LANES), full)
    steps_mlp = iter(range(1, far))
    steps_round = iter(range(far))
    own_mlp, round_mlp, waiting, grads_mlp = None, None, [], None

    def advance_mlp(token):
        nonlocal sends_mlp, own_mlp, round_mlp, waiting
        t = next(steps_mlp, None)
        if t is not None:
            sends_mlp = scatter_step(terms_mlp, t, sends_mlp, token)
            if t < far - 1:
                return zero(sends_mlp[0])
            own_mlp, round_mlp = sends_mlp, (sends_mlp, sends_mlp)
            waiting += gather_start(own_mlp)
            return zero(own_mlp)
        t = next(steps_round, None)
        if t is None:
            return nothing
        round_mlp, found = gather_step(t, round_mlp, None)
        waiting += found
        return zero(round_mlp[0])

    sends_att = scatter_start(terms_att, nothing)
    for t in range(far):
        sends_att = scatter_step(terms_att, t, sends_att, advance_mlp(nothing))
    round_att, waiting_att, grads_att = (sends_att, sends_att), gather_start(sends_att), None
    token = finish_token
    distance = 1
    for t in range(far):
        if distance < owners:
            small = small + zero(round_att[0])[:, :1]
            small = small + lax.ppermute(small, "ctx", [(c, c ^ distance) for c in range(owners)])
            distance *= 2
        later = advance_mlp(nothing)
        round_att, found = gather_step(t, round_att, token)
        if waiting:
            ready, waiting = waiting, []
            grads_mlp, token = unpack_mlp(ready, grads_mlp)
        token = token + later + zero(small)[:, :LANES]
        waiting_att += found
        if t == far - 2:
            grads_att, more = unpack_att(waiting_att[:-4], None)
            waiting_att = waiting_att[-4:]
            token = token + more
    while distance < owners:
        small = small + lax.ppermute(small, "ctx", [(c, c ^ distance) for c in range(owners)])
        distance *= 2
    while next(steps_round, None) is not None:
        raise ValueError("rounds left")
    if waiting:
        grads_mlp, _ = unpack_mlp(waiting, grads_mlp)
    grads_att, _ = unpack_att(waiting_att, grads_att)

    norm_sums = small[:, : 4 * width]
    norm_sums = (norm_sums + across(norm_sums)).reshape(4, width)
    at = 4 * width
    d_bias = small[0, at : at + width]
    d_b_up = small[0, at + width : at + width + hidden_units]
    d_b_qkv = small[0, at + width + hidden_units :].reshape(3, local_width)
    d_w_up, d_w_down = grads_mlp
    d_w_qkv, d_w_out = grads_att
    return (
        output,
        d_hidden,
        norm_sums[0],
        norm_sums[1],
        norm_sums[2],
        norm_sums[3],
        d_w_qkv,
        d_b_qkv,
        d_w_out,
        d_bias,
        d_w_up,
        d_b_up,
        d_w_down,
        d_bias,
    )


def solution(mesh):
    placed = (
        P("ctx", None),
        P(),
        P(),
        P(),
        P(),
        P(),
        P(None, None, "tp"),
        P(None, "tp"),
        P("tp", None),
        P(),
        P(None, "tp"),
        P("tp"),
        P("tp", None),
        P(),
        P("ctx", None),
    )
    return jax.shard_map(
        local,
        mesh=mesh,
        in_specs=placed,
        out_specs=(
            P("ctx", None),
            P("ctx", None),
            P(),
            P(),
            P(),
            P(),
            P(None, None, "tp"),
            P(None, "tp"),
            P("tp", None),
            P(),
            P(None, "tp"),
            P("tp"),
            P("tp", None),
            P(),
        ),
        check_vma=False,
    )
```

```python
import functools

import jax
import jax.numpy as jnp
import numpy as np
from jax import lax
from jax.experimental import pallas as pl
from jax.experimental.pallas import tpu as pltpu
from jax.sharding import PartitionSpec as P

HEAD_DIM = 64
ROT = 16
HALF = ROT // 2
BLOCK = 128
LANES = 128
KEYS = 512
MIB = 1 << 20

norm_eps = 1e-05
masked_score = -1e30
score_scale = HEAD_DIM ** (-0.5)
low = jnp.bfloat16
full = jnp.float32


def mm(left, right):
    return lax.dot_general(left, right, (((1,), (0,)), ((), ())), preferred_element_type=full)


def mm_nt(left, right):
    return lax.dot_general(left, right, (((1,), (1,)), ((), ())), preferred_element_type=full)


def turn(tensor):
    return tensor.astype(full).T.astype(low)


def lane_ids(shape):
    return lax.broadcasted_iota(jnp.int32, shape, len(shape) - 1)


def row_ids(shape):
    return lax.broadcasted_iota(jnp.int32, shape, len(shape) - 2)


def rotary_partner(tensor):
    lanes = lane_ids(tensor.shape)
    ahead = pltpu.roll(tensor, LANES - HALF, 1)
    behind = pltpu.roll(tensor, HALF, 1)
    return jnp.where(lanes % ROT < HALF, ahead, behind)


def spec_vmem():
    return pl.BlockSpec(memory_space=pltpu.VMEM)


def spec_smem():
    return pl.BlockSpec(memory_space=pltpu.SMEM)


def spec_hbm():
    return pl.BlockSpec(memory_space=pltpu.HBM)


def params(mib):
    return pltpu.CompilerParams(vmem_limit_bytes=mib * MIB)


def shape_of(shape, kind):
    return jax.ShapeDtypeStruct(shape, kind)


def block_tables(inverse, blocks):
    row = row_ids((BLOCK, LANES)).astype(full)
    start = blocks.astype(full) * float(BLOCK)
    return jnp.cos(row * inverse), jnp.sin(row * inverse), jnp.cos(start * inverse), jnp.sin(start * inverse)


def project_kernel(heads, pair_ref, inv_ref, *rest):
    given, rest = rest[:5], rest[5:]
    send_ref, held, sems = rest[0], rest[1:-1], rest[-1]
    copies = [pltpu.make_async_copy(src, dst, sems.at[i]) for i, (src, dst) in enumerate(zip(given, held))]
    for copy in copies:
        copy.start()
    h1_ref, w_qkv_ref, b_qkv_ref, cot_ref, w_out_ref = held
    rows = h1_ref.shape[0]
    pair = pair_ref[lax.axis_index("ctx")]
    total_blocks = 2 * pair_ref.shape[0]

    first = jnp.where(row_ids((8, LANES)) == 0, pair, total_blocks - 1 - pair)
    cos_row, sin_row, cos_block, sin_block = block_tables(inv_ref[...], first)
    in_head = lane_ids((BLOCK, LANES)) % HEAD_DIM
    tables = []
    for half in range(2):
        cos_at, sin_at = cos_block[half : half + 1], sin_block[half : half + 1]
        cosine = cos_row * cos_at - sin_row * sin_at
        sine = sin_row * cos_at + cos_row * sin_at
        cosine = jnp.where(in_head < ROT, cosine, 1.0)
        sine = jnp.where(in_head < HALF, -sine, jnp.where(in_head < ROT, sine, 0.0))
        tables.append((cosine, sine))
    cosine = jnp.concatenate([tables[0][0], tables[1][0]], axis=0)
    sine = jnp.concatenate([tables[0][1], tables[1][1]], axis=0)
    lane = lane_ids((rows, LANES))

    def turned(tile):
        return tile * cosine + rotary_partner(tile) * sine

    for copy in copies[:3]:
        copy.wait()
    h1 = h1_ref[...]

    def projected(s):
        return mm(h1, w_qkv_ref[s]) + b_qkv_ref[s : s + 1].astype(full)

    queries, keys, values = projected(0), projected(1), projected(2)
    for copy in copies[3:]:
        copy.wait()
    grads = mm_nt(cot_ref[...], w_out_ref[...])
    left = lane < HEAD_DIM
    for i in range(heads // 2):
        cut = slice(i * LANES, (i + 1) * LANES)
        q = turned(queries[:, cut]).astype(low).astype(full) * score_scale
        k = turned(keys[:, cut])
        v = values[:, cut]
        g = grads[:, cut]
        send_ref[2 * i, :, :LANES] = jnp.where(left, g, pltpu.roll(q, HEAD_DIM, 1)).astype(low)
        send_ref[2 * i, :, LANES:] = jnp.where(left, v, pltpu.roll(k, HEAD_DIM, 1)).astype(low)
        send_ref[2 * i + 1, :, :LANES] = jnp.where(left, pltpu.roll(g, HEAD_DIM, 1), q).astype(low)
        send_ref[2 * i + 1, :, LANES:] = jnp.where(left, pltpu.roll(v, HEAD_DIM, 1), k).astype(low)


def project(heads, pair_of, inverse, *given):
    rows, width = given[0].shape
    return pl.pallas_call(
        functools.partial(project_kernel, heads),
        out_shape=shape_of((heads, rows, 2 * LANES), low),
        in_specs=[spec_smem(), spec_vmem()] + [spec_hbm()] * len(given),
        out_specs=spec_vmem(),
        scratch_shapes=[pltpu.VMEM(array.shape, array.dtype) for array in given]
        + [pltpu.SemaphoreType.DMA((len(given),))],
        compiler_params=params(60),
        cost_estimate=pl.CostEstimate(
            flops=8 * rows * width * heads * HEAD_DIM, bytes_accessed=8 * MIB, transcendentals=0
        ),
        name="project",
    )(pair_of, inverse, *given)


def mlp_kernel(early, ids_ref, *rest):
    given, rest = rest[:11], rest[11:]
    (
        h1_ref,
        xhat_ref,
        std_ref,
        d_bias_ref,
        gains_ref,
        bias_ref,
        part_ref,
        back_ref,
        sums_ref,
        d_b_up_ref,
        keep_ref,
        early_ref,
        send_ref,
    ) = rest[:13]
    h2_held, h2_turned, part_acc, back_acc, b_up = rest[13:18]
    held, sems = rest[18:-1], rest[-1]
    copies = [pltpu.make_async_copy(src, dst, sems.at[i]) for i, (src, dst) in enumerate(zip(given, held))]
    hidden_ref, g1_ref, c1_ref, g2_ref, c2_ref, b_up_ref, b_out_ref, b_down_ref, w_up_ref, cot_ref, w_down_ref = held
    step = pl.program_id(0)
    steps = pl.num_programs(0)

    def as_row(ref):
        return ref[...].astype(full)[None, :]

    @pl.when(step == 0)
    def _():
        for copy in copies:
            copy.start()
        for copy in copies[:8]:
            copy.wait()
        x = hidden_ref[...].astype(full)
        centred = x - jnp.mean(x, axis=-1, keepdims=True)
        spread = jnp.mean(centred * centred, axis=-1, keepdims=True)
        inv_std = lax.rsqrt(spread + norm_eps)
        xhat = centred * inv_std
        xhat_ref[...] = xhat
        std_ref[...] = jnp.broadcast_to(inv_std, std_ref.shape)
        gain1, gain2 = as_row(g1_ref), as_row(g2_ref)
        h1_ref[...] = (xhat * gain1 + as_row(c1_ref)).astype(low)
        h2 = xhat * gain2 + as_row(c2_ref)
        h2_held[...] = h2.astype(low)
        h2_turned[...] = h2.T.astype(low)
        gains_ref[0:1] = gain1
        gains_ref[1:2] = gain2
        b_up[...] = as_row(b_up_ref)
        bias_ref[0:1] = as_row(b_out_ref)
        bias_ref[1:2] = as_row(b_down_ref)
        part_acc[...] = jnp.zeros_like(part_acc)
        back_acc[...] = jnp.zeros_like(back_acc)
        for copy in copies[8:]:
            copy.wait()
        d_bias_ref[...] = jnp.sum(cot_ref[...].astype(full), axis=0, keepdims=True)

    cot = cot_ref[...]
    at = [pl.multiple_of(ids_ref[b * steps + step] * LANES, LANES) for b in range(2)]
    w_up = jnp.concatenate([w_up_ref[:, pl.ds(i, LANES)] for i in at], axis=1)
    w_down = jnp.concatenate([w_down_ref[pl.ds(i, LANES), :] for i in at], axis=0)
    u = mm(h2_held[...], w_up) + jnp.concatenate([b_up[:, pl.ds(i, LANES)] for i in at], axis=1)
    cdf = 0.5 * (1.0 + lax.erf(u * np.float32(np.sqrt(0.5))))
    active = u * cdf
    active_low = active.astype(low)
    slope = cdf + u * jnp.exp(-0.5 * u * u) * np.float32(1.0 / np.sqrt(2.0 * np.pi))
    du = (mm_nt(cot, w_down) * slope).astype(low)
    part_acc[...] += mm(active_low, w_down)
    back_acc[...] += mm_nt(du, w_up)
    d_b_up = jnp.sum(du.astype(full), axis=0, keepdims=True)
    up = mm(h2_turned[...], du).astype(low)
    down = mm(active.T.astype(low), cot).astype(low)
    depth = up.shape[0]

    def put(b, grad_ref):
        grad_ref[:depth] = up[:, b * LANES : (b + 1) * LANES]
        for t in range(down.shape[1] // LANES):
            grad_ref[depth + t * LANES : depth + (t + 1) * LANES] = down[
                b * LANES : (b + 1) * LANES, t * LANES : (t + 1) * LANES
            ]

    for b in range(2):
        d_b_up_ref[:, pl.ds(at[b], LANES)] = d_b_up[:, b * LANES : (b + 1) * LANES]
    put(0, keep_ref)

    @pl.when(step < early)
    def _():
        put(1, early_ref)

    @pl.when(step >= early)
    def _():
        put(1, send_ref)

    @pl.when(step == steps - 1)
    def _():
        part_ref[...] = part_acc[...]
        back = back_acc[...]
        back_ref[...] = back.astype(low)
        sums_ref[0:1] = jnp.sum(back * xhat_ref[...], axis=0, keepdims=True)
        sums_ref[1:2] = jnp.sum(back, axis=0, keepdims=True)


def mlp(ids, early, *given):
    rows, width = given[0].shape
    hidden_units = given[8].shape[1]
    steps = hidden_units // LANES // 2
    whole = lambda shape: pl.BlockSpec(shape, lambda f, c: (0,) * len(shape))
    grads = lambda at: pl.BlockSpec((2 * width, LANES), lambda f, c: (at(f), 0))
    outs = [
        shape_of((rows, width), low),
        shape_of((rows, width), full),
        shape_of((rows, LANES), full),
        shape_of((1, width), full),
        shape_of((2, width), full),
        shape_of((2, width), full),
        shape_of((rows, width), full),
        shape_of((rows, width), low),
        shape_of((2, width), full),
        shape_of((1, hidden_units), full),
        shape_of((steps * 2 * width, LANES), low),
        shape_of((early * 2 * width, LANES), low),
        shape_of(((steps - early) * 2 * width, LANES), low),
    ]
    return pl.pallas_call(
        functools.partial(mlp_kernel, early),
        grid_spec=pltpu.PrefetchScalarGridSpec(
            num_scalar_prefetch=1,
            grid=(steps,),
            in_specs=[spec_hbm()] * len(given),
            out_specs=[whole(array.shape) for array in outs[:10]]
            + [
                grads(lambda f: f),
                grads(lambda f: jnp.minimum(f, early - 1)),
                grads(lambda f: jnp.maximum(f - early, 0)),
            ],
            scratch_shapes=[
                pltpu.VMEM((rows, width), low),
                pltpu.VMEM((width, rows), low),
                pltpu.VMEM((rows, width), full),
                pltpu.VMEM((rows, width), full),
                pltpu.VMEM((1, hidden_units), full),
            ]
            + [pltpu.VMEM(array.shape, array.dtype) for array in given]
            + [pltpu.SemaphoreType.DMA((len(given),))],
        ),
        out_shape=outs,
        compiler_params=params(60),
        cost_estimate=pl.CostEstimate(
            flops=12 * rows * width * hidden_units, bytes_accessed=20 * MIB, transcendentals=0
        ),
        name="feed_forward",
    )(ids, *given)


def attention_kernel(heads, group, places, is_first, is_last, pair_ref, inv_ref, token_ref, *rest):
    del token_ref
    if is_first:
        got_ref, rest = rest[0], rest[1:]
        if group > 1:
            other_ref, rest = rest[0], rest[1:]
    else:
        rest = rest[4:]
    out_ref, rest = rest[0], rest[1:]
    if is_last:
        d_own_ref, rest = rest[0], rest[1:]
        if group > 1:
            d_other_ref, rest = rest[0], rest[1:]
    (values_keys, turned_keys, sums, queries), rest = rest[:4], rest[4:]
    token_out, rest = rest[0], rest[1:]
    weights_in, weights_out, peaks, totals, weighted, finals, block_cos, block_sin = rest
    token_out[...] = jnp.zeros_like(token_out)

    rows = queries.shape[1]
    owners = pair_ref.shape[0]
    total_blocks = 2 * owners
    per_chunk = KEYS // BLOCK
    tasks = (total_blocks + 1 + per_chunk - 1) // per_chunk
    me = lax.axis_index("ctx")
    own_sub = lax.rem(me, group)

    def blocks_of(r, d):
        owner = r * group + lax.rem(own_sub + d, group)
        pair = pair_ref[owner]
        return pair, total_blocks - 1 - pair

    def place(tile, block):
        at = pl.multiple_of(block * BLOCK, BLOCK)
        values_keys[pl.ds(at, BLOCK), :] = tile
        turned_keys[:, pl.ds(at, BLOCK)] = turn(tile)

    if is_first:
        for r in range(heads):
            queries[r] = got_ref[r, :, :LANES]
            for half, block in enumerate(blocks_of(r, 0)):
                place(got_ref[r, half * BLOCK : (half + 1) * BLOCK, LANES:], block)
            for d in range(1, group):
                for half, block in enumerate(blocks_of(r, d)):
                    at = r * rows + half * BLOCK
                    place(other_ref[d - 1, at : at + BLOCK, :], block)
        sums[...] = jnp.zeros_like(sums)

    lane = lane_ids((BLOCK, LANES))
    left = lane < HEAD_DIM
    in_key = lane - HEAD_DIM
    moving = (in_key >= 0) & (in_key < ROT)
    forward = (in_key >= 0) & (in_key < HALF)
    cos_row, sin_row, block_cos[...], block_sin[...] = block_tables(inv_ref[...], row_ids(block_cos.shape))

    def rotated_back(tile, block):
        cos_at, sin_at = block_cos[pl.ds(block, 1), :], block_sin[pl.ds(block, 1), :]
        cosine = jnp.where(moving, cos_row * cos_at - sin_row * sin_at, 1.0)
        sine = sin_row * cos_at + cos_row * sin_at
        sine = jnp.where(moving, jnp.where(forward, sine, -sine), 0.0)
        return tile * cosine + rotary_partner(tile) * sine

    offset = row_ids((BLOCK, BLOCK)) - lane_ids((BLOCK, BLOCK))

    def one_pair(i, carry):
        blocks = blocks_of(places[0] + i, 0)
        first = blocks[0] // per_chunk + 1
        for half in range(2):
            both = queries[places[0] + i, half * BLOCK : (half + 1) * BLOCK, :]
            both_turned = turn(both)
            upper = row_ids((LANES, BLOCK)) < HEAD_DIM
            zero = jnp.zeros_like(both_turned)
            weights_in[half, :, :BLOCK] = jnp.where(upper, both_turned, zero)
            weights_in[half, :, BLOCK:] = jnp.where(upper, zero, both_turned)
            weights_out[half, :BLOCK, :] = jnp.where(left, both, zero)
            weights_out[half, BLOCK:, :] = jnp.where(left, zero, both)
        finals[...] = jnp.zeros_like(finals)

        def task(t):
            is_low = t < first
            chunk = jnp.where(is_low, first - 1 - t, t - first)
            return is_low, chunk

        wide = 2 * BLOCK
        runs = KEYS // wide

        def products(t, is_low, chunk, v):
            at = pl.multiple_of(chunk * KEYS + v * wide, wide)
            both = mm(values_keys[pl.ds(at, wide), :], weights_in[jnp.where(is_low, 0, 1)])
            found = []
            for u in range(2):
                sub = slice(u * BLOCK, (u + 1) * BLOCK)
                scores = both[sub, BLOCK:]
                if t in (0, tasks - 1):
                    query_at = blocks[0 if t == 0 else 1] * BLOCK
                    scores = jnp.where(offset <= query_at - at - u * BLOCK, scores, masked_score)
                found.append((scores, both[sub, :BLOCK]))
            return at, found

        for t in range(tasks):
            is_low, chunk = task(t)
            for v in range(runs):
                _, found = products(t, is_low, chunk, v)
                for u, (scores, grads) in enumerate(found):
                    peak = jnp.max(scores, axis=0, keepdims=True)
                    raised = jnp.exp(scores - peak)
                    line = (t * runs + v) * 2 + u
                    peaks[line : line + 1] = peak
                    totals[line : line + 1] = jnp.sum(raised, axis=0, keepdims=True)
                    weighted[line : line + 1] = jnp.sum(raised * grads, axis=0, keepdims=True)

        lines = tasks * runs * 2
        in_low = row_ids((lines, BLOCK)) < first * (runs * 2)

        def finish(mine):
            peak = jnp.where(mine, peaks[...], masked_score)
            top = jnp.max(peak, axis=0, keepdims=True)
            factor = jnp.where(mine, jnp.exp(peak - top), 0.0)
            total = jnp.sum(totals[...] * factor, axis=0, keepdims=True)
            delta = jnp.sum(weighted[...] * factor, axis=0, keepdims=True) / total
            return top + jnp.log(total), delta

        ends = (finish(in_low), finish(jnp.logical_not(in_low)))

        for t in range(tasks):
            is_low, chunk = task(t)
            half = jnp.where(is_low, 0, 1)
            lse, delta = (jnp.where(is_low, a, b) for a, b in zip(*ends))
            last = None
            for v in range(runs):
                at, found = products(t, is_low, chunk, v)
                tiles = []
                for scores, grads in found:
                    probs = jnp.exp(scores - lse)
                    d_scores = probs * (grads - delta)
                    tiles.append(jnp.concatenate([probs.astype(low), d_scores.astype(low)], axis=1))
                both = jnp.concatenate(tiles, axis=0)
                sums[pl.ds(at, wide), :] += mm(both, weights_out[half])
                new = mm(turned_keys[:, pl.ds(at, wide)], both)
                last = new if last is None else last + new
            finals[half] += last

        for half in range(2):
            both = jnp.concatenate(
                [finals[half, :HEAD_DIM, :BLOCK], finals[half, HEAD_DIM:, BLOCK:] * score_scale], axis=0
            ).T
            out_ref[i, half * BLOCK : (half + 1) * BLOCK, :] = rotated_back(both, blocks[half]).astype(low)
        return carry

    lax.fori_loop(0, len(places), one_pair, 0)

    if is_last:
        for r in range(heads):
            for d in range(group):
                for half, block in enumerate(blocks_of(r, d)):
                    at = r * rows + half * BLOCK
                    tile = rotated_back(sums[pl.ds(pl.multiple_of(block * BLOCK, BLOCK), BLOCK), :], block)
                    if d == 0:
                        d_own_ref[at : at + BLOCK, :] = tile
                    else:
                        d_other_ref[d - 1, at : at + BLOCK, :] = tile


def attention(heads, group, places, pair_of, inverse, token, got, other, state):
    is_first, is_last = state is None, places[-1] == heads - 1
    rows = got.shape[1]
    owners = pair_of.shape[0]
    total_keys = owners * rows
    tasks = (2 * owners + KEYS // BLOCK) // (KEYS // BLOCK)
    operands = [pair_of, inverse, token]
    outs = [shape_of((len(places), rows, LANES), low)]
    if is_first:
        operands += [got] if other is None else [got, other]
    else:
        operands += list(state)
    if is_last:
        outs.append(shape_of((heads * rows, LANES), full))
        if group > 1:
            outs.append(shape_of((group - 1, heads * rows, LANES), full))
    kept = [
        shape_of((total_keys, LANES), low),
        shape_of((LANES, total_keys), low),
        shape_of((total_keys, LANES), full),
        shape_of((heads, rows, LANES), low),
    ]
    aliases = {} if is_first else {len(operands) - 4 + i: len(outs) + i for i in range(4)}
    found = pl.pallas_call(
        functools.partial(attention_kernel, heads, group, places, is_first, is_last),
        out_shape=outs + kept + [shape_of((1, LANES), full)],
        in_specs=[spec_smem()] + [spec_vmem()] * (len(operands) - 1),
        out_specs=[spec_vmem()] * (len(outs) + 5),
        input_output_aliases=aliases,
        scratch_shapes=[
            pltpu.VMEM((2, LANES, 2 * BLOCK), low),
            pltpu.VMEM((2, 2 * BLOCK, LANES), low),
            pltpu.VMEM((tasks * KEYS // BLOCK, BLOCK), full),
            pltpu.VMEM((tasks * KEYS // BLOCK, BLOCK), full),
            pltpu.VMEM((tasks * KEYS // BLOCK, BLOCK), full),
            pltpu.VMEM((2, LANES, 2 * BLOCK), full),
            pltpu.VMEM((2 * owners, LANES), full),
            pltpu.VMEM((2 * owners, LANES), full),
        ],
        compiler_params=params(12),
        cost_estimate=pl.CostEstimate(
            flops=2_500_000_000 * len(places), bytes_accessed=2 * MIB, transcendentals=0
        ),
        name="attention",
    )(*operands)
    return found[0], found[1 : len(outs)], found[len(outs) : len(outs) + 4], found[-1]


def combine_kernel(heads, terms, *refs):
    out_ref = refs[-1]
    rows = out_ref.shape[1]
    for r in range(heads):
        cut = slice(r * rows, (r + 1) * rows)
        total = refs[0][cut, :]
        for term in refs[1:terms]:
            total = total + term[cut, :]
        out_ref[r, :, LANES:] = total.astype(low)
    at = 0
    for first_ref in refs[terms:-1]:
        out_ref[at : at + first_ref.shape[0], :, :LANES] = first_ref[...]
        at += first_ref.shape[0]


def combine(heads, terms, firsts):
    rows = firsts[0].shape[1]
    return pl.pallas_call(
        functools.partial(combine_kernel, heads, len(terms)),
        out_shape=shape_of((heads, rows, 2 * LANES), low),
        in_specs=[spec_vmem()] * (len(firsts) + len(terms)),
        out_specs=spec_vmem(),
        compiler_params=params(24),
        cost_estimate=pl.CostEstimate(flops=10**7, bytes_accessed=3 * MIB, transcendentals=0),
        name="combine",
    )(*terms, *firsts)


def return_kernel(heads, early, ids_ref, *rest):
    given, rest = rest[:7], rest[7:]
    both_ref, sums_ref, d_b_ref, keep_ref, early_ref, send_ref = rest[:6]
    attended, d_proj, grads = rest[6:9]
    held, sems = rest[9:-1], rest[-1]
    copies = [pltpu.make_async_copy(src, dst, sems.at[i]) for i, (src, dst) in enumerate(zip(given, held))]
    for copy in copies:
        copy.start()
    got_ref, w_out_ref, part_ref, w_qkv_ref, xhat_ref, h1_ref, cot_ref = held
    copies[0].wait()
    chunk_rows = grads.shape[1]
    chips = keep_ref.shape[0]

    def put(at, tile):
        step = min(chunk_rows, tile.shape[0])
        for off in range(0, tile.shape[0], step):
            chunk, inside = divmod(at + off, chunk_rows)
            grads[chunk, inside : inside + step] = tile[off : off + step]

    rows = h1_ref.shape[0]
    left = lane_ids((rows, LANES)) < HEAD_DIM
    for i in range(heads // 2):
        cut = slice(i * LANES, (i + 1) * LANES)
        a, b = got_ref[2 * i, :, :LANES].astype(full), got_ref[2 * i + 1, :, :LANES].astype(full)
        attended[:, cut] = jnp.where(left, a, pltpu.roll(b, HEAD_DIM, 1)).astype(low)
        d_proj[0, :, cut] = jnp.where(left, pltpu.roll(a, HEAD_DIM, 1), b).astype(low)
        a, b = got_ref[2 * i, :, LANES:].astype(full), got_ref[2 * i + 1, :, LANES:].astype(full)
        d_proj[2, :, cut] = jnp.where(left, a, pltpu.roll(b, HEAD_DIM, 1)).astype(low)
        d_proj[1, :, cut] = jnp.where(left, pltpu.roll(a, HEAD_DIM, 1), b).astype(low)
    for copy in copies[1:3]:
        copy.wait()
    both_ref[:rows] = (part_ref[...] + mm(attended[...], w_out_ref[...])).astype(low)
    for copy in copies[3:]:
        copy.wait()
    back = mm_nt(d_proj[0], w_qkv_ref[0]) + mm_nt(d_proj[1], w_qkv_ref[1]) + mm_nt(d_proj[2], w_qkv_ref[2])
    both_ref[rows:] = back.astype(low)
    sums_ref[0:1] = jnp.sum(back * xhat_ref[...], axis=0, keepdims=True)
    sums_ref[1:2] = jnp.sum(back, axis=0, keepdims=True)
    h1_turned = turn(h1_ref[...])
    depth, tiles = h1_turned.shape[0], heads // 2
    for s in range(3):
        d_b_ref[s : s + 1] = jnp.sum(d_proj[s].astype(full), axis=0, keepdims=True)
        grad = mm(h1_turned, d_proj[s]).astype(low)
        for t in range(tiles):
            put((s * tiles + t) * depth, grad[:, t * LANES : (t + 1) * LANES])
    grad = mm(turn(attended[...]), cot_ref[...]).astype(low)
    height = grad.shape[0]
    for t in range(depth // LANES):
        put(3 * tiles * depth + t * height, grad[:, t * LANES : (t + 1) * LANES])
    for t in range(chips):
        keep_ref[t] = grads[ids_ref[t]]
        target = early_ref.at[t] if t < early else send_ref.at[t - early]
        target[...] = grads[ids_ref[chips + t]]


def back_projections(heads, early, ids, *given):
    rows, width = given[2].shape
    local_width = given[1].shape[0]
    chips = ids.shape[0] // 2
    chunk_rows = 4 * width * local_width // LANES // (2 * chips)
    outs = [
        shape_of((2 * rows, width), low),
        shape_of((2, width), full),
        shape_of((3, local_width), full),
        shape_of((chips, chunk_rows, LANES), low),
        shape_of((early, chunk_rows, LANES), low),
        shape_of((chips - early, chunk_rows, LANES), low),
    ]
    return pl.pallas_call(
        functools.partial(return_kernel, heads, early),
        out_shape=outs,
        in_specs=[spec_smem()] + [spec_hbm()] * len(given),
        out_specs=[spec_vmem()] * len(outs),
        scratch_shapes=[
            pltpu.VMEM((rows, local_width), low),
            pltpu.VMEM((3, rows, local_width), low),
            pltpu.VMEM((2 * chips, chunk_rows, LANES), low),
        ]
        + [pltpu.VMEM(array.shape, array.dtype) for array in given]
        + [pltpu.SemaphoreType.DMA((len(given),))],
        compiler_params=params(60),
        cost_estimate=pl.CostEstimate(
            flops=16 * rows * width * local_width, bytes_accessed=14 * MIB, transcendentals=0
        ),
        name="back_projections",
    )(ids, *given)


def finish_kernel(
    hidden_ref, cot_ref, xhat_ref, std_ref, gains_ref, bias_ref, ours_ref, theirs_ref, e2_ours_ref, e2_theirs_ref, out_ref, grad_ref, token_ref
):
    rows = hidden_ref.shape[0]
    gains = gains_ref[...]
    biases = bias_ref[...]
    summed = ours_ref[:rows].astype(full) + theirs_ref[:rows].astype(full)
    out_ref[...] = (hidden_ref[...].astype(full) + summed + biases[0:1] + biases[1:2]).astype(low)
    e1 = ours_ref[rows:].astype(full) + theirs_ref[rows:].astype(full)
    e2 = e2_ours_ref[...].astype(full) + e2_theirs_ref[...].astype(full)
    f = e1 * gains[0:1] + e2 * gains[1:2]
    xhat = xhat_ref[...]
    inv_std = std_ref[:, 0:1]
    grad_ref[...] = cot_ref[...].astype(full) + inv_std * (
        f - jnp.mean(f, axis=-1, keepdims=True) - xhat * jnp.mean(f * xhat, axis=-1, keepdims=True)
    )
    token_ref[...] = jnp.zeros_like(token_ref)


def finish(*operands):
    rows, width = operands[0].shape
    return pl.pallas_call(
        finish_kernel,
        out_shape=[shape_of((rows, width), low), shape_of((rows, width), full), shape_of((1, LANES), full)],
        in_specs=[spec_vmem()] * len(operands),
        out_specs=[spec_vmem()] * 3,
        compiler_params=params(24),
        cost_estimate=pl.CostEstimate(flops=10**7, bytes_accessed=8 * MIB, transcendentals=0),
        name="finish",
    )(*operands)


def to_attention(width, local_width, source, refs, base, unit):
    qkv_ref, out_ref = refs
    tiles = local_width // LANES
    split = 3 * tiles * width
    tile = base // width
    row = pl.multiple_of(lax.rem(base, width), unit)
    column = pl.multiple_of(lax.rem(tile, tiles) * LANES, LANES)
    yield base < split, source, qkv_ref.at[jnp.minimum(tile // tiles, 2), pl.ds(row, unit), pl.ds(column, LANES)]
    after = jnp.maximum(base - split, 0)
    row = pl.multiple_of(lax.rem(after, local_width), unit)
    column = pl.multiple_of(after // local_width * LANES, LANES)
    yield base >= split, source, out_ref.at[pl.ds(row, unit), pl.ds(column, LANES)]


def to_mlp(width, source, refs, base, unit):
    up_ref, down_ref = refs
    block, inside = base // (2 * width), lax.rem(base, 2 * width)
    block_at = pl.multiple_of(block * LANES, LANES)
    row = pl.multiple_of(jnp.minimum(inside, width - unit), unit)
    yield inside < width, source, up_ref.at[pl.ds(row, unit), pl.ds(block_at, LANES)]
    for t in range(unit // LANES):
        column = pl.multiple_of(jnp.maximum(inside - width, 0) + t * LANES, LANES)
        cut = source.at[pl.ds(t * LANES, LANES), :]
        yield inside >= width, cut, down_ref.at[pl.ds(block_at, LANES), pl.ds(column, LANES)]


def unpack_kernel(route, count, unit, has_old, ids_ref, *rest):
    parts, rest = rest[:count], rest[count:]
    rest = rest[2:] if has_old else rest
    targets, (token_ref, held, sems) = rest[:2], rest[2:]
    token_ref[...] = jnp.zeros_like(token_ref)
    chunk_rows = parts[0].shape[0]
    units = chunk_rows // unit
    per_unit = sems.shape[0] // (count * units)

    def moves():
        for i in range(count):
            for j in range(units):
                source = held.at[i, pl.ds(j * unit, unit), :]
                base = ids_ref[i] * chunk_rows + j * unit
                for n, (applies, piece, target) in enumerate(route(source, targets, base, unit)):
                    sem = sems.at[(i * units + j) * per_unit + n]
                    yield i, applies, pltpu.make_async_copy(piece, target, sem)

    done = -1
    for i, applies, copy in moves():
        if i != done:
            held[i] = parts[i][...].astype(full)
            done = i
        pl.when(applies)(copy.start)
    for i, applies, copy in moves():
        pl.when(applies)(copy.wait)


def unpack(name, route, cases, unit, shapes, ids, parts, old):
    count = len(parts)
    chunk_rows = parts[0].shape[0]
    operands = [ids, *parts, *(old or ())]
    return pl.pallas_call(
        functools.partial(unpack_kernel, route, count, unit, old is not None),
        out_shape=[shape_of(shape, full) for shape in shapes] + [shape_of((1, LANES), full)],
        in_specs=[spec_smem()] + [spec_vmem()] * count + [spec_hbm()] * (len(operands) - 1 - count),
        out_specs=[spec_hbm()] * 2 + [spec_vmem()],
        input_output_aliases={} if old is None else {1 + count: 0, 2 + count: 1},
        scratch_shapes=[
            pltpu.VMEM((count, chunk_rows, LANES), full),
            pltpu.SemaphoreType.DMA((count * (chunk_rows // unit) * cases,)),
        ],
        compiler_params=params(8 + count * chunk_rows * 3 * LANES * 2 // MIB),
        cost_estimate=pl.CostEstimate(
            flops=10**6, bytes_accessed=count * chunk_rows * LANES * 6, transcendentals=0
        ),
        name=name,
    )(*operands)


def local(
    hidden,
    pair_of,
    ln1_gain,
    ln1_bias,
    ln2_gain,
    ln2_bias,
    w_qkv,
    b_qkv,
    w_out,
    b_out,
    w_up,
    b_up,
    w_down,
    b_down,
    cotangent,
):
    owners = lax.axis_size("ctx")
    sides = lax.axis_size("tp")
    rows, width = hidden.shape
    local_width = w_qkv.shape[2]
    hidden_units = w_up.shape[1]
    heads = local_width // HEAD_DIM
    group = owners // heads

    exponent = np.arange(0, ROT, 2, dtype=np.float32) / np.float32(ROT)
    inverse = jnp.asarray(np.tile(np.float32(10000.0) ** (-exponent), LANES // HALF)[None, :], full)
    order = (0, 2, 4, 6, 7, 5, 3, 1) if owners == 16 else tuple(range(owners // 2))
    chips = len(order)

    def to_heads(array):
        groups = [[h * group + g for h in range(heads)] for g in range(group)]
        return lax.all_to_all(array, "ctx", 0, 0, axis_index_groups=groups, tiled=True)

    def group_shift(array, d):
        pairs = [(c, c // group * group + (c % group + d) % group) for c in range(owners)]
        return lax.ppermute(array, "ctx", pairs)

    me = lax.axis_index("ctx")
    chip, core = me // 2, lax.rem(me, 2)
    place = sum(jnp.where(chip == c, i, 0) for i, c in enumerate(order))
    way = 1 - 2 * core
    far, near = chips // 2, chips - 1 - chips // 2

    def ring(array, forward):
        pairs = []
        for i, c in enumerate(order):
            for k in range(2):
                step = 1 if (k == 0) == forward else -1
                pairs.append((2 * c + k, 2 * order[(i + step) % chips] + k))
        return lax.ppermute(array, "ctx", pairs)

    def other_core(array):
        return lax.ppermute(array, "ctx", [(c, c ^ 1) for c in range(owners)])

    def across(array):
        return lax.ppermute(array, "tp", [(t, (t + 1) % sides) for t in range(sides)])

    def target(distance):
        return lax.rem(place + way * distance + chips, chips)

    def zero(array):
        return array[:1].astype(full) * 0.0

    slots = [far, -near]
    for t in range(1, far):
        slots += [far - t] if t >= near else [far - t, t - near]
    slots.append(0)
    early = 2
    slot_ids = jnp.stack(
        [core * chips + target(d) for d in slots] + [(1 - core) * chips + target(-d) for d in slots]
    )

    def terms_of(keep, came):
        def term(i):
            return keep[i].astype(full) + came[i].astype(full)

        return {d: term(i) for i, d in enumerate(slots)}

    def scatter_start(terms, token):
        return (terms[far] + token).astype(low), (terms[-near] + token).astype(low)

    def scatter_step(terms, t, sends, token):
        long_send, short_send = sends
        long_got = ring(long_send, True).astype(full) + token
        last = t == far - 1
        long_next = long_got if last else (long_got + terms[far - 1 - t]).astype(low)
        short_next = short_send
        if t < near:
            short_got = ring(short_send, False).astype(full) + token
            short_next = short_got if t == near - 1 else (short_got + terms[t + 1 - near]).astype(low)
        if last:
            return (terms[0] + long_next + short_next).astype(low)
        return long_next, short_next

    base, other_base = core * chips, (1 - core) * chips

    def gather_start(own):
        return [(own, base + place), (other_core(own), other_base + place)]

    def gather_step(t, sends, token):
        long_send, short_send = sends
        if token is not None:
            long_send = (long_send.astype(full) + token).astype(low)
        long_got = ring(long_send, True)
        found = [(long_got, base + target(-t - 1)), (other_core(long_got), other_base + target(t + 1))]
        short_got = short_send
        if t < near:
            if token is not None:
                short_send = (short_send.astype(full) + token).astype(low)
            short_got = ring(short_send, False)
            found += [(short_got, base + target(t + 1)), (other_core(short_got), other_base + target(-t - 1))]
        return (long_got, short_got), found

    blocks = hidden_units // LANES // 2
    in_slots = blocks == chips
    mlp_ids = slot_ids if in_slots else jnp.concatenate(
        [core * blocks + jnp.arange(blocks), (1 - core) * blocks + jnp.arange(blocks)]
    )
    (h1, xhat, inv_std, d_bias, gains, biases, part, back2, sums2, d_b_up, keep_mlp, early_mlp, send_mlp) = mlp(
        mlp_ids.astype(jnp.int32),
        early,
        hidden,
        ln1_gain,
        ln1_bias,
        ln2_gain,
        ln2_bias,
        b_up,
        b_out,
        b_down,
        w_up,
        cotangent,
        w_down,
    )
    chunk = keep_mlp.shape[0] // chips
    came_mlp = jnp.concatenate([other_core(early_mlp), other_core(send_mlp)]) if not in_slots else None
    if in_slots:
        halves = [other_core(array).reshape(-1, chunk, LANES) for array in (early_mlp, send_mlp)]
        came_mlp = [half[i] for half in halves for i in range(half.shape[0])]
        terms_mlp = terms_of(keep_mlp.reshape(chips, chunk, LANES), came_mlp)
    else:
        summed = (keep_mlp.astype(full) + came_mlp.astype(full)).reshape(chips, chunk, LANES)
        terms_mlp = {d: lax.dynamic_index_in_dim(summed, target(d), 0, keepdims=False) for d in slots}
    theirs2 = across(back2)
    nothing = jnp.zeros((1, LANES), full)
    sends_mlp = scatter_start(terms_mlp, nothing)

    got = to_heads(project(heads, pair_of, inverse, h1, w_qkv, b_qkv, cotangent, w_out))
    other = None
    if group > 1:
        mine = got[:, :, LANES:].reshape(heads * rows, LANES)
        other = jnp.stack([group_shift(mine, group - d) for d in range(1, group)])

    cuts = (0, 3, 6, heads)
    firsts, state, token = [], None, nothing
    for t in range(3):
        sends_mlp = scatter_step(terms_mlp, t, sends_mlp, token)
        token = zero(sends_mlp[0]) + zero(sends_mlp[1])
        found, ends, state, token = attention(
            heads, group, tuple(range(cuts[t], cuts[t + 1])), pair_of, inverse, token, got, other, state
        )
        firsts.append(found)
    d_own, d_other = ends[0], (ends[1] if group > 1 else None)
    terms = [d_own] + [group_shift(d_other[d - 1], d) for d in range(1, group)]
    backs = to_heads(combine(heads, terms, firsts))
    token = token + zero(theirs2)[:, :LANES]
    for t in range(3, far):
        sends_mlp = scatter_step(terms_mlp, t, sends_mlp, token)
    own_mlp = sends_mlp

    both, sums1, d_b_qkv, keep, early_att, send_att = back_projections(
        heads, early, slot_ids.astype(jnp.int32), backs, w_out, part, w_qkv, xhat, h1, cotangent
    )
    theirs = across(both)
    output, d_hidden, finish_token = finish(
        hidden, cotangent, xhat, inv_std, gains, biases, both, theirs, back2, theirs2
    )
    halves = [other_core(array) for array in (early_att, send_att)]
    terms_att = terms_of(keep, [half[i] for half in halves for i in range(half.shape[0])])

    small = jnp.concatenate(
        [sums1.reshape(1, -1), sums2.reshape(1, -1), d_bias, d_b_up, d_b_qkv.reshape(1, -1)], axis=1
    )

    def unpack_some(name, route, cases, unit, shapes, found, old):
        parts, ids = zip(*found)
        *old, token = unpack(name, route, cases, unit, shapes, jnp.stack(ids), parts, old)
        return old, token

    unit_mlp = min(chunk, local_width)
    unit_att = min(keep.shape[1], local_width)
    unpack_mlp = functools.partial(
        unpack_some,
        "unpack_feed_forward",
        functools.partial(to_mlp, width),
        1 + unit_mlp // LANES,
        unit_mlp,
        ((width, hidden_units), (hidden_units, width)),
    )
    unpack_att = functools.partial(
        unpack_some,
        "unpack_attention",
        functools.partial(to_attention, width, local_width),
        2,
        unit_att,
        ((3, width, local_width), (local_width, width)),
    )

    steps_round = iter(range(far))
    round_mlp, waiting, grads_mlp = (own_mlp, own_mlp), gather_start(own_mlp), None

    def advance_mlp():
        nonlocal round_mlp, waiting
        t = next(steps_round, None)
        if t is None:
            return nothing
        round_mlp, found = gather_step(t, round_mlp, None)
        waiting += found
        return zero(round_mlp[0])

    sends_att = scatter_start(terms_att, nothing)
    for t in range(far):
        sends_att = scatter_step(terms_att, t, sends_att, advance_mlp())
    round_att, waiting_att, grads_att = (sends_att, sends_att), gather_start(sends_att), None
    token = finish_token
    distance = 1
    for t in range(far):
        if distance < owners:
            small = small + zero(round_att[0])[:, :1]
            small = small + lax.ppermute(small, "ctx", [(c, c ^ distance) for c in range(owners)])
            distance *= 2
        later = advance_mlp()
        round_att, found = gather_step(t, round_att, token)
        if waiting:
            ready, waiting = waiting, []
            grads_mlp, token = unpack_mlp(ready, grads_mlp)
        token = token + later + zero(small)[:, :LANES]
        waiting_att += found
        if t == far - 2:
            grads_att, more = unpack_att(waiting_att[:-4], None)
            waiting_att = waiting_att[-4:]
            token = token + more
    while distance < owners:
        small = small + lax.ppermute(small, "ctx", [(c, c ^ distance) for c in range(owners)])
        distance *= 2
    if waiting:
        grads_mlp, _ = unpack_mlp(waiting, grads_mlp)
    grads_att, _ = unpack_att(waiting_att, grads_att)

    norm_sums = small[:, : 4 * width]
    norm_sums = (norm_sums + across(norm_sums)).reshape(4, width)
    at = 4 * width
    d_bias = small[0, at : at + width]
    d_b_up = small[0, at + width : at + width + hidden_units]
    d_b_qkv = small[0, at + width + hidden_units :].reshape(3, local_width)
    d_w_up, d_w_down = grads_mlp
    d_w_qkv, d_w_out = grads_att
    return (
        output,
        d_hidden,
        norm_sums[0],
        norm_sums[1],
        norm_sums[2],
        norm_sums[3],
        d_w_qkv,
        d_b_qkv,
        d_w_out,
        d_bias,
        d_w_up,
        d_b_up,
        d_w_down,
        d_bias,
    )


def solution(mesh):
    placed = (
        P("ctx", None),
        P(),
        P(),
        P(),
        P(),
        P(),
        P(None, None, "tp"),
        P(None, "tp"),
        P("tp", None),
        P(),
        P(None, "tp"),
        P("tp"),
        P("tp", None),
        P(),
        P("ctx", None),
    )
    return jax.shard_map(
        local,
        mesh=mesh,
        in_specs=placed,
        out_specs=(
            P("ctx", None),
            P("ctx", None),
            P(),
            P(),
            P(),
            P(),
            P(None, None, "tp"),
            P(None, "tp"),
            P("tp", None),
            P(),
            P(None, "tp"),
            P("tp"),
            P("tp", None),
            P(),
        ),
        check_vma=False,
    )
```

```python
import functools

import jax
import jax.numpy as jnp
import numpy as np
from jax import lax
from jax.experimental import pallas as pl
from jax.experimental.pallas import tpu as pltpu
from jax.sharding import PartitionSpec as P

HEAD_DIM = 64
ROT = 16
HALF = ROT // 2
BLOCK = 128
LANES = 128
KEYS = 512
MIB = 1 << 20

norm_eps = 1e-05
masked_score = -1e30
score_scale = HEAD_DIM ** (-0.5)
low = jnp.bfloat16
full = jnp.float32


def mm(left, right):
    return lax.dot_general(left, right, (((1,), (0,)), ((), ())), preferred_element_type=full)


def mm_nt(left, right):
    return lax.dot_general(left, right, (((1,), (1,)), ((), ())), preferred_element_type=full)


def turn(tensor):
    return tensor.astype(full).T.astype(low)


def lane_ids(shape):
    return lax.broadcasted_iota(jnp.int32, shape, len(shape) - 1)


def row_ids(shape):
    return lax.broadcasted_iota(jnp.int32, shape, len(shape) - 2)


def rotary_partner(tensor):
    lanes = lane_ids(tensor.shape)
    ahead = pltpu.roll(tensor, LANES - HALF, 1)
    behind = pltpu.roll(tensor, HALF, 1)
    return jnp.where(lanes % ROT < HALF, ahead, behind)


def spec_vmem():
    return pl.BlockSpec(memory_space=pltpu.VMEM)


def spec_smem():
    return pl.BlockSpec(memory_space=pltpu.SMEM)


def spec_hbm():
    return pl.BlockSpec(memory_space=pltpu.HBM)


def params(mib):
    return pltpu.CompilerParams(vmem_limit_bytes=mib * MIB)


def shape_of(shape, kind):
    return jax.ShapeDtypeStruct(shape, kind)


def block_tables(inverse, blocks):
    row = row_ids((BLOCK, LANES)).astype(full)
    start = blocks.astype(full) * float(BLOCK)
    return jnp.cos(row * inverse), jnp.sin(row * inverse), jnp.cos(start * inverse), jnp.sin(start * inverse)


def project_kernel(heads, pair_ref, inv_ref, *rest):
    given, rest = rest[:12], rest[12:]
    h1_ref, h2_ref, xhat_ref, std_ref, d_bias_ref, gains_ref, bias_ref, b_up_out_ref, packed = rest[:9]
    held, sems = rest[9:-1], rest[-1]
    copies = [pltpu.make_async_copy(src, dst, sems.at[i]) for i, (src, dst) in enumerate(zip(given, held))]
    for copy in copies:
        copy.start()
    (
        hidden_ref,
        g1_ref,
        c1_ref,
        g2_ref,
        c2_ref,
        cot_ref,
        w_out_ref,
        w_qkv_ref,
        b_qkv_ref,
        b_up_ref,
        b_out_ref,
        b_down_ref,
    ) = held
    rows = hidden_ref.shape[0]
    me = lax.axis_index("ctx")
    pair = pair_ref[me]
    total_blocks = 2 * pair_ref.shape[0]

    first = jnp.where(row_ids((8, LANES)) == 0, pair, total_blocks - 1 - pair)
    inverse = inv_ref[...]
    cos_row, sin_row, cos_block, sin_block = block_tables(inverse, first)
    in_head = lane_ids((BLOCK, LANES)) % HEAD_DIM
    tables = []
    for half in range(2):
        cos_at, sin_at = cos_block[half : half + 1], sin_block[half : half + 1]
        cosine = cos_row * cos_at - sin_row * sin_at
        sine = sin_row * cos_at + cos_row * sin_at
        cosine = jnp.where(in_head < ROT, cosine, 1.0)
        sine = jnp.where(in_head < HALF, -sine, jnp.where(in_head < ROT, sine, 0.0))
        tables.append((cosine, sine))
    cosine = jnp.concatenate([tables[0][0], tables[1][0]], axis=0)
    sine = jnp.concatenate([tables[0][1], tables[1][1]], axis=0)

    for copy in copies[:5]:
        copy.wait()
    x = hidden_ref[...].astype(full)
    centred = x - jnp.mean(x, axis=-1, keepdims=True)
    spread = jnp.mean(centred * centred, axis=-1, keepdims=True)
    inv_std = lax.rsqrt(spread + norm_eps)
    xhat = centred * inv_std
    xhat_ref[...] = xhat
    std_ref[...] = jnp.broadcast_to(inv_std, std_ref.shape)

    def as_row(ref):
        return ref[...].astype(full)[None, :]

    gain1, gain2 = as_row(g1_ref), as_row(g2_ref)
    h1 = (xhat * gain1 + as_row(c1_ref)).astype(low)
    h1_ref[...] = h1
    h2_ref[...] = (xhat * gain2 + as_row(c2_ref)).astype(low)
    gains_ref[0:1] = gain1
    gains_ref[1:2] = gain2
    for copy in copies[5:]:
        copy.wait()
    b_up_out_ref[...] = as_row(b_up_ref)
    bias_ref[0:1] = as_row(b_out_ref)
    bias_ref[1:2] = as_row(b_down_ref)
    d_bias_ref[...] = jnp.sum(cot_ref[...].astype(full), axis=0, keepdims=True)

    lane = lane_ids((rows, LANES))

    def projected(s):
        return mm(h1, w_qkv_ref[s]) + b_qkv_ref[s : s + 1].astype(full)

    def turned(tile):
        return tile * cosine + rotary_partner(tile) * sine

    queries, keys, values = projected(0), projected(1), projected(2)
    grads = mm_nt(cot_ref[...], w_out_ref[...])
    left = lane < HEAD_DIM
    for i in range(heads // 2):
        cut = slice(i * LANES, (i + 1) * LANES)
        q = turned(queries[:, cut]).astype(low).astype(full) * score_scale
        k = turned(keys[:, cut])
        v = values[:, cut]
        g = grads[:, cut]
        packed[2 * i, :, :LANES] = jnp.where(left, g, pltpu.roll(q, HEAD_DIM, 1)).astype(low)
        packed[2 * i, :, LANES:] = jnp.where(left, v, pltpu.roll(k, HEAD_DIM, 1)).astype(low)
        packed[2 * i + 1, :, :LANES] = jnp.where(left, pltpu.roll(g, HEAD_DIM, 1), q).astype(low)
        packed[2 * i + 1, :, LANES:] = jnp.where(left, pltpu.roll(v, HEAD_DIM, 1), k).astype(low)


def project(heads, pair_of, inverse, given):
    hidden, w_out, b_up = given[0], given[6], given[9]
    rows, width = hidden.shape
    outs = [
        shape_of((rows, width), low),
        shape_of((rows, width), low),
        shape_of((rows, width), full),
        shape_of((rows, LANES), full),
        shape_of((1, width), full),
        shape_of((2, width), full),
        shape_of((2, width), full),
        shape_of((1, b_up.shape[0]), full),
        shape_of((heads, rows, 2 * LANES), low),
    ]
    return pl.pallas_call(
        functools.partial(project_kernel, heads),
        out_shape=outs,
        in_specs=[spec_smem(), spec_vmem()] + [spec_hbm()] * len(given),
        out_specs=[spec_vmem()] * len(outs),
        scratch_shapes=[pltpu.VMEM(array.shape, array.dtype) for array in given]
        + [pltpu.SemaphoreType.DMA((len(given),))],
        compiler_params=params(60),
        cost_estimate=pl.CostEstimate(
            flops=2 * rows * width * 4 * w_out.shape[0], bytes_accessed=8 * MIB, transcendentals=0
        ),
        name="project",
    )(pair_of, inverse, *given)


def mlp_kernel(ids_ref, *rest):
    given, rest = rest[:6], rest[6:]
    part_ref, back_ref, sums_ref, d_b_up_ref, keep_ref, send_ref = rest[:6]
    h2_turned, part_acc, back_acc = rest[6:9]
    held, sems = rest[9:-1], rest[-1]
    copies = [pltpu.make_async_copy(src, dst, sems.at[i]) for i, (src, dst) in enumerate(zip(given, held))]
    h2_held, w_up_ref, b_up, cot_ref, w_down_ref, xhat_ref = held
    step = pl.program_id(0)
    steps = pl.num_programs(0)

    @pl.when(step == 0)
    def _():
        for copy in copies:
            copy.start()
        part_acc[...] = jnp.zeros_like(part_acc)
        back_acc[...] = jnp.zeros_like(back_acc)
        copies[0].wait()
        h2_turned[...] = turn(h2_held[...])
        for copy in copies[1:]:
            copy.wait()

    cot = cot_ref[...]
    at = [pl.multiple_of(ids_ref[b * steps + step] * LANES, LANES) for b in range(2)]
    w_up = jnp.concatenate([w_up_ref[:, pl.ds(i, LANES)] for i in at], axis=1)
    w_down = jnp.concatenate([w_down_ref[pl.ds(i, LANES), :] for i in at], axis=0)
    u = mm(h2_held[...], w_up) + jnp.concatenate([b_up[:, pl.ds(i, LANES)] for i in at], axis=1)
    cdf = 0.5 * (1.0 + lax.erf(u * np.float32(np.sqrt(0.5))))
    active = u * cdf
    active_low = active.astype(low)
    slope = cdf + u * jnp.exp(-0.5 * u * u) * np.float32(1.0 / np.sqrt(2.0 * np.pi))
    du = (mm_nt(cot, w_down) * slope).astype(low)
    part_acc[...] += mm(active_low, w_down)
    back_acc[...] += mm_nt(du, w_up)
    d_b_up = jnp.sum(du.astype(full), axis=0, keepdims=True)
    up = mm(h2_turned[...], du).astype(low)
    down = mm(active.T.astype(low), cot).astype(low)
    depth = up.shape[0]

    def put(b, grad_ref):
        grad_ref[:depth] = up[:, b * LANES : (b + 1) * LANES]
        for t in range(down.shape[1] // LANES):
            grad_ref[depth + t * LANES : depth + (t + 1) * LANES] = down[
                b * LANES : (b + 1) * LANES, t * LANES : (t + 1) * LANES
            ]

    for b in range(2):
        d_b_up_ref[:, pl.ds(at[b], LANES)] = d_b_up[:, b * LANES : (b + 1) * LANES]
    put(0, keep_ref)
    put(1, send_ref)

    @pl.when(step == steps - 1)
    def _():
        part_ref[...] = part_acc[...]
        back = back_acc[...]
        back_ref[...] = back.astype(low)
        sums_ref[0:1] = jnp.sum(back * xhat_ref[...], axis=0, keepdims=True)
        sums_ref[1:2] = jnp.sum(back, axis=0, keepdims=True)


def mlp(ids, *given):
    rows, width = given[0].shape
    hidden_units = given[1].shape[1]
    steps = hidden_units // LANES // 2
    whole = lambda shape: pl.BlockSpec(shape, lambda f, c: (0,) * len(shape))
    grads = pl.BlockSpec((2 * width, LANES), lambda f, c: (f, 0))
    outs = [
        shape_of((rows, width), full),
        shape_of((rows, width), low),
        shape_of((2, width), full),
        shape_of((1, hidden_units), full),
        shape_of((steps * 2 * width, LANES), low),
        shape_of((steps * 2 * width, LANES), low),
    ]
    return pl.pallas_call(
        mlp_kernel,
        grid_spec=pltpu.PrefetchScalarGridSpec(
            num_scalar_prefetch=1,
            grid=(steps,),
            in_specs=[spec_hbm()] * len(given),
            out_specs=[whole(array.shape) for array in outs[:4]] + [grads, grads],
            scratch_shapes=[
                pltpu.VMEM((width, rows), low),
                pltpu.VMEM((rows, width), full),
                pltpu.VMEM((rows, width), full),
            ]
            + [pltpu.VMEM(array.shape, array.dtype) for array in given]
            + [pltpu.SemaphoreType.DMA((len(given),))],
        ),
        out_shape=outs,
        compiler_params=params(60),
        cost_estimate=pl.CostEstimate(
            flops=12 * rows * width * hidden_units, bytes_accessed=20 * MIB, transcendentals=0
        ),
        name="feed_forward",
    )(ids, *given)


def attention_kernel(heads, group, pair_ref, inv_ref, token_ref, got_ref, *rest):
    del token_ref
    if group > 1:
        other_ref, out_ref, d_own_ref, d_other_ref, *rest = rest
    else:
        out_ref, d_own_ref, *rest = rest
    values_keys, turned_keys, sums, *rest = rest
    weights_in, weights_out, stored, peaks, totals, weighted, finals, block_cos, block_sin = rest

    rows = got_ref.shape[1]
    owners = pair_ref.shape[0]
    total_blocks = 2 * owners
    per_chunk = KEYS // BLOCK
    tasks = (total_blocks + 1 + per_chunk - 1) // per_chunk
    me = lax.axis_index("ctx")
    own_sub = lax.rem(me, group)

    def blocks_of(r, d):
        owner = r * group + lax.rem(own_sub + d, group)
        pair = pair_ref[owner]
        return pair, total_blocks - 1 - pair

    def place(tile, block):
        at = pl.multiple_of(block * BLOCK, BLOCK)
        values_keys[pl.ds(at, BLOCK), :] = tile
        turned_keys[:, pl.ds(at, BLOCK)] = turn(tile)

    for r in range(heads):
        for half, block in enumerate(blocks_of(r, 0)):
            place(got_ref[r, half * BLOCK : (half + 1) * BLOCK, LANES:], block)
        for d in range(1, group):
            for half, block in enumerate(blocks_of(r, d)):
                at = r * rows + half * BLOCK
                place(other_ref[d - 1, at : at + BLOCK, :], block)
    sums[...] = jnp.zeros_like(sums)

    lane = lane_ids((BLOCK, LANES))
    left = lane < HEAD_DIM
    in_key = lane - HEAD_DIM
    moving = (in_key >= 0) & (in_key < ROT)
    forward = (in_key >= 0) & (in_key < HALF)
    cos_row, sin_row, block_cos[...], block_sin[...] = block_tables(inv_ref[...], row_ids(block_cos.shape))

    def rotated_back(tile, block):
        cos_at, sin_at = block_cos[pl.ds(block, 1), :], block_sin[pl.ds(block, 1), :]
        cosine = jnp.where(moving, cos_row * cos_at - sin_row * sin_at, 1.0)
        sine = sin_row * cos_at + cos_row * sin_at
        sine = jnp.where(moving, jnp.where(forward, sine, -sine), 0.0)
        return tile * cosine + rotary_partner(tile) * sine

    offset = row_ids((BLOCK, BLOCK)) - lane_ids((BLOCK, BLOCK))

    def one_pair(i, carry):
        blocks = blocks_of(i, 0)
        first = blocks[0] // per_chunk + 1
        for half in range(2):
            both = got_ref[i, half * BLOCK : (half + 1) * BLOCK, :LANES]
            both_turned = turn(both)
            upper = row_ids((LANES, BLOCK)) < HEAD_DIM
            zero = jnp.zeros_like(both_turned)
            weights_in[half, :, :BLOCK] = jnp.where(upper, both_turned, zero)
            weights_in[half, :, BLOCK:] = jnp.where(upper, zero, both_turned)
            weights_out[half, :BLOCK, :] = jnp.where(left, both, zero)
            weights_out[half, BLOCK:, :] = jnp.where(left, zero, both)
        finals[...] = jnp.zeros_like(finals)

        def task(t):
            is_low = t < first
            chunk = jnp.where(is_low, first - 1 - t, t - first)
            return is_low, chunk

        runs = KEYS // BLOCK
        for t in range(tasks):
            is_low, chunk = task(t)
            weights = weights_in[jnp.where(is_low, 0, 1)]
            for u in range(runs):
                at = pl.multiple_of(chunk * KEYS + u * BLOCK, BLOCK)
                sub = slice(u * BLOCK, (u + 1) * BLOCK)
                both = mm(values_keys[pl.ds(at, BLOCK), :], weights)
                grads = both[:, :BLOCK]
                scores = both[:, BLOCK:]
                if t in (0, tasks - 1):
                    query_at = blocks[0 if t == 0 else 1] * BLOCK
                    scores = jnp.where(offset <= query_at - at, scores, masked_score)
                peak = jnp.max(scores, axis=0, keepdims=True)
                raised = jnp.exp(scores - peak)
                stored[t, sub, :BLOCK] = raised
                stored[t, sub, BLOCK:] = grads
                line = t * runs + u
                peaks[line : line + 1] = peak
                totals[line : line + 1] = jnp.sum(raised, axis=0, keepdims=True)
                weighted[line : line + 1] = jnp.sum(raised * grads, axis=0, keepdims=True)

        in_low = row_ids((tasks * runs, BLOCK)) < first * runs

        def finish(mine):
            top = jnp.max(jnp.where(mine, peaks[...], masked_score), axis=0, keepdims=True)
            factor = jnp.where(mine, jnp.exp(peaks[...] - top), 0.0)
            inverse = 1.0 / jnp.sum(totals[...] * factor, axis=0, keepdims=True)
            return factor * inverse, jnp.sum(weighted[...] * factor, axis=0, keepdims=True) * inverse

        (low_factor, low_delta), (high_factor, high_delta) = finish(in_low), finish(jnp.logical_not(in_low))
        peaks[...] = low_factor + high_factor

        for t in range(tasks):
            is_low, chunk = task(t)
            half = jnp.where(is_low, 0, 1)
            weights = weights_out[half]
            delta = jnp.where(is_low, low_delta, high_delta)
            parts = []
            for u in range(runs):
                sub = slice(u * BLOCK, (u + 1) * BLOCK)
                probs = stored[t, sub, :BLOCK] * peaks[t * runs + u : t * runs + u + 1]
                d_scores = probs * (stored[t, sub, BLOCK:] - delta)
                both = jnp.concatenate([probs, d_scores], axis=1).astype(low)
                at = pl.multiple_of(chunk * KEYS + u * BLOCK, BLOCK)
                sums[pl.ds(at, BLOCK), :] += mm(both, weights)
                parts.append(both)
            at = pl.multiple_of(chunk * KEYS, KEYS)
            finals[half] += mm(turned_keys[:, pl.ds(at, KEYS)], jnp.concatenate(parts, axis=0))

        for half in range(2):
            both = jnp.concatenate(
                [finals[half, :HEAD_DIM, :BLOCK], finals[half, HEAD_DIM:, BLOCK:] * score_scale], axis=0
            ).T
            out_ref[i, half * BLOCK : (half + 1) * BLOCK, :] = rotated_back(both, blocks[half]).astype(low)
        return carry

    lax.fori_loop(0, heads, one_pair, 0)

    for r in range(heads):
        for d in range(group):
            for half, block in enumerate(blocks_of(r, d)):
                at = r * rows + half * BLOCK
                tile = rotated_back(sums[pl.ds(pl.multiple_of(block * BLOCK, BLOCK), BLOCK), :], block)
                if d == 0:
                    d_own_ref[at : at + BLOCK, :] = tile
                else:
                    d_other_ref[d - 1, at : at + BLOCK, :] = tile


def attention(heads, group, pair_of, inverse, token, got, other):
    rows = got.shape[1]
    owners = pair_of.shape[0]
    total_keys = owners * rows
    tasks = (2 * owners + KEYS // BLOCK) // (KEYS // BLOCK)
    operands = [pair_of, inverse, token, got]
    outs = [shape_of((heads, rows, LANES), low), shape_of((heads * rows, LANES), full)]
    if group > 1:
        operands.append(other)
        outs.append(shape_of((group - 1, heads * rows, LANES), full))
    return pl.pallas_call(
        functools.partial(attention_kernel, heads, group),
        out_shape=outs,
        in_specs=[spec_smem()] + [spec_vmem()] * (len(operands) - 1),
        out_specs=[spec_vmem()] * len(outs),
        scratch_shapes=[
            pltpu.VMEM((total_keys, LANES), low),
            pltpu.VMEM((LANES, total_keys), low),
            pltpu.VMEM((total_keys, LANES), full),
            pltpu.VMEM((2, LANES, 2 * BLOCK), low),
            pltpu.VMEM((2, 2 * BLOCK, LANES), low),
            pltpu.VMEM((tasks, KEYS, 2 * BLOCK), full),
            pltpu.VMEM((tasks * KEYS // BLOCK, BLOCK), full),
            pltpu.VMEM((tasks * KEYS // BLOCK, BLOCK), full),
            pltpu.VMEM((tasks * KEYS // BLOCK, BLOCK), full),
            pltpu.VMEM((2, LANES, 2 * BLOCK), full),
            pltpu.VMEM((2 * owners, LANES), full),
            pltpu.VMEM((2 * owners, LANES), full),
        ],
        compiler_params=params(12 + total_keys * 9 * 256 // MIB),
        cost_estimate=pl.CostEstimate(
            flops=2_500_000_000 * heads, bytes_accessed=2 * MIB, transcendentals=0
        ),
        name="attention",
    )(*operands)


def combine_kernel(heads, terms, *refs):
    out_ref = refs[-1]
    rows = out_ref.shape[1]
    for r in range(heads):
        cut = slice(r * rows, (r + 1) * rows)
        total = refs[0][cut, :]
        for term in refs[1:terms]:
            total = total + term[cut, :]
        out_ref[r, :, LANES:] = total.astype(low)
    at = 0
    for first_ref in refs[terms:-1]:
        out_ref[at : at + first_ref.shape[0], :, :LANES] = first_ref[...]
        at += first_ref.shape[0]


def combine(heads, terms, firsts):
    rows = firsts[0].shape[1]
    return pl.pallas_call(
        functools.partial(combine_kernel, heads, len(terms)),
        out_shape=shape_of((heads, rows, 2 * LANES), low),
        in_specs=[spec_vmem()] * (len(firsts) + len(terms)),
        out_specs=spec_vmem(),
        compiler_params=params(24),
        cost_estimate=pl.CostEstimate(flops=10**7, bytes_accessed=3 * MIB, transcendentals=0),
        name="combine",
    )(*terms, *firsts)


def return_kernel(heads, early, ids_ref, *rest):
    given, rest = rest[:7], rest[7:]
    both_ref, sums_ref, d_b_ref, keep_ref, early_ref, send_ref = rest[:6]
    attended, d_proj, grads = rest[6:9]
    held, sems = rest[9:-1], rest[-1]
    copies = [pltpu.make_async_copy(src, dst, sems.at[i]) for i, (src, dst) in enumerate(zip(given, held))]
    for copy in copies:
        copy.start()
    got_ref, w_out_ref, part_ref, w_qkv_ref, xhat_ref, h1_ref, cot_ref = held
    copies[0].wait()
    chunk_rows = grads.shape[1]
    chips = keep_ref.shape[0]

    def put(at, tile):
        step = min(chunk_rows, tile.shape[0])
        for off in range(0, tile.shape[0], step):
            chunk, inside = divmod(at + off, chunk_rows)
            grads[chunk, inside : inside + step] = tile[off : off + step]

    rows = h1_ref.shape[0]
    left = lane_ids((rows, LANES)) < HEAD_DIM
    for i in range(heads // 2):
        cut = slice(i * LANES, (i + 1) * LANES)
        a, b = got_ref[2 * i, :, :LANES].astype(full), got_ref[2 * i + 1, :, :LANES].astype(full)
        attended[:, cut] = jnp.where(left, a, pltpu.roll(b, HEAD_DIM, 1)).astype(low)
        d_proj[0, :, cut] = jnp.where(left, pltpu.roll(a, HEAD_DIM, 1), b).astype(low)
        a, b = got_ref[2 * i, :, LANES:].astype(full), got_ref[2 * i + 1, :, LANES:].astype(full)
        d_proj[2, :, cut] = jnp.where(left, a, pltpu.roll(b, HEAD_DIM, 1)).astype(low)
        d_proj[1, :, cut] = jnp.where(left, pltpu.roll(a, HEAD_DIM, 1), b).astype(low)
    for copy in copies[1:3]:
        copy.wait()
    both_ref[:rows] = (part_ref[...] + mm(attended[...], w_out_ref[...])).astype(low)
    for copy in copies[3:]:
        copy.wait()
    back = mm_nt(d_proj[0], w_qkv_ref[0]) + mm_nt(d_proj[1], w_qkv_ref[1]) + mm_nt(d_proj[2], w_qkv_ref[2])
    both_ref[rows:] = back.astype(low)
    sums_ref[0:1] = jnp.sum(back * xhat_ref[...], axis=0, keepdims=True)
    sums_ref[1:2] = jnp.sum(back, axis=0, keepdims=True)
    h1_turned = turn(h1_ref[...])
    depth, tiles = h1_turned.shape[0], heads // 2
    for s in range(3):
        d_b_ref[s : s + 1] = jnp.sum(d_proj[s].astype(full), axis=0, keepdims=True)
        grad = mm(h1_turned, d_proj[s]).astype(low)
        for t in range(tiles):
            put((s * tiles + t) * depth, grad[:, t * LANES : (t + 1) * LANES])
    grad = mm(turn(attended[...]), cot_ref[...]).astype(low)
    height = grad.shape[0]
    for t in range(depth // LANES):
        put(3 * tiles * depth + t * height, grad[:, t * LANES : (t + 1) * LANES])
    for t in range(chips):
        keep_ref[t] = grads[ids_ref[t]]
        target = early_ref.at[t] if t < early else send_ref.at[t - early]
        target[...] = grads[ids_ref[chips + t]]


def back_projections(heads, early, ids, *given):
    rows, width = given[2].shape
    local_width = given[1].shape[0]
    chips = ids.shape[0] // 2
    chunk_rows = 4 * width * local_width // LANES // (2 * chips)
    outs = [
        shape_of((2 * rows, width), low),
        shape_of((2, width), full),
        shape_of((3, local_width), full),
        shape_of((chips, chunk_rows, LANES), low),
        shape_of((early, chunk_rows, LANES), low),
        shape_of((chips - early, chunk_rows, LANES), low),
    ]
    return pl.pallas_call(
        functools.partial(return_kernel, heads, early),
        out_shape=outs,
        in_specs=[spec_smem()] + [spec_hbm()] * len(given),
        out_specs=[spec_vmem()] * len(outs),
        scratch_shapes=[
            pltpu.VMEM((rows, local_width), low),
            pltpu.VMEM((3, rows, local_width), low),
            pltpu.VMEM((2 * chips, chunk_rows, LANES), low),
        ]
        + [pltpu.VMEM(array.shape, array.dtype) for array in given]
        + [pltpu.SemaphoreType.DMA((len(given),))],
        compiler_params=params(60),
        cost_estimate=pl.CostEstimate(
            flops=16 * rows * width * local_width, bytes_accessed=14 * MIB, transcendentals=0
        ),
        name="back_projections",
    )(ids, *given)


def finish_kernel(
    hidden_ref, cot_ref, xhat_ref, std_ref, gains_ref, bias_ref, ours_ref, theirs_ref, e2_ours_ref, e2_theirs_ref, out_ref, grad_ref, token_ref
):
    rows = hidden_ref.shape[0]
    gains = gains_ref[...]
    biases = bias_ref[...]
    summed = ours_ref[:rows].astype(full) + theirs_ref[:rows].astype(full)
    out_ref[...] = (hidden_ref[...].astype(full) + summed + biases[0:1] + biases[1:2]).astype(low)
    e1 = ours_ref[rows:].astype(full) + theirs_ref[rows:].astype(full)
    e2 = e2_ours_ref[...].astype(full) + e2_theirs_ref[...].astype(full)
    f = e1 * gains[0:1] + e2 * gains[1:2]
    xhat = xhat_ref[...]
    inv_std = std_ref[:, 0:1]
    grad_ref[...] = cot_ref[...].astype(full) + inv_std * (
        f - jnp.mean(f, axis=-1, keepdims=True) - xhat * jnp.mean(f * xhat, axis=-1, keepdims=True)
    )
    token_ref[...] = jnp.zeros_like(token_ref)


def finish(*operands):
    rows, width = operands[0].shape
    return pl.pallas_call(
        finish_kernel,
        out_shape=[shape_of((rows, width), low), shape_of((rows, width), full), shape_of((1, LANES), full)],
        in_specs=[spec_vmem()] * len(operands),
        out_specs=[spec_vmem()] * 3,
        compiler_params=params(24),
        cost_estimate=pl.CostEstimate(flops=10**7, bytes_accessed=8 * MIB, transcendentals=0),
        name="finish",
    )(*operands)


def to_attention(width, local_width, source, refs, base, unit):
    qkv_ref, out_ref = refs
    tiles = local_width // LANES
    split = 3 * tiles * width
    tile = base // width
    row = pl.multiple_of(lax.rem(base, width), unit)
    column = pl.multiple_of(lax.rem(tile, tiles) * LANES, LANES)
    yield base < split, source, qkv_ref.at[jnp.minimum(tile // tiles, 2), pl.ds(row, unit), pl.ds(column, LANES)]
    after = jnp.maximum(base - split, 0)
    row = pl.multiple_of(lax.rem(after, local_width), unit)
    column = pl.multiple_of(after // local_width * LANES, LANES)
    yield base >= split, source, out_ref.at[pl.ds(row, unit), pl.ds(column, LANES)]


def unpack_mlp(core, ours, theirs, width, hidden_units):
    blocks = hidden_units // LANES // 2

    def body(core_ref, ours_ref, theirs_ref, up_ref, down_ref):
        def put(in_ref):
            up_ref[...] = in_ref[:width].astype(full)
            for t in range(width // LANES):
                at = width + t * LANES
                down_ref[:, t * LANES : (t + 1) * LANES] = in_ref[at : at + LANES].astype(full)

        step = pl.program_id(0)
        pl.when(step < blocks)(functools.partial(put, ours_ref))
        pl.when(step >= blocks)(functools.partial(put, theirs_ref))

    def place(f, core_ref):
        return jnp.where(f < blocks, core_ref[0] * blocks + f, (1 - core_ref[0]) * blocks + f - blocks)

    return pl.pallas_call(
        body,
        grid_spec=pltpu.PrefetchScalarGridSpec(
            num_scalar_prefetch=1,
            grid=(2 * blocks,),
            in_specs=[
                pl.BlockSpec((2 * width, LANES), lambda f, c: (jnp.minimum(f, blocks - 1), 0)),
                pl.BlockSpec((2 * width, LANES), lambda f, c: (jnp.maximum(f - blocks, 0), 0)),
            ],
            out_specs=[
                pl.BlockSpec((width, LANES), lambda f, c: (0, place(f, c))),
                pl.BlockSpec((LANES, width), lambda f, c: (place(f, c), 0)),
            ],
        ),
        out_shape=[shape_of((width, hidden_units), full), shape_of((hidden_units, width), full)],
        compiler_params=params(24),
        cost_estimate=pl.CostEstimate(
            flops=10**6, bytes_accessed=12 * width * hidden_units, transcendentals=0
        ),
        name="unpack_feed_forward",
    )(core[None], ours, theirs)


def unpack_kernel(route, count, unit, has_old, ids_ref, *rest):
    parts, rest = rest[:count], rest[count:]
    rest = rest[2:] if has_old else rest
    targets, (token_ref, held, sems) = rest[:2], rest[2:]
    token_ref[...] = jnp.zeros_like(token_ref)
    chunk_rows = parts[0].shape[0]
    units = chunk_rows // unit
    per_unit = sems.shape[0] // (count * units)

    def moves():
        for i in range(count):
            for j in range(units):
                source = held.at[i, pl.ds(j * unit, unit), :]
                base = ids_ref[i] * chunk_rows + j * unit
                for n, (applies, piece, target) in enumerate(route(source, targets, base, unit)):
                    sem = sems.at[(i * units + j) * per_unit + n]
                    yield i, applies, pltpu.make_async_copy(piece, target, sem)

    done = -1
    for i, applies, copy in moves():
        if i != done:
            held[i] = parts[i][...].astype(full)
            done = i
        pl.when(applies)(copy.start)
    for i, applies, copy in moves():
        pl.when(applies)(copy.wait)


def unpack(name, route, cases, unit, shapes, ids, parts, old):
    count = len(parts)
    chunk_rows = parts[0].shape[0]
    operands = [ids, *parts, *(old or ())]
    return pl.pallas_call(
        functools.partial(unpack_kernel, route, count, unit, old is not None),
        out_shape=[shape_of(shape, full) for shape in shapes] + [shape_of((1, LANES), full)],
        in_specs=[spec_smem()] + [spec_vmem()] * count + [spec_hbm()] * (len(operands) - 1 - count),
        out_specs=[spec_hbm()] * 2 + [spec_vmem()],
        input_output_aliases={} if old is None else {1 + count: 0, 2 + count: 1},
        scratch_shapes=[
            pltpu.VMEM((count, chunk_rows, LANES), full),
            pltpu.SemaphoreType.DMA((count * (chunk_rows // unit) * cases,)),
        ],
        compiler_params=params(8 + count * chunk_rows * 3 * LANES * 2 // MIB),
        cost_estimate=pl.CostEstimate(
            flops=10**6, bytes_accessed=count * chunk_rows * LANES * 6, transcendentals=0
        ),
        name=name,
    )(*operands)


def local(
    hidden,
    pair_of,
    ln1_gain,
    ln1_bias,
    ln2_gain,
    ln2_bias,
    w_qkv,
    b_qkv,
    w_out,
    b_out,
    w_up,
    b_up,
    w_down,
    b_down,
    cotangent,
):
    owners = lax.axis_size("ctx")
    sides = lax.axis_size("tp")
    rows, width = hidden.shape
    local_width = w_qkv.shape[2]
    hidden_units = w_up.shape[1]
    heads = local_width // HEAD_DIM
    group = owners // heads

    exponent = np.arange(0, ROT, 2, dtype=np.float32) / np.float32(ROT)
    inverse = jnp.asarray(np.tile(np.float32(10000.0) ** (-exponent), LANES // HALF)[None, :], full)
    order = (0, 2, 4, 6, 7, 5, 3, 1) if owners == 16 else tuple(range(owners // 2))
    chips = len(order)

    def to_heads(array):
        groups = [[h * group + g for h in range(heads)] for g in range(group)]
        return lax.all_to_all(array, "ctx", 0, 0, axis_index_groups=groups, tiled=True)

    def group_shift(array, d):
        pairs = [(c, c // group * group + (c % group + d) % group) for c in range(owners)]
        return lax.ppermute(array, "ctx", pairs)

    me = lax.axis_index("ctx")
    chip, core = me // 2, lax.rem(me, 2)
    place = sum(jnp.where(chip == c, i, 0) for i, c in enumerate(order))
    way = 1 - 2 * core
    far, near = chips // 2, chips - 1 - chips // 2

    def ring(array, forward):
        pairs = []
        for i, c in enumerate(order):
            for k in range(2):
                step = 1 if (k == 0) == forward else -1
                pairs.append((2 * c + k, 2 * order[(i + step) % chips] + k))
        return lax.ppermute(array, "ctx", pairs)

    def other_core(array):
        return lax.ppermute(array, "ctx", [(c, c ^ 1) for c in range(owners)])

    def across(array):
        return lax.ppermute(array, "tp", [(t, (t + 1) % sides) for t in range(sides)])

    def target(distance):
        return lax.rem(place + way * distance + chips, chips)

    def zero(array):
        return array[:1].astype(full) * 0.0

    slots = [far, -near]
    for t in range(1, far):
        slots += [far - t] if t >= near else [far - t, t - near]
    slots.append(0)
    early = 2
    slot_ids = jnp.stack(
        [core * chips + target(d) for d in slots] + [(1 - core) * chips + target(-d) for d in slots]
    )

    def terms_of(keep, came):
        def term(i):
            return keep[i].astype(full) + came[i].astype(full)

        return {d: term(i) for i, d in enumerate(slots)}

    def scatter_start(terms, token):
        return (terms[far] + token).astype(low), (terms[-near] + token).astype(low)

    def scatter_step(terms, t, sends, token):
        long_send, short_send = sends
        long_got = ring(long_send, True).astype(full) + token
        last = t == far - 1
        long_next = long_got if last else (long_got + terms[far - 1 - t]).astype(low)
        short_next = short_send
        if t < near:
            short_got = ring(short_send, False).astype(full) + token
            short_next = short_got if t == near - 1 else (short_got + terms[t + 1 - near]).astype(low)
        if last:
            return (terms[0] + long_next + short_next).astype(low)
        return long_next, short_next

    base, other_base = core * chips, (1 - core) * chips

    def gather_start(own):
        return [(own, base + place), (other_core(own), other_base + place)]

    def gather_step(t, sends, token):
        long_send, short_send = sends
        if token is not None:
            long_send = (long_send.astype(full) + token).astype(low)
        long_got = ring(long_send, True)
        found = [(long_got, base + target(-t - 1)), (other_core(long_got), other_base + target(t + 1))]
        short_got = short_send
        if t < near:
            if token is not None:
                short_send = (short_send.astype(full) + token).astype(low)
            short_got = ring(short_send, False)
            found += [(short_got, base + target(t + 1)), (other_core(short_got), other_base + target(-t - 1))]
        return (long_got, short_got), found

    h1, h2, xhat, inv_std, d_bias, gains, biases, b_up_row, packed = project(
        heads,
        pair_of,
        inverse,
        (hidden, ln1_gain, ln1_bias, ln2_gain, ln2_bias, cotangent, w_out, w_qkv, b_qkv, b_up, b_out, b_down),
    )
    got = to_heads(packed)

    blocks = hidden_units // LANES // 2
    mlp_ids = jnp.concatenate([core * blocks + jnp.arange(blocks), (1 - core) * blocks + jnp.arange(blocks)])
    part, back2, sums2, d_b_up, keep_mlp, send_mlp = mlp(
        mlp_ids.astype(jnp.int32), h2, w_up, b_up_row, cotangent, w_down, xhat
    )
    same_core = [[2 * i + k for i in range(chips)] for k in range(2)]
    half_mlp = (keep_mlp.astype(full) + other_core(send_mlp).astype(full)).astype(low)
    own_mlp = lax.psum_scatter(half_mlp, "ctx", scatter_dimension=0, axis_index_groups=same_core, tiled=True)
    theirs2 = across(back2)
    nothing = jnp.zeros((1, LANES), full)

    other = None
    if group > 1:
        mine = got[:, :, LANES:].reshape(heads * rows, LANES)
        other = jnp.stack([group_shift(mine, group - d) for d in range(1, group)])
    first, d_own, *d_other = attention(heads, group, pair_of, inverse, half_mlp[:16], got, other)
    terms = [d_own] + [group_shift(d_other[0][d - 1], d) for d in range(1, group)]
    backs = to_heads(combine(heads, terms, [first]))
    xhat_later = xhat + zero(own_mlp)[:, :1]

    both, sums1, d_b_qkv, keep, early_att, send_att = back_projections(
        heads, early, slot_ids.astype(jnp.int32), backs, w_out, part, w_qkv, xhat_later, h1, cotangent
    )
    half_mlp = lax.all_gather(own_mlp, "ctx", axis=0, axis_index_groups=same_core, tiled=True)
    other_half = other_core(half_mlp)
    theirs = across(both)
    output, d_hidden, finish_token = finish(
        hidden, cotangent, xhat, inv_std, gains, biases, both, theirs, back2, theirs2
    )
    halves = [other_core(array) for array in (early_att, send_att)]
    terms_att = terms_of(keep, [half[i] for half in halves for i in range(half.shape[0])])

    small = jnp.concatenate(
        [sums1.reshape(1, -1), sums2.reshape(1, -1), d_bias, d_b_up, d_b_qkv.reshape(1, -1)], axis=1
    )

    def unpack_some(name, route, cases, unit, shapes, found, old):
        parts, ids = zip(*found)
        *old, token = unpack(name, route, cases, unit, shapes, jnp.stack(ids), parts, old)
        return old, token

    unit_att = min(keep.shape[1], local_width)
    unpack_att = functools.partial(
        unpack_some,
        "unpack_attention",
        functools.partial(to_attention, width, local_width),
        2,
        unit_att,
        ((3, width, local_width), (local_width, width)),
    )

    sends_att = scatter_start(terms_att, nothing)
    for t in range(far):
        sends_att = scatter_step(terms_att, t, sends_att, nothing)
    round_att, waiting_att, grads_att = (sends_att, sends_att), gather_start(sends_att), None
    token = finish_token
    distance = 1
    for t in range(far):
        if distance < owners:
            small = small + zero(round_att[0])[:, :1]
            small = small + lax.ppermute(small, "ctx", [(c, c ^ distance) for c in range(owners)])
            distance *= 2
        round_att, found = gather_step(t, round_att, token)
        token = zero(small)[:, :LANES]
        waiting_att += found
        if t == far - 2:
            grads_att, more = unpack_att(waiting_att[:-4], None)
            waiting_att = waiting_att[-4:]
            token = token + more
    while distance < owners:
        small = small + lax.ppermute(small, "ctx", [(c, c ^ distance) for c in range(owners)])
        distance *= 2
    grads_att, _ = unpack_att(waiting_att, grads_att)
    d_w_up, d_w_down = unpack_mlp(core, half_mlp, other_half, width, hidden_units)

    norm_sums = small[:, : 4 * width]
    norm_sums = (norm_sums + across(norm_sums)).reshape(4, width)
    at = 4 * width
    d_bias = small[0, at : at + width]
    d_b_up = small[0, at + width : at + width + hidden_units]
    d_b_qkv = small[0, at + width + hidden_units :].reshape(3, local_width)
    d_w_qkv, d_w_out = grads_att
    return (
        output,
        d_hidden,
        norm_sums[0],
        norm_sums[1],
        norm_sums[2],
        norm_sums[3],
        d_w_qkv,
        d_b_qkv,
        d_w_out,
        d_bias,
        d_w_up,
        d_b_up,
        d_w_down,
        d_bias,
    )


def solution(mesh):
    placed = (
        P("ctx", None),
        P(),
        P(),
        P(),
        P(),
        P(),
        P(None, None, "tp"),
        P(None, "tp"),
        P("tp", None),
        P(),
        P(None, "tp"),
        P("tp"),
        P("tp", None),
        P(),
        P("ctx", None),
    )
    return jax.shard_map(
        local,
        mesh=mesh,
        in_specs=placed,
        out_specs=(
            P("ctx", None),
            P("ctx", None),
            P(),
            P(),
            P(),
            P(),
            P(None, None, "tp"),
            P(None, "tp"),
            P("tp", None),
            P(),
            P(None, "tp"),
            P("tp"),
            P("tp", None),
            P(),
        ),
        check_vma=False,
    )
```

```python
import functools

import jax
import jax.numpy as jnp
import numpy as np
from jax import lax
from jax.experimental import pallas as pl
from jax.experimental.pallas import tpu as pltpu
from jax.sharding import PartitionSpec as P

HEAD_DIM = 64
ROT = 16
HALF = ROT // 2
BLOCK = 128
LANES = 128
KEYS = 512
MIB = 1 << 20

norm_eps = 1e-05
masked_score = -1e30
score_scale = HEAD_DIM ** (-0.5)
low = jnp.bfloat16
full = jnp.float32


def mm(left, right):
    return lax.dot_general(left, right, (((1,), (0,)), ((), ())), preferred_element_type=full)


def mm_nt(left, right):
    return lax.dot_general(left, right, (((1,), (1,)), ((), ())), preferred_element_type=full)


def turn(tensor):
    return tensor.astype(full).T.astype(low)


def lane_ids(shape):
    return lax.broadcasted_iota(jnp.int32, shape, len(shape) - 1)


def row_ids(shape):
    return lax.broadcasted_iota(jnp.int32, shape, len(shape) - 2)


def rotary_partner(tensor):
    lanes = lane_ids(tensor.shape)
    ahead = pltpu.roll(tensor, LANES - HALF, 1)
    behind = pltpu.roll(tensor, HALF, 1)
    return jnp.where(lanes % ROT < HALF, ahead, behind)


def spec_vmem():
    return pl.BlockSpec(memory_space=pltpu.VMEM)


def spec_smem():
    return pl.BlockSpec(memory_space=pltpu.SMEM)


def spec_hbm():
    return pl.BlockSpec(memory_space=pltpu.HBM)


def params(mib):
    return pltpu.CompilerParams(vmem_limit_bytes=mib * MIB)


def shape_of(shape, kind):
    return jax.ShapeDtypeStruct(shape, kind)


def block_tables(inverse, blocks):
    row = row_ids((BLOCK, LANES)).astype(full)
    start = blocks.astype(full) * float(BLOCK)
    return jnp.cos(row * inverse), jnp.sin(row * inverse), jnp.cos(start * inverse), jnp.sin(start * inverse)


def project_kernel(heads, pair_ref, inv_ref, *rest):
    given, rest = rest[:12], rest[12:]
    h1_ref, h2_ref, xhat_ref, std_ref, d_bias_ref, gains_ref, bias_ref, b_up_out_ref, packed = rest[:9]
    held, sems = rest[9:-1], rest[-1]
    copies = [pltpu.make_async_copy(src, dst, sems.at[i]) for i, (src, dst) in enumerate(zip(given, held))]
    for copy in copies:
        copy.start()
    (
        hidden_ref,
        g1_ref,
        c1_ref,
        g2_ref,
        c2_ref,
        cot_ref,
        w_out_ref,
        w_qkv_ref,
        b_qkv_ref,
        b_up_ref,
        b_out_ref,
        b_down_ref,
    ) = held
    rows = hidden_ref.shape[0]
    me = lax.axis_index("ctx")
    pair = pair_ref[me]
    total_blocks = 2 * pair_ref.shape[0]

    first = jnp.where(row_ids((8, LANES)) == 0, pair, total_blocks - 1 - pair)
    inverse = inv_ref[...]
    cos_row, sin_row, cos_block, sin_block = block_tables(inverse, first)
    in_head = lane_ids((BLOCK, LANES)) % HEAD_DIM
    tables = []
    for half in range(2):
        cos_at, sin_at = cos_block[half : half + 1], sin_block[half : half + 1]
        cosine = cos_row * cos_at - sin_row * sin_at
        sine = sin_row * cos_at + cos_row * sin_at
        cosine = jnp.where(in_head < ROT, cosine, 1.0)
        sine = jnp.where(in_head < HALF, -sine, jnp.where(in_head < ROT, sine, 0.0))
        tables.append((cosine, sine))
    cosine = jnp.concatenate([tables[0][0], tables[1][0]], axis=0)
    sine = jnp.concatenate([tables[0][1], tables[1][1]], axis=0)

    for copy in copies[:5]:
        copy.wait()
    x = hidden_ref[...].astype(full)
    centred = x - jnp.mean(x, axis=-1, keepdims=True)
    spread = jnp.mean(centred * centred, axis=-1, keepdims=True)
    inv_std = lax.rsqrt(spread + norm_eps)
    xhat = centred * inv_std
    xhat_ref[...] = xhat
    std_ref[...] = jnp.broadcast_to(inv_std, std_ref.shape)

    def as_row(ref):
        return ref[...].astype(full)[None, :]

    gain1, gain2 = as_row(g1_ref), as_row(g2_ref)
    h1 = (xhat * gain1 + as_row(c1_ref)).astype(low)
    h1_ref[...] = h1
    h2_ref[...] = (xhat * gain2 + as_row(c2_ref)).astype(low)
    gains_ref[0:1] = gain1
    gains_ref[1:2] = gain2
    for copy in copies[5:]:
        copy.wait()
    b_up_out_ref[...] = as_row(b_up_ref)
    bias_ref[0:1] = as_row(b_out_ref)
    bias_ref[1:2] = as_row(b_down_ref)
    d_bias_ref[...] = jnp.sum(cot_ref[...].astype(full), axis=0, keepdims=True)

    lane = lane_ids((rows, LANES))

    def projected(s):
        return mm(h1, w_qkv_ref[s]) + b_qkv_ref[s : s + 1].astype(full)

    def turned(tile):
        return tile * cosine + rotary_partner(tile) * sine

    queries, keys, values = projected(0), projected(1), projected(2)
    grads = mm_nt(cot_ref[...], w_out_ref[...])
    left = lane < HEAD_DIM
    for i in range(heads // 2):
        cut = slice(i * LANES, (i + 1) * LANES)
        q = turned(queries[:, cut]).astype(low).astype(full) * score_scale
        k = turned(keys[:, cut])
        v = values[:, cut]
        g = grads[:, cut]
        packed[2 * i, :, :LANES] = jnp.where(left, g, pltpu.roll(q, HEAD_DIM, 1)).astype(low)
        packed[2 * i, :, LANES:] = jnp.where(left, v, pltpu.roll(k, HEAD_DIM, 1)).astype(low)
        packed[2 * i + 1, :, :LANES] = jnp.where(left, pltpu.roll(g, HEAD_DIM, 1), q).astype(low)
        packed[2 * i + 1, :, LANES:] = jnp.where(left, pltpu.roll(v, HEAD_DIM, 1), k).astype(low)


def project(heads, pair_of, inverse, given):
    hidden, w_out, b_up = given[0], given[6], given[9]
    rows, width = hidden.shape
    outs = [
        shape_of((rows, width), low),
        shape_of((rows, width), low),
        shape_of((rows, width), full),
        shape_of((rows, LANES), full),
        shape_of((1, width), full),
        shape_of((2, width), full),
        shape_of((2, width), full),
        shape_of((1, b_up.shape[0]), full),
        shape_of((heads, rows, 2 * LANES), low),
    ]
    return pl.pallas_call(
        functools.partial(project_kernel, heads),
        out_shape=outs,
        in_specs=[spec_smem(), spec_vmem()] + [spec_hbm()] * len(given),
        out_specs=[spec_vmem()] * len(outs),
        scratch_shapes=[pltpu.VMEM(array.shape, array.dtype) for array in given]
        + [pltpu.SemaphoreType.DMA((len(given),))],
        compiler_params=params(60),
        cost_estimate=pl.CostEstimate(
            flops=2 * rows * width * 4 * w_out.shape[0], bytes_accessed=8 * MIB, transcendentals=0
        ),
        name="project",
    )(pair_of, inverse, *given)


def mlp_kernel(early, ids_ref, *rest):
    given, rest = rest[:6], rest[6:]
    part_ref, back_ref, sums_ref, d_b_up_ref, keep_ref, early_ref, send_ref = rest[:7]
    h2_turned, part_acc, back_acc = rest[7:10]
    held, sems = rest[10:-1], rest[-1]
    copies = [pltpu.make_async_copy(src, dst, sems.at[i]) for i, (src, dst) in enumerate(zip(given, held))]
    h2_held, w_up_ref, b_up, cot_ref, w_down_ref, xhat_ref = held
    step = pl.program_id(0)
    steps = pl.num_programs(0)

    @pl.when(step == 0)
    def _():
        for copy in copies:
            copy.start()
        part_acc[...] = jnp.zeros_like(part_acc)
        back_acc[...] = jnp.zeros_like(back_acc)
        copies[0].wait()
        h2_turned[...] = turn(h2_held[...])
        for copy in copies[1:3]:
            copy.wait()

    at = [pl.multiple_of(ids_ref[b * steps + step] * LANES, LANES) for b in range(2)]
    w_up = jnp.concatenate([w_up_ref[:, pl.ds(i, LANES)] for i in at], axis=1)
    u = mm(h2_held[...], w_up) + jnp.concatenate([b_up[:, pl.ds(i, LANES)] for i in at], axis=1)

    @pl.when(step == 0)
    def _():
        for copy in copies[3:5]:
            copy.wait()

    cot = cot_ref[...]
    w_down = jnp.concatenate([w_down_ref[pl.ds(i, LANES), :] for i in at], axis=0)
    cdf = 0.5 * (1.0 + lax.erf(u * np.float32(np.sqrt(0.5))))
    active = u * cdf
    active_low = active.astype(low)
    slope = cdf + u * jnp.exp(-0.5 * u * u) * np.float32(1.0 / np.sqrt(2.0 * np.pi))
    du = (mm_nt(cot, w_down) * slope).astype(low)
    part_acc[...] += mm(active_low, w_down)
    back_acc[...] += mm_nt(du, w_up)
    d_b_up = jnp.sum(du.astype(full), axis=0, keepdims=True)
    up = mm(h2_turned[...], du).astype(low)
    down = mm(active.T.astype(low), cot).astype(low)
    depth = up.shape[0]

    def put(b, grad_ref):
        grad_ref[:depth] = up[:, b * LANES : (b + 1) * LANES]
        for t in range(down.shape[1] // LANES):
            grad_ref[depth + t * LANES : depth + (t + 1) * LANES] = down[
                b * LANES : (b + 1) * LANES, t * LANES : (t + 1) * LANES
            ]

    for b in range(2):
        d_b_up_ref[:, pl.ds(at[b], LANES)] = d_b_up[:, b * LANES : (b + 1) * LANES]
    put(0, keep_ref)

    @pl.when(step < early)
    def _():
        put(1, early_ref)

    @pl.when(step >= early)
    def _():
        put(1, send_ref)

    @pl.when(step == steps - 1)
    def _():
        copies[5].wait()
        part_ref[...] = part_acc[...]
        back = back_acc[...]
        back_ref[...] = back.astype(low)
        sums_ref[0:1] = jnp.sum(back * xhat_ref[...], axis=0, keepdims=True)
        sums_ref[1:2] = jnp.sum(back, axis=0, keepdims=True)


def mlp(ids, early, *given):
    rows, width = given[0].shape
    hidden_units = given[1].shape[1]
    steps = hidden_units // LANES // 2
    whole = lambda shape: pl.BlockSpec(shape, lambda f, c: (0,) * len(shape))
    grads = lambda at: pl.BlockSpec((2 * width, LANES), lambda f, c: (at(f), 0))
    outs = [
        shape_of((rows, width), full),
        shape_of((rows, width), low),
        shape_of((2, width), full),
        shape_of((1, hidden_units), full),
        shape_of((steps * 2 * width, LANES), low),
        shape_of((early * 2 * width, LANES), low),
        shape_of(((steps - early) * 2 * width, LANES), low),
    ]
    return pl.pallas_call(
        functools.partial(mlp_kernel, early),
        grid_spec=pltpu.PrefetchScalarGridSpec(
            num_scalar_prefetch=1,
            grid=(steps,),
            in_specs=[spec_hbm()] * len(given),
            out_specs=[whole(array.shape) for array in outs[:4]]
            + [
                grads(lambda f: f),
                grads(lambda f: jnp.minimum(f, early - 1)),
                grads(lambda f: jnp.maximum(f - early, 0)),
            ],
            scratch_shapes=[
                pltpu.VMEM((width, rows), low),
                pltpu.VMEM((rows, width), full),
                pltpu.VMEM((rows, width), full),
            ]
            + [pltpu.VMEM(array.shape, array.dtype) for array in given]
            + [pltpu.SemaphoreType.DMA((len(given),))],
        ),
        out_shape=outs,
        compiler_params=params(60),
        cost_estimate=pl.CostEstimate(
            flops=12 * rows * width * hidden_units, bytes_accessed=20 * MIB, transcendentals=0
        ),
        name="feed_forward",
    )(ids, *given)


def attention_kernel(heads, group, places, is_first, is_last, pair_ref, inv_ref, token_ref, *rest):
    del token_ref
    if is_first:
        got_ref, rest = rest[0], rest[1:]
        if group > 1:
            other_ref, rest = rest[0], rest[1:]
    else:
        rest = rest[4:]
    out_ref, rest = rest[0], rest[1:]
    if is_last:
        d_own_ref, rest = rest[0], rest[1:]
        if group > 1:
            d_other_ref, rest = rest[0], rest[1:]
    (values_keys, turned_keys, sums, queries), rest = rest[:4], rest[4:]
    token_out, rest = rest[0], rest[1:]
    weights_in, weights_out, stored, peaks, totals, weighted, finals, block_cos, block_sin = rest
    token_out[...] = jnp.zeros_like(token_out)

    rows = queries.shape[1]
    owners = pair_ref.shape[0]
    total_blocks = 2 * owners
    per_chunk = KEYS // BLOCK
    tasks = (total_blocks + 1 + per_chunk - 1) // per_chunk
    me = lax.axis_index("ctx")
    own_sub = lax.rem(me, group)

    def blocks_of(r, d):
        owner = r * group + lax.rem(own_sub + d, group)
        pair = pair_ref[owner]
        return pair, total_blocks - 1 - pair

    def place(tile, block):
        at = pl.multiple_of(block * BLOCK, BLOCK)
        values_keys[pl.ds(at, BLOCK), :] = tile
        turned_keys[:, pl.ds(at, BLOCK)] = turn(tile)

    if is_first:
        for r in range(heads):
            queries[r] = got_ref[r, :, :LANES]
            for half, block in enumerate(blocks_of(r, 0)):
                place(got_ref[r, half * BLOCK : (half + 1) * BLOCK, LANES:], block)
            for d in range(1, group):
                for half, block in enumerate(blocks_of(r, d)):
                    at = r * rows + half * BLOCK
                    place(other_ref[d - 1, at : at + BLOCK, :], block)
        sums[...] = jnp.zeros_like(sums)

    lane = lane_ids((BLOCK, LANES))
    left = lane < HEAD_DIM
    in_key = lane - HEAD_DIM
    moving = (in_key >= 0) & (in_key < ROT)
    forward = (in_key >= 0) & (in_key < HALF)
    cos_row, sin_row, block_cos[...], block_sin[...] = block_tables(inv_ref[...], row_ids(block_cos.shape))

    def rotated_back(tile, block):
        cos_at, sin_at = block_cos[pl.ds(block, 1), :], block_sin[pl.ds(block, 1), :]
        cosine = jnp.where(moving, cos_row * cos_at - sin_row * sin_at, 1.0)
        sine = sin_row * cos_at + cos_row * sin_at
        sine = jnp.where(moving, jnp.where(forward, sine, -sine), 0.0)
        return tile * cosine + rotary_partner(tile) * sine

    offset = row_ids((BLOCK, BLOCK)) - lane_ids((BLOCK, BLOCK))

    def one_pair(i, carry):
        blocks = blocks_of(places[0] + i, 0)
        first = blocks[0] // per_chunk + 1
        for half in range(2):
            both = queries[places[0] + i, half * BLOCK : (half + 1) * BLOCK, :]
            both_turned = turn(both)
            upper = row_ids((LANES, BLOCK)) < HEAD_DIM
            zero = jnp.zeros_like(both_turned)
            weights_in[half, :, :BLOCK] = jnp.where(upper, both_turned, zero)
            weights_in[half, :, BLOCK:] = jnp.where(upper, zero, both_turned)
            weights_out[half, :BLOCK, :] = jnp.where(left, both, zero)
            weights_out[half, BLOCK:, :] = jnp.where(left, zero, both)
        finals[...] = jnp.zeros_like(finals)

        def task(t):
            is_low = t < first
            chunk = jnp.where(is_low, first - 1 - t, t - first)
            return is_low, chunk

        runs = KEYS // BLOCK
        for t in range(tasks):
            is_low, chunk = task(t)
            weights = weights_in[jnp.where(is_low, 0, 1)]
            for u in range(runs):
                at = pl.multiple_of(chunk * KEYS + u * BLOCK, BLOCK)
                sub = slice(u * BLOCK, (u + 1) * BLOCK)
                both = mm(values_keys[pl.ds(at, BLOCK), :], weights)
                grads = both[:, :BLOCK]
                scores = both[:, BLOCK:]
                if t in (0, tasks - 1):
                    query_at = blocks[0 if t == 0 else 1] * BLOCK
                    scores = jnp.where(offset <= query_at - at, scores, masked_score)
                peak = jnp.max(scores, axis=0, keepdims=True)
                raised = jnp.exp(scores - peak)
                stored[t, sub, :BLOCK] = raised
                stored[t, sub, BLOCK:] = grads
                line = t * runs + u
                peaks[line : line + 1] = peak
                totals[line : line + 1] = jnp.sum(raised, axis=0, keepdims=True)
                weighted[line : line + 1] = jnp.sum(raised * grads, axis=0, keepdims=True)

        in_low = row_ids((tasks * runs, BLOCK)) < first * runs

        def finish(mine):
            top = jnp.max(jnp.where(mine, peaks[...], masked_score), axis=0, keepdims=True)
            factor = jnp.where(mine, jnp.exp(peaks[...] - top), 0.0)
            inverse = 1.0 / jnp.sum(totals[...] * factor, axis=0, keepdims=True)
            return factor * inverse, jnp.sum(weighted[...] * factor, axis=0, keepdims=True) * inverse

        (low_factor, low_delta), (high_factor, high_delta) = finish(in_low), finish(jnp.logical_not(in_low))
        peaks[...] = low_factor + high_factor

        for t in range(tasks):
            is_low, chunk = task(t)
            half = jnp.where(is_low, 0, 1)
            weights = weights_out[half]
            delta = jnp.where(is_low, low_delta, high_delta)
            parts = []
            for u in range(runs):
                sub = slice(u * BLOCK, (u + 1) * BLOCK)
                probs = stored[t, sub, :BLOCK] * peaks[t * runs + u : t * runs + u + 1]
                d_scores = probs * (stored[t, sub, BLOCK:] - delta)
                both = jnp.concatenate([probs, d_scores], axis=1).astype(low)
                at = pl.multiple_of(chunk * KEYS + u * BLOCK, BLOCK)
                sums[pl.ds(at, BLOCK), :] += mm(both, weights)
                parts.append(both)
            at = pl.multiple_of(chunk * KEYS, KEYS)
            finals[half] += mm(turned_keys[:, pl.ds(at, KEYS)], jnp.concatenate(parts, axis=0))

        for half in range(2):
            both = jnp.concatenate(
                [finals[half, :HEAD_DIM, :BLOCK], finals[half, HEAD_DIM:, BLOCK:] * score_scale], axis=0
            ).T
            out_ref[i, half * BLOCK : (half + 1) * BLOCK, :] = rotated_back(both, blocks[half]).astype(low)
        return carry

    lax.fori_loop(0, len(places), one_pair, 0)

    if is_last:
        for r in range(heads):
            for d in range(group):
                for half, block in enumerate(blocks_of(r, d)):
                    at = r * rows + half * BLOCK
                    tile = rotated_back(sums[pl.ds(pl.multiple_of(block * BLOCK, BLOCK), BLOCK), :], block)
                    if d == 0:
                        d_own_ref[at : at + BLOCK, :] = tile
                    else:
                        d_other_ref[d - 1, at : at + BLOCK, :] = tile


def attention(heads, group, places, pair_of, inverse, token, got, other, state):
    is_first, is_last = state is None, places[-1] == heads - 1
    rows = got.shape[1]
    owners = pair_of.shape[0]
    total_keys = owners * rows
    tasks = (2 * owners + KEYS // BLOCK) // (KEYS // BLOCK)
    operands = [pair_of, inverse, token]
    outs = [shape_of((len(places), rows, LANES), low)]
    if is_first:
        operands += [got] if other is None else [got, other]
    else:
        operands += list(state)
    if is_last:
        outs.append(shape_of((heads * rows, LANES), full))
        if group > 1:
            outs.append(shape_of((group - 1, heads * rows, LANES), full))
    kept = [
        shape_of((total_keys, LANES), low),
        shape_of((LANES, total_keys), low),
        shape_of((total_keys, LANES), full),
        shape_of((heads, rows, LANES), low),
    ]
    aliases = {} if is_first else {len(operands) - 4 + i: len(outs) + i for i in range(4)}
    found = pl.pallas_call(
        functools.partial(attention_kernel, heads, group, places, is_first, is_last),
        out_shape=outs + kept + [shape_of((1, LANES), full)],
        in_specs=[spec_smem()] + [spec_vmem()] * (len(operands) - 1),
        out_specs=[spec_vmem()] * (len(outs) + 5),
        input_output_aliases=aliases,
        scratch_shapes=[
            pltpu.VMEM((2, LANES, 2 * BLOCK), low),
            pltpu.VMEM((2, 2 * BLOCK, LANES), low),
            pltpu.VMEM((tasks, KEYS, 2 * BLOCK), full),
            pltpu.VMEM((tasks * KEYS // BLOCK, BLOCK), full),
            pltpu.VMEM((tasks * KEYS // BLOCK, BLOCK), full),
            pltpu.VMEM((tasks * KEYS // BLOCK, BLOCK), full),
            pltpu.VMEM((2, LANES, 2 * BLOCK), full),
            pltpu.VMEM((2 * owners, LANES), full),
            pltpu.VMEM((2 * owners, LANES), full),
        ],
        compiler_params=params(6 + total_keys * 5 * 256 // MIB),
        cost_estimate=pl.CostEstimate(
            flops=2_500_000_000 * len(places), bytes_accessed=2 * MIB, transcendentals=0
        ),
        name="attention",
    )(*operands)
    return found[0], found[1 : len(outs)], found[len(outs) : len(outs) + 4], found[-1]


def combine_kernel(heads, terms, *refs):
    out_ref = refs[-1]
    rows = out_ref.shape[1]
    for r in range(heads):
        cut = slice(r * rows, (r + 1) * rows)
        total = refs[0][cut, :]
        for term in refs[1:terms]:
            total = total + term[cut, :]
        out_ref[r, :, LANES:] = total.astype(low)
    at = 0
    for first_ref in refs[terms:-1]:
        out_ref[at : at + first_ref.shape[0], :, :LANES] = first_ref[...]
        at += first_ref.shape[0]


def combine(heads, terms, firsts):
    rows = firsts[0].shape[1]
    return pl.pallas_call(
        functools.partial(combine_kernel, heads, len(terms)),
        out_shape=shape_of((heads, rows, 2 * LANES), low),
        in_specs=[spec_vmem()] * (len(firsts) + len(terms)),
        out_specs=spec_vmem(),
        compiler_params=params(24),
        cost_estimate=pl.CostEstimate(flops=10**7, bytes_accessed=3 * MIB, transcendentals=0),
        name="combine",
    )(*terms, *firsts)


def return_kernel(heads, early, ids_ref, *rest):
    given, rest = rest[:7], rest[7:]
    both_ref, sums_ref, d_b_ref, keep_ref, early_ref, send_ref = rest[:6]
    attended, d_proj, grads = rest[6:9]
    held, sems = rest[9:-1], rest[-1]
    copies = [pltpu.make_async_copy(src, dst, sems.at[i]) for i, (src, dst) in enumerate(zip(given, held))]
    for copy in copies:
        copy.start()
    got_ref, w_out_ref, part_ref, w_qkv_ref, xhat_ref, h1_ref, cot_ref = held
    copies[0].wait()
    chunk_rows = grads.shape[1]
    chips = keep_ref.shape[0]

    def put(at, tile):
        step = min(chunk_rows, tile.shape[0])
        for off in range(0, tile.shape[0], step):
            chunk, inside = divmod(at + off, chunk_rows)
            grads[chunk, inside : inside + step] = tile[off : off + step]

    rows = h1_ref.shape[0]
    left = lane_ids((rows, LANES)) < HEAD_DIM
    for i in range(heads // 2):
        cut = slice(i * LANES, (i + 1) * LANES)
        a, b = got_ref[2 * i, :, :LANES].astype(full), got_ref[2 * i + 1, :, :LANES].astype(full)
        attended[:, cut] = jnp.where(left, a, pltpu.roll(b, HEAD_DIM, 1)).astype(low)
        d_proj[0, :, cut] = jnp.where(left, pltpu.roll(a, HEAD_DIM, 1), b).astype(low)
        a, b = got_ref[2 * i, :, LANES:].astype(full), got_ref[2 * i + 1, :, LANES:].astype(full)
        d_proj[2, :, cut] = jnp.where(left, a, pltpu.roll(b, HEAD_DIM, 1)).astype(low)
        d_proj[1, :, cut] = jnp.where(left, pltpu.roll(a, HEAD_DIM, 1), b).astype(low)
    for copy in copies[1:3]:
        copy.wait()
    both_ref[:rows] = (part_ref[...] + mm(attended[...], w_out_ref[...])).astype(low)
    for copy in copies[3:]:
        copy.wait()
    back = mm_nt(d_proj[0], w_qkv_ref[0]) + mm_nt(d_proj[1], w_qkv_ref[1]) + mm_nt(d_proj[2], w_qkv_ref[2])
    both_ref[rows:] = back.astype(low)
    sums_ref[0:1] = jnp.sum(back * xhat_ref[...], axis=0, keepdims=True)
    sums_ref[1:2] = jnp.sum(back, axis=0, keepdims=True)
    h1_turned = turn(h1_ref[...])
    depth, tiles = h1_turned.shape[0], heads // 2
    for s in range(3):
        d_b_ref[s : s + 1] = jnp.sum(d_proj[s].astype(full), axis=0, keepdims=True)
        grad = mm(h1_turned, d_proj[s]).astype(low)
        for t in range(tiles):
            put((s * tiles + t) * depth, grad[:, t * LANES : (t + 1) * LANES])
    grad = mm(turn(attended[...]), cot_ref[...]).astype(low)
    height = grad.shape[0]
    for t in range(depth // LANES):
        put(3 * tiles * depth + t * height, grad[:, t * LANES : (t + 1) * LANES])
    for t in range(chips):
        keep_ref[t] = grads[ids_ref[t]]
        target = early_ref.at[t] if t < early else send_ref.at[t - early]
        target[...] = grads[ids_ref[chips + t]]


def back_projections(heads, early, ids, *given):
    rows, width = given[2].shape
    local_width = given[1].shape[0]
    chips = ids.shape[0] // 2
    chunk_rows = 4 * width * local_width // LANES // (2 * chips)
    outs = [
        shape_of((2 * rows, width), low),
        shape_of((2, width), full),
        shape_of((3, local_width), full),
        shape_of((chips, chunk_rows, LANES), low),
        shape_of((early, chunk_rows, LANES), low),
        shape_of((chips - early, chunk_rows, LANES), low),
    ]
    return pl.pallas_call(
        functools.partial(return_kernel, heads, early),
        out_shape=outs,
        in_specs=[spec_smem()] + [spec_hbm()] * len(given),
        out_specs=[spec_vmem()] * len(outs),
        scratch_shapes=[
            pltpu.VMEM((rows, local_width), low),
            pltpu.VMEM((3, rows, local_width), low),
            pltpu.VMEM((2 * chips, chunk_rows, LANES), low),
        ]
        + [pltpu.VMEM(array.shape, array.dtype) for array in given]
        + [pltpu.SemaphoreType.DMA((len(given),))],
        compiler_params=params(60),
        cost_estimate=pl.CostEstimate(
            flops=16 * rows * width * local_width, bytes_accessed=14 * MIB, transcendentals=0
        ),
        name="back_projections",
    )(ids, *given)


def finish_kernel(
    hidden_ref, cot_ref, xhat_ref, std_ref, gains_ref, bias_ref, ours_ref, theirs_ref, e2_ours_ref, e2_theirs_ref, out_ref, grad_ref, token_ref
):
    rows = hidden_ref.shape[0]
    gains = gains_ref[...]
    biases = bias_ref[...]
    summed = ours_ref[:rows].astype(full) + theirs_ref[:rows].astype(full)
    out_ref[...] = (hidden_ref[...].astype(full) + summed + biases[0:1] + biases[1:2]).astype(low)
    e1 = ours_ref[rows:].astype(full) + theirs_ref[rows:].astype(full)
    e2 = e2_ours_ref[...].astype(full) + e2_theirs_ref[...].astype(full)
    f = e1 * gains[0:1] + e2 * gains[1:2]
    xhat = xhat_ref[...]
    inv_std = std_ref[:, 0:1]
    grad_ref[...] = cot_ref[...].astype(full) + inv_std * (
        f - jnp.mean(f, axis=-1, keepdims=True) - xhat * jnp.mean(f * xhat, axis=-1, keepdims=True)
    )
    token_ref[...] = jnp.zeros_like(token_ref)


def finish(*operands):
    rows, width = operands[0].shape
    return pl.pallas_call(
        finish_kernel,
        out_shape=[shape_of((rows, width), low), shape_of((rows, width), full), shape_of((1, LANES), full)],
        in_specs=[spec_vmem()] * len(operands),
        out_specs=[spec_vmem()] * 3,
        compiler_params=params(24),
        cost_estimate=pl.CostEstimate(flops=10**7, bytes_accessed=8 * MIB, transcendentals=0),
        name="finish",
    )(*operands)


def to_attention(width, local_width, source, refs, base, unit):
    qkv_ref, out_ref = refs
    tiles = local_width // LANES
    split = 3 * tiles * width
    tile = base // width
    row = pl.multiple_of(lax.rem(base, width), unit)
    column = pl.multiple_of(lax.rem(tile, tiles) * LANES, LANES)
    yield base < split, source, qkv_ref.at[jnp.minimum(tile // tiles, 2), pl.ds(row, unit), pl.ds(column, LANES)]
    after = jnp.maximum(base - split, 0)
    row = pl.multiple_of(lax.rem(after, local_width), unit)
    column = pl.multiple_of(after // local_width * LANES, LANES)
    yield base >= split, source, out_ref.at[pl.ds(row, unit), pl.ds(column, LANES)]


def to_mlp(width, source, refs, base, unit):
    up_ref, down_ref = refs
    block, inside = base // (2 * width), lax.rem(base, 2 * width)
    block_at = pl.multiple_of(block * LANES, LANES)
    row = pl.multiple_of(jnp.minimum(inside, width - unit), unit)
    yield inside < width, source, up_ref.at[pl.ds(row, unit), pl.ds(block_at, LANES)]
    for t in range(unit // LANES):
        column = pl.multiple_of(jnp.maximum(inside - width, 0) + t * LANES, LANES)
        cut = source.at[pl.ds(t * LANES, LANES), :]
        yield inside >= width, cut, down_ref.at[pl.ds(block_at, LANES), pl.ds(column, LANES)]


def unpack_kernel(route, count, unit, has_old, ids_ref, *rest):
    parts, rest = rest[:count], rest[count:]
    rest = rest[2:] if has_old else rest
    targets, (token_ref, held, sems) = rest[:2], rest[2:]
    token_ref[...] = jnp.zeros_like(token_ref)
    chunk_rows = parts[0].shape[0]
    units = chunk_rows // unit
    per_unit = sems.shape[0] // (count * units)

    def moves():
        for i in range(count):
            for j in range(units):
                source = held.at[i, pl.ds(j * unit, unit), :]
                base = ids_ref[i] * chunk_rows + j * unit
                for n, (applies, piece, target) in enumerate(route(source, targets, base, unit)):
                    sem = sems.at[(i * units + j) * per_unit + n]
                    yield i, applies, pltpu.make_async_copy(piece, target, sem)

    done = -1
    for i, applies, copy in moves():
        if i != done:
            held[i] = parts[i][...].astype(full)
            done = i
        pl.when(applies)(copy.start)
    for i, applies, copy in moves():
        pl.when(applies)(copy.wait)


def unpack(name, route, cases, unit, shapes, ids, parts, old):
    count = len(parts)
    chunk_rows = parts[0].shape[0]
    operands = [ids, *parts, *(old or ())]
    return pl.pallas_call(
        functools.partial(unpack_kernel, route, count, unit, old is not None),
        out_shape=[shape_of(shape, full) for shape in shapes] + [shape_of((1, LANES), full)],
        in_specs=[spec_smem()] + [spec_vmem()] * count + [spec_hbm()] * (len(operands) - 1 - count),
        out_specs=[spec_hbm()] * 2 + [spec_vmem()],
        input_output_aliases={} if old is None else {1 + count: 0, 2 + count: 1},
        scratch_shapes=[
            pltpu.VMEM((count, chunk_rows, LANES), full),
            pltpu.SemaphoreType.DMA((count * (chunk_rows // unit) * cases,)),
        ],
        compiler_params=params(8 + count * chunk_rows * 3 * LANES * 2 // MIB),
        cost_estimate=pl.CostEstimate(
            flops=10**6, bytes_accessed=count * chunk_rows * LANES * 6, transcendentals=0
        ),
        name=name,
    )(*operands)


def local(
    hidden,
    pair_of,
    ln1_gain,
    ln1_bias,
    ln2_gain,
    ln2_bias,
    w_qkv,
    b_qkv,
    w_out,
    b_out,
    w_up,
    b_up,
    w_down,
    b_down,
    cotangent,
):
    owners = lax.axis_size("ctx")
    sides = lax.axis_size("tp")
    rows, width = hidden.shape
    local_width = w_qkv.shape[2]
    hidden_units = w_up.shape[1]
    heads = local_width // HEAD_DIM
    group = owners // heads

    exponent = np.arange(0, ROT, 2, dtype=np.float32) / np.float32(ROT)
    inverse = jnp.asarray(np.tile(np.float32(10000.0) ** (-exponent), LANES // HALF)[None, :], full)
    order = (0, 2, 4, 6, 7, 5, 3, 1) if owners == 16 else tuple(range(owners // 2))
    chips = len(order)

    def to_heads(array):
        groups = [[h * group + g for h in range(heads)] for g in range(group)]
        return lax.all_to_all(array, "ctx", 0, 0, axis_index_groups=groups, tiled=True)

    def group_shift(array, d):
        pairs = [(c, c // group * group + (c % group + d) % group) for c in range(owners)]
        return lax.ppermute(array, "ctx", pairs)

    me = lax.axis_index("ctx")
    chip, core = me // 2, lax.rem(me, 2)
    place = sum(jnp.where(chip == c, i, 0) for i, c in enumerate(order))
    way = 1 - 2 * core
    far, near = chips // 2, chips - 1 - chips // 2

    def ring(array, forward):
        pairs = []
        for i, c in enumerate(order):
            for k in range(2):
                step = 1 if (k == 0) == forward else -1
                pairs.append((2 * c + k, 2 * order[(i + step) % chips] + k))
        return lax.ppermute(array, "ctx", pairs)

    def other_core(array):
        return lax.ppermute(array, "ctx", [(c, c ^ 1) for c in range(owners)])

    def across(array):
        return lax.ppermute(array, "tp", [(t, (t + 1) % sides) for t in range(sides)])

    def target(distance):
        return lax.rem(place + way * distance + chips, chips)

    def zero(array):
        return array[:1].astype(full) * 0.0

    slots = [far, -near]
    for t in range(1, far):
        slots += [far - t] if t >= near else [far - t, t - near]
    slots.append(0)
    early = 2
    slot_ids = jnp.stack(
        [core * chips + target(d) for d in slots] + [(1 - core) * chips + target(-d) for d in slots]
    )

    def terms_of(keep, came):
        def term(i):
            return keep[i].astype(full) + came[i].astype(full)

        return {d: term(i) for i, d in enumerate(slots)}

    def scatter_start(terms, token):
        return (terms[far] + token).astype(low), (terms[-near] + token).astype(low)

    def scatter_step(terms, t, sends, token):
        long_send, short_send = sends
        long_got = ring(long_send, True).astype(full) + token
        last = t == far - 1
        long_next = long_got if last else (long_got + terms[far - 1 - t]).astype(low)
        short_next = short_send
        if t < near:
            short_got = ring(short_send, False).astype(full) + token
            short_next = short_got if t == near - 1 else (short_got + terms[t + 1 - near]).astype(low)
        if last:
            return (terms[0] + long_next + short_next).astype(low)
        return long_next, short_next

    base, other_base = core * chips, (1 - core) * chips

    def gather_start(own):
        return [(own, base + place), (other_core(own), other_base + place)]

    def gather_step(t, sends, token):
        long_send, short_send = sends
        if token is not None:
            long_send = (long_send.astype(full) + token).astype(low)
        long_got = ring(long_send, True)
        found = [(long_got, base + target(-t - 1)), (other_core(long_got), other_base + target(t + 1))]
        short_got = short_send
        if t < near:
            if token is not None:
                short_send = (short_send.astype(full) + token).astype(low)
            short_got = ring(short_send, False)
            found += [(short_got, base + target(t + 1)), (other_core(short_got), other_base + target(-t - 1))]
        return (long_got, short_got), found

    blocks = hidden_units // LANES // 2
    in_slots = blocks == chips
    mlp_ids = slot_ids if in_slots else jnp.concatenate(
        [core * blocks + jnp.arange(blocks), (1 - core) * blocks + jnp.arange(blocks)]
    )
    h1, h2, xhat, inv_std, d_bias, gains, biases, b_up_row, packed = project(
        heads,
        pair_of,
        inverse,
        (hidden, ln1_gain, ln1_bias, ln2_gain, ln2_bias, cotangent, w_out, w_qkv, b_qkv, b_up, b_out, b_down),
    )
    got = to_heads(packed)
    part, back2, sums2, d_b_up, keep_mlp, early_mlp, send_mlp = mlp(
        mlp_ids.astype(jnp.int32), early, h2, w_up, b_up_row, cotangent, w_down, xhat
    )
    chunk = keep_mlp.shape[0] // chips
    came_mlp = jnp.concatenate([other_core(early_mlp), other_core(send_mlp)]) if not in_slots else None
    if in_slots:
        halves = [other_core(array).reshape(-1, chunk, LANES) for array in (early_mlp, send_mlp)]
        came_mlp = [half[i] for half in halves for i in range(half.shape[0])]
        terms_mlp = terms_of(keep_mlp.reshape(chips, chunk, LANES), came_mlp)
    else:
        summed = (keep_mlp.astype(full) + came_mlp.astype(full)).reshape(chips, chunk, LANES)
        terms_mlp = {d: lax.dynamic_index_in_dim(summed, target(d), 0, keepdims=False) for d in slots}
    nothing = jnp.zeros((1, LANES), full)

    other = None
    if group > 1:
        mine = got[:, :, LANES:].reshape(heads * rows, LANES)
        other = jnp.stack([group_shift(mine, group - d) for d in range(1, group)])

    middle = heads // 4
    first, _, state, token = attention(
        heads, group, tuple(range(middle)), pair_of, inverse, sums2, got, other, None
    )
    sends_mlp = scatter_start(terms_mlp, token)
    token = zero(sends_mlp[0]) + zero(sends_mlp[1])
    second, ends, _, token = attention(
        heads, group, tuple(range(middle, heads)), pair_of, inverse, token, got, other, state
    )
    d_own, d_other = ends[0], (ends[1] if group > 1 else None)
    terms = [d_own] + [group_shift(d_other[d - 1], d) for d in range(1, group)]
    backs = to_heads(combine(heads, terms, [first, second]))
    theirs2 = across((back2.astype(full) + token[:, :1]).astype(low))
    sends_mlp = scatter_step(terms_mlp, 0, sends_mlp, token)
    sends_mlp = scatter_step(terms_mlp, 1, sends_mlp, nothing)
    xhat_later = xhat + (zero(sends_mlp[0]) + zero(sends_mlp[1]) + zero(theirs2)[:, :LANES])[:, :1]

    both, sums1, d_b_qkv, keep, early_att, send_att = back_projections(
        heads, early, slot_ids.astype(jnp.int32), backs, w_out, part, w_qkv, xhat_later, h1, cotangent
    )
    theirs = across(both)
    output, d_hidden, finish_token = finish(
        hidden, cotangent, xhat, inv_std, gains, biases, both, theirs, back2, theirs2
    )
    halves = [other_core(array) for array in (early_att, send_att)]
    terms_att = terms_of(keep, [half[i] for half in halves for i in range(half.shape[0])])

    small = jnp.concatenate(
        [sums1.reshape(1, -1), sums2.reshape(1, -1), d_bias, d_b_up, d_b_qkv.reshape(1, -1)], axis=1
    )

    def unpack_some(name, route, cases, unit, shapes, found, old):
        parts, ids = zip(*found)
        *old, token = unpack(name, route, cases, unit, shapes, jnp.stack(ids), parts, old)
        return old, token

    unit_mlp = min(chunk, local_width)
    unit_att = min(keep.shape[1], local_width)
    unpack_mlp = functools.partial(
        unpack_some,
        "unpack_feed_forward",
        functools.partial(to_mlp, width),
        1 + unit_mlp // LANES,
        unit_mlp,
        ((width, hidden_units), (hidden_units, width)),
    )
    unpack_att = functools.partial(
        unpack_some,
        "unpack_attention",
        functools.partial(to_attention, width, local_width),
        2,
        unit_att,
        ((3, width, local_width), (local_width, width)),
    )

    steps_mlp, steps_round = iter(range(2, far)), iter(range(far))
    own_mlp, round_mlp, waiting, grads_mlp = None, None, [], None

    def advance_mlp():
        nonlocal sends_mlp, own_mlp, round_mlp, waiting
        t = next(steps_mlp, None)
        if t is not None:
            sends_mlp = scatter_step(terms_mlp, t, sends_mlp, nothing)
            if t < far - 1:
                return zero(sends_mlp[0])
            own_mlp, round_mlp = sends_mlp, (sends_mlp, sends_mlp)
            waiting += gather_start(own_mlp)
            return zero(own_mlp)
        t = next(steps_round, None)
        if t is None:
            return nothing
        round_mlp, found = gather_step(t, round_mlp, None)
        waiting += found
        return zero(round_mlp[0])

    sends_att = scatter_start(terms_att, nothing)
    for t in range(far):
        sends_att = scatter_step(terms_att, t, sends_att, advance_mlp())
    round_att, waiting_att, grads_att = (sends_att, sends_att), gather_start(sends_att), None
    token = nothing
    distance = 1
    for t in range(far):
        if distance < owners:
            small = small + zero(round_att[0])[:, :1]
            small = small + lax.ppermute(small, "ctx", [(c, c ^ distance) for c in range(owners)])
            distance *= 2
        later = advance_mlp()
        round_att, found = gather_step(t, round_att, token)
        if waiting:
            ready, waiting = waiting, []
            grads_mlp, token = unpack_mlp(ready, grads_mlp)
        token = token + later + zero(small)[:, :LANES]
        if t == 0:
            token = token + finish_token
        waiting_att += found
        if t == far - 2:
            grads_att, more = unpack_att(waiting_att[:-4], None)
            waiting_att = waiting_att[-4:]
            token = token + more
    while distance < owners:
        small = small + lax.ppermute(small, "ctx", [(c, c ^ distance) for c in range(owners)])
        distance *= 2
    if waiting:
        grads_mlp, _ = unpack_mlp(waiting, grads_mlp)
    grads_att, _ = unpack_att(waiting_att, grads_att)

    norm_sums = small[:, : 4 * width]
    norm_sums = (norm_sums + across(norm_sums)).reshape(4, width)
    at = 4 * width
    d_bias = small[0, at : at + width]
    d_b_up = small[0, at + width : at + width + hidden_units]
    d_b_qkv = small[0, at + width + hidden_units :].reshape(3, local_width)
    d_w_up, d_w_down = grads_mlp
    d_w_qkv, d_w_out = grads_att
    return (
        output,
        d_hidden,
        norm_sums[0],
        norm_sums[1],
        norm_sums[2],
        norm_sums[3],
        d_w_qkv,
        d_b_qkv,
        d_w_out,
        d_bias,
        d_w_up,
        d_b_up,
        d_w_down,
        d_bias,
    )


def solution(mesh):
    placed = (
        P("ctx", None),
        P(),
        P(),
        P(),
        P(),
        P(),
        P(None, None, "tp"),
        P(None, "tp"),
        P("tp", None),
        P(),
        P(None, "tp"),
        P("tp"),
        P("tp", None),
        P(),
        P("ctx", None),
    )
    return jax.shard_map(
        local,
        mesh=mesh,
        in_specs=placed,
        out_specs=(
            P("ctx", None),
            P("ctx", None),
            P(),
            P(),
            P(),
            P(),
            P(None, None, "tp"),
            P(None, "tp"),
            P("tp", None),
            P(),
            P(None, "tp"),
            P("tp"),
            P("tp", None),
            P(),
        ),
        check_vma=False,
    )
```

```python
import functools

import jax
import jax.numpy as jnp
import numpy as np
from jax import lax
from jax.experimental import pallas as pl
from jax.experimental.pallas import tpu as pltpu
from jax.sharding import PartitionSpec as P

HEAD_DIM = 64
ROT = 16
HALF = ROT // 2
BLOCK = 128
LANES = 128
KEYS = 512
MIB = 1 << 20

norm_eps = 1e-05
masked_score = -1e30
score_scale = HEAD_DIM ** (-0.5)
low = jnp.bfloat16
full = jnp.float32


def mm(left, right):
    return lax.dot_general(left, right, (((1,), (0,)), ((), ())), preferred_element_type=full)


def mm_nt(left, right):
    return lax.dot_general(left, right, (((1,), (1,)), ((), ())), preferred_element_type=full)


def turn(tensor):
    return tensor.astype(full).T.astype(low)


def lane_ids(shape):
    return lax.broadcasted_iota(jnp.int32, shape, len(shape) - 1)


def row_ids(shape):
    return lax.broadcasted_iota(jnp.int32, shape, len(shape) - 2)


def rotary_partner(tensor):
    lanes = lane_ids(tensor.shape)
    ahead = pltpu.roll(tensor, LANES - HALF, 1)
    behind = pltpu.roll(tensor, HALF, 1)
    return jnp.where(lanes % ROT < HALF, ahead, behind)


def spec_vmem():
    return pl.BlockSpec(memory_space=pltpu.VMEM)


def spec_smem():
    return pl.BlockSpec(memory_space=pltpu.SMEM)


def spec_hbm():
    return pl.BlockSpec(memory_space=pltpu.HBM)


def params(mib):
    return pltpu.CompilerParams(vmem_limit_bytes=mib * MIB)


def shape_of(shape, kind):
    return jax.ShapeDtypeStruct(shape, kind)


def block_tables(inverse, blocks):
    row = row_ids((BLOCK, LANES)).astype(full)
    start = blocks.astype(full) * float(BLOCK)
    return jnp.cos(row * inverse), jnp.sin(row * inverse), jnp.cos(start * inverse), jnp.sin(start * inverse)


def project_kernel(heads, pair_ref, inv_ref, *rest):
    given, rest = rest[:12], rest[12:]
    h1_ref, h2_ref, xhat_ref, std_ref, d_bias_ref, gains_ref, bias_ref, b_up_out_ref, packed = rest[:9]
    held, sems = rest[9:-1], rest[-1]
    copies = [pltpu.make_async_copy(src, dst, sems.at[i]) for i, (src, dst) in enumerate(zip(given, held))]
    for copy in copies:
        copy.start()
    (
        hidden_ref,
        g1_ref,
        c1_ref,
        g2_ref,
        c2_ref,
        cot_ref,
        w_out_ref,
        w_qkv_ref,
        b_qkv_ref,
        b_up_ref,
        b_out_ref,
        b_down_ref,
    ) = held
    rows = hidden_ref.shape[0]
    me = lax.axis_index("ctx")
    pair = pair_ref[me]
    total_blocks = 2 * pair_ref.shape[0]

    first = jnp.where(row_ids((8, LANES)) == 0, pair, total_blocks - 1 - pair)
    inverse = inv_ref[...]
    cos_row, sin_row, cos_block, sin_block = block_tables(inverse, first)
    in_head = lane_ids((BLOCK, LANES)) % HEAD_DIM
    tables = []
    for half in range(2):
        cos_at, sin_at = cos_block[half : half + 1], sin_block[half : half + 1]
        cosine = cos_row * cos_at - sin_row * sin_at
        sine = sin_row * cos_at + cos_row * sin_at
        cosine = jnp.where(in_head < ROT, cosine, 1.0)
        sine = jnp.where(in_head < HALF, -sine, jnp.where(in_head < ROT, sine, 0.0))
        tables.append((cosine, sine))
    cosine = jnp.concatenate([tables[0][0], tables[1][0]], axis=0)
    sine = jnp.concatenate([tables[0][1], tables[1][1]], axis=0)

    for copy in copies[:5]:
        copy.wait()
    x = hidden_ref[...].astype(full)
    centred = x - jnp.mean(x, axis=-1, keepdims=True)
    spread = jnp.mean(centred * centred, axis=-1, keepdims=True)
    inv_std = lax.rsqrt(spread + norm_eps)
    xhat = centred * inv_std
    xhat_ref[...] = xhat
    std_ref[...] = jnp.broadcast_to(inv_std, std_ref.shape)

    def as_row(ref):
        return ref[...].astype(full)[None, :]

    gain1, gain2 = as_row(g1_ref), as_row(g2_ref)
    h1 = (xhat * gain1 + as_row(c1_ref)).astype(low)
    h1_ref[...] = h1
    h2_ref[...] = (xhat * gain2 + as_row(c2_ref)).astype(low)
    gains_ref[0:1] = gain1
    gains_ref[1:2] = gain2
    for copy in copies[5:]:
        copy.wait()
    b_up_out_ref[...] = as_row(b_up_ref)
    bias_ref[0:1] = as_row(b_out_ref)
    bias_ref[1:2] = as_row(b_down_ref)
    d_bias_ref[...] = jnp.sum(cot_ref[...].astype(full), axis=0, keepdims=True)

    lane = lane_ids((rows, LANES))

    def projected(s):
        return mm(h1, w_qkv_ref[s]) + b_qkv_ref[s : s + 1].astype(full)

    def turned(tile):
        return tile * cosine + rotary_partner(tile) * sine

    queries, keys, values = projected(0), projected(1), projected(2)
    grads = mm_nt(cot_ref[...], w_out_ref[...])
    left = lane < HEAD_DIM
    for i in range(heads // 2):
        cut = slice(i * LANES, (i + 1) * LANES)
        q = turned(queries[:, cut]).astype(low).astype(full) * score_scale
        k = turned(keys[:, cut])
        v = values[:, cut]
        g = grads[:, cut]
        packed[2 * i, :, :LANES] = jnp.where(left, g, pltpu.roll(q, HEAD_DIM, 1)).astype(low)
        packed[2 * i, :, LANES:] = jnp.where(left, v, pltpu.roll(k, HEAD_DIM, 1)).astype(low)
        packed[2 * i + 1, :, :LANES] = jnp.where(left, pltpu.roll(g, HEAD_DIM, 1), q).astype(low)
        packed[2 * i + 1, :, LANES:] = jnp.where(left, pltpu.roll(v, HEAD_DIM, 1), k).astype(low)


def project(heads, pair_of, inverse, given):
    hidden, w_out, b_up = given[0], given[6], given[9]
    rows, width = hidden.shape
    outs = [
        shape_of((rows, width), low),
        shape_of((rows, width), low),
        shape_of((rows, width), full),
        shape_of((rows, LANES), full),
        shape_of((1, width), full),
        shape_of((2, width), full),
        shape_of((2, width), full),
        shape_of((1, b_up.shape[0]), full),
        shape_of((heads, rows, 2 * LANES), low),
    ]
    return pl.pallas_call(
        functools.partial(project_kernel, heads),
        out_shape=outs,
        in_specs=[spec_smem(), spec_vmem()] + [spec_hbm()] * len(given),
        out_specs=[spec_vmem()] * len(outs),
        scratch_shapes=[pltpu.VMEM(array.shape, array.dtype) for array in given]
        + [pltpu.SemaphoreType.DMA((len(given),))],
        compiler_params=params(60),
        cost_estimate=pl.CostEstimate(
            flops=2 * rows * width * 4 * w_out.shape[0], bytes_accessed=8 * MIB, transcendentals=0
        ),
        name="project",
    )(pair_of, inverse, *given)


def mlp_kernel(early, ids_ref, *rest):
    given, rest = rest[:6], rest[6:]
    part_ref, back_ref, sums_ref, d_b_up_ref, keep_ref, early_ref, send_ref = rest[:7]
    h2_turned, part_acc, back_acc = rest[7:10]
    held, sems = rest[10:-1], rest[-1]
    copies = [pltpu.make_async_copy(src, dst, sems.at[i]) for i, (src, dst) in enumerate(zip(given, held))]
    h2_held, w_up_ref, b_up, cot_ref, w_down_ref, xhat_ref = held
    step = pl.program_id(0)
    steps = pl.num_programs(0)

    @pl.when(step == 0)
    def _():
        for copy in copies:
            copy.start()
        part_acc[...] = jnp.zeros_like(part_acc)
        back_acc[...] = jnp.zeros_like(back_acc)
        copies[0].wait()
        h2_turned[...] = turn(h2_held[...])
        for copy in copies[1:3]:
            copy.wait()

    at = [pl.multiple_of(ids_ref[b * steps + step] * LANES, LANES) for b in range(2)]
    w_up = jnp.concatenate([w_up_ref[:, pl.ds(i, LANES)] for i in at], axis=1)
    u = mm(h2_held[...], w_up) + jnp.concatenate([b_up[:, pl.ds(i, LANES)] for i in at], axis=1)

    @pl.when(step == 0)
    def _():
        for copy in copies[3:5]:
            copy.wait()

    cot = cot_ref[...]
    w_down = jnp.concatenate([w_down_ref[pl.ds(i, LANES), :] for i in at], axis=0)
    cdf = 0.5 * (1.0 + lax.erf(u * np.float32(np.sqrt(0.5))))
    active = u * cdf
    active_low = active.astype(low)
    slope = cdf + u * jnp.exp(-0.5 * u * u) * np.float32(1.0 / np.sqrt(2.0 * np.pi))
    du = (mm_nt(cot, w_down) * slope).astype(low)
    part_acc[...] += mm(active_low, w_down)
    back_acc[...] += mm_nt(du, w_up)
    d_b_up = jnp.sum(du.astype(full), axis=0, keepdims=True)
    up = mm(h2_turned[...], du).astype(low)
    down = mm(active.T.astype(low), cot).astype(low)
    depth = up.shape[0]

    def put(b, grad_ref):
        grad_ref[:depth] = up[:, b * LANES : (b + 1) * LANES]
        for t in range(down.shape[1] // LANES):
            grad_ref[depth + t * LANES : depth + (t + 1) * LANES] = down[
                b * LANES : (b + 1) * LANES, t * LANES : (t + 1) * LANES
            ]

    for b in range(2):
        d_b_up_ref[:, pl.ds(at[b], LANES)] = d_b_up[:, b * LANES : (b + 1) * LANES]
    put(0, keep_ref)

    @pl.when(step < early)
    def _():
        put(1, early_ref)

    @pl.when(step >= early)
    def _():
        put(1, send_ref)

    @pl.when(step == steps - 1)
    def _():
        copies[5].wait()
        part_ref[...] = part_acc[...]
        back = back_acc[...]
        back_ref[...] = back.astype(low)
        sums_ref[0:1] = jnp.sum(back * xhat_ref[...], axis=0, keepdims=True)
        sums_ref[1:2] = jnp.sum(back, axis=0, keepdims=True)


def mlp(ids, early, *given):
    rows, width = given[0].shape
    hidden_units = given[1].shape[1]
    steps = hidden_units // LANES // 2
    whole = lambda shape: pl.BlockSpec(shape, lambda f, c: (0,) * len(shape))
    grads = lambda at: pl.BlockSpec((2 * width, LANES), lambda f, c: (at(f), 0))
    outs = [
        shape_of((rows, width), full),
        shape_of((rows, width), low),
        shape_of((2, width), full),
        shape_of((1, hidden_units), full),
        shape_of((steps * 2 * width, LANES), low),
        shape_of((early * 2 * width, LANES), low),
        shape_of(((steps - early) * 2 * width, LANES), low),
    ]
    return pl.pallas_call(
        functools.partial(mlp_kernel, early),
        grid_spec=pltpu.PrefetchScalarGridSpec(
            num_scalar_prefetch=1,
            grid=(steps,),
            in_specs=[spec_hbm()] * len(given),
            out_specs=[whole(array.shape) for array in outs[:4]]
            + [
                grads(lambda f: f),
                grads(lambda f: jnp.minimum(f, early - 1)),
                grads(lambda f: jnp.maximum(f - early, 0)),
            ],
            scratch_shapes=[
                pltpu.VMEM((width, rows), low),
                pltpu.VMEM((rows, width), full),
                pltpu.VMEM((rows, width), full),
            ]
            + [pltpu.VMEM(array.shape, array.dtype) for array in given]
            + [pltpu.SemaphoreType.DMA((len(given),))],
        ),
        out_shape=outs,
        compiler_params=params(60),
        cost_estimate=pl.CostEstimate(
            flops=12 * rows * width * hidden_units, bytes_accessed=20 * MIB, transcendentals=0
        ),
        name="feed_forward",
    )(ids, *given)


def attention_kernel(heads, group, places, is_first, is_last, pair_ref, inv_ref, token_ref, *rest):
    del token_ref
    if is_first:
        got_ref, rest = rest[0], rest[1:]
        if group > 1:
            other_ref, rest = rest[0], rest[1:]
    else:
        rest = rest[4:]
    out_ref, rest = rest[0], rest[1:]
    if is_last:
        d_own_ref, rest = rest[0], rest[1:]
        if group > 1:
            d_other_ref, rest = rest[0], rest[1:]
    (values_keys, turned_keys, sums, queries), rest = rest[:4], rest[4:]
    token_out, rest = rest[0], rest[1:]
    weights_in, weights_out, stored, peaks, totals, weighted, finals, block_cos, block_sin = rest
    token_out[...] = jnp.zeros_like(token_out)

    rows = queries.shape[1]
    owners = pair_ref.shape[0]
    total_blocks = 2 * owners
    per_chunk = KEYS // BLOCK
    tasks = (total_blocks + 1 + per_chunk - 1) // per_chunk
    me = lax.axis_index("ctx")
    own_sub = lax.rem(me, group)

    def blocks_of(r, d):
        owner = r * group + lax.rem(own_sub + d, group)
        pair = pair_ref[owner]
        return pair, total_blocks - 1 - pair

    def place(tile, block):
        at = pl.multiple_of(block * BLOCK, BLOCK)
        values_keys[pl.ds(at, BLOCK), :] = tile
        turned_keys[:, pl.ds(at, BLOCK)] = turn(tile)

    if is_first:
        for r in range(heads):
            queries[r] = got_ref[r, :, :LANES]
            for half, block in enumerate(blocks_of(r, 0)):
                place(got_ref[r, half * BLOCK : (half + 1) * BLOCK, LANES:], block)
            for d in range(1, group):
                for half, block in enumerate(blocks_of(r, d)):
                    at = r * rows + half * BLOCK
                    place(other_ref[d - 1, at : at + BLOCK, :], block)
        sums[...] = jnp.zeros_like(sums)

    lane = lane_ids((BLOCK, LANES))
    left = lane < HEAD_DIM
    in_key = lane - HEAD_DIM
    moving = (in_key >= 0) & (in_key < ROT)
    forward = (in_key >= 0) & (in_key < HALF)
    cos_row, sin_row, block_cos[...], block_sin[...] = block_tables(inv_ref[...], row_ids(block_cos.shape))

    def rotated_back(tile, block):
        cos_at, sin_at = block_cos[pl.ds(block, 1), :], block_sin[pl.ds(block, 1), :]
        cosine = jnp.where(moving, cos_row * cos_at - sin_row * sin_at, 1.0)
        sine = sin_row * cos_at + cos_row * sin_at
        sine = jnp.where(moving, jnp.where(forward, sine, -sine), 0.0)
        return tile * cosine + rotary_partner(tile) * sine

    offset = row_ids((BLOCK, BLOCK)) - lane_ids((BLOCK, BLOCK))

    def one_pair(i, carry):
        blocks = blocks_of(places[0] + i, 0)
        first = blocks[0] // per_chunk + 1
        for half in range(2):
            both = queries[places[0] + i, half * BLOCK : (half + 1) * BLOCK, :]
            both_turned = turn(both)
            upper = row_ids((LANES, BLOCK)) < HEAD_DIM
            zero = jnp.zeros_like(both_turned)
            weights_in[half, :, :BLOCK] = jnp.where(upper, both_turned, zero)
            weights_in[half, :, BLOCK:] = jnp.where(upper, zero, both_turned)
            weights_out[half, :BLOCK, :] = jnp.where(left, both, zero)
            weights_out[half, BLOCK:, :] = jnp.where(left, zero, both)
        finals[...] = jnp.zeros_like(finals)

        def task(t):
            is_low = t < first
            chunk = jnp.where(is_low, first - 1 - t, t - first)
            return is_low, chunk

        runs = KEYS // BLOCK
        for t in range(tasks):
            is_low, chunk = task(t)
            weights = weights_in[jnp.where(is_low, 0, 1)]
            for u in range(runs):
                at = pl.multiple_of(chunk * KEYS + u * BLOCK, BLOCK)
                sub = slice(u * BLOCK, (u + 1) * BLOCK)
                both = mm(values_keys[pl.ds(at, BLOCK), :], weights)
                grads = both[:, :BLOCK]
                scores = both[:, BLOCK:]
                if t in (0, tasks - 1):
                    query_at = blocks[0 if t == 0 else 1] * BLOCK
                    scores = jnp.where(offset <= query_at - at, scores, masked_score)
                peak = jnp.max(scores, axis=0, keepdims=True)
                raised = jnp.exp(scores - peak)
                stored[t, sub, :BLOCK] = raised
                stored[t, sub, BLOCK:] = grads
                line = t * runs + u
                peaks[line : line + 1] = peak
                totals[line : line + 1] = jnp.sum(raised, axis=0, keepdims=True)
                weighted[line : line + 1] = jnp.sum(raised * grads, axis=0, keepdims=True)

        in_low = row_ids((tasks * runs, BLOCK)) < first * runs

        def finish(mine):
            top = jnp.max(jnp.where(mine, peaks[...], masked_score), axis=0, keepdims=True)
            factor = jnp.where(mine, jnp.exp(peaks[...] - top), 0.0)
            inverse = 1.0 / jnp.sum(totals[...] * factor, axis=0, keepdims=True)
            return factor * inverse, jnp.sum(weighted[...] * factor, axis=0, keepdims=True) * inverse

        (low_factor, low_delta), (high_factor, high_delta) = finish(in_low), finish(jnp.logical_not(in_low))
        peaks[...] = low_factor + high_factor

        for t in range(tasks):
            is_low, chunk = task(t)
            half = jnp.where(is_low, 0, 1)
            weights = weights_out[half]
            delta = jnp.where(is_low, low_delta, high_delta)
            parts = []
            for u in range(runs):
                sub = slice(u * BLOCK, (u + 1) * BLOCK)
                probs = stored[t, sub, :BLOCK] * peaks[t * runs + u : t * runs + u + 1]
                d_scores = probs * (stored[t, sub, BLOCK:] - delta)
                both = jnp.concatenate([probs, d_scores], axis=1).astype(low)
                at = pl.multiple_of(chunk * KEYS + u * BLOCK, BLOCK)
                sums[pl.ds(at, BLOCK), :] += mm(both, weights)
                parts.append(both)
            at = pl.multiple_of(chunk * KEYS, KEYS)
            finals[half] += mm(turned_keys[:, pl.ds(at, KEYS)], jnp.concatenate(parts, axis=0))

        for half in range(2):
            both = jnp.concatenate(
                [finals[half, :HEAD_DIM, :BLOCK], finals[half, HEAD_DIM:, BLOCK:] * score_scale], axis=0
            ).T
            out_ref[i, half * BLOCK : (half + 1) * BLOCK, :] = rotated_back(both, blocks[half]).astype(low)
        return carry

    lax.fori_loop(0, len(places), one_pair, 0)

    if is_last:
        for r in range(heads):
            for d in range(group):
                for half, block in enumerate(blocks_of(r, d)):
                    at = r * rows + half * BLOCK
                    tile = rotated_back(sums[pl.ds(pl.multiple_of(block * BLOCK, BLOCK), BLOCK), :], block)
                    if d == 0:
                        d_own_ref[at : at + BLOCK, :] = tile
                    else:
                        d_other_ref[d - 1, at : at + BLOCK, :] = tile


def attention(heads, group, places, pair_of, inverse, token, got, other, state):
    is_first, is_last = state is None, places[-1] == heads - 1
    rows = got.shape[1]
    owners = pair_of.shape[0]
    total_keys = owners * rows
    tasks = (2 * owners + KEYS // BLOCK) // (KEYS // BLOCK)
    operands = [pair_of, inverse, token]
    outs = [shape_of((len(places), rows, LANES), low)]
    if is_first:
        operands += [got] if other is None else [got, other]
    else:
        operands += list(state)
    if is_last:
        outs.append(shape_of((heads * rows, LANES), full))
        if group > 1:
            outs.append(shape_of((group - 1, heads * rows, LANES), full))
    kept = [
        shape_of((total_keys, LANES), low),
        shape_of((LANES, total_keys), low),
        shape_of((total_keys, LANES), full),
        shape_of((heads, rows, LANES), low),
    ]
    aliases = {} if is_first else {len(operands) - 4 + i: len(outs) + i for i in range(4)}
    found = pl.pallas_call(
        functools.partial(attention_kernel, heads, group, places, is_first, is_last),
        out_shape=outs + kept + [shape_of((1, LANES), full)],
        in_specs=[spec_smem()] + [spec_vmem()] * (len(operands) - 1),
        out_specs=[spec_vmem()] * (len(outs) + 5),
        input_output_aliases=aliases,
        scratch_shapes=[
            pltpu.VMEM((2, LANES, 2 * BLOCK), low),
            pltpu.VMEM((2, 2 * BLOCK, LANES), low),
            pltpu.VMEM((tasks, KEYS, 2 * BLOCK), full),
            pltpu.VMEM((tasks * KEYS // BLOCK, BLOCK), full),
            pltpu.VMEM((tasks * KEYS // BLOCK, BLOCK), full),
            pltpu.VMEM((tasks * KEYS // BLOCK, BLOCK), full),
            pltpu.VMEM((2, LANES, 2 * BLOCK), full),
            pltpu.VMEM((2 * owners, LANES), full),
            pltpu.VMEM((2 * owners, LANES), full),
        ],
        compiler_params=params(6 + total_keys * 5 * 256 // MIB),
        cost_estimate=pl.CostEstimate(
            flops=2_500_000_000 * len(places), bytes_accessed=2 * MIB, transcendentals=0
        ),
        name="attention",
    )(*operands)
    return found[0], found[1 : len(outs)], found[len(outs) : len(outs) + 4], found[-1]


def combine_kernel(heads, terms, *refs):
    out_ref = refs[-1]
    rows = out_ref.shape[1]
    for r in range(heads):
        cut = slice(r * rows, (r + 1) * rows)
        total = refs[0][cut, :]
        for term in refs[1:terms]:
            total = total + term[cut, :]
        out_ref[r, :, LANES:] = total.astype(low)
    at = 0
    for first_ref in refs[terms:-1]:
        out_ref[at : at + first_ref.shape[0], :, :LANES] = first_ref[...]
        at += first_ref.shape[0]


def combine(heads, terms, firsts):
    rows = firsts[0].shape[1]
    return pl.pallas_call(
        functools.partial(combine_kernel, heads, len(terms)),
        out_shape=shape_of((heads, rows, 2 * LANES), low),
        in_specs=[spec_vmem()] * (len(firsts) + len(terms)),
        out_specs=spec_vmem(),
        compiler_params=params(24),
        cost_estimate=pl.CostEstimate(flops=10**7, bytes_accessed=3 * MIB, transcendentals=0),
        name="combine",
    )(*terms, *firsts)


def return_kernel(heads, early, ids_ref, *rest):
    given, rest = rest[:7], rest[7:]
    both_ref, sums_ref, d_b_ref, keep_ref, early_ref, send_ref = rest[:6]
    attended, d_proj, grads = rest[6:9]
    held, sems = rest[9:-1], rest[-1]
    copies = [pltpu.make_async_copy(src, dst, sems.at[i]) for i, (src, dst) in enumerate(zip(given, held))]
    for copy in copies:
        copy.start()
    got_ref, w_out_ref, part_ref, w_qkv_ref, xhat_ref, h1_ref, cot_ref = held
    copies[0].wait()
    chunk_rows = grads.shape[1]
    chips = keep_ref.shape[0]

    def put(at, tile):
        step = min(chunk_rows, tile.shape[0])
        for off in range(0, tile.shape[0], step):
            chunk, inside = divmod(at + off, chunk_rows)
            grads[chunk, inside : inside + step] = tile[off : off + step]

    rows = h1_ref.shape[0]
    left = lane_ids((rows, LANES)) < HEAD_DIM
    for i in range(heads // 2):
        cut = slice(i * LANES, (i + 1) * LANES)
        a, b = got_ref[2 * i, :, :LANES].astype(full), got_ref[2 * i + 1, :, :LANES].astype(full)
        attended[:, cut] = jnp.where(left, a, pltpu.roll(b, HEAD_DIM, 1)).astype(low)
        d_proj[0, :, cut] = jnp.where(left, pltpu.roll(a, HEAD_DIM, 1), b).astype(low)
        a, b = got_ref[2 * i, :, LANES:].astype(full), got_ref[2 * i + 1, :, LANES:].astype(full)
        d_proj[2, :, cut] = jnp.where(left, a, pltpu.roll(b, HEAD_DIM, 1)).astype(low)
        d_proj[1, :, cut] = jnp.where(left, pltpu.roll(a, HEAD_DIM, 1), b).astype(low)
    for copy in copies[1:3]:
        copy.wait()
    both_ref[:rows] = (part_ref[...] + mm(attended[...], w_out_ref[...])).astype(low)
    for copy in copies[3:]:
        copy.wait()
    back = mm_nt(d_proj[0], w_qkv_ref[0]) + mm_nt(d_proj[1], w_qkv_ref[1]) + mm_nt(d_proj[2], w_qkv_ref[2])
    both_ref[rows:] = back.astype(low)
    sums_ref[0:1] = jnp.sum(back * xhat_ref[...], axis=0, keepdims=True)
    sums_ref[1:2] = jnp.sum(back, axis=0, keepdims=True)
    h1_turned = turn(h1_ref[...])
    depth, tiles = h1_turned.shape[0], heads // 2
    for s in range(3):
        d_b_ref[s : s + 1] = jnp.sum(d_proj[s].astype(full), axis=0, keepdims=True)
        grad = mm(h1_turned, d_proj[s]).astype(low)
        for t in range(tiles):
            put((s * tiles + t) * depth, grad[:, t * LANES : (t + 1) * LANES])
    grad = mm(turn(attended[...]), cot_ref[...]).astype(low)
    height = grad.shape[0]
    for t in range(depth // LANES):
        put(3 * tiles * depth + t * height, grad[:, t * LANES : (t + 1) * LANES])
    for t in range(chips):
        keep_ref[t] = grads[ids_ref[t]]
        target = early_ref.at[t] if t < early else send_ref.at[t - early]
        target[...] = grads[ids_ref[chips + t]]


def back_projections(heads, early, ids, *given):
    rows, width = given[2].shape
    local_width = given[1].shape[0]
    chips = ids.shape[0] // 2
    chunk_rows = 4 * width * local_width // LANES // (2 * chips)
    outs = [
        shape_of((2 * rows, width), low),
        shape_of((2, width), full),
        shape_of((3, local_width), full),
        shape_of((chips, chunk_rows, LANES), low),
        shape_of((early, chunk_rows, LANES), low),
        shape_of((chips - early, chunk_rows, LANES), low),
    ]
    return pl.pallas_call(
        functools.partial(return_kernel, heads, early),
        out_shape=outs,
        in_specs=[spec_smem()] + [spec_hbm()] * len(given),
        out_specs=[spec_vmem()] * len(outs),
        scratch_shapes=[
            pltpu.VMEM((rows, local_width), low),
            pltpu.VMEM((3, rows, local_width), low),
            pltpu.VMEM((2 * chips, chunk_rows, LANES), low),
        ]
        + [pltpu.VMEM(array.shape, array.dtype) for array in given]
        + [pltpu.SemaphoreType.DMA((len(given),))],
        compiler_params=params(60),
        cost_estimate=pl.CostEstimate(
            flops=16 * rows * width * local_width, bytes_accessed=14 * MIB, transcendentals=0
        ),
        name="back_projections",
    )(ids, *given)


def finish_kernel(
    hidden_ref, cot_ref, xhat_ref, std_ref, gains_ref, bias_ref, ours_ref, theirs_ref, e2_ours_ref, e2_theirs_ref, out_ref, grad_ref, token_ref
):
    rows = hidden_ref.shape[0]
    gains = gains_ref[...]
    biases = bias_ref[...]
    summed = ours_ref[:rows].astype(full) + theirs_ref[:rows].astype(full)
    out_ref[...] = (hidden_ref[...].astype(full) + summed + biases[0:1] + biases[1:2]).astype(low)
    e1 = ours_ref[rows:].astype(full) + theirs_ref[rows:].astype(full)
    e2 = e2_ours_ref[...].astype(full) + e2_theirs_ref[...].astype(full)
    f = e1 * gains[0:1] + e2 * gains[1:2]
    xhat = xhat_ref[...]
    inv_std = std_ref[:, 0:1]
    grad_ref[...] = cot_ref[...].astype(full) + inv_std * (
        f - jnp.mean(f, axis=-1, keepdims=True) - xhat * jnp.mean(f * xhat, axis=-1, keepdims=True)
    )
    token_ref[...] = jnp.zeros_like(token_ref)


def finish(*operands):
    rows, width = operands[0].shape
    return pl.pallas_call(
        finish_kernel,
        out_shape=[shape_of((rows, width), low), shape_of((rows, width), full), shape_of((1, LANES), full)],
        in_specs=[spec_vmem()] * len(operands),
        out_specs=[spec_vmem()] * 3,
        compiler_params=params(24),
        cost_estimate=pl.CostEstimate(flops=10**7, bytes_accessed=8 * MIB, transcendentals=0),
        name="finish",
    )(*operands)


def to_attention(width, local_width, source, refs, base, unit):
    qkv_ref, out_ref = refs
    tiles = local_width // LANES
    split = 3 * tiles * width
    tile = base // width
    row = pl.multiple_of(lax.rem(base, width), unit)
    column = pl.multiple_of(lax.rem(tile, tiles) * LANES, LANES)
    yield base < split, source, qkv_ref.at[jnp.minimum(tile // tiles, 2), pl.ds(row, unit), pl.ds(column, LANES)]
    after = jnp.maximum(base - split, 0)
    row = pl.multiple_of(lax.rem(after, local_width), unit)
    column = pl.multiple_of(after // local_width * LANES, LANES)
    yield base >= split, source, out_ref.at[pl.ds(row, unit), pl.ds(column, LANES)]


def to_mlp(width, source, refs, base, unit):
    up_ref, down_ref = refs
    block, inside = base // (2 * width), lax.rem(base, 2 * width)
    block_at = pl.multiple_of(block * LANES, LANES)
    row = pl.multiple_of(jnp.minimum(inside, width - unit), unit)
    yield inside < width, source, up_ref.at[pl.ds(row, unit), pl.ds(block_at, LANES)]
    for t in range(unit // LANES):
        column = pl.multiple_of(jnp.maximum(inside - width, 0) + t * LANES, LANES)
        cut = source.at[pl.ds(t * LANES, LANES), :]
        yield inside >= width, cut, down_ref.at[pl.ds(block_at, LANES), pl.ds(column, LANES)]


def unpack_kernel(route, count, unit, has_old, ids_ref, *rest):
    parts, rest = rest[:count], rest[count:]
    rest = rest[2:] if has_old else rest
    targets, (token_ref, held, sems) = rest[:2], rest[2:]
    token_ref[...] = jnp.zeros_like(token_ref)
    chunk_rows = parts[0].shape[0]
    units = chunk_rows // unit
    per_unit = sems.shape[0] // (count * units)

    def moves():
        for i in range(count):
            for j in range(units):
                source = held.at[i, pl.ds(j * unit, unit), :]
                base = ids_ref[i] * chunk_rows + j * unit
                for n, (applies, piece, target) in enumerate(route(source, targets, base, unit)):
                    sem = sems.at[(i * units + j) * per_unit + n]
                    yield i, applies, pltpu.make_async_copy(piece, target, sem)

    done = -1
    for i, applies, copy in moves():
        if i != done:
            held[i] = parts[i][...].astype(full)
            done = i
        pl.when(applies)(copy.start)
    for i, applies, copy in moves():
        pl.when(applies)(copy.wait)


def unpack(name, route, cases, unit, shapes, ids, parts, old):
    count = len(parts)
    chunk_rows = parts[0].shape[0]
    operands = [ids, *parts, *(old or ())]
    return pl.pallas_call(
        functools.partial(unpack_kernel, route, count, unit, old is not None),
        out_shape=[shape_of(shape, full) for shape in shapes] + [shape_of((1, LANES), full)],
        in_specs=[spec_smem()] + [spec_vmem()] * count + [spec_hbm()] * (len(operands) - 1 - count),
        out_specs=[spec_hbm()] * 2 + [spec_vmem()],
        input_output_aliases={} if old is None else {1 + count: 0, 2 + count: 1},
        scratch_shapes=[
            pltpu.VMEM((count, chunk_rows, LANES), full),
            pltpu.SemaphoreType.DMA((count * (chunk_rows // unit) * cases,)),
        ],
        compiler_params=params(8 + count * chunk_rows * 3 * LANES * 2 // MIB),
        cost_estimate=pl.CostEstimate(
            flops=10**6, bytes_accessed=count * chunk_rows * LANES * 6, transcendentals=0
        ),
        name=name,
    )(*operands)


def local(
    hidden,
    pair_of,
    ln1_gain,
    ln1_bias,
    ln2_gain,
    ln2_bias,
    w_qkv,
    b_qkv,
    w_out,
    b_out,
    w_up,
    b_up,
    w_down,
    b_down,
    cotangent,
):
    owners = lax.axis_size("ctx")
    sides = lax.axis_size("tp")
    rows, width = hidden.shape
    local_width = w_qkv.shape[2]
    hidden_units = w_up.shape[1]
    heads = local_width // HEAD_DIM
    group = owners // heads

    exponent = np.arange(0, ROT, 2, dtype=np.float32) / np.float32(ROT)
    inverse = jnp.asarray(np.tile(np.float32(10000.0) ** (-exponent), LANES // HALF)[None, :], full)
    order = (0, 2, 4, 6, 7, 5, 3, 1) if owners == 16 else tuple(range(owners // 2))
    chips = len(order)

    def to_heads(array):
        groups = [[h * group + g for h in range(heads)] for g in range(group)]
        return lax.all_to_all(array, "ctx", 0, 0, axis_index_groups=groups, tiled=True)

    def group_shift(array, d):
        pairs = [(c, c // group * group + (c % group + d) % group) for c in range(owners)]
        return lax.ppermute(array, "ctx", pairs)

    me = lax.axis_index("ctx")
    chip, core = me // 2, lax.rem(me, 2)
    place = sum(jnp.where(chip == c, i, 0) for i, c in enumerate(order))
    way = 1 - 2 * core
    far, near = chips // 2, chips - 1 - chips // 2

    def ring(array, forward):
        pairs = []
        for i, c in enumerate(order):
            for k in range(2):
                step = 1 if (k == 0) == forward else -1
                pairs.append((2 * c + k, 2 * order[(i + step) % chips] + k))
        return lax.ppermute(array, "ctx", pairs)

    def other_core(array):
        return lax.ppermute(array, "ctx", [(c, c ^ 1) for c in range(owners)])

    def across(array):
        return lax.ppermute(array, "tp", [(t, (t + 1) % sides) for t in range(sides)])

    def target(distance):
        return lax.rem(place + way * distance + chips, chips)

    def zero(array):
        return array[:1].astype(full) * 0.0

    slots = [far, -near]
    for t in range(1, far):
        slots += [far - t] if t >= near else [far - t, t - near]
    slots.append(0)
    early = 2
    slot_ids = jnp.stack(
        [core * chips + target(d) for d in slots] + [(1 - core) * chips + target(-d) for d in slots]
    )

    def terms_of(keep, came):
        def term(i):
            return keep[i].astype(full) + came[i].astype(full)

        return {d: term(i) for i, d in enumerate(slots)}

    def scatter_start(terms, token):
        return (terms[far] + token).astype(low), (terms[-near] + token).astype(low)

    def scatter_step(terms, t, sends, token):
        long_send, short_send = sends
        long_got = ring(long_send, True).astype(full) + token
        last = t == far - 1
        long_next = long_got if last else (long_got + terms[far - 1 - t]).astype(low)
        short_next = short_send
        if t < near:
            short_got = ring(short_send, False).astype(full) + token
            short_next = short_got if t == near - 1 else (short_got + terms[t + 1 - near]).astype(low)
        if last:
            return (terms[0] + long_next + short_next).astype(low)
        return long_next, short_next

    base, other_base = core * chips, (1 - core) * chips

    def gather_start(own):
        return [(own, base + place), (other_core(own), other_base + place)]

    def gather_step(t, sends, token):
        long_send, short_send = sends
        if token is not None:
            long_send = (long_send.astype(full) + token).astype(low)
        long_got = ring(long_send, True)
        found = [(long_got, base + target(-t - 1)), (other_core(long_got), other_base + target(t + 1))]
        short_got = short_send
        if t < near:
            if token is not None:
                short_send = (short_send.astype(full) + token).astype(low)
            short_got = ring(short_send, False)
            found += [(short_got, base + target(t + 1)), (other_core(short_got), other_base + target(-t - 1))]
        return (long_got, short_got), found

    blocks = hidden_units // LANES // 2
    in_slots = blocks == chips
    mlp_ids = slot_ids if in_slots else jnp.concatenate(
        [core * blocks + jnp.arange(blocks), (1 - core) * blocks + jnp.arange(blocks)]
    )
    h1, h2, xhat, inv_std, d_bias, gains, biases, b_up_row, packed = project(
        heads,
        pair_of,
        inverse,
        (hidden, ln1_gain, ln1_bias, ln2_gain, ln2_bias, cotangent, w_out, w_qkv, b_qkv, b_up, b_out, b_down),
    )
    got = to_heads(packed)
    part, back2, sums2, d_b_up, keep_mlp, early_mlp, send_mlp = mlp(
        mlp_ids.astype(jnp.int32), early, h2, w_up, b_up_row, cotangent, w_down, xhat
    )
    chunk = keep_mlp.shape[0] // chips
    came_mlp = jnp.concatenate([other_core(early_mlp), other_core(send_mlp)]) if not in_slots else None
    if in_slots:
        halves = [other_core(array).reshape(-1, chunk, LANES) for array in (early_mlp, send_mlp)]
        came_mlp = [half[i] for half in halves for i in range(half.shape[0])]
        terms_mlp = terms_of(keep_mlp.reshape(chips, chunk, LANES), came_mlp)
    else:
        summed = (keep_mlp.astype(full) + came_mlp.astype(full)).reshape(chips, chunk, LANES)
        terms_mlp = {d: lax.dynamic_index_in_dim(summed, target(d), 0, keepdims=False) for d in slots}
    nothing = jnp.zeros((1, LANES), full)

    other = None
    if group > 1:
        mine = got[:, :, LANES:].reshape(heads * rows, LANES)
        other = jnp.stack([group_shift(mine, group - d) for d in range(1, group)])

    middle = heads // 4
    first, _, state, token = attention(
        heads, group, tuple(range(middle)), pair_of, inverse, sums2, got, other, None
    )
    sends_mlp = scatter_start(terms_mlp, token)
    token = zero(sends_mlp[0]) + zero(sends_mlp[1])
    second, ends, _, token = attention(
        heads, group, tuple(range(middle, heads)), pair_of, inverse, token, got, other, state
    )
    d_own, d_other = ends[0], (ends[1] if group > 1 else None)
    terms = [d_own] + [group_shift(d_other[d - 1], d) for d in range(1, group)]
    combined = combine(heads, terms, [first, second])
    backs = to_heads(combined)
    token = zero(combined[0])[:, :LANES]
    theirs2 = across((back2.astype(full) + token[:, :1]).astype(low))
    sends_mlp = scatter_step(terms_mlp, 0, sends_mlp, token)
    xhat_later = xhat + (zero(sends_mlp[0]) + zero(sends_mlp[1]) + zero(theirs2)[:, :LANES])[:, :1]

    both, sums1, d_b_qkv, keep, early_att, send_att = back_projections(
        heads, early, slot_ids.astype(jnp.int32), backs, w_out, part, w_qkv, xhat_later, h1, cotangent
    )
    theirs = across(both)
    output, d_hidden, finish_token = finish(
        hidden, cotangent, xhat, inv_std, gains, biases, both, theirs, back2, theirs2
    )
    halves = [other_core(array) for array in (early_att, send_att)]
    terms_att = terms_of(keep, [half[i] for half in halves for i in range(half.shape[0])])

    small = jnp.concatenate(
        [sums1.reshape(1, -1), sums2.reshape(1, -1), d_bias, d_b_up, d_b_qkv.reshape(1, -1)], axis=1
    )

    def unpack_some(name, route, cases, unit, shapes, found, old):
        parts, ids = zip(*found)
        *old, token = unpack(name, route, cases, unit, shapes, jnp.stack(ids), parts, old)
        return old, token

    unit_mlp = min(chunk, local_width)
    unit_att = min(keep.shape[1], local_width)
    unpack_mlp = functools.partial(
        unpack_some,
        "unpack_feed_forward",
        functools.partial(to_mlp, width),
        1 + unit_mlp // LANES,
        unit_mlp,
        ((width, hidden_units), (hidden_units, width)),
    )
    unpack_att = functools.partial(
        unpack_some,
        "unpack_attention",
        functools.partial(to_attention, width, local_width),
        2,
        unit_att,
        ((3, width, local_width), (local_width, width)),
    )

    steps_mlp, steps_round = iter(range(1, far)), iter(range(far))
    own_mlp, round_mlp, waiting, grads_mlp = None, None, [], None

    def advance_mlp(token):
        nonlocal sends_mlp, own_mlp, round_mlp, waiting
        t = next(steps_mlp, None)
        if t is not None:
            sends_mlp = scatter_step(terms_mlp, t, sends_mlp, token)
            if t < far - 1:
                return zero(sends_mlp[0])
            own_mlp, round_mlp = sends_mlp, (sends_mlp, sends_mlp)
            waiting += gather_start(own_mlp)
            return zero(own_mlp)
        t = next(steps_round, None)
        if t is None:
            return nothing
        round_mlp, found = gather_step(t, round_mlp, None)
        waiting += found
        return zero(round_mlp[0])

    gathered = lax.all_gather(small, ("ctx", "tp"), axis=0, tiled=True).reshape(owners, sides, -1)

    sends_att = scatter_start(terms_att, nothing)
    before = nothing
    after = zero(sums1)[:, :LANES]
    for t in range(far):
        later = advance_mlp(after)
        sends_att = scatter_step(terms_att, t, sends_att, before)
        before = later
    round_att, waiting_att, grads_att = (sends_att, sends_att), gather_start(sends_att), None
    for t in range(far):
        ready, waiting = waiting, []
        later = advance_mlp(after)
        round_att, found = gather_step(t, round_att, before)
        before = later
        if ready:
            grads_mlp, more = unpack_mlp(ready, grads_mlp)
            before = before + more
        if t == 0:
            before = before + finish_token
        waiting_att += found
        if t == far - 2:
            grads_att, more = unpack_att(waiting_att[:-4], None)
            waiting_att = waiting_att[-4:]
            before = before + more
    while waiting:
        grads_mlp, _ = unpack_mlp(waiting, grads_mlp)
        waiting = []
        advance_mlp(after)
    grads_att, _ = unpack_att(waiting_att, grads_att)

    side_sums = jnp.sum(gathered, axis=0)
    norm_sums = jnp.sum(side_sums[:, : 4 * width], axis=0).reshape(4, width)
    small = lax.dynamic_index_in_dim(side_sums, lax.axis_index("tp"), 0)
    at = 4 * width
    d_bias = small[0, at : at + width]
    d_b_up = small[0, at + width : at + width + hidden_units]
    d_b_qkv = small[0, at + width + hidden_units :].reshape(3, local_width)
    d_w_up, d_w_down = grads_mlp
    d_w_qkv, d_w_out = grads_att
    return (
        output,
        d_hidden,
        norm_sums[0],
        norm_sums[1],
        norm_sums[2],
        norm_sums[3],
        d_w_qkv,
        d_b_qkv,
        d_w_out,
        d_bias,
        d_w_up,
        d_b_up,
        d_w_down,
        d_bias,
    )


def solution(mesh):
    placed = (
        P("ctx", None),
        P(),
        P(),
        P(),
        P(),
        P(),
        P(None, None, "tp"),
        P(None, "tp"),
        P("tp", None),
        P(),
        P(None, "tp"),
        P("tp"),
        P("tp", None),
        P(),
        P("ctx", None),
    )
    return jax.shard_map(
        local,
        mesh=mesh,
        in_specs=placed,
        out_specs=(
            P("ctx", None),
            P("ctx", None),
            P(),
            P(),
            P(),
            P(),
            P(None, None, "tp"),
            P(None, "tp"),
            P("tp", None),
            P(),
            P(None, "tp"),
            P("tp"),
            P("tp", None),
            P(),
        ),
        check_vma=False,
    )
```

```python
import functools

import jax
import jax.numpy as jnp
import numpy as np
from jax import lax
from jax.experimental import pallas as pl
from jax.experimental.pallas import tpu as pltpu
from jax.sharding import PartitionSpec as P

HEAD_DIM = 64
ROT = 16
HALF = ROT // 2
BLOCK = 128
LANES = 128
KEYS = 512
MIB = 1 << 20

norm_eps = 1e-05
masked_score = -1e30
score_scale = HEAD_DIM ** (-0.5)
low = jnp.bfloat16
full = jnp.float32


def mm(left, right):
    return lax.dot_general(left, right, (((1,), (0,)), ((), ())), preferred_element_type=full)


def mm_nt(left, right):
    return lax.dot_general(left, right, (((1,), (1,)), ((), ())), preferred_element_type=full)


def turn(tensor):
    return tensor.astype(full).T.astype(low)


def lane_ids(shape):
    return lax.broadcasted_iota(jnp.int32, shape, len(shape) - 1)


def row_ids(shape):
    return lax.broadcasted_iota(jnp.int32, shape, len(shape) - 2)


def rotary_partner(tensor):
    lanes = lane_ids(tensor.shape)
    ahead = pltpu.roll(tensor, LANES - HALF, 1)
    behind = pltpu.roll(tensor, HALF, 1)
    return jnp.where(lanes % ROT < HALF, ahead, behind)


def spec_vmem():
    return pl.BlockSpec(memory_space=pltpu.VMEM)


def spec_smem():
    return pl.BlockSpec(memory_space=pltpu.SMEM)


def spec_hbm():
    return pl.BlockSpec(memory_space=pltpu.HBM)


def params(mib):
    return pltpu.CompilerParams(vmem_limit_bytes=mib * MIB)


def shape_of(shape, kind):
    return jax.ShapeDtypeStruct(shape, kind)


def block_tables(inverse, blocks):
    row = row_ids((BLOCK, LANES)).astype(full)
    start = blocks.astype(full) * float(BLOCK)
    return jnp.cos(row * inverse), jnp.sin(row * inverse), jnp.cos(start * inverse), jnp.sin(start * inverse)


def project_kernel(heads, pair_ref, inv_ref, *rest):
    given, rest = rest[:12], rest[12:]
    h1_ref, h2_ref, xhat_ref, std_ref, d_bias_ref, gains_ref, bias_ref, b_up_out_ref, packed = rest[:9]
    held, sems = rest[9:-1], rest[-1]
    copies = [pltpu.make_async_copy(src, dst, sems.at[i]) for i, (src, dst) in enumerate(zip(given, held))]
    for copy in copies:
        copy.start()
    (
        hidden_ref,
        g1_ref,
        c1_ref,
        g2_ref,
        c2_ref,
        cot_ref,
        w_out_ref,
        w_qkv_ref,
        b_qkv_ref,
        b_up_ref,
        b_out_ref,
        b_down_ref,
    ) = held
    rows = hidden_ref.shape[0]
    me = lax.axis_index("ctx")
    pair = pair_ref[me]
    total_blocks = 2 * pair_ref.shape[0]

    first = jnp.where(row_ids((8, LANES)) == 0, pair, total_blocks - 1 - pair)
    inverse = inv_ref[...]
    cos_row, sin_row, cos_block, sin_block = block_tables(inverse, first)
    in_head = lane_ids((BLOCK, LANES)) % HEAD_DIM
    tables = []
    for half in range(2):
        cos_at, sin_at = cos_block[half : half + 1], sin_block[half : half + 1]
        cosine = cos_row * cos_at - sin_row * sin_at
        sine = sin_row * cos_at + cos_row * sin_at
        cosine = jnp.where(in_head < ROT, cosine, 1.0)
        sine = jnp.where(in_head < HALF, -sine, jnp.where(in_head < ROT, sine, 0.0))
        tables.append((cosine, sine))
    cosine = jnp.concatenate([tables[0][0], tables[1][0]], axis=0)
    sine = jnp.concatenate([tables[0][1], tables[1][1]], axis=0)

    for copy in copies[:5]:
        copy.wait()
    x = hidden_ref[...].astype(full)
    centred = x - jnp.mean(x, axis=-1, keepdims=True)
    spread = jnp.mean(centred * centred, axis=-1, keepdims=True)
    inv_std = lax.rsqrt(spread + norm_eps)
    xhat = centred * inv_std
    xhat_ref[...] = xhat
    std_ref[...] = jnp.broadcast_to(inv_std, std_ref.shape)

    def as_row(ref):
        return ref[...].astype(full)[None, :]

    gain1, gain2 = as_row(g1_ref), as_row(g2_ref)
    h1 = (xhat * gain1 + as_row(c1_ref)).astype(low)
    h1_ref[...] = h1
    h2_ref[...] = (xhat * gain2 + as_row(c2_ref)).astype(low)
    gains_ref[0:1] = gain1
    gains_ref[1:2] = gain2
    for copy in copies[5:]:
        copy.wait()
    b_up_out_ref[...] = as_row(b_up_ref)
    bias_ref[0:1] = as_row(b_out_ref)
    bias_ref[1:2] = as_row(b_down_ref)
    d_bias_ref[...] = jnp.sum(cot_ref[...].astype(full), axis=0, keepdims=True)

    lane = lane_ids((rows, LANES))

    def projected(s):
        return mm(h1, w_qkv_ref[s]) + b_qkv_ref[s : s + 1].astype(full)

    def turned(tile):
        return tile * cosine + rotary_partner(tile) * sine

    queries, keys, values = projected(0), projected(1), projected(2)
    grads = mm_nt(cot_ref[...], w_out_ref[...])
    left = lane < HEAD_DIM
    for i in range(heads // 2):
        cut = slice(i * LANES, (i + 1) * LANES)
        q = turned(queries[:, cut]).astype(low).astype(full) * score_scale
        k = turned(keys[:, cut])
        v = values[:, cut]
        g = grads[:, cut]
        packed[2 * i, :, :LANES] = jnp.where(left, g, pltpu.roll(q, HEAD_DIM, 1)).astype(low)
        packed[2 * i, :, LANES:] = jnp.where(left, v, pltpu.roll(k, HEAD_DIM, 1)).astype(low)
        packed[2 * i + 1, :, :LANES] = jnp.where(left, pltpu.roll(g, HEAD_DIM, 1), q).astype(low)
        packed[2 * i + 1, :, LANES:] = jnp.where(left, pltpu.roll(v, HEAD_DIM, 1), k).astype(low)


def project(heads, pair_of, inverse, given):
    hidden, w_out, b_up = given[0], given[6], given[9]
    rows, width = hidden.shape
    outs = [
        shape_of((rows, width), low),
        shape_of((rows, width), low),
        shape_of((rows, width), full),
        shape_of((rows, LANES), full),
        shape_of((1, width), full),
        shape_of((2, width), full),
        shape_of((2, width), full),
        shape_of((1, b_up.shape[0]), full),
        shape_of((heads, rows, 2 * LANES), low),
    ]
    return pl.pallas_call(
        functools.partial(project_kernel, heads),
        out_shape=outs,
        in_specs=[spec_smem(), spec_vmem()] + [spec_hbm()] * len(given),
        out_specs=[spec_vmem()] * len(outs),
        scratch_shapes=[pltpu.VMEM(array.shape, array.dtype) for array in given]
        + [pltpu.SemaphoreType.DMA((len(given),))],
        compiler_params=params(60),
        cost_estimate=pl.CostEstimate(
            flops=2 * rows * width * 4 * w_out.shape[0], bytes_accessed=8 * MIB, transcendentals=0
        ),
        name="project",
    )(pair_of, inverse, *given)


def mlp_kernel(early, ids_ref, *rest):
    given, rest = rest[:6], rest[6:]
    part_ref, back_ref, sums_ref, d_b_up_ref, keep_ref, early_ref, send_ref = rest[:7]
    h2_turned, part_acc, back_acc = rest[7:10]
    held, sems = rest[10:-1], rest[-1]
    copies = [pltpu.make_async_copy(src, dst, sems.at[i]) for i, (src, dst) in enumerate(zip(given, held))]
    h2_held, w_up_ref, b_up, cot_ref, w_down_ref, xhat_ref = held
    step = pl.program_id(0)
    steps = pl.num_programs(0)

    @pl.when(step == 0)
    def _():
        for copy in copies:
            copy.start()
        part_acc[...] = jnp.zeros_like(part_acc)
        back_acc[...] = jnp.zeros_like(back_acc)
        copies[0].wait()
        h2_turned[...] = turn(h2_held[...])
        for copy in copies[1:3]:
            copy.wait()

    at = [pl.multiple_of(ids_ref[b * steps + step] * LANES, LANES) for b in range(2)]
    w_up = jnp.concatenate([w_up_ref[:, pl.ds(i, LANES)] for i in at], axis=1)
    u = mm(h2_held[...], w_up) + jnp.concatenate([b_up[:, pl.ds(i, LANES)] for i in at], axis=1)

    @pl.when(step == 0)
    def _():
        for copy in copies[3:5]:
            copy.wait()

    cot = cot_ref[...]
    w_down = jnp.concatenate([w_down_ref[pl.ds(i, LANES), :] for i in at], axis=0)
    cdf = 0.5 * (1.0 + lax.erf(u * np.float32(np.sqrt(0.5))))
    active = u * cdf
    active_low = active.astype(low)
    slope = cdf + u * jnp.exp(-0.5 * u * u) * np.float32(1.0 / np.sqrt(2.0 * np.pi))
    du = (mm_nt(cot, w_down) * slope).astype(low)
    part_acc[...] += mm(active_low, w_down)
    back_acc[...] += mm_nt(du, w_up)
    d_b_up = jnp.sum(du.astype(full), axis=0, keepdims=True)
    up = mm(h2_turned[...], du).astype(low)
    down = mm(active.T.astype(low), cot).astype(low)
    depth = up.shape[0]

    def put(b, grad_ref):
        grad_ref[:depth] = up[:, b * LANES : (b + 1) * LANES]
        for t in range(down.shape[1] // LANES):
            grad_ref[depth + t * LANES : depth + (t + 1) * LANES] = down[
                b * LANES : (b + 1) * LANES, t * LANES : (t + 1) * LANES
            ]

    for b in range(2):
        d_b_up_ref[:, pl.ds(at[b], LANES)] = d_b_up[:, b * LANES : (b + 1) * LANES]
    put(0, keep_ref)

    @pl.when(step < early)
    def _():
        put(1, early_ref)

    @pl.when(step >= early)
    def _():
        put(1, send_ref)

    @pl.when(step == steps - 1)
    def _():
        copies[5].wait()
        part_ref[...] = part_acc[...]
        back = back_acc[...]
        back_ref[...] = back.astype(low)
        sums_ref[0:1] = jnp.sum(back * xhat_ref[...], axis=0, keepdims=True)
        sums_ref[1:2] = jnp.sum(back, axis=0, keepdims=True)


def mlp(ids, early, *given):
    rows, width = given[0].shape
    hidden_units = given[1].shape[1]
    steps = hidden_units // LANES // 2
    whole = lambda shape: pl.BlockSpec(shape, lambda f, c: (0,) * len(shape))
    grads = lambda at: pl.BlockSpec((2 * width, LANES), lambda f, c: (at(f), 0))
    outs = [
        shape_of((rows, width), full),
        shape_of((rows, width), low),
        shape_of((2, width), full),
        shape_of((1, hidden_units), full),
        shape_of((steps * 2 * width, LANES), low),
        shape_of((early * 2 * width, LANES), low),
        shape_of(((steps - early) * 2 * width, LANES), low),
    ]
    return pl.pallas_call(
        functools.partial(mlp_kernel, early),
        grid_spec=pltpu.PrefetchScalarGridSpec(
            num_scalar_prefetch=1,
            grid=(steps,),
            in_specs=[spec_hbm()] * len(given),
            out_specs=[whole(array.shape) for array in outs[:4]]
            + [
                grads(lambda f: f),
                grads(lambda f: jnp.minimum(f, early - 1)),
                grads(lambda f: jnp.maximum(f - early, 0)),
            ],
            scratch_shapes=[
                pltpu.VMEM((width, rows), low),
                pltpu.VMEM((rows, width), full),
                pltpu.VMEM((rows, width), full),
            ]
            + [pltpu.VMEM(array.shape, array.dtype) for array in given]
            + [pltpu.SemaphoreType.DMA((len(given),))],
        ),
        out_shape=outs,
        compiler_params=params(60),
        cost_estimate=pl.CostEstimate(
            flops=12 * rows * width * hidden_units, bytes_accessed=20 * MIB, transcendentals=0
        ),
        name="feed_forward",
    )(ids, *given)


def attention_kernel(heads, group, places, is_first, is_last, pair_ref, inv_ref, token_ref, *rest):
    del token_ref
    if is_first:
        got_ref, rest = rest[0], rest[1:]
        if group > 1:
            other_ref, rest = rest[0], rest[1:]
    else:
        rest = rest[4:]
    out_ref, rest = rest[0], rest[1:]
    if is_last:
        d_own_ref, rest = rest[0], rest[1:]
        if group > 1:
            d_other_ref, rest = rest[0], rest[1:]
    (values_keys, turned_keys, sums, queries), rest = rest[:4], rest[4:]
    token_out, rest = rest[0], rest[1:]
    weights_in, weights_out, stored, peaks, totals, weighted, finals, block_cos, block_sin = rest
    token_out[...] = jnp.zeros_like(token_out)

    rows = queries.shape[1]
    owners = pair_ref.shape[0]
    total_blocks = 2 * owners
    per_chunk = KEYS // BLOCK
    tasks = (total_blocks + 1 + per_chunk - 1) // per_chunk
    me = lax.axis_index("ctx")
    own_sub = lax.rem(me, group)

    def blocks_of(r, d):
        owner = r * group + lax.rem(own_sub + d, group)
        pair = pair_ref[owner]
        return pair, total_blocks - 1 - pair

    def place(tile, block):
        at = pl.multiple_of(block * BLOCK, BLOCK)
        values_keys[pl.ds(at, BLOCK), :] = tile
        turned_keys[:, pl.ds(at, BLOCK)] = turn(tile)

    if is_first:
        for r in range(heads):
            queries[r] = got_ref[r, :, :LANES]
            for half, block in enumerate(blocks_of(r, 0)):
                place(got_ref[r, half * BLOCK : (half + 1) * BLOCK, LANES:], block)
            for d in range(1, group):
                for half, block in enumerate(blocks_of(r, d)):
                    at = r * rows + half * BLOCK
                    place(other_ref[d - 1, at : at + BLOCK, :], block)
        sums[...] = jnp.zeros_like(sums)

    lane = lane_ids((BLOCK, LANES))
    left = lane < HEAD_DIM
    in_key = lane - HEAD_DIM
    moving = (in_key >= 0) & (in_key < ROT)
    forward = (in_key >= 0) & (in_key < HALF)
    cos_row, sin_row, block_cos[...], block_sin[...] = block_tables(inv_ref[...], row_ids(block_cos.shape))

    def rotated_back(tile, block):
        cos_at, sin_at = block_cos[pl.ds(block, 1), :], block_sin[pl.ds(block, 1), :]
        cosine = jnp.where(moving, cos_row * cos_at - sin_row * sin_at, 1.0)
        sine = sin_row * cos_at + cos_row * sin_at
        sine = jnp.where(moving, jnp.where(forward, sine, -sine), 0.0)
        return tile * cosine + rotary_partner(tile) * sine

    offset = row_ids((BLOCK, BLOCK)) - lane_ids((BLOCK, BLOCK))

    def one_pair(i, carry):
        blocks = blocks_of(places[0] + i, 0)
        first = blocks[0] // per_chunk + 1
        for half in range(2):
            both = queries[places[0] + i, half * BLOCK : (half + 1) * BLOCK, :]
            both_turned = turn(both)
            upper = row_ids((LANES, BLOCK)) < HEAD_DIM
            zero = jnp.zeros_like(both_turned)
            weights_in[half, :, :BLOCK] = jnp.where(upper, both_turned, zero)
            weights_in[half, :, BLOCK:] = jnp.where(upper, zero, both_turned)
            weights_out[half, :BLOCK, :] = jnp.where(left, both, zero)
            weights_out[half, BLOCK:, :] = jnp.where(left, zero, both)
        finals[...] = jnp.zeros_like(finals)

        def task(t):
            is_low = t < first
            chunk = jnp.where(is_low, first - 1 - t, t - first)
            return is_low, chunk

        runs = KEYS // BLOCK
        for t in range(tasks):
            is_low, chunk = task(t)
            weights = weights_in[jnp.where(is_low, 0, 1)]
            for u in range(runs):
                at = pl.multiple_of(chunk * KEYS + u * BLOCK, BLOCK)
                sub = slice(u * BLOCK, (u + 1) * BLOCK)
                both = mm(values_keys[pl.ds(at, BLOCK), :], weights)
                grads = both[:, :BLOCK]
                scores = both[:, BLOCK:]
                if t in (0, tasks - 1):
                    query_at = blocks[0 if t == 0 else 1] * BLOCK
                    scores = jnp.where(offset <= query_at - at, scores, masked_score)
                peak = jnp.max(scores, axis=0, keepdims=True)
                raised = jnp.exp(scores - peak)
                stored[t, sub, :BLOCK] = raised
                stored[t, sub, BLOCK:] = grads
                line = t * runs + u
                peaks[line : line + 1] = peak
                totals[line : line + 1] = jnp.sum(raised, axis=0, keepdims=True)
                weighted[line : line + 1] = jnp.sum(raised * grads, axis=0, keepdims=True)

        in_low = row_ids((tasks * runs, BLOCK)) < first * runs

        def finish(mine):
            top = jnp.max(jnp.where(mine, peaks[...], masked_score), axis=0, keepdims=True)
            factor = jnp.where(mine, jnp.exp(peaks[...] - top), 0.0)
            inverse = 1.0 / jnp.sum(totals[...] * factor, axis=0, keepdims=True)
            return factor * inverse, jnp.sum(weighted[...] * factor, axis=0, keepdims=True) * inverse

        (low_factor, low_delta), (high_factor, high_delta) = finish(in_low), finish(jnp.logical_not(in_low))
        peaks[...] = low_factor + high_factor

        for t in range(tasks):
            is_low, chunk = task(t)
            half = jnp.where(is_low, 0, 1)
            weights = weights_out[half]
            delta = jnp.where(is_low, low_delta, high_delta)
            parts = []
            for u in range(runs):
                sub = slice(u * BLOCK, (u + 1) * BLOCK)
                probs = stored[t, sub, :BLOCK] * peaks[t * runs + u : t * runs + u + 1]
                d_scores = probs * (stored[t, sub, BLOCK:] - delta)
                both = jnp.concatenate([probs, d_scores], axis=1).astype(low)
                at = pl.multiple_of(chunk * KEYS + u * BLOCK, BLOCK)
                sums[pl.ds(at, BLOCK), :] += mm(both, weights)
                parts.append(both)
            at = pl.multiple_of(chunk * KEYS, KEYS)
            finals[half] += mm(turned_keys[:, pl.ds(at, KEYS)], jnp.concatenate(parts, axis=0))

        for half in range(2):
            both = jnp.concatenate(
                [finals[half, :HEAD_DIM, :BLOCK], finals[half, HEAD_DIM:, BLOCK:] * score_scale], axis=0
            ).T
            out_ref[i, half * BLOCK : (half + 1) * BLOCK, :] = rotated_back(both, blocks[half]).astype(low)
        return carry

    lax.fori_loop(0, len(places), one_pair, 0)

    if is_last:
        for r in range(heads):
            for d in range(group):
                for half, block in enumerate(blocks_of(r, d)):
                    at = r * rows + half * BLOCK
                    tile = rotated_back(sums[pl.ds(pl.multiple_of(block * BLOCK, BLOCK), BLOCK), :], block)
                    if d == 0:
                        d_own_ref[at : at + BLOCK, :] = tile
                    else:
                        d_other_ref[d - 1, at : at + BLOCK, :] = tile


def attention(heads, group, places, pair_of, inverse, token, got, other, state):
    is_first, is_last = state is None, places[-1] == heads - 1
    rows = got.shape[1]
    owners = pair_of.shape[0]
    total_keys = owners * rows
    tasks = (2 * owners + KEYS // BLOCK) // (KEYS // BLOCK)
    operands = [pair_of, inverse, token]
    outs = [shape_of((len(places), rows, LANES), low)]
    if is_first:
        operands += [got] if other is None else [got, other]
    else:
        operands += list(state)
    if is_last:
        outs.append(shape_of((heads * rows, LANES), full))
        if group > 1:
            outs.append(shape_of((group - 1, heads * rows, LANES), full))
    kept = [
        shape_of((total_keys, LANES), low),
        shape_of((LANES, total_keys), low),
        shape_of((total_keys, LANES), full),
        shape_of((heads, rows, LANES), low),
    ]
    aliases = {} if is_first else {len(operands) - 4 + i: len(outs) + i for i in range(4)}
    found = pl.pallas_call(
        functools.partial(attention_kernel, heads, group, places, is_first, is_last),
        out_shape=outs + kept + [shape_of((1, LANES), full)],
        in_specs=[spec_smem()] + [spec_vmem()] * (len(operands) - 1),
        out_specs=[spec_vmem()] * (len(outs) + 5),
        input_output_aliases=aliases,
        scratch_shapes=[
            pltpu.VMEM((2, LANES, 2 * BLOCK), low),
            pltpu.VMEM((2, 2 * BLOCK, LANES), low),
            pltpu.VMEM((tasks, KEYS, 2 * BLOCK), full),
            pltpu.VMEM((tasks * KEYS // BLOCK, BLOCK), full),
            pltpu.VMEM((tasks * KEYS // BLOCK, BLOCK), full),
            pltpu.VMEM((tasks * KEYS // BLOCK, BLOCK), full),
            pltpu.VMEM((2, LANES, 2 * BLOCK), full),
            pltpu.VMEM((2 * owners, LANES), full),
            pltpu.VMEM((2 * owners, LANES), full),
        ],
        compiler_params=params(6 + total_keys * 5 * 256 // MIB),
        cost_estimate=pl.CostEstimate(
            flops=2_500_000_000 * len(places), bytes_accessed=2 * MIB, transcendentals=0
        ),
        name="attention",
    )(*operands)
    return found[0], found[1 : len(outs)], found[len(outs) : len(outs) + 4], found[-1]


def combine_kernel(heads, terms, *refs):
    out_ref = refs[-1]
    rows = out_ref.shape[1]
    for r in range(heads):
        cut = slice(r * rows, (r + 1) * rows)
        total = refs[0][cut, :]
        for term in refs[1:terms]:
            total = total + term[cut, :]
        out_ref[r, :, LANES:] = total.astype(low)
    at = 0
    for first_ref in refs[terms:-1]:
        out_ref[at : at + first_ref.shape[0], :, :LANES] = first_ref[...]
        at += first_ref.shape[0]


def combine(heads, terms, firsts):
    rows = firsts[0].shape[1]
    return pl.pallas_call(
        functools.partial(combine_kernel, heads, len(terms)),
        out_shape=shape_of((heads, rows, 2 * LANES), low),
        in_specs=[spec_vmem()] * (len(firsts) + len(terms)),
        out_specs=spec_vmem(),
        compiler_params=params(24),
        cost_estimate=pl.CostEstimate(flops=10**7, bytes_accessed=3 * MIB, transcendentals=0),
        name="combine",
    )(*terms, *firsts)


def weight_grads_kernel(
    heads, early, ids_ref, got_ref, h1_ref, cot_ref, low_ref, d_b_ref, keep_ref, early_ref, send_ref, token_ref, grads
):
    chips, chunk_rows = keep_ref.shape[:2]

    def put(at, tile):
        step = min(chunk_rows, tile.shape[0])
        for off in range(0, tile.shape[0], step):
            chunk, inside = divmod(at + off, chunk_rows)
            grads[chunk, inside : inside + step] = tile[off : off + step]

    rows = h1_ref.shape[0]
    left = lane_ids((rows, LANES)) < HEAD_DIM
    for i in range(heads // 2):
        cut = slice(i * LANES, (i + 1) * LANES)
        for first, second, half in ((0, 1, slice(0, LANES)), (3, 2, slice(LANES, 2 * LANES))):
            a, b = got_ref[2 * i, :, half].astype(full), got_ref[2 * i + 1, :, half].astype(full)
            low_ref[first, :, cut] = jnp.where(left, a, pltpu.roll(b, HEAD_DIM, 1)).astype(low)
            low_ref[second, :, cut] = jnp.where(left, pltpu.roll(a, HEAD_DIM, 1), b).astype(low)
    h1_turned = turn(h1_ref[...])
    depth, tiles = h1_turned.shape[0], heads // 2
    for s in range(3):
        d_proj = low_ref[1 + s]
        d_b_ref[s : s + 1] = jnp.sum(d_proj.astype(full), axis=0, keepdims=True)
        grad = mm(h1_turned, d_proj).astype(low)
        for t in range(tiles):
            put((s * tiles + t) * depth, grad[:, t * LANES : (t + 1) * LANES])
    grad = mm(turn(low_ref[0]), cot_ref[...]).astype(low)
    height = grad.shape[0]
    for t in range(depth // LANES):
        put(3 * tiles * depth + t * height, grad[:, t * LANES : (t + 1) * LANES])
    for t in range(chips):
        target = early_ref.at[t] if t < early else send_ref.at[t - early]
        target[...] = grads[ids_ref[chips + t]]
        keep_ref[t] = grads[ids_ref[t]]
    token_ref[...] = jnp.zeros_like(token_ref)


def weight_grads(heads, early, ids, got, h1, cot):
    rows, width = h1.shape
    local_width = heads * HEAD_DIM
    chips = ids.shape[0] // 2
    chunk_rows = 4 * width * local_width // LANES // (2 * chips)
    outs = [
        shape_of((4, rows, local_width), low),
        shape_of((3, local_width), full),
        shape_of((chips, chunk_rows, LANES), low),
        shape_of((early, chunk_rows, LANES), low),
        shape_of((chips - early, chunk_rows, LANES), low),
        shape_of((1, LANES), full),
    ]
    return pl.pallas_call(
        functools.partial(weight_grads_kernel, heads, early),
        out_shape=outs,
        in_specs=[spec_smem()] + [spec_vmem()] * 3,
        out_specs=[spec_vmem()] * len(outs),
        scratch_shapes=[pltpu.VMEM((2 * chips, chunk_rows, LANES), low)],
        compiler_params=params(20),
        cost_estimate=pl.CostEstimate(
            flops=8 * rows * width * local_width, bytes_accessed=8 * MIB, transcendentals=0
        ),
        name="weight_grads",
    )(ids, got, h1, cot)


def return_kernel(low_ref, part_ref, w_out_ref, w_qkv_ref, xhat_ref, e2_ref, both_ref, sums_ref):
    rows = xhat_ref.shape[0]
    both_ref[:rows] = (part_ref[...] + mm(low_ref[0], w_out_ref[...])).astype(low)
    back = mm_nt(low_ref[1], w_qkv_ref[0]) + mm_nt(low_ref[2], w_qkv_ref[1]) + mm_nt(low_ref[3], w_qkv_ref[2])
    both_ref[rows : 2 * rows] = back.astype(low)
    both_ref[2 * rows :] = e2_ref[...]
    sums_ref[0:1] = jnp.sum(back * xhat_ref[...], axis=0, keepdims=True)
    sums_ref[1:2] = jnp.sum(back, axis=0, keepdims=True)


def back_projections(*given):
    rows, width = given[1].shape
    return pl.pallas_call(
        return_kernel,
        out_shape=[shape_of((3 * rows, width), low), shape_of((2, width), full)],
        in_specs=[spec_vmem()] * len(given),
        out_specs=[spec_vmem()] * 2,
        compiler_params=params(16),
        cost_estimate=pl.CostEstimate(
            flops=8 * rows * width * given[2].shape[0], bytes_accessed=8 * MIB, transcendentals=0
        ),
        name="back_projections",
    )(*given)


def finish_kernel(
    hidden_ref, cot_ref, xhat_ref, std_ref, gains_ref, bias_ref, ours_ref, theirs_ref, out_ref, grad_ref, token_ref
):
    rows = hidden_ref.shape[0]
    gains = gains_ref[...]
    biases = bias_ref[...]
    summed = ours_ref[:rows].astype(full) + theirs_ref[:rows].astype(full)
    out_ref[...] = (hidden_ref[...].astype(full) + summed + biases[0:1] + biases[1:2]).astype(low)
    e1 = ours_ref[rows : 2 * rows].astype(full) + theirs_ref[rows : 2 * rows].astype(full)
    e2 = ours_ref[2 * rows :].astype(full) + theirs_ref[2 * rows :].astype(full)
    f = e1 * gains[0:1] + e2 * gains[1:2]
    xhat = xhat_ref[...]
    inv_std = std_ref[:, 0:1]
    grad_ref[...] = cot_ref[...].astype(full) + inv_std * (
        f - jnp.mean(f, axis=-1, keepdims=True) - xhat * jnp.mean(f * xhat, axis=-1, keepdims=True)
    )
    token_ref[...] = jnp.zeros_like(token_ref)


def finish(*operands):
    rows, width = operands[0].shape
    return pl.pallas_call(
        finish_kernel,
        out_shape=[shape_of((rows, width), low), shape_of((rows, width), full), shape_of((1, LANES), full)],
        in_specs=[spec_vmem()] * len(operands),
        out_specs=[spec_vmem()] * 3,
        compiler_params=params(24),
        cost_estimate=pl.CostEstimate(flops=10**7, bytes_accessed=8 * MIB, transcendentals=0),
        name="finish",
    )(*operands)


def to_attention(width, local_width, source, refs, base, unit):
    qkv_ref, out_ref = refs
    tiles = local_width // LANES
    split = 3 * tiles * width
    tile = base // width
    row = pl.multiple_of(lax.rem(base, width), unit)
    column = pl.multiple_of(lax.rem(tile, tiles) * LANES, LANES)
    yield base < split, source, qkv_ref.at[jnp.minimum(tile // tiles, 2), pl.ds(row, unit), pl.ds(column, LANES)]
    after = jnp.maximum(base - split, 0)
    row = pl.multiple_of(lax.rem(after, local_width), unit)
    column = pl.multiple_of(after // local_width * LANES, LANES)
    yield base >= split, source, out_ref.at[pl.ds(row, unit), pl.ds(column, LANES)]


def to_mlp(width, source, refs, base, unit):
    up_ref, down_ref = refs
    block, inside = base // (2 * width), lax.rem(base, 2 * width)
    block_at = pl.multiple_of(block * LANES, LANES)
    row = pl.multiple_of(jnp.minimum(inside, width - unit), unit)
    yield inside < width, source, up_ref.at[pl.ds(row, unit), pl.ds(block_at, LANES)]
    for t in range(unit // LANES):
        column = pl.multiple_of(jnp.maximum(inside - width, 0) + t * LANES, LANES)
        cut = source.at[pl.ds(t * LANES, LANES), :]
        yield inside >= width, cut, down_ref.at[pl.ds(block_at, LANES), pl.ds(column, LANES)]


def unpack_kernel(route, count, unit, has_old, ids_ref, *rest):
    parts, rest = rest[:count], rest[count:]
    rest = rest[2:] if has_old else rest
    targets, (token_ref, held, sems) = rest[:2], rest[2:]
    token_ref[...] = jnp.zeros_like(token_ref)
    chunk_rows = parts[0].shape[0]
    units = chunk_rows // unit
    per_unit = sems.shape[0] // (count * units)

    def moves():
        for i in range(count):
            for j in range(units):
                source = held.at[i, pl.ds(j * unit, unit), :]
                base = ids_ref[i] * chunk_rows + j * unit
                for n, (applies, piece, target) in enumerate(route(source, targets, base, unit)):
                    sem = sems.at[(i * units + j) * per_unit + n]
                    yield i, applies, pltpu.make_async_copy(piece, target, sem)

    done = -1
    for i, applies, copy in moves():
        if i != done:
            held[i] = parts[i][...].astype(full)
            done = i
        pl.when(applies)(copy.start)
    for i, applies, copy in moves():
        pl.when(applies)(copy.wait)


def unpack(name, route, cases, unit, shapes, ids, parts, old):
    count = len(parts)
    chunk_rows = parts[0].shape[0]
    operands = [ids, *parts, *(old or ())]
    return pl.pallas_call(
        functools.partial(unpack_kernel, route, count, unit, old is not None),
        out_shape=[shape_of(shape, full) for shape in shapes] + [shape_of((1, LANES), full)],
        in_specs=[spec_smem()] + [spec_vmem()] * count + [spec_hbm()] * (len(operands) - 1 - count),
        out_specs=[spec_hbm()] * 2 + [spec_vmem()],
        input_output_aliases={} if old is None else {1 + count: 0, 2 + count: 1},
        scratch_shapes=[
            pltpu.VMEM((count, chunk_rows, LANES), full),
            pltpu.SemaphoreType.DMA((count * (chunk_rows // unit) * cases,)),
        ],
        compiler_params=params(8 + count * chunk_rows * 3 * LANES * 2 // MIB),
        cost_estimate=pl.CostEstimate(
            flops=10**6, bytes_accessed=count * chunk_rows * LANES * 6, transcendentals=0
        ),
        name=name,
    )(*operands)


def local(
    hidden,
    pair_of,
    ln1_gain,
    ln1_bias,
    ln2_gain,
    ln2_bias,
    w_qkv,
    b_qkv,
    w_out,
    b_out,
    w_up,
    b_up,
    w_down,
    b_down,
    cotangent,
):
    owners = lax.axis_size("ctx")
    sides = lax.axis_size("tp")
    rows, width = hidden.shape
    local_width = w_qkv.shape[2]
    hidden_units = w_up.shape[1]
    heads = local_width // HEAD_DIM
    group = owners // heads

    exponent = np.arange(0, ROT, 2, dtype=np.float32) / np.float32(ROT)
    inverse = jnp.asarray(np.tile(np.float32(10000.0) ** (-exponent), LANES // HALF)[None, :], full)
    order = (0, 2, 4, 6, 7, 5, 3, 1) if owners == 16 else tuple(range(owners // 2))
    chips = len(order)

    def to_heads(array):
        groups = [[h * group + g for h in range(heads)] for g in range(group)]
        return lax.all_to_all(array, "ctx", 0, 0, axis_index_groups=groups, tiled=True)

    def group_shift(array, d):
        pairs = [(c, c // group * group + (c % group + d) % group) for c in range(owners)]
        return lax.ppermute(array, "ctx", pairs)

    me = lax.axis_index("ctx")
    chip, core = me // 2, lax.rem(me, 2)
    place = sum(jnp.where(chip == c, i, 0) for i, c in enumerate(order))
    way = 1 - 2 * core
    far, near = chips // 2, chips - 1 - chips // 2

    def ring(array, forward):
        pairs = []
        for i, c in enumerate(order):
            for k in range(2):
                step = 1 if (k == 0) == forward else -1
                pairs.append((2 * c + k, 2 * order[(i + step) % chips] + k))
        return lax.ppermute(array, "ctx", pairs)

    def other_core(array):
        return lax.ppermute(array, "ctx", [(c, c ^ 1) for c in range(owners)])

    def across(array):
        return lax.ppermute(array, "tp", [(t, (t + 1) % sides) for t in range(sides)])

    def target(distance):
        return lax.rem(place + way * distance + chips, chips)

    def zero(array):
        return array[:1].astype(full) * 0.0

    slots = [far, -near]
    for t in range(1, far):
        slots += [far - t] if t >= near else [far - t, t - near]
    slots.append(0)
    early = 2
    slot_ids = jnp.stack(
        [core * chips + target(d) for d in slots] + [(1 - core) * chips + target(-d) for d in slots]
    )

    def terms_of(keep, came):
        def term(i):
            return keep[i].astype(full) + came[i].astype(full)

        return {d: term(i) for i, d in enumerate(slots)}

    def scatter_start(terms, token):
        return (terms[far] + token).astype(low), (terms[-near] + token).astype(low)

    def scatter_step(terms, t, sends, token):
        long_send, short_send = sends
        long_got = ring(long_send, True).astype(full) + token
        last = t == far - 1
        long_next = long_got if last else (long_got + terms[far - 1 - t]).astype(low)
        short_next = short_send
        if t < near:
            short_got = ring(short_send, False).astype(full) + token
            short_next = short_got if t == near - 1 else (short_got + terms[t + 1 - near]).astype(low)
        if last:
            return (terms[0] + long_next + short_next).astype(low)
        return long_next, short_next

    base, other_base = core * chips, (1 - core) * chips

    def gather_start(own):
        return [(own, base + place), (other_core(own), other_base + place)]

    def gather_step(t, sends, token):
        long_send, short_send = sends
        if token is not None:
            long_send = (long_send.astype(full) + token).astype(low)
        long_got = ring(long_send, True)
        found = [(long_got, base + target(-t - 1)), (other_core(long_got), other_base + target(t + 1))]
        short_got = short_send
        if t < near:
            short_got = ring(short_send, False)
            found += [(short_got, base + target(t + 1)), (other_core(short_got), other_base + target(-t - 1))]
        return (long_got, short_got), found

    blocks = hidden_units // LANES // 2
    in_slots = blocks == chips
    mlp_ids = slot_ids if in_slots else jnp.concatenate(
        [core * blocks + jnp.arange(blocks), (1 - core) * blocks + jnp.arange(blocks)]
    )
    h1, h2, xhat, inv_std, d_bias, gains, biases, b_up_row, packed = project(
        heads,
        pair_of,
        inverse,
        (hidden, ln1_gain, ln1_bias, ln2_gain, ln2_bias, cotangent, w_out, w_qkv, b_qkv, b_up, b_out, b_down),
    )
    got = to_heads(packed)
    part, back2, sums2, d_b_up, keep_mlp, early_mlp, send_mlp = mlp(
        mlp_ids.astype(jnp.int32), early, h2, w_up, b_up_row, cotangent, w_down, xhat
    )
    chunk = keep_mlp.shape[0] // chips
    came_mlp = jnp.concatenate([other_core(early_mlp), other_core(send_mlp)]) if not in_slots else None
    if in_slots:
        halves = [other_core(array).reshape(-1, chunk, LANES) for array in (early_mlp, send_mlp)]
        came_mlp = [half[i] for half in halves for i in range(half.shape[0])]
        terms_mlp = terms_of(keep_mlp.reshape(chips, chunk, LANES), came_mlp)
    else:
        summed = (keep_mlp.astype(full) + came_mlp.astype(full)).reshape(chips, chunk, LANES)
        terms_mlp = {d: lax.dynamic_index_in_dim(summed, target(d), 0, keepdims=False) for d in slots}
    nothing = jnp.zeros((1, LANES), full)

    other = None
    if group > 1:
        mine = got[:, :, LANES:].reshape(heads * rows, LANES)
        other = jnp.stack([group_shift(mine, group - d) for d in range(1, group)])

    middle = heads // 4
    first, _, state, token = attention(
        heads, group, tuple(range(middle)), pair_of, inverse, sums2, got, other, None
    )
    sends_mlp = scatter_start(terms_mlp, token)
    token = zero(sends_mlp[0]) + zero(sends_mlp[1])
    second, ends, _, token = attention(
        heads, group, tuple(range(middle, heads)), pair_of, inverse, token, got, other, state
    )
    d_own, d_other = ends[0], (ends[1] if group > 1 else None)
    terms = [d_own] + [group_shift(d_other[d - 1], d) for d in range(1, group)]
    backs = to_heads(combine(heads, terms, [first, second]))
    sends_mlp = scatter_step(terms_mlp, 0, sends_mlp, token)
    h1_later = (h1.astype(full) + (zero(sends_mlp[0]) + zero(sends_mlp[1]))[:, :1]).astype(low)

    lows, d_b_qkv, keep, early_att, send_att, after = weight_grads(
        heads, early, slot_ids.astype(jnp.int32), backs, h1_later, cotangent
    )
    both, sums1 = back_projections(lows, part, w_out, w_qkv, xhat, back2)
    theirs = across(both)
    output, d_hidden, finish_token = finish(
        hidden, cotangent, xhat, inv_std, gains, biases, both, theirs
    )
    halves = [other_core(array) for array in (early_att, send_att)]
    terms_att = terms_of(keep, [half[i] for half in halves for i in range(half.shape[0])])

    small = jnp.concatenate(
        [sums1.reshape(1, -1), sums2.reshape(1, -1), d_bias, d_b_up, d_b_qkv.reshape(1, -1)], axis=1
    )

    def unpack_some(name, route, cases, unit, shapes, found, old):
        parts, ids = zip(*found)
        *old, token = unpack(name, route, cases, unit, shapes, jnp.stack(ids), parts, old)
        return old, token

    unit_mlp = min(chunk, local_width)
    unit_att = min(keep.shape[1], local_width)
    unpack_mlp = functools.partial(
        unpack_some,
        "unpack_feed_forward",
        functools.partial(to_mlp, width),
        1 + unit_mlp // LANES,
        unit_mlp,
        ((width, hidden_units), (hidden_units, width)),
    )
    unpack_att = functools.partial(
        unpack_some,
        "unpack_attention",
        functools.partial(to_attention, width, local_width),
        2,
        unit_att,
        ((3, width, local_width), (local_width, width)),
    )

    steps_mlp, steps_round = iter(range(1, far)), iter(range(far))
    own_mlp, round_mlp, waiting, grads_mlp = None, None, [], None

    def advance_mlp(token):
        nonlocal sends_mlp, own_mlp, round_mlp, waiting
        t = next(steps_mlp, None)
        if t is not None:
            sends_mlp = scatter_step(terms_mlp, t, sends_mlp, token)
            if t < far - 1:
                return zero(sends_mlp[0])
            own_mlp, round_mlp = sends_mlp, (sends_mlp, sends_mlp)
            waiting += gather_start(own_mlp)
            return zero(own_mlp)
        t = next(steps_round, None)
        if t is None:
            return nothing
        round_mlp, found = gather_step(t, round_mlp, None)
        waiting += found
        return zero(round_mlp[0])

    sends_att = scatter_start(terms_att, nothing)
    before = nothing
    for t in range(far):
        later = advance_mlp(after)
        sends_att = scatter_step(terms_att, t, sends_att, before)
        before = later
    round_att, waiting_att, grads_att = (sends_att, sends_att), gather_start(sends_att), None
    distance = 1
    for t in range(far):
        ready, waiting = waiting, []
        later = advance_mlp(after)
        round_att, found = gather_step(t, round_att, before if t > 0 else None)
        if distance < owners:
            small = small + zero(round_att[0])[:, :1]
            small = small + lax.ppermute(small, "ctx", [(c, c ^ distance) for c in range(owners)])
            distance *= 2
        before = later + zero(small)[:, :LANES]
        if ready:
            grads_mlp, more = unpack_mlp(ready, grads_mlp)
            before = before + more
        if t == 0:
            before = before + finish_token
        waiting_att += found
        if t == far - 2:
            grads_att, more = unpack_att(waiting_att[:-4], None)
            waiting_att = waiting_att[-4:]
            before = before + more
    while distance < owners:
        small = small + lax.ppermute(small, "ctx", [(c, c ^ distance) for c in range(owners)])
        distance *= 2
    if waiting:
        grads_mlp, _ = unpack_mlp(waiting, grads_mlp)
    grads_att, _ = unpack_att(waiting_att, grads_att)

    norm_sums = small[:, : 4 * width]
    norm_sums = (norm_sums + across(norm_sums)).reshape(4, width)
    at = 4 * width
    d_bias = small[0, at : at + width]
    d_b_up = small[0, at + width : at + width + hidden_units]
    d_b_qkv = small[0, at + width + hidden_units :].reshape(3, local_width)
    d_w_up, d_w_down = grads_mlp
    d_w_qkv, d_w_out = grads_att
    return (
        output,
        d_hidden,
        norm_sums[0],
        norm_sums[1],
        norm_sums[2],
        norm_sums[3],
        d_w_qkv,
        d_b_qkv,
        d_w_out,
        d_bias,
        d_w_up,
        d_b_up,
        d_w_down,
        d_bias,
    )


def solution(mesh):
    placed = (
        P("ctx", None),
        P(),
        P(),
        P(),
        P(),
        P(),
        P(None, None, "tp"),
        P(None, "tp"),
        P("tp", None),
        P(),
        P(None, "tp"),
        P("tp"),
        P("tp", None),
        P(),
        P("ctx", None),
    )
    return jax.shard_map(
        local,
        mesh=mesh,
        in_specs=placed,
        out_specs=(
            P("ctx", None),
            P("ctx", None),
            P(),
            P(),
            P(),
            P(),
            P(None, None, "tp"),
            P(None, "tp"),
            P("tp", None),
            P(),
            P(None, "tp"),
            P("tp"),
            P("tp", None),
            P(),
        ),
        check_vma=False,
    )
```

```python
import functools

import jax
import jax.numpy as jnp
import numpy as np
from jax import lax
from jax.experimental import pallas as pl
from jax.experimental.pallas import tpu as pltpu
from jax.sharding import PartitionSpec as P

HEAD_DIM = 64
ROT = 16
HALF = ROT // 2
BLOCK = 128
LANES = 128
KEYS = 512
MIB = 1 << 20

norm_eps = 1e-05
masked_score = -1e30
score_scale = HEAD_DIM ** (-0.5)
low = jnp.bfloat16
full = jnp.float32


def mm(left, right):
    return lax.dot_general(left, right, (((1,), (0,)), ((), ())), preferred_element_type=full)


def mm_nt(left, right):
    return lax.dot_general(left, right, (((1,), (1,)), ((), ())), preferred_element_type=full)


def turn(tensor):
    return tensor.astype(full).T.astype(low)


def lane_ids(shape):
    return lax.broadcasted_iota(jnp.int32, shape, len(shape) - 1)


def row_ids(shape):
    return lax.broadcasted_iota(jnp.int32, shape, len(shape) - 2)


def rotary_partner(tensor):
    lanes = lane_ids(tensor.shape)
    ahead = pltpu.roll(tensor, LANES - HALF, 1)
    behind = pltpu.roll(tensor, HALF, 1)
    return jnp.where(lanes % ROT < HALF, ahead, behind)


def spec_vmem():
    return pl.BlockSpec(memory_space=pltpu.VMEM)


def spec_smem():
    return pl.BlockSpec(memory_space=pltpu.SMEM)


def spec_hbm():
    return pl.BlockSpec(memory_space=pltpu.HBM)


def params(mib):
    return pltpu.CompilerParams(vmem_limit_bytes=mib * MIB)


def shape_of(shape, kind):
    return jax.ShapeDtypeStruct(shape, kind)


def block_tables(inverse, blocks):
    row = row_ids((BLOCK, LANES)).astype(full)
    start = blocks.astype(full) * float(BLOCK)
    return jnp.cos(row * inverse), jnp.sin(row * inverse), jnp.cos(start * inverse), jnp.sin(start * inverse)


def project_kernel(heads, pair_ref, inv_ref, *rest):
    given, rest = rest[:12], rest[12:]
    h1_ref, h2_ref, xhat_ref, std_ref, d_bias_ref, gains_ref, bias_ref, b_up_out_ref, packed = rest[:9]
    held, sems = rest[9:-1], rest[-1]
    copies = [pltpu.make_async_copy(src, dst, sems.at[i]) for i, (src, dst) in enumerate(zip(given, held))]
    for copy in copies:
        copy.start()
    (
        hidden_ref,
        g1_ref,
        c1_ref,
        g2_ref,
        c2_ref,
        cot_ref,
        w_out_ref,
        w_qkv_ref,
        b_qkv_ref,
        b_up_ref,
        b_out_ref,
        b_down_ref,
    ) = held
    rows = hidden_ref.shape[0]
    me = lax.axis_index("ctx")
    pair = pair_ref[me]
    total_blocks = 2 * pair_ref.shape[0]

    first = jnp.where(row_ids((8, LANES)) == 0, pair, total_blocks - 1 - pair)
    inverse = inv_ref[...]
    cos_row, sin_row, cos_block, sin_block = block_tables(inverse, first)
    in_head = lane_ids((BLOCK, LANES)) % HEAD_DIM
    tables = []
    for half in range(2):
        cos_at, sin_at = cos_block[half : half + 1], sin_block[half : half + 1]
        cosine = cos_row * cos_at - sin_row * sin_at
        sine = sin_row * cos_at + cos_row * sin_at
        cosine = jnp.where(in_head < ROT, cosine, 1.0)
        sine = jnp.where(in_head < HALF, -sine, jnp.where(in_head < ROT, sine, 0.0))
        tables.append((cosine, sine))
    cosine = jnp.concatenate([tables[0][0], tables[1][0]], axis=0)
    sine = jnp.concatenate([tables[0][1], tables[1][1]], axis=0)

    for copy in copies[:5]:
        copy.wait()
    x = hidden_ref[...].astype(full)
    centred = x - jnp.mean(x, axis=-1, keepdims=True)
    spread = jnp.mean(centred * centred, axis=-1, keepdims=True)
    inv_std = lax.rsqrt(spread + norm_eps)
    xhat = centred * inv_std
    xhat_ref[...] = xhat
    std_ref[...] = jnp.broadcast_to(inv_std, std_ref.shape)

    def as_row(ref):
        return ref[...].astype(full)[None, :]

    gain1, gain2 = as_row(g1_ref), as_row(g2_ref)
    h1 = (xhat * gain1 + as_row(c1_ref)).astype(low)
    h1_ref[...] = h1
    h2_ref[...] = (xhat * gain2 + as_row(c2_ref)).astype(low)
    gains_ref[0:1] = gain1
    gains_ref[1:2] = gain2
    for copy in copies[5:]:
        copy.wait()
    b_up_out_ref[...] = as_row(b_up_ref)
    bias_ref[0:1] = as_row(b_out_ref)
    bias_ref[1:2] = as_row(b_down_ref)
    d_bias_ref[...] = jnp.sum(cot_ref[...].astype(full), axis=0, keepdims=True)

    lane = lane_ids((rows, LANES))

    def projected(s):
        return mm(h1, w_qkv_ref[s]) + b_qkv_ref[s : s + 1].astype(full)

    def turned(tile):
        return tile * cosine + rotary_partner(tile) * sine

    queries, keys, values = projected(0), projected(1), projected(2)
    grads = mm_nt(cot_ref[...], w_out_ref[...])
    left = lane < HEAD_DIM
    for i in range(heads // 2):
        cut = slice(i * LANES, (i + 1) * LANES)
        q = turned(queries[:, cut]).astype(low).astype(full) * score_scale
        k = turned(keys[:, cut])
        v = values[:, cut]
        g = grads[:, cut]
        packed[2 * i, :, :LANES] = jnp.where(left, g, pltpu.roll(q, HEAD_DIM, 1)).astype(low)
        packed[2 * i, :, LANES:] = jnp.where(left, v, pltpu.roll(k, HEAD_DIM, 1)).astype(low)
        packed[2 * i + 1, :, :LANES] = jnp.where(left, pltpu.roll(g, HEAD_DIM, 1), q).astype(low)
        packed[2 * i + 1, :, LANES:] = jnp.where(left, pltpu.roll(v, HEAD_DIM, 1), k).astype(low)


def project(heads, pair_of, inverse, given):
    hidden, w_out, b_up = given[0], given[6], given[9]
    rows, width = hidden.shape
    outs = [
        shape_of((rows, width), low),
        shape_of((rows, width), low),
        shape_of((rows, width), full),
        shape_of((rows, LANES), full),
        shape_of((1, width), full),
        shape_of((2, width), full),
        shape_of((2, width), full),
        shape_of((1, b_up.shape[0]), full),
        shape_of((heads, rows, 2 * LANES), low),
    ]
    return pl.pallas_call(
        functools.partial(project_kernel, heads),
        out_shape=outs,
        in_specs=[spec_smem(), spec_vmem()] + [spec_hbm()] * len(given),
        out_specs=[spec_vmem()] * len(outs),
        scratch_shapes=[pltpu.VMEM(array.shape, array.dtype) for array in given]
        + [pltpu.SemaphoreType.DMA((len(given),))],
        compiler_params=params(60),
        cost_estimate=pl.CostEstimate(
            flops=2 * rows * width * 4 * w_out.shape[0], bytes_accessed=8 * MIB, transcendentals=0
        ),
        name="project",
    )(pair_of, inverse, *given)


def mlp_kernel(early, ids_ref, *rest):
    given, rest = rest[:6], rest[6:]
    part_ref, back_ref, sums_ref, d_b_up_ref, keep_ref, early_ref, send_ref = rest[:7]
    h2_turned, part_acc, back_acc = rest[7:10]
    held, sems = rest[10:-1], rest[-1]
    copies = [pltpu.make_async_copy(src, dst, sems.at[i]) for i, (src, dst) in enumerate(zip(given, held))]
    h2_held, w_up_ref, b_up, cot_ref, w_down_ref, xhat_ref = held
    step = pl.program_id(0)
    steps = pl.num_programs(0)

    @pl.when(step == 0)
    def _():
        for copy in copies:
            copy.start()
        part_acc[...] = jnp.zeros_like(part_acc)
        back_acc[...] = jnp.zeros_like(back_acc)
        copies[0].wait()
        h2_turned[...] = turn(h2_held[...])
        for copy in copies[1:3]:
            copy.wait()

    at = [pl.multiple_of(ids_ref[b * steps + step] * LANES, LANES) for b in range(2)]
    w_up = jnp.concatenate([w_up_ref[:, pl.ds(i, LANES)] for i in at], axis=1)
    u = mm(h2_held[...], w_up) + jnp.concatenate([b_up[:, pl.ds(i, LANES)] for i in at], axis=1)

    @pl.when(step == 0)
    def _():
        for copy in copies[3:5]:
            copy.wait()

    cot = cot_ref[...]
    w_down = jnp.concatenate([w_down_ref[pl.ds(i, LANES), :] for i in at], axis=0)
    cdf = 0.5 * (1.0 + lax.erf(u * np.float32(np.sqrt(0.5))))
    active = u * cdf
    active_low = active.astype(low)
    slope = cdf + u * jnp.exp(-0.5 * u * u) * np.float32(1.0 / np.sqrt(2.0 * np.pi))
    du = (mm_nt(cot, w_down) * slope).astype(low)
    part_acc[...] += mm(active_low, w_down)
    back_acc[...] += mm_nt(du, w_up)
    d_b_up = jnp.sum(du.astype(full), axis=0, keepdims=True)
    up = mm(h2_turned[...], du).astype(low)
    down = mm(active.T.astype(low), cot).astype(low)
    depth = up.shape[0]

    def put(b, grad_ref):
        grad_ref[:depth] = up[:, b * LANES : (b + 1) * LANES]
        for t in range(down.shape[1] // LANES):
            grad_ref[depth + t * LANES : depth + (t + 1) * LANES] = down[
                b * LANES : (b + 1) * LANES, t * LANES : (t + 1) * LANES
            ]

    for b in range(2):
        d_b_up_ref[:, pl.ds(at[b], LANES)] = d_b_up[:, b * LANES : (b + 1) * LANES]
    put(0, keep_ref)

    @pl.when(step < early)
    def _():
        put(1, early_ref)

    @pl.when(step >= early)
    def _():
        put(1, send_ref)

    @pl.when(step == steps - 1)
    def _():
        copies[5].wait()
        part_ref[...] = part_acc[...]
        back = back_acc[...]
        back_ref[...] = back.astype(low)
        sums_ref[0:1] = jnp.sum(back * xhat_ref[...], axis=0, keepdims=True)
        sums_ref[1:2] = jnp.sum(back, axis=0, keepdims=True)


def mlp(ids, early, *given):
    rows, width = given[0].shape
    hidden_units = given[1].shape[1]
    steps = hidden_units // LANES // 2
    whole = lambda shape: pl.BlockSpec(shape, lambda f, c: (0,) * len(shape))
    grads = lambda at: pl.BlockSpec((2 * width, LANES), lambda f, c: (at(f), 0))
    outs = [
        shape_of((rows, width), full),
        shape_of((rows, width), low),
        shape_of((2, width), full),
        shape_of((1, hidden_units), full),
        shape_of((steps * 2 * width, LANES), low),
        shape_of((early * 2 * width, LANES), low),
        shape_of(((steps - early) * 2 * width, LANES), low),
    ]
    return pl.pallas_call(
        functools.partial(mlp_kernel, early),
        grid_spec=pltpu.PrefetchScalarGridSpec(
            num_scalar_prefetch=1,
            grid=(steps,),
            in_specs=[spec_hbm()] * len(given),
            out_specs=[whole(array.shape) for array in outs[:4]]
            + [
                grads(lambda f: f),
                grads(lambda f: jnp.minimum(f, early - 1)),
                grads(lambda f: jnp.maximum(f - early, 0)),
            ],
            scratch_shapes=[
                pltpu.VMEM((width, rows), low),
                pltpu.VMEM((rows, width), full),
                pltpu.VMEM((rows, width), full),
            ]
            + [pltpu.VMEM(array.shape, array.dtype) for array in given]
            + [pltpu.SemaphoreType.DMA((len(given),))],
        ),
        out_shape=outs,
        compiler_params=params(60),
        cost_estimate=pl.CostEstimate(
            flops=12 * rows * width * hidden_units, bytes_accessed=20 * MIB, transcendentals=0
        ),
        name="feed_forward",
    )(ids, *given)


def attention_kernel(heads, group, places, is_first, is_last, pair_ref, inv_ref, token_ref, *rest):
    del token_ref
    if is_first:
        got_ref, rest = rest[0], rest[1:]
        if group > 1:
            other_ref, rest = rest[0], rest[1:]
    else:
        rest = rest[4:]
    out_ref, rest = rest[0], rest[1:]
    if is_last:
        d_own_ref, rest = rest[0], rest[1:]
        if group > 1:
            d_other_ref, rest = rest[0], rest[1:]
    (values_keys, turned_keys, sums, queries), rest = rest[:4], rest[4:]
    token_out, rest = rest[0], rest[1:]
    weights_in, weights_out, stored, peaks, totals, weighted, finals, block_cos, block_sin = rest
    token_out[...] = jnp.zeros_like(token_out)

    rows = queries.shape[1]
    owners = pair_ref.shape[0]
    total_blocks = 2 * owners
    per_chunk = KEYS // BLOCK
    tasks = (total_blocks + 1 + per_chunk - 1) // per_chunk
    me = lax.axis_index("ctx")
    own_sub = lax.rem(me, group)

    def blocks_of(r, d):
        owner = r * group + lax.rem(own_sub + d, group)
        pair = pair_ref[owner]
        return pair, total_blocks - 1 - pair

    def place(tile, block):
        at = pl.multiple_of(block * BLOCK, BLOCK)
        values_keys[pl.ds(at, BLOCK), :] = tile
        turned_keys[:, pl.ds(at, BLOCK)] = turn(tile)

    if is_first:
        for r in range(heads):
            queries[r] = got_ref[r, :, :LANES]
            for half, block in enumerate(blocks_of(r, 0)):
                place(got_ref[r, half * BLOCK : (half + 1) * BLOCK, LANES:], block)
            for d in range(1, group):
                for half, block in enumerate(blocks_of(r, d)):
                    at = r * rows + half * BLOCK
                    place(other_ref[d - 1, at : at + BLOCK, :], block)
        sums[...] = jnp.zeros_like(sums)

    lane = lane_ids((BLOCK, LANES))
    left = lane < HEAD_DIM
    in_key = lane - HEAD_DIM
    moving = (in_key >= 0) & (in_key < ROT)
    forward = (in_key >= 0) & (in_key < HALF)
    cos_row, sin_row, block_cos[...], block_sin[...] = block_tables(inv_ref[...], row_ids(block_cos.shape))

    def rotated_back(tile, block):
        cos_at, sin_at = block_cos[pl.ds(block, 1), :], block_sin[pl.ds(block, 1), :]
        cosine = jnp.where(moving, cos_row * cos_at - sin_row * sin_at, 1.0)
        sine = sin_row * cos_at + cos_row * sin_at
        sine = jnp.where(moving, jnp.where(forward, sine, -sine), 0.0)
        return tile * cosine + rotary_partner(tile) * sine

    offset = row_ids((BLOCK, BLOCK)) - lane_ids((BLOCK, BLOCK))

    def one_pair(i, carry):
        blocks = blocks_of(places[0] + i, 0)
        first = blocks[0] // per_chunk + 1
        for half in range(2):
            both = queries[places[0] + i, half * BLOCK : (half + 1) * BLOCK, :]
            both_turned = turn(both)
            upper = row_ids((LANES, BLOCK)) < HEAD_DIM
            zero = jnp.zeros_like(both_turned)
            weights_in[half, :, :BLOCK] = jnp.where(upper, both_turned, zero)
            weights_in[half, :, BLOCK:] = jnp.where(upper, zero, both_turned)
            weights_out[half, :BLOCK, :] = jnp.where(left, both, zero)
            weights_out[half, BLOCK:, :] = jnp.where(left, zero, both)
        finals[...] = jnp.zeros_like(finals)

        def task(t):
            is_low = t < first
            chunk = jnp.where(is_low, first - 1 - t, t - first)
            return is_low, chunk

        runs = KEYS // BLOCK
        for t in range(tasks):
            is_low, chunk = task(t)
            weights = weights_in[jnp.where(is_low, 0, 1)]
            for u in range(runs):
                at = pl.multiple_of(chunk * KEYS + u * BLOCK, BLOCK)
                sub = slice(u * BLOCK, (u + 1) * BLOCK)
                both = mm(values_keys[pl.ds(at, BLOCK), :], weights)
                grads = both[:, :BLOCK]
                scores = both[:, BLOCK:]
                if t in (0, tasks - 1):
                    query_at = blocks[0 if t == 0 else 1] * BLOCK
                    scores = jnp.where(offset <= query_at - at, scores, masked_score)
                peak = jnp.max(scores, axis=0, keepdims=True)
                raised = jnp.exp(scores - peak)
                stored[t, sub, :BLOCK] = raised
                stored[t, sub, BLOCK:] = grads
                line = t * runs + u
                peaks[line : line + 1] = peak
                totals[line : line + 1] = jnp.sum(raised, axis=0, keepdims=True)
                weighted[line : line + 1] = jnp.sum(raised * grads, axis=0, keepdims=True)

        in_low = row_ids((tasks * runs, BLOCK)) < first * runs

        def finish(mine):
            top = jnp.max(jnp.where(mine, peaks[...], masked_score), axis=0, keepdims=True)
            factor = jnp.where(mine, jnp.exp(peaks[...] - top), 0.0)
            inverse = 1.0 / jnp.sum(totals[...] * factor, axis=0, keepdims=True)
            return factor * inverse, jnp.sum(weighted[...] * factor, axis=0, keepdims=True) * inverse

        (low_factor, low_delta), (high_factor, high_delta) = finish(in_low), finish(jnp.logical_not(in_low))
        peaks[...] = low_factor + high_factor

        for t in range(tasks):
            is_low, chunk = task(t)
            half = jnp.where(is_low, 0, 1)
            weights = weights_out[half]
            delta = jnp.where(is_low, low_delta, high_delta)
            parts = []
            for u in range(runs):
                sub = slice(u * BLOCK, (u + 1) * BLOCK)
                probs = stored[t, sub, :BLOCK] * peaks[t * runs + u : t * runs + u + 1]
                d_scores = probs * (stored[t, sub, BLOCK:] - delta)
                both = jnp.concatenate([probs, d_scores], axis=1).astype(low)
                at = pl.multiple_of(chunk * KEYS + u * BLOCK, BLOCK)
                sums[pl.ds(at, BLOCK), :] += mm(both, weights)
                parts.append(both)
            at = pl.multiple_of(chunk * KEYS, KEYS)
            finals[half] += mm(turned_keys[:, pl.ds(at, KEYS)], jnp.concatenate(parts, axis=0))

        for half in range(2):
            both = jnp.concatenate(
                [finals[half, :HEAD_DIM, :BLOCK], finals[half, HEAD_DIM:, BLOCK:] * score_scale], axis=0
            ).T
            out_ref[i, half * BLOCK : (half + 1) * BLOCK, :] = rotated_back(both, blocks[half]).astype(low)
        return carry

    lax.fori_loop(0, len(places), one_pair, 0)

    if is_last:
        for r in range(heads):
            for d in range(group):
                for half, block in enumerate(blocks_of(r, d)):
                    at = r * rows + half * BLOCK
                    tile = rotated_back(sums[pl.ds(pl.multiple_of(block * BLOCK, BLOCK), BLOCK), :], block)
                    if d == 0:
                        d_own_ref[at : at + BLOCK, :] = tile
                    else:
                        d_other_ref[d - 1, at : at + BLOCK, :] = tile


def attention(heads, group, places, pair_of, inverse, token, got, other, state):
    is_first, is_last = state is None, places[-1] == heads - 1
    rows = got.shape[1]
    owners = pair_of.shape[0]
    total_keys = owners * rows
    tasks = (2 * owners + KEYS // BLOCK) // (KEYS // BLOCK)
    operands = [pair_of, inverse, token]
    outs = [shape_of((len(places), rows, LANES), low)]
    if is_first:
        operands += [got] if other is None else [got, other]
    else:
        operands += list(state)
    if is_last:
        outs.append(shape_of((heads * rows, LANES), full))
        if group > 1:
            outs.append(shape_of((group - 1, heads * rows, LANES), full))
    kept = [
        shape_of((total_keys, LANES), low),
        shape_of((LANES, total_keys), low),
        shape_of((total_keys, LANES), full),
        shape_of((heads, rows, LANES), low),
    ]
    aliases = {} if is_first else {len(operands) - 4 + i: len(outs) + i for i in range(4)}
    found = pl.pallas_call(
        functools.partial(attention_kernel, heads, group, places, is_first, is_last),
        out_shape=outs + kept + [shape_of((1, LANES), full)],
        in_specs=[spec_smem()] + [spec_vmem()] * (len(operands) - 1),
        out_specs=[spec_vmem()] * (len(outs) + 5),
        input_output_aliases=aliases,
        scratch_shapes=[
            pltpu.VMEM((2, LANES, 2 * BLOCK), low),
            pltpu.VMEM((2, 2 * BLOCK, LANES), low),
            pltpu.VMEM((tasks, KEYS, 2 * BLOCK), full),
            pltpu.VMEM((tasks * KEYS // BLOCK, BLOCK), full),
            pltpu.VMEM((tasks * KEYS // BLOCK, BLOCK), full),
            pltpu.VMEM((tasks * KEYS // BLOCK, BLOCK), full),
            pltpu.VMEM((2, LANES, 2 * BLOCK), full),
            pltpu.VMEM((2 * owners, LANES), full),
            pltpu.VMEM((2 * owners, LANES), full),
        ],
        compiler_params=params(6 + total_keys * 5 * 256 // MIB),
        cost_estimate=pl.CostEstimate(
            flops=2_500_000_000 * len(places), bytes_accessed=2 * MIB, transcendentals=0
        ),
        name="attention",
    )(*operands)
    return found[0], found[1 : len(outs)], found[len(outs) : len(outs) + 4], found[-1]


def combine_kernel(heads, terms, *refs):
    out_ref = refs[-1]
    rows = out_ref.shape[1]
    for r in range(heads):
        cut = slice(r * rows, (r + 1) * rows)
        total = refs[0][cut, :]
        for term in refs[1:terms]:
            total = total + term[cut, :]
        out_ref[r, :, LANES:] = total.astype(low)
    at = 0
    for first_ref in refs[terms:-1]:
        out_ref[at : at + first_ref.shape[0], :, :LANES] = first_ref[...]
        at += first_ref.shape[0]


def combine(heads, terms, firsts):
    rows = firsts[0].shape[1]
    return pl.pallas_call(
        functools.partial(combine_kernel, heads, len(terms)),
        out_shape=shape_of((heads, rows, 2 * LANES), low),
        in_specs=[spec_vmem()] * (len(firsts) + len(terms)),
        out_specs=spec_vmem(),
        compiler_params=params(24),
        cost_estimate=pl.CostEstimate(flops=10**7, bytes_accessed=3 * MIB, transcendentals=0),
        name="combine",
    )(*terms, *firsts)


def weight_grads_kernel(
    heads, early, ids_ref, got_ref, h1_ref, cot_ref, low_ref, d_b_ref, keep_ref, early_ref, send_ref, token_ref, grads
):
    chips, chunk_rows = keep_ref.shape[:2]

    def put(at, tile):
        step = min(chunk_rows, tile.shape[0])
        for off in range(0, tile.shape[0], step):
            chunk, inside = divmod(at + off, chunk_rows)
            grads[chunk, inside : inside + step] = tile[off : off + step]

    rows = h1_ref.shape[0]
    left = lane_ids((rows, LANES)) < HEAD_DIM
    for i in range(heads // 2):
        cut = slice(i * LANES, (i + 1) * LANES)
        for first, second, half in ((0, 1, slice(0, LANES)), (3, 2, slice(LANES, 2 * LANES))):
            a, b = got_ref[2 * i, :, half].astype(full), got_ref[2 * i + 1, :, half].astype(full)
            low_ref[first, :, cut] = jnp.where(left, a, pltpu.roll(b, HEAD_DIM, 1)).astype(low)
            low_ref[second, :, cut] = jnp.where(left, pltpu.roll(a, HEAD_DIM, 1), b).astype(low)
    h1_turned = turn(h1_ref[...])
    depth, tiles = h1_turned.shape[0], heads // 2
    for s in range(3):
        d_proj = low_ref[1 + s]
        d_b_ref[s : s + 1] = jnp.sum(d_proj.astype(full), axis=0, keepdims=True)
        grad = mm(h1_turned, d_proj).astype(low)
        for t in range(tiles):
            put((s * tiles + t) * depth, grad[:, t * LANES : (t + 1) * LANES])
    grad = mm(turn(low_ref[0]), cot_ref[...]).astype(low)
    height = grad.shape[0]
    for t in range(depth // LANES):
        put(3 * tiles * depth + t * height, grad[:, t * LANES : (t + 1) * LANES])
    for t in range(chips):
        target = early_ref.at[t] if t < early else send_ref.at[t - early]
        target[...] = grads[ids_ref[chips + t]]
        keep_ref[t] = grads[ids_ref[t]]
    token_ref[...] = jnp.zeros_like(token_ref)


def weight_grads(heads, early, ids, got, h1, cot):
    rows, width = h1.shape
    local_width = heads * HEAD_DIM
    chips = ids.shape[0] // 2
    chunk_rows = 4 * width * local_width // LANES // (2 * chips)
    outs = [
        shape_of((4, rows, local_width), low),
        shape_of((3, local_width), full),
        shape_of((chips, chunk_rows, LANES), low),
        shape_of((early, chunk_rows, LANES), low),
        shape_of((chips - early, chunk_rows, LANES), low),
        shape_of((1, LANES), full),
    ]
    return pl.pallas_call(
        functools.partial(weight_grads_kernel, heads, early),
        out_shape=outs,
        in_specs=[spec_smem()] + [spec_vmem()] * 3,
        out_specs=[spec_vmem()] * len(outs),
        scratch_shapes=[pltpu.VMEM((2 * chips, chunk_rows, LANES), low)],
        compiler_params=params(20),
        cost_estimate=pl.CostEstimate(
            flops=8 * rows * width * local_width, bytes_accessed=8 * MIB, transcendentals=0
        ),
        name="weight_grads",
    )(ids, got, h1, cot)


def return_kernel(low_ref, part_ref, w_out_ref, w_qkv_ref, xhat_ref, e2_ref, both_ref, sums_ref):
    rows = xhat_ref.shape[0]
    both_ref[:rows] = (part_ref[...] + mm(low_ref[0], w_out_ref[...])).astype(low)
    back = mm_nt(low_ref[1], w_qkv_ref[0]) + mm_nt(low_ref[2], w_qkv_ref[1]) + mm_nt(low_ref[3], w_qkv_ref[2])
    both_ref[rows : 2 * rows] = back.astype(low)
    both_ref[2 * rows :] = e2_ref[...]
    sums_ref[0:1] = jnp.sum(back * xhat_ref[...], axis=0, keepdims=True)
    sums_ref[1:2] = jnp.sum(back, axis=0, keepdims=True)


def back_projections(*given):
    rows, width = given[1].shape
    return pl.pallas_call(
        return_kernel,
        out_shape=[shape_of((3 * rows, width), low), shape_of((2, width), full)],
        in_specs=[spec_vmem()] * len(given),
        out_specs=[spec_vmem()] * 2,
        compiler_params=params(16),
        cost_estimate=pl.CostEstimate(
            flops=8 * rows * width * given[2].shape[0], bytes_accessed=8 * MIB, transcendentals=0
        ),
        name="back_projections",
    )(*given)


def finish_kernel(
    hidden_ref, cot_ref, xhat_ref, std_ref, gains_ref, bias_ref, ours_ref, theirs_ref, out_ref, grad_ref, token_ref
):
    rows = hidden_ref.shape[0]
    gains = gains_ref[...]
    biases = bias_ref[...]
    summed = ours_ref[:rows].astype(full) + theirs_ref[:rows].astype(full)
    out_ref[...] = (hidden_ref[...].astype(full) + summed + biases[0:1] + biases[1:2]).astype(low)
    e1 = ours_ref[rows : 2 * rows].astype(full) + theirs_ref[rows : 2 * rows].astype(full)
    e2 = ours_ref[2 * rows :].astype(full) + theirs_ref[2 * rows :].astype(full)
    f = e1 * gains[0:1] + e2 * gains[1:2]
    xhat = xhat_ref[...]
    inv_std = std_ref[:, 0:1]
    grad_ref[...] = cot_ref[...].astype(full) + inv_std * (
        f - jnp.mean(f, axis=-1, keepdims=True) - xhat * jnp.mean(f * xhat, axis=-1, keepdims=True)
    )
    token_ref[...] = jnp.zeros_like(token_ref)


def finish(*operands):
    rows, width = operands[0].shape
    return pl.pallas_call(
        finish_kernel,
        out_shape=[shape_of((rows, width), low), shape_of((rows, width), full), shape_of((1, LANES), full)],
        in_specs=[spec_vmem()] * len(operands),
        out_specs=[spec_vmem()] * 3,
        compiler_params=params(24),
        cost_estimate=pl.CostEstimate(flops=10**7, bytes_accessed=8 * MIB, transcendentals=0),
        name="finish",
    )(*operands)


def to_attention(width, local_width, source, refs, base, unit):
    qkv_ref, out_ref = refs
    tiles = local_width // LANES
    split = 3 * tiles * width
    tile = base // width
    row = pl.multiple_of(lax.rem(base, width), unit)
    column = pl.multiple_of(lax.rem(tile, tiles) * LANES, LANES)
    yield base < split, source, qkv_ref.at[jnp.minimum(tile // tiles, 2), pl.ds(row, unit), pl.ds(column, LANES)]
    after = jnp.maximum(base - split, 0)
    row = pl.multiple_of(lax.rem(after, local_width), unit)
    column = pl.multiple_of(after // local_width * LANES, LANES)
    yield base >= split, source, out_ref.at[pl.ds(row, unit), pl.ds(column, LANES)]


def to_mlp(width, source, refs, base, unit):
    up_ref, down_ref = refs
    block, inside = base // (2 * width), lax.rem(base, 2 * width)
    block_at = pl.multiple_of(block * LANES, LANES)
    row = pl.multiple_of(jnp.minimum(inside, width - unit), unit)
    yield inside < width, source, up_ref.at[pl.ds(row, unit), pl.ds(block_at, LANES)]
    for t in range(unit // LANES):
        column = pl.multiple_of(jnp.maximum(inside - width, 0) + t * LANES, LANES)
        cut = source.at[pl.ds(t * LANES, LANES), :]
        yield inside >= width, cut, down_ref.at[pl.ds(block_at, LANES), pl.ds(column, LANES)]


def unpack_kernel(route, count, unit, has_old, ids_ref, *rest):
    parts, rest = rest[:count], rest[count:]
    rest = rest[2:] if has_old else rest
    targets, (token_ref, held, sems) = rest[:2], rest[2:]
    token_ref[...] = jnp.zeros_like(token_ref)
    chunk_rows = parts[0].shape[0]
    units = chunk_rows // unit
    per_unit = sems.shape[0] // (count * units)

    def moves():
        for i in range(count):
            for j in range(units):
                source = held.at[i, pl.ds(j * unit, unit), :]
                base = ids_ref[i] * chunk_rows + j * unit
                for n, (applies, piece, target) in enumerate(route(source, targets, base, unit)):
                    sem = sems.at[(i * units + j) * per_unit + n]
                    yield i, applies, pltpu.make_async_copy(piece, target, sem)

    done = -1
    for i, applies, copy in moves():
        if i != done:
            held[i] = parts[i][...].astype(full)
            done = i
        pl.when(applies)(copy.start)
    for i, applies, copy in moves():
        pl.when(applies)(copy.wait)


def unpack(name, route, cases, unit, shapes, ids, parts, old):
    count = len(parts)
    chunk_rows = parts[0].shape[0]
    operands = [ids, *parts, *(old or ())]
    return pl.pallas_call(
        functools.partial(unpack_kernel, route, count, unit, old is not None),
        out_shape=[shape_of(shape, full) for shape in shapes] + [shape_of((1, LANES), full)],
        in_specs=[spec_smem()] + [spec_vmem()] * count + [spec_hbm()] * (len(operands) - 1 - count),
        out_specs=[spec_hbm()] * 2 + [spec_vmem()],
        input_output_aliases={} if old is None else {1 + count: 0, 2 + count: 1},
        scratch_shapes=[
            pltpu.VMEM((count, chunk_rows, LANES), full),
            pltpu.SemaphoreType.DMA((count * (chunk_rows // unit) * cases,)),
        ],
        compiler_params=params(8 + count * chunk_rows * 3 * LANES * 2 // MIB),
        cost_estimate=pl.CostEstimate(
            flops=10**6, bytes_accessed=count * chunk_rows * LANES * 6, transcendentals=0
        ),
        name=name,
    )(*operands)


def local(
    hidden,
    pair_of,
    ln1_gain,
    ln1_bias,
    ln2_gain,
    ln2_bias,
    w_qkv,
    b_qkv,
    w_out,
    b_out,
    w_up,
    b_up,
    w_down,
    b_down,
    cotangent,
):
    owners = lax.axis_size("ctx")
    sides = lax.axis_size("tp")
    rows, width = hidden.shape
    local_width = w_qkv.shape[2]
    hidden_units = w_up.shape[1]
    heads = local_width // HEAD_DIM
    group = owners // heads

    exponent = np.arange(0, ROT, 2, dtype=np.float32) / np.float32(ROT)
    inverse = jnp.asarray(np.tile(np.float32(10000.0) ** (-exponent), LANES // HALF)[None, :], full)
    order = (0, 2, 4, 6, 7, 5, 3, 1) if owners == 16 else tuple(range(owners // 2))
    chips = len(order)

    def to_heads(array):
        groups = [[h * group + g for h in range(heads)] for g in range(group)]
        return lax.all_to_all(array, "ctx", 0, 0, axis_index_groups=groups, tiled=True)

    def group_shift(array, d):
        pairs = [(c, c // group * group + (c % group + d) % group) for c in range(owners)]
        return lax.ppermute(array, "ctx", pairs)

    me = lax.axis_index("ctx")
    chip, core = me // 2, lax.rem(me, 2)
    place = sum(jnp.where(chip == c, i, 0) for i, c in enumerate(order))
    way = 1 - 2 * core
    far, near = chips // 2, chips - 1 - chips // 2

    def ring(array, forward):
        pairs = []
        for i, c in enumerate(order):
            for k in range(2):
                step = 1 if (k == 0) == forward else -1
                pairs.append((2 * c + k, 2 * order[(i + step) % chips] + k))
        return lax.ppermute(array, "ctx", pairs)

    def other_core(array):
        return lax.ppermute(array, "ctx", [(c, c ^ 1) for c in range(owners)])

    def across(array):
        return lax.ppermute(array, "tp", [(t, (t + 1) % sides) for t in range(sides)])

    def target(distance):
        return lax.rem(place + way * distance + chips, chips)

    def zero(array):
        return array[:1].astype(full) * 0.0

    slots = [far, -near]
    for t in range(1, far):
        slots += [far - t] if t >= near else [far - t, t - near]
    slots.append(0)
    early = 2
    slot_ids = jnp.stack(
        [core * chips + target(d) for d in slots] + [(1 - core) * chips + target(-d) for d in slots]
    )

    def terms_of(keep, came):
        def term(i):
            return keep[i].astype(full) + came[i].astype(full)

        return {d: term(i) for i, d in enumerate(slots)}

    def scatter_start(terms, token):
        return (terms[far] + token).astype(low), (terms[-near] + token).astype(low)

    def scatter_step(terms, t, sends, token):
        long_send, short_send = sends
        long_got = ring(long_send, True).astype(full) + token
        last = t == far - 1
        long_next = long_got if last else (long_got + terms[far - 1 - t]).astype(low)
        short_next = short_send
        if t < near:
            short_got = ring(short_send, False).astype(full) + token
            short_next = short_got if t == near - 1 else (short_got + terms[t + 1 - near]).astype(low)
        if last:
            return (terms[0] + long_next + short_next).astype(low)
        return long_next, short_next

    base, other_base = core * chips, (1 - core) * chips

    def gather_start(own):
        return [(own, base + place), (other_core(own), other_base + place)]

    def gather_step(t, sends, token):
        long_send, short_send = sends
        if token is not None:
            long_send = (long_send.astype(full) + token).astype(low)
        long_got = ring(long_send, True)
        found = [(long_got, base + target(-t - 1)), (other_core(long_got), other_base + target(t + 1))]
        short_got = short_send
        if t < near:
            short_got = ring(short_send, False)
            found += [(short_got, base + target(t + 1)), (other_core(short_got), other_base + target(-t - 1))]
        return (long_got, short_got), found

    blocks = hidden_units // LANES // 2
    in_slots = blocks == chips
    mlp_ids = slot_ids if in_slots else jnp.concatenate(
        [core * blocks + jnp.arange(blocks), (1 - core) * blocks + jnp.arange(blocks)]
    )
    h1, h2, xhat, inv_std, d_bias, gains, biases, b_up_row, packed = project(
        heads,
        pair_of,
        inverse,
        (hidden, ln1_gain, ln1_bias, ln2_gain, ln2_bias, cotangent, w_out, w_qkv, b_qkv, b_up, b_out, b_down),
    )
    got = to_heads(packed)
    part, back2, sums2, d_b_up, keep_mlp, early_mlp, send_mlp = mlp(
        mlp_ids.astype(jnp.int32), early, h2, w_up, b_up_row, cotangent, w_down, xhat
    )
    chunk = keep_mlp.shape[0] // chips
    came_mlp = jnp.concatenate([other_core(early_mlp), other_core(send_mlp)]) if not in_slots else None
    if in_slots:
        halves = [other_core(array).reshape(-1, chunk, LANES) for array in (early_mlp, send_mlp)]
        came_mlp = [half[i] for half in halves for i in range(half.shape[0])]
        terms_mlp = terms_of(keep_mlp.reshape(chips, chunk, LANES), came_mlp)
    else:
        summed = (keep_mlp.astype(full) + came_mlp.astype(full)).reshape(chips, chunk, LANES)
        terms_mlp = {d: lax.dynamic_index_in_dim(summed, target(d), 0, keepdims=False) for d in slots}
    nothing = jnp.zeros((1, LANES), full)

    other = None
    if group > 1:
        mine = got[:, :, LANES:].reshape(heads * rows, LANES)
        other = jnp.stack([group_shift(mine, group - d) for d in range(1, group)])

    middle = heads // 4
    first, _, state, token = attention(
        heads, group, tuple(range(middle)), pair_of, inverse, sums2, got, other, None
    )
    sends_mlp = scatter_start(terms_mlp, token)
    token = zero(sends_mlp[0]) + zero(sends_mlp[1])
    second, ends, _, token = attention(
        heads, group, tuple(range(middle, heads)), pair_of, inverse, token, got, other, state
    )
    d_own, d_other = ends[0], (ends[1] if group > 1 else None)
    terms = [d_own] + [group_shift(d_other[d - 1], d) for d in range(1, group)]
    sends_mlp = scatter_step(terms_mlp, 0, sends_mlp, token)
    first = (first.astype(full) + zero(sends_mlp[0]) + zero(sends_mlp[1])).astype(low)
    backs = to_heads(combine(heads, terms, [first, second]))
    sends_mlp = scatter_step(terms_mlp, 1, sends_mlp, nothing)
    h1_later = (h1.astype(full) + (zero(sends_mlp[0]) + zero(sends_mlp[1]))[:, :1]).astype(low)

    lows, d_b_qkv, keep, early_att, send_att, after = weight_grads(
        heads, early, slot_ids.astype(jnp.int32), backs, h1_later, cotangent
    )
    both, sums1 = back_projections(lows, part, w_out, w_qkv, xhat, back2)
    theirs = across(both)
    output, d_hidden, finish_token = finish(
        hidden, cotangent, xhat, inv_std, gains, biases, both, theirs
    )
    halves = [other_core(array) for array in (early_att, send_att)]
    terms_att = terms_of(keep, [half[i] for half in halves for i in range(half.shape[0])])

    small = jnp.concatenate(
        [sums1.reshape(1, -1), sums2.reshape(1, -1), d_bias, d_b_up, d_b_qkv.reshape(1, -1)], axis=1
    )

    def unpack_some(name, route, cases, unit, shapes, found, old):
        parts, ids = zip(*found)
        *old, token = unpack(name, route, cases, unit, shapes, jnp.stack(ids), parts, old)
        return old, token

    unit_mlp = min(chunk, local_width)
    unit_att = min(keep.shape[1], local_width)
    unpack_mlp = functools.partial(
        unpack_some,
        "unpack_feed_forward",
        functools.partial(to_mlp, width),
        1 + unit_mlp // LANES,
        unit_mlp,
        ((width, hidden_units), (hidden_units, width)),
    )
    unpack_att = functools.partial(
        unpack_some,
        "unpack_attention",
        functools.partial(to_attention, width, local_width),
        2,
        unit_att,
        ((3, width, local_width), (local_width, width)),
    )

    steps_mlp, steps_round = iter(range(2, far)), iter(range(far))
    own_mlp, round_mlp, waiting, grads_mlp = None, None, [], None

    def advance_mlp(token):
        nonlocal sends_mlp, own_mlp, round_mlp, waiting
        t = next(steps_mlp, None)
        if t is not None:
            sends_mlp = scatter_step(terms_mlp, t, sends_mlp, token)
            if t < far - 1:
                return zero(sends_mlp[0])
            own_mlp, round_mlp = sends_mlp, (sends_mlp, sends_mlp)
            waiting += gather_start(own_mlp)
            return zero(own_mlp)
        t = next(steps_round, None)
        if t is None:
            return nothing
        round_mlp, found = gather_step(t, round_mlp, None)
        waiting += found
        return zero(round_mlp[0])

    sends_att = scatter_start(terms_att, nothing)
    before = nothing
    for t in range(far):
        later = advance_mlp(after)
        sends_att = scatter_step(terms_att, t, sends_att, before)
        before = later
    round_att, waiting_att, grads_att = (sends_att, sends_att), gather_start(sends_att), None
    distance = 1
    for t in range(far):
        ready, waiting = waiting, []
        later = advance_mlp(after)
        round_att, found = gather_step(t, round_att, before if t > 0 else None)
        if distance < owners:
            small = small + zero(round_att[0])[:, :1]
            small = small + lax.ppermute(small, "ctx", [(c, c ^ distance) for c in range(owners)])
            distance *= 2
        before = later + zero(small)[:, :LANES]
        if ready:
            grads_mlp, more = unpack_mlp(ready, grads_mlp)
            before = before + more
        if t == 0:
            before = before + finish_token
        waiting_att += found
        if t == far - 2:
            grads_att, more = unpack_att(waiting_att[:-4], None)
            waiting_att = waiting_att[-4:]
            before = before + more
    while distance < owners:
        small = small + lax.ppermute(small, "ctx", [(c, c ^ distance) for c in range(owners)])
        distance *= 2
    if waiting:
        grads_mlp, _ = unpack_mlp(waiting, grads_mlp)
    grads_att, _ = unpack_att(waiting_att, grads_att)

    norm_sums = small[:, : 4 * width]
    norm_sums = (norm_sums + across(norm_sums)).reshape(4, width)
    at = 4 * width
    d_bias = small[0, at : at + width]
    d_b_up = small[0, at + width : at + width + hidden_units]
    d_b_qkv = small[0, at + width + hidden_units :].reshape(3, local_width)
    d_w_up, d_w_down = grads_mlp
    d_w_qkv, d_w_out = grads_att
    return (
        output,
        d_hidden,
        norm_sums[0],
        norm_sums[1],
        norm_sums[2],
        norm_sums[3],
        d_w_qkv,
        d_b_qkv,
        d_w_out,
        d_bias,
        d_w_up,
        d_b_up,
        d_w_down,
        d_bias,
    )


def solution(mesh):
    placed = (
        P("ctx", None),
        P(),
        P(),
        P(),
        P(),
        P(),
        P(None, None, "tp"),
        P(None, "tp"),
        P("tp", None),
        P(),
        P(None, "tp"),
        P("tp"),
        P("tp", None),
        P(),
        P("ctx", None),
    )
    return jax.shard_map(
        local,
        mesh=mesh,
        in_specs=placed,
        out_specs=(
            P("ctx", None),
            P("ctx", None),
            P(),
            P(),
            P(),
            P(),
            P(None, None, "tp"),
            P(None, "tp"),
            P("tp", None),
            P(),
            P(None, "tp"),
            P("tp"),
            P("tp", None),
            P(),
        ),
        check_vma=False,
    )
```

```python
import functools

import jax
import jax.numpy as jnp
import numpy as np
from jax import lax
from jax.experimental import pallas as pl
from jax.experimental.pallas import tpu as pltpu
from jax.sharding import PartitionSpec as P

HEAD_DIM = 64
ROT = 16
HALF = ROT // 2
BLOCK = 128
LANES = 128
KEYS = 512
MIB = 1 << 20

norm_eps = 1e-05
masked_score = -1e30
score_scale = HEAD_DIM ** (-0.5)
low = jnp.bfloat16
full = jnp.float32


def mm(left, right):
    return lax.dot_general(left, right, (((1,), (0,)), ((), ())), preferred_element_type=full)


def mm_nt(left, right):
    return lax.dot_general(left, right, (((1,), (1,)), ((), ())), preferred_element_type=full)


def turn(tensor):
    return tensor.astype(full).T.astype(low)


def lane_ids(shape):
    return lax.broadcasted_iota(jnp.int32, shape, len(shape) - 1)


def row_ids(shape):
    return lax.broadcasted_iota(jnp.int32, shape, len(shape) - 2)


def rotary_partner(tensor):
    lanes = lane_ids(tensor.shape)
    ahead = pltpu.roll(tensor, LANES - HALF, 1)
    behind = pltpu.roll(tensor, HALF, 1)
    return jnp.where(lanes % ROT < HALF, ahead, behind)


def spec_vmem():
    return pl.BlockSpec(memory_space=pltpu.VMEM)


def spec_smem():
    return pl.BlockSpec(memory_space=pltpu.SMEM)


def spec_hbm():
    return pl.BlockSpec(memory_space=pltpu.HBM)


def params(mib):
    return pltpu.CompilerParams(vmem_limit_bytes=mib * MIB)


def shape_of(shape, kind):
    return jax.ShapeDtypeStruct(shape, kind)


def block_tables(inverse, blocks):
    row = row_ids((BLOCK, LANES)).astype(full)
    start = blocks.astype(full) * float(BLOCK)
    return jnp.cos(row * inverse), jnp.sin(row * inverse), jnp.cos(start * inverse), jnp.sin(start * inverse)


def project_kernel(heads, pair_ref, inv_ref, *rest):
    given, rest = rest[:12], rest[12:]
    h1_ref, h2_ref, xhat_ref, std_ref, d_bias_ref, gains_ref, bias_ref, b_up_out_ref, packed = rest[:9]
    held, sems = rest[9:-1], rest[-1]
    copies = [pltpu.make_async_copy(src, dst, sems.at[i]) for i, (src, dst) in enumerate(zip(given, held))]
    for copy in copies:
        copy.start()
    (
        hidden_ref,
        g1_ref,
        c1_ref,
        g2_ref,
        c2_ref,
        cot_ref,
        w_out_ref,
        w_qkv_ref,
        b_qkv_ref,
        b_up_ref,
        b_out_ref,
        b_down_ref,
    ) = held
    rows = hidden_ref.shape[0]
    me = lax.axis_index("ctx")
    pair = pair_ref[me]
    total_blocks = 2 * pair_ref.shape[0]

    first = jnp.where(row_ids((8, LANES)) == 0, pair, total_blocks - 1 - pair)
    inverse = inv_ref[...]
    cos_row, sin_row, cos_block, sin_block = block_tables(inverse, first)
    in_head = lane_ids((BLOCK, LANES)) % HEAD_DIM
    tables = []
    for half in range(2):
        cos_at, sin_at = cos_block[half : half + 1], sin_block[half : half + 1]
        cosine = cos_row * cos_at - sin_row * sin_at
        sine = sin_row * cos_at + cos_row * sin_at
        cosine = jnp.where(in_head < ROT, cosine, 1.0)
        sine = jnp.where(in_head < HALF, -sine, jnp.where(in_head < ROT, sine, 0.0))
        tables.append((cosine, sine))
    cosine = jnp.concatenate([tables[0][0], tables[1][0]], axis=0)
    sine = jnp.concatenate([tables[0][1], tables[1][1]], axis=0)

    for copy in copies[:5]:
        copy.wait()
    x = hidden_ref[...].astype(full)
    centred = x - jnp.mean(x, axis=-1, keepdims=True)
    spread = jnp.mean(centred * centred, axis=-1, keepdims=True)
    inv_std = lax.rsqrt(spread + norm_eps)
    xhat = centred * inv_std
    xhat_ref[...] = xhat
    std_ref[...] = jnp.broadcast_to(inv_std, std_ref.shape)

    def as_row(ref):
        return ref[...].astype(full)[None, :]

    gain1, gain2 = as_row(g1_ref), as_row(g2_ref)
    h1 = (xhat * gain1 + as_row(c1_ref)).astype(low)
    h1_ref[...] = h1
    h2_ref[...] = (xhat * gain2 + as_row(c2_ref)).astype(low)
    gains_ref[0:1] = gain1
    gains_ref[1:2] = gain2
    for copy in copies[5:]:
        copy.wait()
    b_up_out_ref[...] = as_row(b_up_ref)
    bias_ref[0:1] = as_row(b_out_ref)
    bias_ref[1:2] = as_row(b_down_ref)
    d_bias_ref[...] = jnp.sum(cot_ref[...].astype(full), axis=0, keepdims=True)

    lane = lane_ids((rows, LANES))

    def projected(s):
        return mm(h1, w_qkv_ref[s]) + b_qkv_ref[s : s + 1].astype(full)

    def turned(tile):
        return tile * cosine + rotary_partner(tile) * sine

    queries, keys, values = projected(0), projected(1), projected(2)
    grads = mm_nt(cot_ref[...], w_out_ref[...])
    left = lane < HEAD_DIM
    for i in range(heads // 2):
        cut = slice(i * LANES, (i + 1) * LANES)
        q = turned(queries[:, cut]).astype(low).astype(full) * score_scale
        k = turned(keys[:, cut])
        v = values[:, cut]
        g = grads[:, cut]
        packed[2 * i, :, :LANES] = jnp.where(left, g, pltpu.roll(q, HEAD_DIM, 1)).astype(low)
        packed[2 * i, :, LANES:] = jnp.where(left, v, pltpu.roll(k, HEAD_DIM, 1)).astype(low)
        packed[2 * i + 1, :, :LANES] = jnp.where(left, pltpu.roll(g, HEAD_DIM, 1), q).astype(low)
        packed[2 * i + 1, :, LANES:] = jnp.where(left, pltpu.roll(v, HEAD_DIM, 1), k).astype(low)


def project(heads, pair_of, inverse, given):
    hidden, w_out, b_up = given[0], given[6], given[9]
    rows, width = hidden.shape
    outs = [
        shape_of((rows, width), low),
        shape_of((rows, width), low),
        shape_of((rows, width), full),
        shape_of((rows, LANES), full),
        shape_of((1, width), full),
        shape_of((2, width), full),
        shape_of((2, width), full),
        shape_of((1, b_up.shape[0]), full),
        shape_of((heads, rows, 2 * LANES), low),
    ]
    return pl.pallas_call(
        functools.partial(project_kernel, heads),
        out_shape=outs,
        in_specs=[spec_smem(), spec_vmem()] + [spec_hbm()] * len(given),
        out_specs=[spec_vmem()] * len(outs),
        scratch_shapes=[pltpu.VMEM(array.shape, array.dtype) for array in given]
        + [pltpu.SemaphoreType.DMA((len(given),))],
        compiler_params=params(60),
        cost_estimate=pl.CostEstimate(
            flops=2 * rows * width * 4 * w_out.shape[0], bytes_accessed=8 * MIB, transcendentals=0
        ),
        name="project",
    )(pair_of, inverse, *given)


def mlp_kernel(early, ids_ref, *rest):
    given, rest = rest[:6], rest[6:]
    part_ref, back_ref, sums_ref, d_b_up_ref, keep_ref, early_ref, send_ref = rest[:7]
    h2_turned, part_acc, back_acc = rest[7:10]
    held, sems = rest[10:-1], rest[-1]
    copies = [pltpu.make_async_copy(src, dst, sems.at[i]) for i, (src, dst) in enumerate(zip(given, held))]
    h2_held, w_up_ref, b_up, cot_ref, w_down_ref, xhat_ref = held
    step = pl.program_id(0)
    steps = pl.num_programs(0)

    @pl.when(step == 0)
    def _():
        for copy in copies:
            copy.start()
        part_acc[...] = jnp.zeros_like(part_acc)
        back_acc[...] = jnp.zeros_like(back_acc)
        copies[0].wait()
        h2_turned[...] = turn(h2_held[...])
        for copy in copies[1:3]:
            copy.wait()

    at = [pl.multiple_of(ids_ref[b * steps + step] * LANES, LANES) for b in range(2)]
    w_up = jnp.concatenate([w_up_ref[:, pl.ds(i, LANES)] for i in at], axis=1)
    u = mm(h2_held[...], w_up) + jnp.concatenate([b_up[:, pl.ds(i, LANES)] for i in at], axis=1)

    @pl.when(step == 0)
    def _():
        for copy in copies[3:5]:
            copy.wait()

    cot = cot_ref[...]
    w_down = jnp.concatenate([w_down_ref[pl.ds(i, LANES), :] for i in at], axis=0)
    cdf = 0.5 * (1.0 + lax.erf(u * np.float32(np.sqrt(0.5))))
    active = u * cdf
    active_low = active.astype(low)
    slope = cdf + u * jnp.exp(-0.5 * u * u) * np.float32(1.0 / np.sqrt(2.0 * np.pi))
    du = (mm_nt(cot, w_down) * slope).astype(low)
    part_acc[...] += mm(active_low, w_down)
    back_acc[...] += mm_nt(du, w_up)
    d_b_up = jnp.sum(du.astype(full), axis=0, keepdims=True)
    up = mm(h2_turned[...], du).astype(low)
    down = mm(active.T.astype(low), cot).astype(low)
    depth = up.shape[0]

    def put(b, grad_ref):
        grad_ref[:depth] = up[:, b * LANES : (b + 1) * LANES]
        for t in range(down.shape[1] // LANES):
            grad_ref[depth + t * LANES : depth + (t + 1) * LANES] = down[
                b * LANES : (b + 1) * LANES, t * LANES : (t + 1) * LANES
            ]

    for b in range(2):
        d_b_up_ref[:, pl.ds(at[b], LANES)] = d_b_up[:, b * LANES : (b + 1) * LANES]
    put(0, keep_ref)

    @pl.when(step < early)
    def _():
        put(1, early_ref)

    @pl.when(step >= early)
    def _():
        put(1, send_ref)

    @pl.when(step == steps - 1)
    def _():
        copies[5].wait()
        part_ref[...] = part_acc[...]
        back = back_acc[...]
        back_ref[...] = back.astype(low)
        sums_ref[0:1] = jnp.sum(back * xhat_ref[...], axis=0, keepdims=True)
        sums_ref[1:2] = jnp.sum(back, axis=0, keepdims=True)


def mlp(ids, early, *given):
    rows, width = given[0].shape
    hidden_units = given[1].shape[1]
    steps = hidden_units // LANES // 2
    whole = lambda shape: pl.BlockSpec(shape, lambda f, c: (0,) * len(shape))
    grads = lambda at: pl.BlockSpec((2 * width, LANES), lambda f, c: (at(f), 0))
    outs = [
        shape_of((rows, width), full),
        shape_of((rows, width), low),
        shape_of((2, width), full),
        shape_of((1, hidden_units), full),
        shape_of((steps * 2 * width, LANES), low),
        shape_of((early * 2 * width, LANES), low),
        shape_of(((steps - early) * 2 * width, LANES), low),
    ]
    return pl.pallas_call(
        functools.partial(mlp_kernel, early),
        grid_spec=pltpu.PrefetchScalarGridSpec(
            num_scalar_prefetch=1,
            grid=(steps,),
            in_specs=[spec_hbm()] * len(given),
            out_specs=[whole(array.shape) for array in outs[:4]]
            + [
                grads(lambda f: f),
                grads(lambda f: jnp.minimum(f, early - 1)),
                grads(lambda f: jnp.maximum(f - early, 0)),
            ],
            scratch_shapes=[
                pltpu.VMEM((width, rows), low),
                pltpu.VMEM((rows, width), full),
                pltpu.VMEM((rows, width), full),
            ]
            + [pltpu.VMEM(array.shape, array.dtype) for array in given]
            + [pltpu.SemaphoreType.DMA((len(given),))],
        ),
        out_shape=outs,
        compiler_params=params(60),
        cost_estimate=pl.CostEstimate(
            flops=12 * rows * width * hidden_units, bytes_accessed=20 * MIB, transcendentals=0
        ),
        name="feed_forward",
    )(ids, *given)


def attention_kernel(heads, group, places, is_first, is_last, pair_ref, inv_ref, token_ref, *rest):
    del token_ref
    if is_first:
        got_ref, rest = rest[0], rest[1:]
        if group > 1:
            other_ref, rest = rest[0], rest[1:]
    else:
        rest = rest[4:]
    out_ref, rest = rest[0], rest[1:]
    if is_last:
        d_own_ref, rest = rest[0], rest[1:]
        if group > 1:
            d_other_ref, rest = rest[0], rest[1:]
    (values_keys, turned_keys, sums, queries), rest = rest[:4], rest[4:]
    token_out, rest = rest[0], rest[1:]
    weights_in, weights_out, stored, peaks, totals, weighted, finals, block_cos, block_sin = rest
    token_out[...] = jnp.zeros_like(token_out)

    rows = queries.shape[1]
    owners = pair_ref.shape[0]
    total_blocks = 2 * owners
    per_chunk = KEYS // BLOCK
    tasks = (total_blocks + 1 + per_chunk - 1) // per_chunk
    me = lax.axis_index("ctx")
    own_sub = lax.rem(me, group)

    def blocks_of(r, d):
        owner = r * group + lax.rem(own_sub + d, group)
        pair = pair_ref[owner]
        return pair, total_blocks - 1 - pair

    def place(tile, block):
        at = pl.multiple_of(block * BLOCK, BLOCK)
        values_keys[pl.ds(at, BLOCK), :] = tile
        turned_keys[:, pl.ds(at, BLOCK)] = turn(tile)

    if is_first:
        for r in range(heads):
            queries[r] = got_ref[r, :, :LANES]
            for half, block in enumerate(blocks_of(r, 0)):
                place(got_ref[r, half * BLOCK : (half + 1) * BLOCK, LANES:], block)
            for d in range(1, group):
                for half, block in enumerate(blocks_of(r, d)):
                    at = r * rows + half * BLOCK
                    place(other_ref[d - 1, at : at + BLOCK, :], block)
        sums[...] = jnp.zeros_like(sums)

    lane = lane_ids((BLOCK, LANES))
    left = lane < HEAD_DIM
    in_key = lane - HEAD_DIM
    moving = (in_key >= 0) & (in_key < ROT)
    forward = (in_key >= 0) & (in_key < HALF)
    cos_row, sin_row, block_cos[...], block_sin[...] = block_tables(inv_ref[...], row_ids(block_cos.shape))

    def rotated_back(tile, block):
        cos_at, sin_at = block_cos[pl.ds(block, 1), :], block_sin[pl.ds(block, 1), :]
        cosine = jnp.where(moving, cos_row * cos_at - sin_row * sin_at, 1.0)
        sine = sin_row * cos_at + cos_row * sin_at
        sine = jnp.where(moving, jnp.where(forward, sine, -sine), 0.0)
        return tile * cosine + rotary_partner(tile) * sine

    offset = row_ids((BLOCK, BLOCK)) - lane_ids((BLOCK, BLOCK))

    def one_pair(i, carry):
        blocks = blocks_of(places[0] + i, 0)
        first = blocks[0] // per_chunk + 1
        for half in range(2):
            both = queries[places[0] + i, half * BLOCK : (half + 1) * BLOCK, :]
            both_turned = turn(both)
            upper = row_ids((LANES, BLOCK)) < HEAD_DIM
            zero = jnp.zeros_like(both_turned)
            weights_in[half, :, :BLOCK] = jnp.where(upper, both_turned, zero)
            weights_in[half, :, BLOCK:] = jnp.where(upper, zero, both_turned)
            weights_out[half, :BLOCK, :] = jnp.where(left, both, zero)
            weights_out[half, BLOCK:, :] = jnp.where(left, zero, both)
        finals[...] = jnp.zeros_like(finals)

        def task(t):
            is_low = t < first
            chunk = jnp.where(is_low, first - 1 - t, t - first)
            return is_low, chunk

        runs = KEYS // BLOCK
        for t in range(tasks):
            is_low, chunk = task(t)
            weights = weights_in[jnp.where(is_low, 0, 1)]
            for u in range(runs):
                at = pl.multiple_of(chunk * KEYS + u * BLOCK, BLOCK)
                sub = slice(u * BLOCK, (u + 1) * BLOCK)
                both = mm(values_keys[pl.ds(at, BLOCK), :], weights)
                grads = both[:, :BLOCK]
                scores = both[:, BLOCK:]
                if t in (0, tasks - 1):
                    query_at = blocks[0 if t == 0 else 1] * BLOCK
                    scores = jnp.where(offset <= query_at - at, scores, masked_score)
                peak = jnp.max(scores, axis=0, keepdims=True)
                raised = jnp.exp(scores - peak)
                stored[t, sub, :BLOCK] = raised
                stored[t, sub, BLOCK:] = grads
                line = t * runs + u
                peaks[line : line + 1] = peak
                totals[line : line + 1] = jnp.sum(raised, axis=0, keepdims=True)
                weighted[line : line + 1] = jnp.sum(raised * grads, axis=0, keepdims=True)

        in_low = row_ids((tasks * runs, BLOCK)) < first * runs

        def finish(mine):
            top = jnp.max(jnp.where(mine, peaks[...], masked_score), axis=0, keepdims=True)
            factor = jnp.where(mine, jnp.exp(peaks[...] - top), 0.0)
            inverse = 1.0 / jnp.sum(totals[...] * factor, axis=0, keepdims=True)
            return factor * inverse, jnp.sum(weighted[...] * factor, axis=0, keepdims=True) * inverse

        (low_factor, low_delta), (high_factor, high_delta) = finish(in_low), finish(jnp.logical_not(in_low))
        peaks[...] = low_factor + high_factor

        for t in range(tasks):
            is_low, chunk = task(t)
            half = jnp.where(is_low, 0, 1)
            weights = weights_out[half]
            delta = jnp.where(is_low, low_delta, high_delta)
            parts = []
            for u in range(runs):
                sub = slice(u * BLOCK, (u + 1) * BLOCK)
                probs = stored[t, sub, :BLOCK] * peaks[t * runs + u : t * runs + u + 1]
                d_scores = probs * (stored[t, sub, BLOCK:] - delta)
                both = jnp.concatenate([probs, d_scores], axis=1).astype(low)
                at = pl.multiple_of(chunk * KEYS + u * BLOCK, BLOCK)
                sums[pl.ds(at, BLOCK), :] += mm(both, weights)
                parts.append(both)
            at = pl.multiple_of(chunk * KEYS, KEYS)
            finals[half] += mm(turned_keys[:, pl.ds(at, KEYS)], jnp.concatenate(parts, axis=0))

        for half in range(2):
            both = jnp.concatenate(
                [finals[half, :HEAD_DIM, :BLOCK], finals[half, HEAD_DIM:, BLOCK:] * score_scale], axis=0
            ).T
            out_ref[i, half * BLOCK : (half + 1) * BLOCK, :] = rotated_back(both, blocks[half]).astype(low)
        return carry

    lax.fori_loop(0, len(places), one_pair, 0)

    if is_last:
        for r in range(heads):
            for d in range(group):
                for half, block in enumerate(blocks_of(r, d)):
                    at = r * rows + half * BLOCK
                    tile = rotated_back(sums[pl.ds(pl.multiple_of(block * BLOCK, BLOCK), BLOCK), :], block)
                    if d == 0:
                        d_own_ref[at : at + BLOCK, :] = tile
                    else:
                        d_other_ref[d - 1, at : at + BLOCK, :] = tile


def attention(heads, group, places, pair_of, inverse, token, got, other, state):
    is_first, is_last = state is None, places[-1] == heads - 1
    rows = got.shape[1]
    owners = pair_of.shape[0]
    total_keys = owners * rows
    tasks = (2 * owners + KEYS // BLOCK) // (KEYS // BLOCK)
    operands = [pair_of, inverse, token]
    outs = [shape_of((len(places), rows, LANES), low)]
    if is_first:
        operands += [got] if other is None else [got, other]
    else:
        operands += list(state)
    if is_last:
        outs.append(shape_of((heads * rows, LANES), full))
        if group > 1:
            outs.append(shape_of((group - 1, heads * rows, LANES), full))
    kept = [
        shape_of((total_keys, LANES), low),
        shape_of((LANES, total_keys), low),
        shape_of((total_keys, LANES), full),
        shape_of((heads, rows, LANES), low),
    ]
    aliases = {} if is_first else {len(operands) - 4 + i: len(outs) + i for i in range(4)}
    found = pl.pallas_call(
        functools.partial(attention_kernel, heads, group, places, is_first, is_last),
        out_shape=outs + kept + [shape_of((1, LANES), full)],
        in_specs=[spec_smem()] + [spec_vmem()] * (len(operands) - 1),
        out_specs=[spec_vmem()] * (len(outs) + 5),
        input_output_aliases=aliases,
        scratch_shapes=[
            pltpu.VMEM((2, LANES, 2 * BLOCK), low),
            pltpu.VMEM((2, 2 * BLOCK, LANES), low),
            pltpu.VMEM((tasks, KEYS, 2 * BLOCK), full),
            pltpu.VMEM((tasks * KEYS // BLOCK, BLOCK), full),
            pltpu.VMEM((tasks * KEYS // BLOCK, BLOCK), full),
            pltpu.VMEM((tasks * KEYS // BLOCK, BLOCK), full),
            pltpu.VMEM((2, LANES, 2 * BLOCK), full),
            pltpu.VMEM((2 * owners, LANES), full),
            pltpu.VMEM((2 * owners, LANES), full),
        ],
        compiler_params=params(6 + total_keys * 5 * 256 // MIB),
        cost_estimate=pl.CostEstimate(
            flops=2_500_000_000 * len(places), bytes_accessed=2 * MIB, transcendentals=0
        ),
        name="attention",
    )(*operands)
    return found[0], found[1 : len(outs)], found[len(outs) : len(outs) + 4], found[-1]


def combine_kernel(heads, terms, *refs):
    out_ref = refs[-1]
    rows = out_ref.shape[1]
    for r in range(heads):
        cut = slice(r * rows, (r + 1) * rows)
        total = refs[0][cut, :]
        for term in refs[1:terms]:
            total = total + term[cut, :]
        out_ref[r, :, LANES:] = total.astype(low)
    at = 0
    for first_ref in refs[terms:-1]:
        out_ref[at : at + first_ref.shape[0], :, :LANES] = first_ref[...]
        at += first_ref.shape[0]


def combine(heads, terms, firsts):
    rows = firsts[0].shape[1]
    return pl.pallas_call(
        functools.partial(combine_kernel, heads, len(terms)),
        out_shape=shape_of((heads, rows, 2 * LANES), low),
        in_specs=[spec_vmem()] * (len(firsts) + len(terms)),
        out_specs=spec_vmem(),
        compiler_params=params(24),
        cost_estimate=pl.CostEstimate(flops=10**7, bytes_accessed=3 * MIB, transcendentals=0),
        name="combine",
    )(*terms, *firsts)


def weight_grads_kernel(
    heads, early, ids_ref, got_ref, h1_ref, cot_ref, low_ref, d_b_ref, keep_ref, early_ref, send_ref, token_ref, grads
):
    chips, chunk_rows = keep_ref.shape[:2]

    def put(at, tile):
        step = min(chunk_rows, tile.shape[0])
        for off in range(0, tile.shape[0], step):
            chunk, inside = divmod(at + off, chunk_rows)
            grads[chunk, inside : inside + step] = tile[off : off + step]

    rows = h1_ref.shape[0]
    left = lane_ids((rows, LANES)) < HEAD_DIM
    for i in range(heads // 2):
        cut = slice(i * LANES, (i + 1) * LANES)
        for first, second, half in ((0, 1, slice(0, LANES)), (3, 2, slice(LANES, 2 * LANES))):
            a, b = got_ref[2 * i, :, half].astype(full), got_ref[2 * i + 1, :, half].astype(full)
            low_ref[first, :, cut] = jnp.where(left, a, pltpu.roll(b, HEAD_DIM, 1)).astype(low)
            low_ref[second, :, cut] = jnp.where(left, pltpu.roll(a, HEAD_DIM, 1), b).astype(low)
    h1_turned = turn(h1_ref[...])
    depth, tiles = h1_turned.shape[0], heads // 2
    for s in range(3):
        d_proj = low_ref[1 + s]
        d_b_ref[s : s + 1] = jnp.sum(d_proj.astype(full), axis=0, keepdims=True)
        grad = mm(h1_turned, d_proj).astype(low)
        for t in range(tiles):
            put((s * tiles + t) * depth, grad[:, t * LANES : (t + 1) * LANES])
    grad = mm(turn(low_ref[0]), cot_ref[...]).astype(low)
    height = grad.shape[0]
    for t in range(depth // LANES):
        put(3 * tiles * depth + t * height, grad[:, t * LANES : (t + 1) * LANES])
    for t in range(chips):
        target = early_ref.at[t] if t < early else send_ref.at[t - early]
        target[...] = grads[ids_ref[chips + t]]
        keep_ref[t] = grads[ids_ref[t]]
    token_ref[...] = jnp.zeros_like(token_ref)


def weight_grads(heads, early, ids, got, h1, cot):
    rows, width = h1.shape
    local_width = heads * HEAD_DIM
    chips = ids.shape[0] // 2
    chunk_rows = 4 * width * local_width // LANES // (2 * chips)
    outs = [
        shape_of((4, rows, local_width), low),
        shape_of((3, local_width), full),
        shape_of((chips, chunk_rows, LANES), low),
        shape_of((early, chunk_rows, LANES), low),
        shape_of((chips - early, chunk_rows, LANES), low),
        shape_of((1, LANES), full),
    ]
    return pl.pallas_call(
        functools.partial(weight_grads_kernel, heads, early),
        out_shape=outs,
        in_specs=[spec_smem()] + [spec_vmem()] * 3,
        out_specs=[spec_vmem()] * len(outs),
        scratch_shapes=[pltpu.VMEM((2 * chips, chunk_rows, LANES), low)],
        compiler_params=params(20),
        cost_estimate=pl.CostEstimate(
            flops=8 * rows * width * local_width, bytes_accessed=8 * MIB, transcendentals=0
        ),
        name="weight_grads",
    )(ids, got, h1, cot)


def return_kernel(low_ref, part_ref, w_out_ref, w_qkv_ref, xhat_ref, e2_ref, both_ref, sums_ref):
    rows = xhat_ref.shape[0]
    both_ref[:rows] = (part_ref[...] + mm(low_ref[0], w_out_ref[...])).astype(low)
    back = mm_nt(low_ref[1], w_qkv_ref[0]) + mm_nt(low_ref[2], w_qkv_ref[1]) + mm_nt(low_ref[3], w_qkv_ref[2])
    both_ref[rows : 2 * rows] = back.astype(low)
    both_ref[2 * rows :] = e2_ref[...]
    sums_ref[0:1] = jnp.sum(back * xhat_ref[...], axis=0, keepdims=True)
    sums_ref[1:2] = jnp.sum(back, axis=0, keepdims=True)


def back_projections(*given):
    rows, width = given[1].shape
    return pl.pallas_call(
        return_kernel,
        out_shape=[shape_of((3 * rows, width), low), shape_of((2, width), full)],
        in_specs=[spec_vmem()] * len(given),
        out_specs=[spec_vmem()] * 2,
        compiler_params=params(16),
        cost_estimate=pl.CostEstimate(
            flops=8 * rows * width * given[2].shape[0], bytes_accessed=8 * MIB, transcendentals=0
        ),
        name="back_projections",
    )(*given)


def finish_kernel(
    hidden_ref, cot_ref, xhat_ref, std_ref, gains_ref, bias_ref, ours_ref, theirs_ref, out_ref, grad_ref, token_ref
):
    rows = hidden_ref.shape[0]
    gains = gains_ref[...]
    biases = bias_ref[...]
    summed = ours_ref[:rows].astype(full) + theirs_ref[:rows].astype(full)
    out_ref[...] = (hidden_ref[...].astype(full) + summed + biases[0:1] + biases[1:2]).astype(low)
    e1 = ours_ref[rows : 2 * rows].astype(full) + theirs_ref[rows : 2 * rows].astype(full)
    e2 = ours_ref[2 * rows :].astype(full) + theirs_ref[2 * rows :].astype(full)
    f = e1 * gains[0:1] + e2 * gains[1:2]
    xhat = xhat_ref[...]
    inv_std = std_ref[:, 0:1]
    grad_ref[...] = cot_ref[...].astype(full) + inv_std * (
        f - jnp.mean(f, axis=-1, keepdims=True) - xhat * jnp.mean(f * xhat, axis=-1, keepdims=True)
    )
    token_ref[...] = jnp.zeros_like(token_ref)


def finish(*operands):
    rows, width = operands[0].shape
    return pl.pallas_call(
        finish_kernel,
        out_shape=[shape_of((rows, width), low), shape_of((rows, width), full), shape_of((1, LANES), full)],
        in_specs=[spec_vmem()] * len(operands),
        out_specs=[spec_vmem()] * 3,
        compiler_params=params(24),
        cost_estimate=pl.CostEstimate(flops=10**7, bytes_accessed=8 * MIB, transcendentals=0),
        name="finish",
    )(*operands)


def to_attention(width, local_width, source, refs, base, unit):
    qkv_ref, out_ref = refs
    tiles = local_width // LANES
    split = 3 * tiles * width
    tile = base // width
    row = pl.multiple_of(lax.rem(base, width), unit)
    column = pl.multiple_of(lax.rem(tile, tiles) * LANES, LANES)
    yield base < split, source, qkv_ref.at[jnp.minimum(tile // tiles, 2), pl.ds(row, unit), pl.ds(column, LANES)]
    after = jnp.maximum(base - split, 0)
    row = pl.multiple_of(lax.rem(after, local_width), unit)
    column = pl.multiple_of(after // local_width * LANES, LANES)
    yield base >= split, source, out_ref.at[pl.ds(row, unit), pl.ds(column, LANES)]


def to_mlp(width, source, refs, base, unit):
    up_ref, down_ref = refs
    block, inside = base // (2 * width), lax.rem(base, 2 * width)
    block_at = pl.multiple_of(block * LANES, LANES)
    row = pl.multiple_of(jnp.minimum(inside, width - unit), unit)
    yield inside < width, source, up_ref.at[pl.ds(row, unit), pl.ds(block_at, LANES)]
    for t in range(unit // LANES):
        column = pl.multiple_of(jnp.maximum(inside - width, 0) + t * LANES, LANES)
        cut = source.at[pl.ds(t * LANES, LANES), :]
        yield inside >= width, cut, down_ref.at[pl.ds(block_at, LANES), pl.ds(column, LANES)]


def unpack_kernel(route, count, unit, joined, has_old, keeps, ids_ref, *rest):
    if joined:
        rows = rest[0].shape[0] // count
        parts, rest = [rest[0].at[pl.ds(i * rows, rows), :] for i in range(count)], rest[1:]
    else:
        parts, rest = rest[:count], rest[count:]
    rest = rest[2:] if has_old else rest
    targets, rest = rest[:2], rest[2:]
    if keeps:
        packed_ref, rest = rest[0], rest[1:]
    token_ref, held, sems = rest
    token_ref[...] = jnp.zeros_like(token_ref)
    chunk_rows = parts[0].shape[0]
    units = chunk_rows // unit
    per_unit = (sems.shape[0] - (count if keeps else 0)) // (count * units)
    kept = []
    if keeps:
        for i in range(count):
            target = packed_ref.at[pl.ds(i * chunk_rows, chunk_rows), :]
            kept.append(pltpu.make_async_copy(parts[i], target, sems.at[count * units * per_unit + i]))
            kept[i].start()

    def moves():
        for i in range(count):
            for j in range(units):
                source = held.at[i, pl.ds(j * unit, unit), :]
                base = ids_ref[i] * chunk_rows + j * unit
                for n, (applies, piece, target) in enumerate(route(source, targets, base, unit)):
                    sem = sems.at[(i * units + j) * per_unit + n]
                    yield i, applies, pltpu.make_async_copy(piece, target, sem)

    done = -1
    for i, applies, copy in moves():
        if i != done:
            held[i] = parts[i][...].astype(full)
            done = i
        pl.when(applies)(copy.start)
    for i, applies, copy in moves():
        pl.when(applies)(copy.wait)
    for copy in kept:
        copy.wait()


def unpack(name, route, cases, unit, shapes, ids, parts, old, keeps=False):
    count = ids.shape[0]
    joined = len(parts) < count
    chunk_rows = parts[0].shape[0] // (count if joined else 1)
    operands = [ids, *parts, *(old or ())]
    outs = [shape_of(shape, full) for shape in shapes]
    if keeps:
        outs.append(shape_of((count * chunk_rows, LANES), low))
    return pl.pallas_call(
        functools.partial(unpack_kernel, route, count, unit, joined, old is not None, keeps),
        out_shape=outs + [shape_of((1, LANES), full)],
        in_specs=[spec_smem()] + [spec_vmem()] * len(parts) + [spec_hbm()] * (len(operands) - 1 - len(parts)),
        out_specs=[spec_hbm()] * len(outs) + [spec_vmem()],
        input_output_aliases={} if old is None else {1 + len(parts): 0, 2 + len(parts): 1},
        scratch_shapes=[
            pltpu.VMEM((count, chunk_rows, LANES), full),
            pltpu.SemaphoreType.DMA((count * (chunk_rows // unit) * cases + (count if keeps else 0),)),
        ],
        compiler_params=params(8 + count * chunk_rows * 3 * LANES * 2 // MIB),
        cost_estimate=pl.CostEstimate(
            flops=10**6, bytes_accessed=count * chunk_rows * LANES * 6, transcendentals=0
        ),
        name=name,
    )(*operands)


def local(
    hidden,
    pair_of,
    ln1_gain,
    ln1_bias,
    ln2_gain,
    ln2_bias,
    w_qkv,
    b_qkv,
    w_out,
    b_out,
    w_up,
    b_up,
    w_down,
    b_down,
    cotangent,
):
    owners = lax.axis_size("ctx")
    sides = lax.axis_size("tp")
    rows, width = hidden.shape
    local_width = w_qkv.shape[2]
    hidden_units = w_up.shape[1]
    heads = local_width // HEAD_DIM
    group = owners // heads

    exponent = np.arange(0, ROT, 2, dtype=np.float32) / np.float32(ROT)
    inverse = jnp.asarray(np.tile(np.float32(10000.0) ** (-exponent), LANES // HALF)[None, :], full)
    order = (0, 2, 4, 6, 7, 5, 3, 1) if owners == 16 else tuple(range(owners // 2))
    chips = len(order)

    def to_heads(array):
        groups = [[h * group + g for h in range(heads)] for g in range(group)]
        return lax.all_to_all(array, "ctx", 0, 0, axis_index_groups=groups, tiled=True)

    def group_shift(array, d):
        pairs = [(c, c // group * group + (c % group + d) % group) for c in range(owners)]
        return lax.ppermute(array, "ctx", pairs)

    me = lax.axis_index("ctx")
    chip, core = me // 2, lax.rem(me, 2)
    place = sum(jnp.where(chip == c, i, 0) for i, c in enumerate(order))
    way = 1 - 2 * core
    far, near = chips // 2, chips - 1 - chips // 2

    def ring(array, forward):
        pairs = []
        for i, c in enumerate(order):
            for k in range(2):
                step = 1 if (k == 0) == forward else -1
                pairs.append((2 * c + k, 2 * order[(i + step) % chips] + k))
        return lax.ppermute(array, "ctx", pairs)

    def other_core(array):
        return lax.ppermute(array, "ctx", [(c, c ^ 1) for c in range(owners)])

    def across(array):
        return lax.ppermute(array, "tp", [(t, (t + 1) % sides) for t in range(sides)])

    def target(distance):
        return lax.rem(place + way * distance + chips, chips)

    def zero(array):
        return array[:1].astype(full) * 0.0

    slots = [far, -near]
    for t in range(1, far):
        slots += [far - t] if t >= near else [far - t, t - near]
    slots.append(0)
    early = 2
    slot_ids = jnp.stack(
        [core * chips + target(d) for d in slots] + [(1 - core) * chips + target(-d) for d in slots]
    )

    def terms_of(keep, came):
        def term(i):
            return keep[i].astype(full) + came[i].astype(full)

        return {d: term(i) for i, d in enumerate(slots)}

    def scatter_start(terms, token):
        return (terms[far] + token).astype(low), (terms[-near] + token).astype(low)

    def scatter_send(t, sends):
        long_send, short_send = sends
        return ring(long_send, True), (ring(short_send, False) if t < near else short_send)

    def scatter_add(terms, t, came, token):
        long_got = came[0].astype(full) + token
        last = t == far - 1
        long_next = long_got if last else (long_got + terms[far - 1 - t]).astype(low)
        short_next = came[1]
        if t < near:
            short_got = came[1].astype(full) + token
            short_next = short_got if t == near - 1 else (short_got + terms[t + 1 - near]).astype(low)
        if last:
            return (terms[0] + long_next + short_next).astype(low)
        return long_next, short_next

    def scatter_step(terms, t, sends, token):
        return scatter_add(terms, t, scatter_send(t, sends), token)

    base, other_base = core * chips, (1 - core) * chips

    def gather_start(own):
        return [(own, base + place), (other_core(own), other_base + place)]

    def gather_step(t, sends, token):
        long_send, short_send = sends
        if token is not None:
            long_send = (long_send.astype(full) + token).astype(low)
        long_got = ring(long_send, True)
        found = [(long_got, base + target(-t - 1)), (other_core(long_got), other_base + target(t + 1))]
        short_got = short_send
        if t < near:
            short_got = ring(short_send, False)
            found += [(short_got, base + target(t + 1)), (other_core(short_got), other_base + target(-t - 1))]
        return (long_got, short_got), found

    blocks = hidden_units // LANES // 2
    in_slots = blocks == chips
    mlp_ids = slot_ids if in_slots else jnp.concatenate(
        [core * blocks + jnp.arange(blocks), (1 - core) * blocks + jnp.arange(blocks)]
    )
    h1, h2, xhat, inv_std, d_bias, gains, biases, b_up_row, packed = project(
        heads,
        pair_of,
        inverse,
        (hidden, ln1_gain, ln1_bias, ln2_gain, ln2_bias, cotangent, w_out, w_qkv, b_qkv, b_up, b_out, b_down),
    )
    got = to_heads(packed)
    part, back2, sums2, d_b_up, keep_mlp, early_mlp, send_mlp = mlp(
        mlp_ids.astype(jnp.int32), early, h2, w_up, b_up_row, cotangent, w_down, xhat
    )
    chunk = keep_mlp.shape[0] // chips
    came_mlp = jnp.concatenate([other_core(early_mlp), other_core(send_mlp)]) if not in_slots else None
    if in_slots:
        halves = [other_core(array).reshape(-1, chunk, LANES) for array in (early_mlp, send_mlp)]
        came_mlp = [half[i] for half in halves for i in range(half.shape[0])]
        terms_mlp = terms_of(keep_mlp.reshape(chips, chunk, LANES), came_mlp)
    else:
        summed = (keep_mlp.astype(full) + came_mlp.astype(full)).reshape(chips, chunk, LANES)
        terms_mlp = {d: lax.dynamic_index_in_dim(summed, target(d), 0, keepdims=False) for d in slots}
    nothing = jnp.zeros((1, LANES), full)

    other = None
    if group > 1:
        mine = got[:, :, LANES:].reshape(heads * rows, LANES)
        other = jnp.stack([group_shift(mine, group - d) for d in range(1, group)])

    middle = heads // 4
    first, _, state, token = attention(
        heads, group, tuple(range(middle)), pair_of, inverse, sums2, got, other, None
    )
    sends_mlp = scatter_start(terms_mlp, token)
    token = zero(sends_mlp[0]) + zero(sends_mlp[1])
    second, ends, _, token = attention(
        heads, group, tuple(range(middle, heads)), pair_of, inverse, token, got, other, state
    )
    d_own, d_other = ends[0], (ends[1] if group > 1 else None)
    terms = [d_own] + [group_shift(d_other[d - 1], d) for d in range(1, group)]
    sends_mlp = scatter_step(terms_mlp, 0, sends_mlp, token)
    first = (first.astype(full) + zero(sends_mlp[0]) + zero(sends_mlp[1])).astype(low)
    backs = to_heads(combine(heads, terms, [first, second]))
    came_mlp = scatter_send(1, sends_mlp)
    h1_later = (h1.astype(full) + (zero(came_mlp[0]) + zero(came_mlp[1]))[:, :1]).astype(low)

    lows, d_b_qkv, keep, early_att, send_att, after = weight_grads(
        heads, early, slot_ids.astype(jnp.int32), backs, h1_later, cotangent
    )
    both, sums1 = back_projections(lows, part, w_out, w_qkv, xhat, back2)
    sends_mlp = scatter_add(terms_mlp, 1, came_mlp, after)
    theirs = across(both)
    output, d_hidden, finish_token = finish(
        hidden, cotangent, xhat, inv_std, gains, biases, both, theirs
    )
    halves = [other_core(array) for array in (early_att, send_att)]
    terms_att = terms_of(keep, [half[i] for half in halves for i in range(half.shape[0])])

    small = jnp.concatenate(
        [sums1.reshape(1, -1), sums2.reshape(1, -1), d_bias, d_b_up, d_b_qkv.reshape(1, -1)], axis=1
    )

    def unpack_some(name, route, cases, unit, shapes, found, old):
        parts, ids = zip(*found)
        *old, token = unpack(name, route, cases, unit, shapes, jnp.stack(ids), parts, old)
        return old, token

    unit_mlp = min(chunk, local_width)
    unit_att = min(keep.shape[1], local_width)
    unpack_mlp = functools.partial(
        unpack,
        "unpack_feed_forward",
        functools.partial(to_mlp, width),
        1 + unit_mlp // LANES,
        unit_mlp,
        ((width, hidden_units), (hidden_units, width)),
    )
    unpack_att = functools.partial(
        unpack_some,
        "unpack_attention",
        functools.partial(to_attention, width, local_width),
        2,
        unit_att,
        ((3, width, local_width), (local_width, width)),
    )

    steps_mlp, steps_round = iter(range(2, far)), iter(range(far))
    own_mlp, round_mlp, waiting = None, None, []

    def advance_mlp(token, gate=None):
        nonlocal sends_mlp, own_mlp, round_mlp, waiting
        t = next(steps_mlp, None)
        if t is not None:
            sends_mlp = scatter_step(terms_mlp, t, sends_mlp, token)
            if t < far - 1:
                return zero(sends_mlp[0])
            own_mlp, round_mlp = sends_mlp, (sends_mlp, sends_mlp)
            waiting.append((own_mlp, base + place, other_base + place))
            return zero(own_mlp)
        t = next(steps_round, None)
        if t is None:
            return nothing
        long_send, short_send = round_mlp
        if gate is not None:
            long_send = (long_send.astype(full) + gate).astype(low)
        long_got = ring(long_send, True)
        waiting.append((long_got, base + target(-t - 1), other_base + target(t + 1)))
        short_got = short_send
        if t < near:
            short_got = ring(short_send, False)
            waiting.append((short_got, base + target(t + 1), other_base + target(-t - 1)))
        round_mlp = (long_got, short_got)
        return zero(round_mlp[0])

    sends_att = scatter_start(terms_att, nothing)
    before = nothing
    for t in range(far):
        later = advance_mlp(after)
        sends_att = scatter_step(terms_att, t, sends_att, before)
        before = later
    round_att, waiting_att, grads_att = (sends_att, sends_att), gather_start(sends_att), None
    small = small + zero(sends_att)[:, :1]
    distance = 1
    for t in range(far):
        advance_mlp(after, zero(round_att[0]))
        round_att, found = gather_step(t, round_att, None)
        waiting_att += found
        if distance < owners:
            small = small + lax.ppermute(small, "ctx", [(c, c ^ distance) for c in range(owners)])
            distance *= 2
        if t == 1:
            small = small + finish_token[:, :1]
        if t == far - 2:
            parts, ids, other_ids = zip(*waiting)
            *halves, packed_mlp, more = unpack_mlp(jnp.stack(ids), parts, None, True)
            small = small + more[:, :1]
            theirs_mlp = other_core(packed_mlp)
            grads_att, more = unpack_att(waiting_att[:-4], None)
            waiting_att = waiting_att[-4:]
            small = small + more[:, :1]
    while distance < owners:
        small = small + lax.ppermute(small, "ctx", [(c, c ^ distance) for c in range(owners)])
        distance *= 2
    d_w_up, d_w_down, _ = unpack_mlp(jnp.stack(other_ids), [theirs_mlp], halves)
    grads_att, _ = unpack_att(waiting_att, grads_att)

    norm_sums = small[:, : 4 * width]
    norm_sums = (norm_sums + across(norm_sums)).reshape(4, width)
    at = 4 * width
    d_bias = small[0, at : at + width]
    d_b_up = small[0, at + width : at + width + hidden_units]
    d_b_qkv = small[0, at + width + hidden_units :].reshape(3, local_width)
    d_w_qkv, d_w_out = grads_att
    return (
        output,
        d_hidden,
        norm_sums[0],
        norm_sums[1],
        norm_sums[2],
        norm_sums[3],
        d_w_qkv,
        d_b_qkv,
        d_w_out,
        d_bias,
        d_w_up,
        d_b_up,
        d_w_down,
        d_bias,
    )


def solution(mesh):
    placed = (
        P("ctx", None),
        P(),
        P(),
        P(),
        P(),
        P(),
        P(None, None, "tp"),
        P(None, "tp"),
        P("tp", None),
        P(),
        P(None, "tp"),
        P("tp"),
        P("tp", None),
        P(),
        P("ctx", None),
    )
    return jax.shard_map(
        local,
        mesh=mesh,
        in_specs=placed,
        out_specs=(
            P("ctx", None),
            P("ctx", None),
            P(),
            P(),
            P(),
            P(),
            P(None, None, "tp"),
            P(None, "tp"),
            P("tp", None),
            P(),
            P(None, "tp"),
            P("tp"),
            P("tp", None),
            P(),
        ),
        check_vma=False,
    )
```

```python
import functools

import jax
import jax.numpy as jnp
import numpy as np
from jax import lax
from jax.experimental import pallas as pl
from jax.experimental.pallas import tpu as pltpu
from jax.sharding import PartitionSpec as P

HEAD_DIM = 64
ROT = 16
HALF = ROT // 2
BLOCK = 128
LANES = 128
KEYS = 512
MIB = 1 << 20

norm_eps = 1e-05
masked_score = -1e30
score_scale = HEAD_DIM ** (-0.5)
low = jnp.bfloat16
full = jnp.float32


def mm(left, right):
    return lax.dot_general(left, right, (((1,), (0,)), ((), ())), preferred_element_type=full)


def mm_nt(left, right):
    return lax.dot_general(left, right, (((1,), (1,)), ((), ())), preferred_element_type=full)


def turn(tensor):
    return tensor.astype(full).T.astype(low)


def lane_ids(shape):
    return lax.broadcasted_iota(jnp.int32, shape, len(shape) - 1)


def row_ids(shape):
    return lax.broadcasted_iota(jnp.int32, shape, len(shape) - 2)


def rotary_partner(tensor):
    lanes = lane_ids(tensor.shape)
    ahead = pltpu.roll(tensor, LANES - HALF, 1)
    behind = pltpu.roll(tensor, HALF, 1)
    return jnp.where(lanes % ROT < HALF, ahead, behind)


def spec_vmem():
    return pl.BlockSpec(memory_space=pltpu.VMEM)


def spec_smem():
    return pl.BlockSpec(memory_space=pltpu.SMEM)


def spec_hbm():
    return pl.BlockSpec(memory_space=pltpu.HBM)


def params(mib):
    return pltpu.CompilerParams(vmem_limit_bytes=mib * MIB)


def shape_of(shape, kind):
    return jax.ShapeDtypeStruct(shape, kind)


def block_tables(inverse, blocks):
    row = row_ids((BLOCK, LANES)).astype(full)
    start = blocks.astype(full) * float(BLOCK)
    return jnp.cos(row * inverse), jnp.sin(row * inverse), jnp.cos(start * inverse), jnp.sin(start * inverse)


def project_kernel(heads, pair_ref, inv_ref, *rest):
    given, rest = rest[:12], rest[12:]
    h1_ref, h2_ref, xhat_ref, std_ref, d_bias_ref, gains_ref, bias_ref, b_up_out_ref, packed = rest[:9]
    held, sems = rest[9:-1], rest[-1]
    copies = [pltpu.make_async_copy(src, dst, sems.at[i]) for i, (src, dst) in enumerate(zip(given, held))]
    for copy in copies:
        copy.start()
    (
        hidden_ref,
        g1_ref,
        c1_ref,
        g2_ref,
        c2_ref,
        cot_ref,
        w_out_ref,
        w_qkv_ref,
        b_qkv_ref,
        b_up_ref,
        b_out_ref,
        b_down_ref,
    ) = held
    rows = hidden_ref.shape[0]
    me = lax.axis_index("ctx")
    pair = pair_ref[me]
    total_blocks = 2 * pair_ref.shape[0]

    first = jnp.where(row_ids((8, LANES)) == 0, pair, total_blocks - 1 - pair)
    inverse = inv_ref[...]
    cos_row, sin_row, cos_block, sin_block = block_tables(inverse, first)
    in_head = lane_ids((BLOCK, LANES)) % HEAD_DIM
    tables = []
    for half in range(2):
        cos_at, sin_at = cos_block[half : half + 1], sin_block[half : half + 1]
        cosine = cos_row * cos_at - sin_row * sin_at
        sine = sin_row * cos_at + cos_row * sin_at
        cosine = jnp.where(in_head < ROT, cosine, 1.0)
        sine = jnp.where(in_head < HALF, -sine, jnp.where(in_head < ROT, sine, 0.0))
        tables.append((cosine, sine))
    cosine = jnp.concatenate([tables[0][0], tables[1][0]], axis=0)
    sine = jnp.concatenate([tables[0][1], tables[1][1]], axis=0)

    for copy in copies[:5]:
        copy.wait()
    x = hidden_ref[...].astype(full)
    centred = x - jnp.mean(x, axis=-1, keepdims=True)
    spread = jnp.mean(centred * centred, axis=-1, keepdims=True)
    inv_std = lax.rsqrt(spread + norm_eps)
    xhat = centred * inv_std
    xhat_ref[...] = xhat
    std_ref[...] = jnp.broadcast_to(inv_std, std_ref.shape)

    def as_row(ref):
        return ref[...].astype(full)[None, :]

    gain1, gain2 = as_row(g1_ref), as_row(g2_ref)
    h1 = (xhat * gain1 + as_row(c1_ref)).astype(low)
    h1_ref[...] = h1
    h2_ref[...] = (xhat * gain2 + as_row(c2_ref)).astype(low)
    gains_ref[0:1] = gain1
    gains_ref[1:2] = gain2
    for copy in copies[5:]:
        copy.wait()
    b_up_out_ref[...] = as_row(b_up_ref)
    bias_ref[0:1] = as_row(b_out_ref)
    bias_ref[1:2] = as_row(b_down_ref)
    d_bias_ref[...] = jnp.sum(cot_ref[...].astype(full), axis=0, keepdims=True)

    lane = lane_ids((rows, LANES))

    def projected(s):
        return mm(h1, w_qkv_ref[s]) + b_qkv_ref[s : s + 1].astype(full)

    def turned(tile):
        return tile * cosine + rotary_partner(tile) * sine

    queries, keys, values = projected(0), projected(1), projected(2)
    grads = mm_nt(cot_ref[...], w_out_ref[...])
    left = lane < HEAD_DIM
    for i in range(heads // 2):
        cut = slice(i * LANES, (i + 1) * LANES)
        q = turned(queries[:, cut]).astype(low).astype(full) * score_scale
        k = turned(keys[:, cut])
        v = values[:, cut]
        g = grads[:, cut]
        packed[2 * i, :, :LANES] = jnp.where(left, g, pltpu.roll(q, HEAD_DIM, 1)).astype(low)
        packed[2 * i, :, LANES:] = jnp.where(left, v, pltpu.roll(k, HEAD_DIM, 1)).astype(low)
        packed[2 * i + 1, :, :LANES] = jnp.where(left, pltpu.roll(g, HEAD_DIM, 1), q).astype(low)
        packed[2 * i + 1, :, LANES:] = jnp.where(left, pltpu.roll(v, HEAD_DIM, 1), k).astype(low)


def project(heads, pair_of, inverse, given):
    hidden, w_out, b_up = given[0], given[6], given[9]
    rows, width = hidden.shape
    outs = [
        shape_of((rows, width), low),
        shape_of((rows, width), low),
        shape_of((rows, width), full),
        shape_of((rows, LANES), full),
        shape_of((1, width), full),
        shape_of((2, width), full),
        shape_of((2, width), full),
        shape_of((1, b_up.shape[0]), full),
        shape_of((heads, rows, 2 * LANES), low),
    ]
    return pl.pallas_call(
        functools.partial(project_kernel, heads),
        out_shape=outs,
        in_specs=[spec_smem(), spec_vmem()] + [spec_hbm()] * len(given),
        out_specs=[spec_vmem()] * len(outs),
        scratch_shapes=[pltpu.VMEM(array.shape, array.dtype) for array in given]
        + [pltpu.SemaphoreType.DMA((len(given),))],
        compiler_params=params(60),
        cost_estimate=pl.CostEstimate(
            flops=2 * rows * width * 4 * w_out.shape[0], bytes_accessed=8 * MIB, transcendentals=0
        ),
        name="project",
    )(pair_of, inverse, *given)


def mlp_kernel(early, ids_ref, *rest):
    given, rest = rest[:6], rest[6:]
    part_ref, back_ref, sums_ref, d_b_up_ref, keep_ref, early_ref, send_ref = rest[:7]
    h2_turned, part_acc, back_acc = rest[7:10]
    held, sems = rest[10:-1], rest[-1]
    copies = [pltpu.make_async_copy(src, dst, sems.at[i]) for i, (src, dst) in enumerate(zip(given, held))]
    h2_held, w_up_ref, b_up, cot_ref, w_down_ref, xhat_ref = held
    step = pl.program_id(0)
    steps = pl.num_programs(0)

    @pl.when(step == 0)
    def _():
        for copy in copies:
            copy.start()
        part_acc[...] = jnp.zeros_like(part_acc)
        back_acc[...] = jnp.zeros_like(back_acc)
        copies[0].wait()
        h2_turned[...] = turn(h2_held[...])
        for copy in copies[1:3]:
            copy.wait()

    at = [pl.multiple_of(ids_ref[b * steps + step] * LANES, LANES) for b in range(2)]
    w_up = jnp.concatenate([w_up_ref[:, pl.ds(i, LANES)] for i in at], axis=1)
    u = mm(h2_held[...], w_up) + jnp.concatenate([b_up[:, pl.ds(i, LANES)] for i in at], axis=1)

    @pl.when(step == 0)
    def _():
        for copy in copies[3:5]:
            copy.wait()

    cot = cot_ref[...]
    w_down = jnp.concatenate([w_down_ref[pl.ds(i, LANES), :] for i in at], axis=0)
    cdf = 0.5 * (1.0 + lax.erf(u * np.float32(np.sqrt(0.5))))
    active = u * cdf
    active_low = active.astype(low)
    slope = cdf + u * jnp.exp(-0.5 * u * u) * np.float32(1.0 / np.sqrt(2.0 * np.pi))
    du = (mm_nt(cot, w_down) * slope).astype(low)
    part_acc[...] += mm(active_low, w_down)
    back_acc[...] += mm_nt(du, w_up)
    d_b_up = jnp.sum(du.astype(full), axis=0, keepdims=True)
    up = mm(h2_turned[...], du).astype(low)
    down = mm(active.T.astype(low), cot).astype(low)
    depth = up.shape[0]

    def put(b, grad_ref):
        grad_ref[:depth] = up[:, b * LANES : (b + 1) * LANES]
        for t in range(down.shape[1] // LANES):
            grad_ref[depth + t * LANES : depth + (t + 1) * LANES] = down[
                b * LANES : (b + 1) * LANES, t * LANES : (t + 1) * LANES
            ]

    for b in range(2):
        d_b_up_ref[:, pl.ds(at[b], LANES)] = d_b_up[:, b * LANES : (b + 1) * LANES]
    put(0, keep_ref)

    @pl.when(step < early)
    def _():
        put(1, early_ref)

    @pl.when(step >= early)
    def _():
        put(1, send_ref)

    @pl.when(step == steps - 1)
    def _():
        copies[5].wait()
        part_ref[...] = part_acc[...]
        back = back_acc[...]
        back_ref[...] = back.astype(low)
        sums_ref[0:1] = jnp.sum(back * xhat_ref[...], axis=0, keepdims=True)
        sums_ref[1:2] = jnp.sum(back, axis=0, keepdims=True)


def mlp(ids, early, *given):
    rows, width = given[0].shape
    hidden_units = given[1].shape[1]
    steps = hidden_units // LANES // 2
    whole = lambda shape: pl.BlockSpec(shape, lambda f, c: (0,) * len(shape))
    grads = lambda at: pl.BlockSpec((2 * width, LANES), lambda f, c: (at(f), 0))
    outs = [
        shape_of((rows, width), full),
        shape_of((rows, width), low),
        shape_of((2, width), full),
        shape_of((1, hidden_units), full),
        shape_of((steps * 2 * width, LANES), low),
        shape_of((early * 2 * width, LANES), low),
        shape_of(((steps - early) * 2 * width, LANES), low),
    ]
    return pl.pallas_call(
        functools.partial(mlp_kernel, early),
        grid_spec=pltpu.PrefetchScalarGridSpec(
            num_scalar_prefetch=1,
            grid=(steps,),
            in_specs=[spec_hbm()] * len(given),
            out_specs=[whole(array.shape) for array in outs[:4]]
            + [
                grads(lambda f: f),
                grads(lambda f: jnp.minimum(f, early - 1)),
                grads(lambda f: jnp.maximum(f - early, 0)),
            ],
            scratch_shapes=[
                pltpu.VMEM((width, rows), low),
                pltpu.VMEM((rows, width), full),
                pltpu.VMEM((rows, width), full),
            ]
            + [pltpu.VMEM(array.shape, array.dtype) for array in given]
            + [pltpu.SemaphoreType.DMA((len(given),))],
        ),
        out_shape=outs,
        compiler_params=params(60),
        cost_estimate=pl.CostEstimate(
            flops=12 * rows * width * hidden_units, bytes_accessed=20 * MIB, transcendentals=0
        ),
        name="feed_forward",
    )(ids, *given)


def attention_kernel(heads, group, places, is_first, is_last, pair_ref, inv_ref, token_ref, *rest):
    del token_ref
    if is_first:
        got_ref, rest = rest[0], rest[1:]
        if group > 1:
            other_ref, rest = rest[0], rest[1:]
    else:
        rest = rest[4:]
    out_ref, rest = rest[0], rest[1:]
    if is_last:
        d_own_ref, rest = rest[0], rest[1:]
        if group > 1:
            d_other_ref, rest = rest[0], rest[1:]
    (values_keys, turned_keys, sums, queries), rest = rest[:4], rest[4:]
    token_out, rest = rest[0], rest[1:]
    weights_in, weights_out, stored, peaks, totals, weighted, finals, block_cos, block_sin = rest
    token_out[...] = jnp.zeros_like(token_out)

    rows = queries.shape[1]
    owners = pair_ref.shape[0]
    total_blocks = 2 * owners
    per_chunk = KEYS // BLOCK
    tasks = (total_blocks + 1 + per_chunk - 1) // per_chunk
    me = lax.axis_index("ctx")
    own_sub = lax.rem(me, group)

    def blocks_of(r, d):
        owner = r * group + lax.rem(own_sub + d, group)
        pair = pair_ref[owner]
        return pair, total_blocks - 1 - pair

    def place(tile, block):
        at = pl.multiple_of(block * BLOCK, BLOCK)
        values_keys[pl.ds(at, BLOCK), :] = tile
        turned_keys[:, pl.ds(at, BLOCK)] = turn(tile)

    if is_first:
        for r in range(heads):
            queries[r] = got_ref[r, :, :LANES]
            for half, block in enumerate(blocks_of(r, 0)):
                place(got_ref[r, half * BLOCK : (half + 1) * BLOCK, LANES:], block)
            for d in range(1, group):
                for half, block in enumerate(blocks_of(r, d)):
                    at = r * rows + half * BLOCK
                    place(other_ref[d - 1, at : at + BLOCK, :], block)
        sums[...] = jnp.zeros_like(sums)

    lane = lane_ids((BLOCK, LANES))
    left = lane < HEAD_DIM
    in_key = lane - HEAD_DIM
    moving = (in_key >= 0) & (in_key < ROT)
    forward = (in_key >= 0) & (in_key < HALF)
    cos_row, sin_row, block_cos[...], block_sin[...] = block_tables(inv_ref[...], row_ids(block_cos.shape))

    def rotated_back(tile, block):
        cos_at, sin_at = block_cos[pl.ds(block, 1), :], block_sin[pl.ds(block, 1), :]
        cosine = jnp.where(moving, cos_row * cos_at - sin_row * sin_at, 1.0)
        sine = sin_row * cos_at + cos_row * sin_at
        sine = jnp.where(moving, jnp.where(forward, sine, -sine), 0.0)
        return tile * cosine + rotary_partner(tile) * sine

    offset = row_ids((BLOCK, BLOCK)) - lane_ids((BLOCK, BLOCK))

    def one_pair(i, carry):
        blocks = blocks_of(places[0] + i, 0)
        first = blocks[0] // per_chunk + 1
        for half in range(2):
            both = queries[places[0] + i, half * BLOCK : (half + 1) * BLOCK, :]
            both_turned = turn(both)
            upper = row_ids((LANES, BLOCK)) < HEAD_DIM
            zero = jnp.zeros_like(both_turned)
            weights_in[half, :, :BLOCK] = jnp.where(upper, both_turned, zero)
            weights_in[half, :, BLOCK:] = jnp.where(upper, zero, both_turned)
            weights_out[half, :BLOCK, :] = jnp.where(left, both, zero)
            weights_out[half, BLOCK:, :] = jnp.where(left, zero, both)
        finals[...] = jnp.zeros_like(finals)

        def task(t):
            is_low = t < first
            chunk = jnp.where(is_low, first - 1 - t, t - first)
            return is_low, chunk

        runs = KEYS // BLOCK
        for t in range(tasks):
            is_low, chunk = task(t)
            weights = weights_in[jnp.where(is_low, 0, 1)]
            for u in range(runs):
                at = pl.multiple_of(chunk * KEYS + u * BLOCK, BLOCK)
                sub = slice(u * BLOCK, (u + 1) * BLOCK)
                both = mm(values_keys[pl.ds(at, BLOCK), :], weights)
                grads = both[:, :BLOCK]
                scores = both[:, BLOCK:]
                if t in (0, tasks - 1):
                    query_at = blocks[0 if t == 0 else 1] * BLOCK
                    scores = jnp.where(offset <= query_at - at, scores, masked_score)
                peak = jnp.max(scores, axis=0, keepdims=True)
                raised = jnp.exp(scores - peak)
                stored[t, sub, :BLOCK] = raised
                stored[t, sub, BLOCK:] = grads
                line = t * runs + u
                peaks[line : line + 1] = peak
                totals[line : line + 1] = jnp.sum(raised, axis=0, keepdims=True)
                weighted[line : line + 1] = jnp.sum(raised * grads, axis=0, keepdims=True)

        in_low = row_ids((tasks * runs, BLOCK)) < first * runs

        def finish(mine):
            top = jnp.max(jnp.where(mine, peaks[...], masked_score), axis=0, keepdims=True)
            factor = jnp.where(mine, jnp.exp(peaks[...] - top), 0.0)
            inverse = 1.0 / jnp.sum(totals[...] * factor, axis=0, keepdims=True)
            return factor * inverse, jnp.sum(weighted[...] * factor, axis=0, keepdims=True) * inverse

        (low_factor, low_delta), (high_factor, high_delta) = finish(in_low), finish(jnp.logical_not(in_low))
        peaks[...] = low_factor + high_factor

        for t in range(tasks):
            is_low, chunk = task(t)
            half = jnp.where(is_low, 0, 1)
            weights = weights_out[half]
            delta = jnp.where(is_low, low_delta, high_delta)
            parts = []
            for u in range(runs):
                sub = slice(u * BLOCK, (u + 1) * BLOCK)
                probs = stored[t, sub, :BLOCK] * peaks[t * runs + u : t * runs + u + 1]
                d_scores = probs * (stored[t, sub, BLOCK:] - delta)
                both = jnp.concatenate([probs, d_scores], axis=1).astype(low)
                at = pl.multiple_of(chunk * KEYS + u * BLOCK, BLOCK)
                sums[pl.ds(at, BLOCK), :] += mm(both, weights)
                parts.append(both)
            at = pl.multiple_of(chunk * KEYS, KEYS)
            finals[half] += mm(turned_keys[:, pl.ds(at, KEYS)], jnp.concatenate(parts, axis=0))

        for half in range(2):
            both = jnp.concatenate(
                [finals[half, :HEAD_DIM, :BLOCK], finals[half, HEAD_DIM:, BLOCK:] * score_scale], axis=0
            ).T
            out_ref[i, half * BLOCK : (half + 1) * BLOCK, :] = rotated_back(both, blocks[half]).astype(low)
        return carry

    lax.fori_loop(0, len(places), one_pair, 0)

    if is_last:
        for r in range(heads):
            for d in range(group):
                for half, block in enumerate(blocks_of(r, d)):
                    at = r * rows + half * BLOCK
                    tile = rotated_back(sums[pl.ds(pl.multiple_of(block * BLOCK, BLOCK), BLOCK), :], block)
                    if d == 0:
                        d_own_ref[at : at + BLOCK, :] = tile
                    else:
                        d_other_ref[d - 1, at : at + BLOCK, :] = tile


def attention(heads, group, places, pair_of, inverse, token, got, other, state):
    is_first, is_last = state is None, places[-1] == heads - 1
    rows = got.shape[1]
    owners = pair_of.shape[0]
    total_keys = owners * rows
    tasks = (2 * owners + KEYS // BLOCK) // (KEYS // BLOCK)
    operands = [pair_of, inverse, token]
    outs = [shape_of((len(places), rows, LANES), low)]
    if is_first:
        operands += [got] if other is None else [got, other]
    else:
        operands += list(state)
    if is_last:
        outs.append(shape_of((heads * rows, LANES), full))
        if group > 1:
            outs.append(shape_of((group - 1, heads * rows, LANES), full))
    kept = [
        shape_of((total_keys, LANES), low),
        shape_of((LANES, total_keys), low),
        shape_of((total_keys, LANES), full),
        shape_of((heads, rows, LANES), low),
    ]
    aliases = {} if is_first else {len(operands) - 4 + i: len(outs) + i for i in range(4)}
    found = pl.pallas_call(
        functools.partial(attention_kernel, heads, group, places, is_first, is_last),
        out_shape=outs + kept + [shape_of((1, LANES), full)],
        in_specs=[spec_smem()] + [spec_vmem()] * (len(operands) - 1),
        out_specs=[spec_vmem()] * (len(outs) + 5),
        input_output_aliases=aliases,
        scratch_shapes=[
            pltpu.VMEM((2, LANES, 2 * BLOCK), low),
            pltpu.VMEM((2, 2 * BLOCK, LANES), low),
            pltpu.VMEM((tasks, KEYS, 2 * BLOCK), full),
            pltpu.VMEM((tasks * KEYS // BLOCK, BLOCK), full),
            pltpu.VMEM((tasks * KEYS // BLOCK, BLOCK), full),
            pltpu.VMEM((tasks * KEYS // BLOCK, BLOCK), full),
            pltpu.VMEM((2, LANES, 2 * BLOCK), full),
            pltpu.VMEM((2 * owners, LANES), full),
            pltpu.VMEM((2 * owners, LANES), full),
        ],
        compiler_params=params(6 + total_keys * 5 * 256 // MIB),
        cost_estimate=pl.CostEstimate(
            flops=2_500_000_000 * len(places), bytes_accessed=2 * MIB, transcendentals=0
        ),
        name="attention",
    )(*operands)
    return found[0], found[1 : len(outs)], found[len(outs) : len(outs) + 4], found[-1]


def combine_kernel(heads, terms, *refs):
    out_ref = refs[-1]
    rows = out_ref.shape[1]
    for r in range(heads):
        cut = slice(r * rows, (r + 1) * rows)
        total = refs[0][cut, :]
        for term in refs[1:terms]:
            total = total + term[cut, :]
        out_ref[r, :, LANES:] = total.astype(low)
    at = 0
    for first_ref in refs[terms:-1]:
        out_ref[at : at + first_ref.shape[0], :, :LANES] = first_ref[...]
        at += first_ref.shape[0]


def combine(heads, terms, firsts):
    rows = firsts[0].shape[1]
    return pl.pallas_call(
        functools.partial(combine_kernel, heads, len(terms)),
        out_shape=shape_of((heads, rows, 2 * LANES), low),
        in_specs=[spec_vmem()] * (len(firsts) + len(terms)),
        out_specs=spec_vmem(),
        compiler_params=params(24),
        cost_estimate=pl.CostEstimate(flops=10**7, bytes_accessed=3 * MIB, transcendentals=0),
        name="combine",
    )(*terms, *firsts)


def weight_grads_kernel(
    heads, early, ids_ref, got_ref, h1_ref, cot_ref, low_ref, d_b_ref, keep_ref, early_ref, send_ref, token_ref, grads
):
    chips, chunk_rows = keep_ref.shape[:2]

    def put(at, tile):
        step = min(chunk_rows, tile.shape[0])
        for off in range(0, tile.shape[0], step):
            chunk, inside = divmod(at + off, chunk_rows)
            grads[chunk, inside : inside + step] = tile[off : off + step]

    rows = h1_ref.shape[0]
    left = lane_ids((rows, LANES)) < HEAD_DIM
    for i in range(heads // 2):
        cut = slice(i * LANES, (i + 1) * LANES)
        for first, second, half in ((0, 1, slice(0, LANES)), (3, 2, slice(LANES, 2 * LANES))):
            a, b = got_ref[2 * i, :, half].astype(full), got_ref[2 * i + 1, :, half].astype(full)
            low_ref[first, :, cut] = jnp.where(left, a, pltpu.roll(b, HEAD_DIM, 1)).astype(low)
            low_ref[second, :, cut] = jnp.where(left, pltpu.roll(a, HEAD_DIM, 1), b).astype(low)
    h1_turned = turn(h1_ref[...])
    depth, tiles = h1_turned.shape[0], heads // 2
    for s in range(3):
        d_proj = low_ref[1 + s]
        d_b_ref[s : s + 1] = jnp.sum(d_proj.astype(full), axis=0, keepdims=True)
        grad = mm(h1_turned, d_proj).astype(low)
        for t in range(tiles):
            put((s * tiles + t) * depth, grad[:, t * LANES : (t + 1) * LANES])
    grad = mm(turn(low_ref[0]), cot_ref[...]).astype(low)
    height = grad.shape[0]
    for t in range(depth // LANES):
        put(3 * tiles * depth + t * height, grad[:, t * LANES : (t + 1) * LANES])
    for t in range(chips):
        target = early_ref.at[t] if t < early else send_ref.at[t - early]
        target[...] = grads[ids_ref[chips + t]]
        keep_ref[t] = grads[ids_ref[t]]
    token_ref[...] = jnp.zeros_like(token_ref)


def weight_grads(heads, early, ids, got, h1, cot):
    rows, width = h1.shape
    local_width = heads * HEAD_DIM
    chips = ids.shape[0] // 2
    chunk_rows = 4 * width * local_width // LANES // (2 * chips)
    outs = [
        shape_of((4, rows, local_width), low),
        shape_of((3, local_width), full),
        shape_of((chips, chunk_rows, LANES), low),
        shape_of((early, chunk_rows, LANES), low),
        shape_of((chips - early, chunk_rows, LANES), low),
        shape_of((1, LANES), full),
    ]
    return pl.pallas_call(
        functools.partial(weight_grads_kernel, heads, early),
        out_shape=outs,
        in_specs=[spec_smem()] + [spec_vmem()] * 3,
        out_specs=[spec_vmem()] * len(outs),
        scratch_shapes=[pltpu.VMEM((2 * chips, chunk_rows, LANES), low)],
        compiler_params=params(20),
        cost_estimate=pl.CostEstimate(
            flops=8 * rows * width * local_width, bytes_accessed=8 * MIB, transcendentals=0
        ),
        name="weight_grads",
    )(ids, got, h1, cot)


def return_kernel(low_ref, part_ref, w_out_ref, w_qkv_ref, xhat_ref, e2_ref, both_ref, sums_ref):
    rows = xhat_ref.shape[0]
    both_ref[:rows] = (part_ref[...] + mm(low_ref[0], w_out_ref[...])).astype(low)
    back = mm_nt(low_ref[1], w_qkv_ref[0]) + mm_nt(low_ref[2], w_qkv_ref[1]) + mm_nt(low_ref[3], w_qkv_ref[2])
    both_ref[rows : 2 * rows] = back.astype(low)
    both_ref[2 * rows :] = e2_ref[...]
    sums_ref[0:1] = jnp.sum(back * xhat_ref[...], axis=0, keepdims=True)
    sums_ref[1:2] = jnp.sum(back, axis=0, keepdims=True)


def back_projections(*given):
    rows, width = given[1].shape
    return pl.pallas_call(
        return_kernel,
        out_shape=[shape_of((3 * rows, width), low), shape_of((2, width), full)],
        in_specs=[spec_vmem()] * len(given),
        out_specs=[spec_vmem()] * 2,
        compiler_params=params(16),
        cost_estimate=pl.CostEstimate(
            flops=8 * rows * width * given[2].shape[0], bytes_accessed=8 * MIB, transcendentals=0
        ),
        name="back_projections",
    )(*given)


def finish_kernel(
    hidden_ref, cot_ref, xhat_ref, std_ref, gains_ref, bias_ref, ours_ref, theirs_ref, out_ref, grad_ref, token_ref
):
    rows = hidden_ref.shape[0]
    gains = gains_ref[...]
    biases = bias_ref[...]
    summed = ours_ref[:rows].astype(full) + theirs_ref[:rows].astype(full)
    out_ref[...] = (hidden_ref[...].astype(full) + summed + biases[0:1] + biases[1:2]).astype(low)
    e1 = ours_ref[rows : 2 * rows].astype(full) + theirs_ref[rows : 2 * rows].astype(full)
    e2 = ours_ref[2 * rows :].astype(full) + theirs_ref[2 * rows :].astype(full)
    f = e1 * gains[0:1] + e2 * gains[1:2]
    xhat = xhat_ref[...]
    inv_std = std_ref[:, 0:1]
    grad_ref[...] = cot_ref[...].astype(full) + inv_std * (
        f - jnp.mean(f, axis=-1, keepdims=True) - xhat * jnp.mean(f * xhat, axis=-1, keepdims=True)
    )
    token_ref[...] = jnp.zeros_like(token_ref)


def finish(*operands):
    rows, width = operands[0].shape
    return pl.pallas_call(
        finish_kernel,
        out_shape=[shape_of((rows, width), low), shape_of((rows, width), full), shape_of((1, LANES), full)],
        in_specs=[spec_vmem()] * len(operands),
        out_specs=[spec_vmem()] * 3,
        compiler_params=params(24),
        cost_estimate=pl.CostEstimate(flops=10**7, bytes_accessed=8 * MIB, transcendentals=0),
        name="finish",
    )(*operands)


def to_attention(width, local_width, source, refs, base, unit):
    qkv_ref, out_ref = refs
    tiles = local_width // LANES
    split = 3 * tiles * width
    tile = base // width
    row = pl.multiple_of(lax.rem(base, width), unit)
    column = pl.multiple_of(lax.rem(tile, tiles) * LANES, LANES)
    yield base < split, source, qkv_ref.at[jnp.minimum(tile // tiles, 2), pl.ds(row, unit), pl.ds(column, LANES)]
    after = jnp.maximum(base - split, 0)
    row = pl.multiple_of(lax.rem(after, local_width), unit)
    column = pl.multiple_of(after // local_width * LANES, LANES)
    yield base >= split, source, out_ref.at[pl.ds(row, unit), pl.ds(column, LANES)]


def to_mlp(width, source, refs, base, unit):
    up_ref, down_ref = refs
    block, inside = base // (2 * width), lax.rem(base, 2 * width)
    block_at = pl.multiple_of(block * LANES, LANES)
    row = pl.multiple_of(jnp.minimum(inside, width - unit), unit)
    yield inside < width, source, up_ref.at[pl.ds(row, unit), pl.ds(block_at, LANES)]
    for t in range(unit // LANES):
        column = pl.multiple_of(jnp.maximum(inside - width, 0) + t * LANES, LANES)
        cut = source.at[pl.ds(t * LANES, LANES), :]
        yield inside >= width, cut, down_ref.at[pl.ds(block_at, LANES), pl.ds(column, LANES)]


def unpack_kernel(route, count, unit, joined, has_old, keeps, ids_ref, *rest):
    if joined:
        rows = rest[0].shape[0] // count
        parts, rest = [rest[0].at[pl.ds(i * rows, rows), :] for i in range(count)], rest[1:]
    else:
        parts, rest = rest[:count], rest[count:]
    rest = rest[2:] if has_old else rest
    targets, rest = rest[:2], rest[2:]
    if keeps:
        packed_ref, rest = rest[0], rest[1:]
    token_ref, held, sems = rest
    token_ref[...] = jnp.zeros_like(token_ref)
    chunk_rows = parts[0].shape[0]
    units = chunk_rows // unit
    per_unit = (sems.shape[0] - (count if keeps else 0)) // (count * units)
    kept = []
    if keeps:
        for i in range(count):
            target = packed_ref.at[pl.ds(i * chunk_rows, chunk_rows), :]
            kept.append(pltpu.make_async_copy(parts[i], target, sems.at[count * units * per_unit + i]))
            kept[i].start()

    def moves():
        for i in range(count):
            for j in range(units):
                source = held.at[i, pl.ds(j * unit, unit), :]
                base = ids_ref[i] * chunk_rows + j * unit
                for n, (applies, piece, target) in enumerate(route(source, targets, base, unit)):
                    sem = sems.at[(i * units + j) * per_unit + n]
                    yield i, applies, pltpu.make_async_copy(piece, target, sem)

    done = -1
    for i, applies, copy in moves():
        if i != done:
            held[i] = parts[i][...].astype(full)
            done = i
        pl.when(applies)(copy.start)
    for i, applies, copy in moves():
        pl.when(applies)(copy.wait)
    for copy in kept:
        copy.wait()


def unpack(name, route, cases, unit, shapes, ids, parts, old, keeps=False):
    count = ids.shape[0]
    joined = len(parts) < count
    chunk_rows = parts[0].shape[0] // (count if joined else 1)
    operands = [ids, *parts, *(old or ())]
    outs = [shape_of(shape, full) for shape in shapes]
    if keeps:
        outs.append(shape_of((count * chunk_rows, LANES), low))
    return pl.pallas_call(
        functools.partial(unpack_kernel, route, count, unit, joined, old is not None, keeps),
        out_shape=outs + [shape_of((1, LANES), full)],
        in_specs=[spec_smem()] + [spec_vmem()] * len(parts) + [spec_hbm()] * (len(operands) - 1 - len(parts)),
        out_specs=[spec_hbm()] * len(outs) + [spec_vmem()],
        input_output_aliases={} if old is None else {1 + len(parts): 0, 2 + len(parts): 1},
        scratch_shapes=[
            pltpu.VMEM((count, chunk_rows, LANES), full),
            pltpu.SemaphoreType.DMA((count * (chunk_rows // unit) * cases + (count if keeps else 0),)),
        ],
        compiler_params=params(8 + count * chunk_rows * 3 * LANES * 2 // MIB),
        cost_estimate=pl.CostEstimate(
            flops=10**6, bytes_accessed=count * chunk_rows * LANES * 6, transcendentals=0
        ),
        name=name,
    )(*operands)


def local(
    hidden,
    pair_of,
    ln1_gain,
    ln1_bias,
    ln2_gain,
    ln2_bias,
    w_qkv,
    b_qkv,
    w_out,
    b_out,
    w_up,
    b_up,
    w_down,
    b_down,
    cotangent,
):
    owners = lax.axis_size("ctx")
    sides = lax.axis_size("tp")
    rows, width = hidden.shape
    local_width = w_qkv.shape[2]
    hidden_units = w_up.shape[1]
    heads = local_width // HEAD_DIM
    group = owners // heads

    exponent = np.arange(0, ROT, 2, dtype=np.float32) / np.float32(ROT)
    inverse = jnp.asarray(np.tile(np.float32(10000.0) ** (-exponent), LANES // HALF)[None, :], full)
    order = (0, 2, 4, 6, 7, 5, 3, 1) if owners == 16 else tuple(range(owners // 2))
    chips = len(order)

    def to_heads(array):
        groups = [[h * group + g for h in range(heads)] for g in range(group)]
        return lax.all_to_all(array, "ctx", 0, 0, axis_index_groups=groups, tiled=True)

    def group_shift(array, d):
        pairs = [(c, c // group * group + (c % group + d) % group) for c in range(owners)]
        return lax.ppermute(array, "ctx", pairs)

    me = lax.axis_index("ctx")
    chip, core = me // 2, lax.rem(me, 2)
    place = sum(jnp.where(chip == c, i, 0) for i, c in enumerate(order))
    way = 1 - 2 * core
    far, near = chips // 2, chips - 1 - chips // 2

    def ring(array, forward):
        pairs = []
        for i, c in enumerate(order):
            for k in range(2):
                step = 1 if (k == 0) == forward else -1
                pairs.append((2 * c + k, 2 * order[(i + step) % chips] + k))
        return lax.ppermute(array, "ctx", pairs)

    def other_core(array):
        return lax.ppermute(array, "ctx", [(c, c ^ 1) for c in range(owners)])

    def across(array):
        return lax.ppermute(array, "tp", [(t, (t + 1) % sides) for t in range(sides)])

    def target(distance):
        return lax.rem(place + way * distance + chips, chips)

    def zero(array):
        return array[:1].astype(full) * 0.0

    slots = [far, -near]
    for t in range(1, far):
        slots += [far - t] if t >= near else [far - t, t - near]
    slots.append(0)
    early = 2
    slot_ids = jnp.stack(
        [core * chips + target(d) for d in slots] + [(1 - core) * chips + target(-d) for d in slots]
    )

    def terms_of(keep, came):
        def term(i):
            return keep[i].astype(full) + came[i].astype(full)

        return {d: term(i) for i, d in enumerate(slots)}

    def scatter_start(terms, token):
        return (terms[far] + token).astype(low), (terms[-near] + token).astype(low)

    def scatter_send(t, sends):
        long_send, short_send = sends
        return ring(long_send, True), (ring(short_send, False) if t < near else short_send)

    def scatter_add(terms, t, came, token):
        long_got = came[0].astype(full) + token
        last = t == far - 1
        long_next = long_got if last else (long_got + terms[far - 1 - t]).astype(low)
        short_next = came[1]
        if t < near:
            short_got = came[1].astype(full) + token
            short_next = short_got if t == near - 1 else (short_got + terms[t + 1 - near]).astype(low)
        if last:
            return (terms[0] + long_next + short_next).astype(low)
        return long_next, short_next

    def scatter_step(terms, t, sends, token):
        return scatter_add(terms, t, scatter_send(t, sends), token)

    base, other_base = core * chips, (1 - core) * chips

    def gather_start(own):
        return [(own, base + place), (other_core(own), other_base + place)]

    def gather_step(t, sends, token):
        long_send, short_send = sends
        if token is not None:
            long_send = (long_send.astype(full) + token).astype(low)
        long_got = ring(long_send, True)
        found = [(long_got, base + target(-t - 1)), (other_core(long_got), other_base + target(t + 1))]
        short_got = short_send
        if t < near:
            short_got = ring(short_send, False)
            found += [(short_got, base + target(t + 1)), (other_core(short_got), other_base + target(-t - 1))]
        return (long_got, short_got), found

    blocks = hidden_units // LANES // 2
    in_slots = blocks == chips
    mlp_ids = slot_ids if in_slots else jnp.concatenate(
        [core * blocks + jnp.arange(blocks), (1 - core) * blocks + jnp.arange(blocks)]
    )
    h1, h2, xhat, inv_std, d_bias, gains, biases, b_up_row, packed = project(
        heads,
        pair_of,
        inverse,
        (hidden, ln1_gain, ln1_bias, ln2_gain, ln2_bias, cotangent, w_out, w_qkv, b_qkv, b_up, b_out, b_down),
    )
    got = to_heads(packed)
    part, back2, sums2, d_b_up, keep_mlp, early_mlp, send_mlp = mlp(
        mlp_ids.astype(jnp.int32), early, h2, w_up, b_up_row, cotangent, w_down, xhat
    )
    chunk = keep_mlp.shape[0] // chips
    came_mlp = jnp.concatenate([other_core(early_mlp), other_core(send_mlp)]) if not in_slots else None
    if in_slots:
        halves = [other_core(array).reshape(-1, chunk, LANES) for array in (early_mlp, send_mlp)]
        came_mlp = [half[i] for half in halves for i in range(half.shape[0])]
        terms_mlp = terms_of(keep_mlp.reshape(chips, chunk, LANES), came_mlp)
    else:
        summed = (keep_mlp.astype(full) + came_mlp.astype(full)).reshape(chips, chunk, LANES)
        terms_mlp = {d: lax.dynamic_index_in_dim(summed, target(d), 0, keepdims=False) for d in slots}
    nothing = jnp.zeros((1, LANES), full)

    other = None
    if group > 1:
        mine = got[:, :, LANES:].reshape(heads * rows, LANES)
        other = jnp.stack([group_shift(mine, group - d) for d in range(1, group)])

    middle = heads // 4
    first, _, state, token = attention(
        heads, group, tuple(range(middle)), pair_of, inverse, sums2, got, other, None
    )
    sends_mlp = scatter_start(terms_mlp, token)
    token = zero(sends_mlp[0]) + zero(sends_mlp[1])
    second, ends, _, token = attention(
        heads, group, tuple(range(middle, heads)), pair_of, inverse, token, got, other, state
    )
    d_own, d_other = ends[0], (ends[1] if group > 1 else None)
    terms = [d_own] + [group_shift(d_other[d - 1], d) for d in range(1, group)]
    sends_mlp = scatter_step(terms_mlp, 0, sends_mlp, token)
    first = (first.astype(full) + zero(sends_mlp[0]) + zero(sends_mlp[1])).astype(low)
    backs = to_heads(combine(heads, terms, [first, second]))
    sends_mlp = scatter_step(terms_mlp, 1, sends_mlp, nothing)
    h1_later = (h1.astype(full) + (zero(sends_mlp[0]) + zero(sends_mlp[1]))[:, :1]).astype(low)

    lows, d_b_qkv, keep, early_att, send_att, after = weight_grads(
        heads, early, slot_ids.astype(jnp.int32), backs, h1_later, cotangent
    )
    both, sums1 = back_projections(lows, part, w_out, w_qkv, xhat, back2)
    theirs = across(both)
    output, d_hidden, finish_token = finish(
        hidden, cotangent, xhat, inv_std, gains, biases, both, theirs
    )
    halves = [other_core(array) for array in (early_att, send_att)]
    terms_att = terms_of(keep, [half[i] for half in halves for i in range(half.shape[0])])

    small = jnp.concatenate(
        [sums1.reshape(1, -1), sums2.reshape(1, -1), d_bias, d_b_up, d_b_qkv.reshape(1, -1)], axis=1
    )

    def unpack_some(name, route, cases, unit, shapes, found, old):
        parts, ids = zip(*found)
        *old, token = unpack(name, route, cases, unit, shapes, jnp.stack(ids), parts, old)
        return old, token

    unit_mlp = min(chunk, local_width)
    unit_att = min(keep.shape[1], local_width)
    unpack_mlp = functools.partial(
        unpack,
        "unpack_feed_forward",
        functools.partial(to_mlp, width),
        1 + unit_mlp // LANES,
        unit_mlp,
        ((width, hidden_units), (hidden_units, width)),
    )
    unpack_att = functools.partial(
        unpack_some,
        "unpack_attention",
        functools.partial(to_attention, width, local_width),
        2,
        unit_att,
        ((3, width, local_width), (local_width, width)),
    )

    steps_mlp, steps_round = iter(range(2, far)), iter(range(far))
    own_mlp, round_mlp, waiting = None, None, []

    def advance_mlp(token, gate=None):
        nonlocal sends_mlp, own_mlp, round_mlp, waiting
        t = next(steps_mlp, None)
        if t is not None:
            sends_mlp = scatter_step(terms_mlp, t, sends_mlp, token)
            if t < far - 1:
                return zero(sends_mlp[0])
            own_mlp, round_mlp = sends_mlp, (sends_mlp, sends_mlp)
            waiting.append((own_mlp, base + place, other_base + place))
            return zero(own_mlp)
        t = next(steps_round, None)
        if t is None:
            return nothing
        long_send, short_send = round_mlp
        if gate is not None:
            long_send = (long_send.astype(full) + gate).astype(low)
        long_got = ring(long_send, True)
        waiting.append((long_got, base + target(-t - 1), other_base + target(t + 1)))
        short_got = short_send
        if t < near:
            short_got = ring(short_send, False)
            waiting.append((short_got, base + target(t + 1), other_base + target(-t - 1)))
        round_mlp = (long_got, short_got)
        return zero(round_mlp[0])

    sends_att = scatter_start(terms_att, nothing)
    before = nothing
    for t in range(far):
        later = advance_mlp(after)
        sends_att = scatter_step(terms_att, t, sends_att, before)
        before = later
    round_att, waiting_att, grads_att = (sends_att, sends_att), gather_start(sends_att), None
    small = small + zero(sends_att)[:, :1]
    distance = 1
    for t in range(far):
        advance_mlp(after, zero(round_att[0]))
        round_att, found = gather_step(t, round_att, None)
        waiting_att += found
        if distance < owners:
            small = small + lax.ppermute(small, "ctx", [(c, c ^ distance) for c in range(owners)])
            distance *= 2
        if t == 1:
            small = small + finish_token[:, :1]
        if t == far - 2:
            parts, ids, other_ids = zip(*waiting)
            *halves, packed_mlp, more = unpack_mlp(jnp.stack(ids), parts, None, True)
            small = small + more[:, :1]
            theirs_mlp = other_core(packed_mlp)
            grads_att, more = unpack_att(waiting_att[:-4], None)
            waiting_att = waiting_att[-4:]
            small = small + more[:, :1]
    while distance < owners:
        small = small + lax.ppermute(small, "ctx", [(c, c ^ distance) for c in range(owners)])
        distance *= 2
    d_w_up, d_w_down, _ = unpack_mlp(jnp.stack(other_ids), [theirs_mlp], halves)
    grads_att, _ = unpack_att(waiting_att, grads_att)

    norm_sums = small[:, : 4 * width]
    norm_sums = (norm_sums + across(norm_sums)).reshape(4, width)
    at = 4 * width
    d_bias = small[0, at : at + width]
    d_b_up = small[0, at + width : at + width + hidden_units]
    d_b_qkv = small[0, at + width + hidden_units :].reshape(3, local_width)
    d_w_qkv, d_w_out = grads_att
    return (
        output,
        d_hidden,
        norm_sums[0],
        norm_sums[1],
        norm_sums[2],
        norm_sums[3],
        d_w_qkv,
        d_b_qkv,
        d_w_out,
        d_bias,
        d_w_up,
        d_b_up,
        d_w_down,
        d_bias,
    )


def solution(mesh):
    placed = (
        P("ctx", None),
        P(),
        P(),
        P(),
        P(),
        P(),
        P(None, None, "tp"),
        P(None, "tp"),
        P("tp", None),
        P(),
        P(None, "tp"),
        P("tp"),
        P("tp", None),
        P(),
        P("ctx", None),
    )
    return jax.shard_map(
        local,
        mesh=mesh,
        in_specs=placed,
        out_specs=(
            P("ctx", None),
            P("ctx", None),
            P(),
            P(),
            P(),
            P(),
            P(None, None, "tp"),
            P(None, "tp"),
            P("tp", None),
            P(),
            P(None, "tp"),
            P("tp"),
            P("tp", None),
            P(),
        ),
        check_vma=False,
    )
```

```python
import functools

import jax
import jax.numpy as jnp
import numpy as np
from jax import lax
from jax.experimental import pallas as pl
from jax.experimental.pallas import tpu as pltpu
from jax.sharding import PartitionSpec as P

HEAD_DIM = 64
ROT = 16
HALF = ROT // 2
BLOCK = 128
LANES = 128
KEYS = 512
MIB = 1 << 20

norm_eps = 1e-05
masked_score = -1e30
score_scale = HEAD_DIM ** (-0.5)
low = jnp.bfloat16
full = jnp.float32


def mm(left, right):
    return lax.dot_general(left, right, (((1,), (0,)), ((), ())), preferred_element_type=full)


def mm_nt(left, right):
    return lax.dot_general(left, right, (((1,), (1,)), ((), ())), preferred_element_type=full)


def turn(tensor):
    return tensor.astype(full).T.astype(low)


def lane_ids(shape):
    return lax.broadcasted_iota(jnp.int32, shape, len(shape) - 1)


def row_ids(shape):
    return lax.broadcasted_iota(jnp.int32, shape, len(shape) - 2)


def rotary_partner(tensor):
    lanes = lane_ids(tensor.shape)
    ahead = pltpu.roll(tensor, LANES - HALF, 1)
    behind = pltpu.roll(tensor, HALF, 1)
    return jnp.where(lanes % ROT < HALF, ahead, behind)


def spec_vmem():
    return pl.BlockSpec(memory_space=pltpu.VMEM)


def spec_smem():
    return pl.BlockSpec(memory_space=pltpu.SMEM)


def spec_hbm():
    return pl.BlockSpec(memory_space=pltpu.HBM)


def params(mib):
    return pltpu.CompilerParams(vmem_limit_bytes=mib * MIB)


def shape_of(shape, kind):
    return jax.ShapeDtypeStruct(shape, kind)


def block_tables(inverse, blocks):
    row = row_ids((BLOCK, LANES)).astype(full)
    start = blocks.astype(full) * float(BLOCK)
    return jnp.cos(row * inverse), jnp.sin(row * inverse), jnp.cos(start * inverse), jnp.sin(start * inverse)


def project_kernel(heads, pair_ref, inv_ref, *rest):
    given, rest = rest[:12], rest[12:]
    h1_ref, h2_ref, xhat_ref, std_ref, d_bias_ref, gains_ref, bias_ref, b_up_out_ref, packed = rest[:9]
    held, sems = rest[9:-1], rest[-1]
    copies = [pltpu.make_async_copy(src, dst, sems.at[i]) for i, (src, dst) in enumerate(zip(given, held))]
    for copy in copies:
        copy.start()
    (
        hidden_ref,
        g1_ref,
        c1_ref,
        g2_ref,
        c2_ref,
        cot_ref,
        w_out_ref,
        w_qkv_ref,
        b_qkv_ref,
        b_up_ref,
        b_out_ref,
        b_down_ref,
    ) = held
    rows = hidden_ref.shape[0]
    me = lax.axis_index("ctx")
    pair = pair_ref[me]
    total_blocks = 2 * pair_ref.shape[0]

    first = jnp.where(row_ids((8, LANES)) == 0, pair, total_blocks - 1 - pair)
    inverse = inv_ref[...]
    cos_row, sin_row, cos_block, sin_block = block_tables(inverse, first)
    in_head = lane_ids((BLOCK, LANES)) % HEAD_DIM
    tables = []
    for half in range(2):
        cos_at, sin_at = cos_block[half : half + 1], sin_block[half : half + 1]
        cosine = cos_row * cos_at - sin_row * sin_at
        sine = sin_row * cos_at + cos_row * sin_at
        cosine = jnp.where(in_head < ROT, cosine, 1.0)
        sine = jnp.where(in_head < HALF, -sine, jnp.where(in_head < ROT, sine, 0.0))
        tables.append((cosine, sine))
    cosine = jnp.concatenate([tables[0][0], tables[1][0]], axis=0)
    sine = jnp.concatenate([tables[0][1], tables[1][1]], axis=0)

    for copy in copies[:5]:
        copy.wait()
    x = hidden_ref[...].astype(full)
    centred = x - jnp.mean(x, axis=-1, keepdims=True)
    spread = jnp.mean(centred * centred, axis=-1, keepdims=True)
    inv_std = lax.rsqrt(spread + norm_eps)
    xhat = centred * inv_std
    xhat_ref[...] = xhat
    std_ref[...] = jnp.broadcast_to(inv_std, std_ref.shape)

    def as_row(ref):
        return ref[...].astype(full)[None, :]

    gain1, gain2 = as_row(g1_ref), as_row(g2_ref)
    h1 = (xhat * gain1 + as_row(c1_ref)).astype(low)
    h1_ref[...] = h1
    h2_ref[...] = (xhat * gain2 + as_row(c2_ref)).astype(low)
    gains_ref[0:1] = gain1
    gains_ref[1:2] = gain2
    for copy in copies[5:]:
        copy.wait()
    b_up_out_ref[...] = as_row(b_up_ref)
    bias_ref[0:1] = as_row(b_out_ref)
    bias_ref[1:2] = as_row(b_down_ref)
    d_bias_ref[...] = jnp.sum(cot_ref[...].astype(full), axis=0, keepdims=True)

    lane = lane_ids((rows, LANES))

    def projected(s):
        return mm(h1, w_qkv_ref[s]) + b_qkv_ref[s : s + 1].astype(full)

    def turned(tile):
        return tile * cosine + rotary_partner(tile) * sine

    queries, keys, values = projected(0), projected(1), projected(2)
    grads = mm_nt(cot_ref[...], w_out_ref[...])
    left = lane < HEAD_DIM
    for i in range(heads // 2):
        cut = slice(i * LANES, (i + 1) * LANES)
        q = turned(queries[:, cut]).astype(low).astype(full) * score_scale
        k = turned(keys[:, cut])
        v = values[:, cut]
        g = grads[:, cut]
        packed[2 * i, :, :LANES] = jnp.where(left, g, pltpu.roll(q, HEAD_DIM, 1)).astype(low)
        packed[2 * i, :, LANES:] = jnp.where(left, v, pltpu.roll(k, HEAD_DIM, 1)).astype(low)
        packed[2 * i + 1, :, :LANES] = jnp.where(left, pltpu.roll(g, HEAD_DIM, 1), q).astype(low)
        packed[2 * i + 1, :, LANES:] = jnp.where(left, pltpu.roll(v, HEAD_DIM, 1), k).astype(low)


def project(heads, pair_of, inverse, given):
    hidden, w_out, b_up = given[0], given[6], given[9]
    rows, width = hidden.shape
    outs = [
        shape_of((rows, width), low),
        shape_of((rows, width), low),
        shape_of((rows, width), full),
        shape_of((rows, LANES), full),
        shape_of((1, width), full),
        shape_of((2, width), full),
        shape_of((2, width), full),
        shape_of((1, b_up.shape[0]), full),
        shape_of((heads, rows, 2 * LANES), low),
    ]
    return pl.pallas_call(
        functools.partial(project_kernel, heads),
        out_shape=outs,
        in_specs=[spec_smem(), spec_vmem()] + [spec_hbm()] * len(given),
        out_specs=[spec_vmem()] * len(outs),
        scratch_shapes=[pltpu.VMEM(array.shape, array.dtype) for array in given]
        + [pltpu.SemaphoreType.DMA((len(given),))],
        compiler_params=params(60),
        cost_estimate=pl.CostEstimate(
            flops=2 * rows * width * 4 * w_out.shape[0], bytes_accessed=8 * MIB, transcendentals=0
        ),
        name="project",
    )(pair_of, inverse, *given)


def mlp_kernel(early, ids_ref, *rest):
    given, rest = rest[:6], rest[6:]
    part_ref, back_ref, sums_ref, d_b_up_ref, keep_ref, early_ref, send_ref = rest[:7]
    h2_turned, part_acc, back_acc = rest[7:10]
    held, sems = rest[10:-1], rest[-1]
    copies = [pltpu.make_async_copy(src, dst, sems.at[i]) for i, (src, dst) in enumerate(zip(given, held))]
    h2_held, w_up_ref, b_up, cot_ref, w_down_ref, xhat_ref = held
    step = pl.program_id(0)
    steps = pl.num_programs(0)

    @pl.when(step == 0)
    def _():
        for copy in copies:
            copy.start()
        part_acc[...] = jnp.zeros_like(part_acc)
        back_acc[...] = jnp.zeros_like(back_acc)
        copies[0].wait()
        h2_turned[...] = turn(h2_held[...])
        for copy in copies[1:3]:
            copy.wait()

    at = [pl.multiple_of(ids_ref[b * steps + step] * LANES, LANES) for b in range(2)]
    w_up = jnp.concatenate([w_up_ref[:, pl.ds(i, LANES)] for i in at], axis=1)
    u = mm(h2_held[...], w_up) + jnp.concatenate([b_up[:, pl.ds(i, LANES)] for i in at], axis=1)

    @pl.when(step == 0)
    def _():
        for copy in copies[3:5]:
            copy.wait()

    cot = cot_ref[...]
    w_down = jnp.concatenate([w_down_ref[pl.ds(i, LANES), :] for i in at], axis=0)
    cdf = 0.5 * (1.0 + lax.erf(u * np.float32(np.sqrt(0.5))))
    active = u * cdf
    active_low = active.astype(low)
    slope = cdf + u * jnp.exp(-0.5 * u * u) * np.float32(1.0 / np.sqrt(2.0 * np.pi))
    du = (mm_nt(cot, w_down) * slope).astype(low)
    part_acc[...] += mm(active_low, w_down)
    back_acc[...] += mm_nt(du, w_up)
    d_b_up = jnp.sum(du.astype(full), axis=0, keepdims=True)
    up = mm(h2_turned[...], du).astype(low)
    down = mm(active.T.astype(low), cot).astype(low)
    depth = up.shape[0]

    def put(b, grad_ref):
        grad_ref[:depth] = up[:, b * LANES : (b + 1) * LANES]
        for t in range(down.shape[1] // LANES):
            grad_ref[depth + t * LANES : depth + (t + 1) * LANES] = down[
                b * LANES : (b + 1) * LANES, t * LANES : (t + 1) * LANES
            ]

    for b in range(2):
        d_b_up_ref[:, pl.ds(at[b], LANES)] = d_b_up[:, b * LANES : (b + 1) * LANES]
    put(0, keep_ref)

    @pl.when(step < early)
    def _():
        put(1, early_ref)

    @pl.when(step >= early)
    def _():
        put(1, send_ref)

    @pl.when(step == steps - 1)
    def _():
        copies[5].wait()
        part_ref[...] = part_acc[...]
        back = back_acc[...]
        back_ref[...] = back.astype(low)
        sums_ref[0:1] = jnp.sum(back * xhat_ref[...], axis=0, keepdims=True)
        sums_ref[1:2] = jnp.sum(back, axis=0, keepdims=True)


def mlp(ids, early, *given):
    rows, width = given[0].shape
    hidden_units = given[1].shape[1]
    steps = hidden_units // LANES // 2
    whole = lambda shape: pl.BlockSpec(shape, lambda f, c: (0,) * len(shape))
    grads = lambda at: pl.BlockSpec((2 * width, LANES), lambda f, c: (at(f), 0))
    outs = [
        shape_of((rows, width), full),
        shape_of((rows, width), low),
        shape_of((2, width), full),
        shape_of((1, hidden_units), full),
        shape_of((steps * 2 * width, LANES), low),
        shape_of((early * 2 * width, LANES), low),
        shape_of(((steps - early) * 2 * width, LANES), low),
    ]
    return pl.pallas_call(
        functools.partial(mlp_kernel, early),
        grid_spec=pltpu.PrefetchScalarGridSpec(
            num_scalar_prefetch=1,
            grid=(steps,),
            in_specs=[spec_hbm()] * len(given),
            out_specs=[whole(array.shape) for array in outs[:4]]
            + [
                grads(lambda f: f),
                grads(lambda f: jnp.minimum(f, early - 1)),
                grads(lambda f: jnp.maximum(f - early, 0)),
            ],
            scratch_shapes=[
                pltpu.VMEM((width, rows), low),
                pltpu.VMEM((rows, width), full),
                pltpu.VMEM((rows, width), full),
            ]
            + [pltpu.VMEM(array.shape, array.dtype) for array in given]
            + [pltpu.SemaphoreType.DMA((len(given),))],
        ),
        out_shape=outs,
        compiler_params=params(60),
        cost_estimate=pl.CostEstimate(
            flops=12 * rows * width * hidden_units, bytes_accessed=20 * MIB, transcendentals=0
        ),
        name="feed_forward",
    )(ids, *given)


def attention_kernel(heads, group, places, is_first, is_last, pair_ref, inv_ref, token_ref, *rest):
    del token_ref
    if is_first:
        got_ref, rest = rest[0], rest[1:]
        if group > 1:
            other_ref, rest = rest[0], rest[1:]
    else:
        rest = rest[4:]
    out_ref, rest = rest[0], rest[1:]
    if is_last:
        d_own_ref, rest = rest[0], rest[1:]
        if group > 1:
            d_other_ref, rest = rest[0], rest[1:]
    (values_keys, turned_keys, sums, queries), rest = rest[:4], rest[4:]
    token_out, rest = rest[0], rest[1:]
    weights_in, weights_out, stored, peaks, totals, weighted, finals, block_cos, block_sin = rest
    token_out[...] = jnp.zeros_like(token_out)

    rows = queries.shape[1]
    owners = pair_ref.shape[0]
    total_blocks = 2 * owners
    per_chunk = KEYS // BLOCK
    tasks = (total_blocks + 1 + per_chunk - 1) // per_chunk
    me = lax.axis_index("ctx")
    own_sub = lax.rem(me, group)

    def blocks_of(r, d):
        owner = r * group + lax.rem(own_sub + d, group)
        pair = pair_ref[owner]
        return pair, total_blocks - 1 - pair

    def place(tile, block):
        at = pl.multiple_of(block * BLOCK, BLOCK)
        values_keys[pl.ds(at, BLOCK), :] = tile
        turned_keys[:, pl.ds(at, BLOCK)] = turn(tile)

    if is_first:
        for r in range(heads):
            queries[r] = got_ref[r, :, :LANES]
            for half, block in enumerate(blocks_of(r, 0)):
                place(got_ref[r, half * BLOCK : (half + 1) * BLOCK, LANES:], block)
            for d in range(1, group):
                for half, block in enumerate(blocks_of(r, d)):
                    at = r * rows + half * BLOCK
                    place(other_ref[d - 1, at : at + BLOCK, :], block)
        sums[...] = jnp.zeros_like(sums)

    lane = lane_ids((BLOCK, LANES))
    left = lane < HEAD_DIM
    in_key = lane - HEAD_DIM
    moving = (in_key >= 0) & (in_key < ROT)
    forward = (in_key >= 0) & (in_key < HALF)
    cos_row, sin_row, block_cos[...], block_sin[...] = block_tables(inv_ref[...], row_ids(block_cos.shape))

    def rotated_back(tile, block):
        cos_at, sin_at = block_cos[pl.ds(block, 1), :], block_sin[pl.ds(block, 1), :]
        cosine = jnp.where(moving, cos_row * cos_at - sin_row * sin_at, 1.0)
        sine = sin_row * cos_at + cos_row * sin_at
        sine = jnp.where(moving, jnp.where(forward, sine, -sine), 0.0)
        return tile * cosine + rotary_partner(tile) * sine

    offset = row_ids((BLOCK, BLOCK)) - lane_ids((BLOCK, BLOCK))

    def one_pair(i, carry):
        blocks = blocks_of(places[0] + i, 0)
        first = blocks[0] // per_chunk + 1
        for half in range(2):
            both = queries[places[0] + i, half * BLOCK : (half + 1) * BLOCK, :]
            both_turned = turn(both)
            upper = row_ids((LANES, BLOCK)) < HEAD_DIM
            zero = jnp.zeros_like(both_turned)
            weights_in[half, :, :BLOCK] = jnp.where(upper, both_turned, zero)
            weights_in[half, :, BLOCK:] = jnp.where(upper, zero, both_turned)
            weights_out[half, :BLOCK, :] = jnp.where(left, both, zero)
            weights_out[half, BLOCK:, :] = jnp.where(left, zero, both)
        finals[...] = jnp.zeros_like(finals)

        def task(t):
            is_low = t < first
            chunk = jnp.where(is_low, first - 1 - t, t - first)
            return is_low, chunk

        runs = KEYS // BLOCK
        for t in range(tasks):
            is_low, chunk = task(t)
            weights = weights_in[jnp.where(is_low, 0, 1)]
            for u in range(runs):
                at = pl.multiple_of(chunk * KEYS + u * BLOCK, BLOCK)
                sub = slice(u * BLOCK, (u + 1) * BLOCK)
                both = mm(values_keys[pl.ds(at, BLOCK), :], weights)
                grads = both[:, :BLOCK]
                scores = both[:, BLOCK:]
                if t in (0, tasks - 1):
                    query_at = blocks[0 if t == 0 else 1] * BLOCK
                    scores = jnp.where(offset <= query_at - at, scores, masked_score)
                peak = jnp.max(scores, axis=0, keepdims=True)
                raised = jnp.exp(scores - peak)
                stored[t, sub, :BLOCK] = raised
                stored[t, sub, BLOCK:] = grads
                line = t * runs + u
                peaks[line : line + 1] = peak
                totals[line : line + 1] = jnp.sum(raised, axis=0, keepdims=True)
                weighted[line : line + 1] = jnp.sum(raised * grads, axis=0, keepdims=True)

        in_low = row_ids((tasks * runs, BLOCK)) < first * runs

        def finish(mine):
            top = jnp.max(jnp.where(mine, peaks[...], masked_score), axis=0, keepdims=True)
            factor = jnp.where(mine, jnp.exp(peaks[...] - top), 0.0)
            inverse = 1.0 / jnp.sum(totals[...] * factor, axis=0, keepdims=True)
            return factor * inverse, jnp.sum(weighted[...] * factor, axis=0, keepdims=True) * inverse

        (low_factor, low_delta), (high_factor, high_delta) = finish(in_low), finish(jnp.logical_not(in_low))
        peaks[...] = low_factor + high_factor

        for t in range(tasks):
            is_low, chunk = task(t)
            half = jnp.where(is_low, 0, 1)
            weights = weights_out[half]
            delta = jnp.where(is_low, low_delta, high_delta)
            parts = []
            for u in range(runs):
                sub = slice(u * BLOCK, (u + 1) * BLOCK)
                probs = stored[t, sub, :BLOCK] * peaks[t * runs + u : t * runs + u + 1]
                d_scores = probs * (stored[t, sub, BLOCK:] - delta)
                both = jnp.concatenate([probs, d_scores], axis=1).astype(low)
                at = pl.multiple_of(chunk * KEYS + u * BLOCK, BLOCK)
                sums[pl.ds(at, BLOCK), :] += mm(both, weights)
                parts.append(both)
            at = pl.multiple_of(chunk * KEYS, KEYS)
            finals[half] += mm(turned_keys[:, pl.ds(at, KEYS)], jnp.concatenate(parts, axis=0))

        for half in range(2):
            both = jnp.concatenate(
                [finals[half, :HEAD_DIM, :BLOCK], finals[half, HEAD_DIM:, BLOCK:] * score_scale], axis=0
            ).T
            out_ref[i, half * BLOCK : (half + 1) * BLOCK, :] = rotated_back(both, blocks[half]).astype(low)
        return carry

    lax.fori_loop(0, len(places), one_pair, 0)

    if is_last:
        for r in range(heads):
            for d in range(group):
                for half, block in enumerate(blocks_of(r, d)):
                    at = r * rows + half * BLOCK
                    tile = rotated_back(sums[pl.ds(pl.multiple_of(block * BLOCK, BLOCK), BLOCK), :], block)
                    if d == 0:
                        d_own_ref[at : at + BLOCK, :] = tile
                    else:
                        d_other_ref[d - 1, at : at + BLOCK, :] = tile


def attention(heads, group, places, pair_of, inverse, token, got, other, state):
    is_first, is_last = state is None, places[-1] == heads - 1
    rows = got.shape[1]
    owners = pair_of.shape[0]
    total_keys = owners * rows
    tasks = (2 * owners + KEYS // BLOCK) // (KEYS // BLOCK)
    operands = [pair_of, inverse, token]
    outs = [shape_of((len(places), rows, LANES), low)]
    if is_first:
        operands += [got] if other is None else [got, other]
    else:
        operands += list(state)
    if is_last:
        outs.append(shape_of((heads * rows, LANES), full))
        if group > 1:
            outs.append(shape_of((group - 1, heads * rows, LANES), full))
    kept = [
        shape_of((total_keys, LANES), low),
        shape_of((LANES, total_keys), low),
        shape_of((total_keys, LANES), full),
        shape_of((heads, rows, LANES), low),
    ]
    aliases = {} if is_first else {len(operands) - 4 + i: len(outs) + i for i in range(4)}
    found = pl.pallas_call(
        functools.partial(attention_kernel, heads, group, places, is_first, is_last),
        out_shape=outs + kept + [shape_of((1, LANES), full)],
        in_specs=[spec_smem()] + [spec_vmem()] * (len(operands) - 1),
        out_specs=[spec_vmem()] * (len(outs) + 5),
        input_output_aliases=aliases,
        scratch_shapes=[
            pltpu.VMEM((2, LANES, 2 * BLOCK), low),
            pltpu.VMEM((2, 2 * BLOCK, LANES), low),
            pltpu.VMEM((tasks, KEYS, 2 * BLOCK), full),
            pltpu.VMEM((tasks * KEYS // BLOCK, BLOCK), full),
            pltpu.VMEM((tasks * KEYS // BLOCK, BLOCK), full),
            pltpu.VMEM((tasks * KEYS // BLOCK, BLOCK), full),
            pltpu.VMEM((2, LANES, 2 * BLOCK), full),
            pltpu.VMEM((2 * owners, LANES), full),
            pltpu.VMEM((2 * owners, LANES), full),
        ],
        compiler_params=params(6 + total_keys * 5 * 256 // MIB),
        cost_estimate=pl.CostEstimate(
            flops=2_500_000_000 * len(places), bytes_accessed=2 * MIB, transcendentals=0
        ),
        name="attention",
    )(*operands)
    return found[0], found[1 : len(outs)], found[len(outs) : len(outs) + 4], found[-1]


def combine_kernel(heads, terms, *refs):
    out_ref = refs[-1]
    rows = out_ref.shape[1]
    for r in range(heads):
        cut = slice(r * rows, (r + 1) * rows)
        total = refs[0][cut, :]
        for term in refs[1:terms]:
            total = total + term[cut, :]
        out_ref[r, :, LANES:] = total.astype(low)
    at = 0
    for first_ref in refs[terms:-1]:
        out_ref[at : at + first_ref.shape[0], :, :LANES] = first_ref[...]
        at += first_ref.shape[0]


def combine(heads, terms, firsts):
    rows = firsts[0].shape[1]
    return pl.pallas_call(
        functools.partial(combine_kernel, heads, len(terms)),
        out_shape=shape_of((heads, rows, 2 * LANES), low),
        in_specs=[spec_vmem()] * (len(firsts) + len(terms)),
        out_specs=spec_vmem(),
        compiler_params=params(24),
        cost_estimate=pl.CostEstimate(flops=10**7, bytes_accessed=3 * MIB, transcendentals=0),
        name="combine",
    )(*terms, *firsts)


def weight_grads_kernel(
    heads, early, ids_ref, got_ref, h1_ref, cot_ref, low_ref, d_b_ref, keep_ref, early_ref, send_ref, token_ref, grads
):
    chips, chunk_rows = keep_ref.shape[:2]

    def put(at, tile):
        step = min(chunk_rows, tile.shape[0])
        for off in range(0, tile.shape[0], step):
            chunk, inside = divmod(at + off, chunk_rows)
            grads[chunk, inside : inside + step] = tile[off : off + step]

    rows = h1_ref.shape[0]
    left = lane_ids((rows, LANES)) < HEAD_DIM
    for i in range(heads // 2):
        cut = slice(i * LANES, (i + 1) * LANES)
        for first, second, half in ((0, 1, slice(0, LANES)), (3, 2, slice(LANES, 2 * LANES))):
            a, b = got_ref[2 * i, :, half].astype(full), got_ref[2 * i + 1, :, half].astype(full)
            low_ref[first, :, cut] = jnp.where(left, a, pltpu.roll(b, HEAD_DIM, 1)).astype(low)
            low_ref[second, :, cut] = jnp.where(left, pltpu.roll(a, HEAD_DIM, 1), b).astype(low)
    h1_turned = turn(h1_ref[...])
    depth, tiles = h1_turned.shape[0], heads // 2
    for s in range(3):
        d_proj = low_ref[1 + s]
        d_b_ref[s : s + 1] = jnp.sum(d_proj.astype(full), axis=0, keepdims=True)
        grad = mm(h1_turned, d_proj).astype(low)
        for t in range(tiles):
            put((s * tiles + t) * depth, grad[:, t * LANES : (t + 1) * LANES])
    grad = mm(turn(low_ref[0]), cot_ref[...]).astype(low)
    height = grad.shape[0]
    for t in range(depth // LANES):
        put(3 * tiles * depth + t * height, grad[:, t * LANES : (t + 1) * LANES])
    for t in range(chips):
        target = early_ref.at[t] if t < early else send_ref.at[t - early]
        target[...] = grads[ids_ref[chips + t]]
        keep_ref[t] = grads[ids_ref[t]]
    token_ref[...] = jnp.zeros_like(token_ref)


def weight_grads(heads, early, ids, got, h1, cot):
    rows, width = h1.shape
    local_width = heads * HEAD_DIM
    chips = ids.shape[0] // 2
    chunk_rows = 4 * width * local_width // LANES // (2 * chips)
    outs = [
        shape_of((4, rows, local_width), low),
        shape_of((3, local_width), full),
        shape_of((chips, chunk_rows, LANES), low),
        shape_of((early, chunk_rows, LANES), low),
        shape_of((chips - early, chunk_rows, LANES), low),
        shape_of((1, LANES), full),
    ]
    return pl.pallas_call(
        functools.partial(weight_grads_kernel, heads, early),
        out_shape=outs,
        in_specs=[spec_smem()] + [spec_vmem()] * 3,
        out_specs=[spec_vmem()] * len(outs),
        scratch_shapes=[pltpu.VMEM((2 * chips, chunk_rows, LANES), low)],
        compiler_params=params(20),
        cost_estimate=pl.CostEstimate(
            flops=8 * rows * width * local_width, bytes_accessed=8 * MIB, transcendentals=0
        ),
        name="weight_grads",
    )(ids, got, h1, cot)


def return_kernel(low_ref, part_ref, w_out_ref, w_qkv_ref, xhat_ref, e2_ref, both_ref, sums_ref):
    rows = xhat_ref.shape[0]
    both_ref[:rows] = (part_ref[...] + mm(low_ref[0], w_out_ref[...])).astype(low)
    back = mm_nt(low_ref[1], w_qkv_ref[0]) + mm_nt(low_ref[2], w_qkv_ref[1]) + mm_nt(low_ref[3], w_qkv_ref[2])
    both_ref[rows : 2 * rows] = back.astype(low)
    both_ref[2 * rows :] = e2_ref[...]
    sums_ref[0:1] = jnp.sum(back * xhat_ref[...], axis=0, keepdims=True)
    sums_ref[1:2] = jnp.sum(back, axis=0, keepdims=True)


def back_projections(*given):
    rows, width = given[1].shape
    return pl.pallas_call(
        return_kernel,
        out_shape=[shape_of((3 * rows, width), low), shape_of((2, width), full)],
        in_specs=[spec_vmem()] * len(given),
        out_specs=[spec_vmem()] * 2,
        compiler_params=params(16),
        cost_estimate=pl.CostEstimate(
            flops=8 * rows * width * given[2].shape[0], bytes_accessed=8 * MIB, transcendentals=0
        ),
        name="back_projections",
    )(*given)


def finish_kernel(
    hidden_ref, cot_ref, xhat_ref, std_ref, gains_ref, bias_ref, ours_ref, theirs_ref, out_ref, grad_ref, token_ref
):
    rows = hidden_ref.shape[0]
    gains = gains_ref[...]
    biases = bias_ref[...]
    summed = ours_ref[:rows].astype(full) + theirs_ref[:rows].astype(full)
    out_ref[...] = (hidden_ref[...].astype(full) + summed + biases[0:1] + biases[1:2]).astype(low)
    e1 = ours_ref[rows : 2 * rows].astype(full) + theirs_ref[rows : 2 * rows].astype(full)
    e2 = ours_ref[2 * rows :].astype(full) + theirs_ref[2 * rows :].astype(full)
    f = e1 * gains[0:1] + e2 * gains[1:2]
    xhat = xhat_ref[...]
    inv_std = std_ref[:, 0:1]
    grad_ref[...] = cot_ref[...].astype(full) + inv_std * (
        f - jnp.mean(f, axis=-1, keepdims=True) - xhat * jnp.mean(f * xhat, axis=-1, keepdims=True)
    )
    token_ref[...] = jnp.zeros_like(token_ref)


def finish(*operands):
    rows, width = operands[0].shape
    return pl.pallas_call(
        finish_kernel,
        out_shape=[shape_of((rows, width), low), shape_of((rows, width), full), shape_of((1, LANES), full)],
        in_specs=[spec_vmem()] * len(operands),
        out_specs=[spec_vmem()] * 3,
        compiler_params=params(24),
        cost_estimate=pl.CostEstimate(flops=10**7, bytes_accessed=8 * MIB, transcendentals=0),
        name="finish",
    )(*operands)


def to_attention(width, local_width, source, refs, base, unit):
    qkv_ref, out_ref = refs
    tiles = local_width // LANES
    split = 3 * tiles * width
    tile = base // width
    row = pl.multiple_of(lax.rem(base, width), unit)
    column = pl.multiple_of(lax.rem(tile, tiles) * LANES, LANES)
    yield base < split, source, qkv_ref.at[jnp.minimum(tile // tiles, 2), pl.ds(row, unit), pl.ds(column, LANES)]
    after = jnp.maximum(base - split, 0)
    row = pl.multiple_of(lax.rem(after, local_width), unit)
    column = pl.multiple_of(after // local_width * LANES, LANES)
    yield base >= split, source, out_ref.at[pl.ds(row, unit), pl.ds(column, LANES)]


def to_mlp(width, source, refs, base, unit):
    up_ref, down_ref = refs
    block, inside = base // (2 * width), lax.rem(base, 2 * width)
    block_at = pl.multiple_of(block * LANES, LANES)
    row = pl.multiple_of(jnp.minimum(inside, width - unit), unit)
    yield inside < width, source, up_ref.at[pl.ds(row, unit), pl.ds(block_at, LANES)]
    for t in range(unit // LANES):
        column = pl.multiple_of(jnp.maximum(inside - width, 0) + t * LANES, LANES)
        cut = source.at[pl.ds(t * LANES, LANES), :]
        yield inside >= width, cut, down_ref.at[pl.ds(block_at, LANES), pl.ds(column, LANES)]


def unpack_kernel(route, count, unit, has_old, ids_ref, *rest):
    parts, rest = rest[:count], rest[count:]
    rest = rest[2:] if has_old else rest
    targets, (token_ref, held, sems) = rest[:2], rest[2:]
    token_ref[...] = jnp.zeros_like(token_ref)
    chunk_rows = parts[0].shape[0]
    units = chunk_rows // unit
    per_unit = sems.shape[0] // (count * units)

    def moves():
        for i in range(count):
            for j in range(units):
                source = held.at[i, pl.ds(j * unit, unit), :]
                base = ids_ref[i] * chunk_rows + j * unit
                for n, (applies, piece, target) in enumerate(route(source, targets, base, unit)):
                    sem = sems.at[(i * units + j) * per_unit + n]
                    yield i, applies, pltpu.make_async_copy(piece, target, sem)

    done = -1
    for i, applies, copy in moves():
        if i != done:
            held[i] = parts[i][...].astype(full)
            done = i
        pl.when(applies)(copy.start)
    for i, applies, copy in moves():
        pl.when(applies)(copy.wait)


def unpack(name, route, cases, unit, shapes, ids, parts, old):
    count = len(parts)
    chunk_rows = parts[0].shape[0]
    operands = [ids, *parts, *(old or ())]
    return pl.pallas_call(
        functools.partial(unpack_kernel, route, count, unit, old is not None),
        out_shape=[shape_of(shape, full) for shape in shapes] + [shape_of((1, LANES), full)],
        in_specs=[spec_smem()] + [spec_vmem()] * count + [spec_hbm()] * (len(operands) - 1 - count),
        out_specs=[spec_hbm()] * 2 + [spec_vmem()],
        input_output_aliases={} if old is None else {1 + count: 0, 2 + count: 1},
        scratch_shapes=[
            pltpu.VMEM((count, chunk_rows, LANES), full),
            pltpu.SemaphoreType.DMA((count * (chunk_rows // unit) * cases,)),
        ],
        compiler_params=params(8 + count * chunk_rows * 3 * LANES * 2 // MIB),
        cost_estimate=pl.CostEstimate(
            flops=10**6, bytes_accessed=count * chunk_rows * LANES * 6, transcendentals=0
        ),
        name=name,
    )(*operands)


def local(
    hidden,
    pair_of,
    ln1_gain,
    ln1_bias,
    ln2_gain,
    ln2_bias,
    w_qkv,
    b_qkv,
    w_out,
    b_out,
    w_up,
    b_up,
    w_down,
    b_down,
    cotangent,
):
    owners = lax.axis_size("ctx")
    sides = lax.axis_size("tp")
    rows, width = hidden.shape
    local_width = w_qkv.shape[2]
    hidden_units = w_up.shape[1]
    heads = local_width // HEAD_DIM
    group = owners // heads

    exponent = np.arange(0, ROT, 2, dtype=np.float32) / np.float32(ROT)
    inverse = jnp.asarray(np.tile(np.float32(10000.0) ** (-exponent), LANES // HALF)[None, :], full)
    order = (0, 2, 4, 6, 7, 5, 3, 1) if owners == 16 else tuple(range(owners // 2))
    chips = len(order)

    def to_heads(array):
        groups = [[h * group + g for h in range(heads)] for g in range(group)]
        return lax.all_to_all(array, "ctx", 0, 0, axis_index_groups=groups, tiled=True)

    def group_shift(array, d):
        pairs = [(c, c // group * group + (c % group + d) % group) for c in range(owners)]
        return lax.ppermute(array, "ctx", pairs)

    me = lax.axis_index("ctx")
    chip, core = me // 2, lax.rem(me, 2)
    place = sum(jnp.where(chip == c, i, 0) for i, c in enumerate(order))
    way = 1 - 2 * core
    far, near = chips // 2, chips - 1 - chips // 2

    def ring(array, forward):
        pairs = []
        for i, c in enumerate(order):
            for k in range(2):
                step = 1 if (k == 0) == forward else -1
                pairs.append((2 * c + k, 2 * order[(i + step) % chips] + k))
        return lax.ppermute(array, "ctx", pairs)

    def other_core(array):
        return lax.ppermute(array, "ctx", [(c, c ^ 1) for c in range(owners)])

    def across(array):
        return lax.ppermute(array, "tp", [(t, (t + 1) % sides) for t in range(sides)])

    def target(distance):
        return lax.rem(place + way * distance + chips, chips)

    def zero(array):
        return array[:1].astype(full) * 0.0

    slots = [far, -near]
    for t in range(1, far):
        slots += [far - t] if t >= near else [far - t, t - near]
    slots.append(0)
    early = 2
    slot_ids = jnp.stack(
        [core * chips + target(d) for d in slots] + [(1 - core) * chips + target(-d) for d in slots]
    )

    def terms_of(keep, came):
        def term(i):
            return keep[i].astype(full) + came[i].astype(full)

        return {d: term(i) for i, d in enumerate(slots)}

    def scatter_start(terms, token):
        return (terms[far] + token).astype(low), (terms[-near] + token).astype(low)

    def scatter_step(terms, t, sends, token):
        long_send, short_send = sends
        long_got = ring(long_send, True).astype(full) + token
        last = t == far - 1
        long_next = long_got if last else (long_got + terms[far - 1 - t]).astype(low)
        short_next = short_send
        if t < near:
            short_got = ring(short_send, False).astype(full) + token
            short_next = short_got if t == near - 1 else (short_got + terms[t + 1 - near]).astype(low)
        if last:
            return (terms[0] + long_next + short_next).astype(low)
        return long_next, short_next

    base, other_base = core * chips, (1 - core) * chips

    def gather_start(own):
        return [(own, base + place), (other_core(own), other_base + place)]

    def gather_step(t, sends, token):
        long_send, short_send = sends
        if token is not None:
            long_send = (long_send.astype(full) + token).astype(low)
        long_got = ring(long_send, True)
        found = [(long_got, base + target(-t - 1)), (other_core(long_got), other_base + target(t + 1))]
        short_got = short_send
        if t < near:
            short_got = ring(short_send, False)
            found += [(short_got, base + target(t + 1)), (other_core(short_got), other_base + target(-t - 1))]
        return (long_got, short_got), found

    blocks = hidden_units // LANES // 2
    in_slots = blocks == chips
    mlp_ids = slot_ids if in_slots else jnp.concatenate(
        [core * blocks + jnp.arange(blocks), (1 - core) * blocks + jnp.arange(blocks)]
    )
    h1, h2, xhat, inv_std, d_bias, gains, biases, b_up_row, packed = project(
        heads,
        pair_of,
        inverse,
        (hidden, ln1_gain, ln1_bias, ln2_gain, ln2_bias, cotangent, w_out, w_qkv, b_qkv, b_up, b_out, b_down),
    )
    got = to_heads(packed)
    part, back2, sums2, d_b_up, keep_mlp, early_mlp, send_mlp = mlp(
        mlp_ids.astype(jnp.int32), early, h2, w_up, b_up_row, cotangent, w_down, xhat
    )
    chunk = keep_mlp.shape[0] // chips
    came_mlp = jnp.concatenate([other_core(early_mlp), other_core(send_mlp)]) if not in_slots else None
    if in_slots:
        halves = [other_core(array).reshape(-1, chunk, LANES) for array in (early_mlp, send_mlp)]
        came_mlp = [half[i] for half in halves for i in range(half.shape[0])]
        terms_mlp = terms_of(keep_mlp.reshape(chips, chunk, LANES), came_mlp)
    else:
        summed = (keep_mlp.astype(full) + came_mlp.astype(full)).reshape(chips, chunk, LANES)
        terms_mlp = {d: lax.dynamic_index_in_dim(summed, target(d), 0, keepdims=False) for d in slots}
    nothing = jnp.zeros((1, LANES), full)

    other = None
    if group > 1:
        mine = got[:, :, LANES:].reshape(heads * rows, LANES)
        other = jnp.stack([group_shift(mine, group - d) for d in range(1, group)])

    middle = heads // 4
    first, _, state, token = attention(
        heads, group, tuple(range(middle)), pair_of, inverse, sums2, got, other, None
    )
    sends_mlp = scatter_start(terms_mlp, token)
    token = zero(sends_mlp[0]) + zero(sends_mlp[1])
    second, ends, _, token = attention(
        heads, group, tuple(range(middle, heads)), pair_of, inverse, token, got, other, state
    )
    d_own, d_other = ends[0], (ends[1] if group > 1 else None)
    terms = [d_own] + [group_shift(d_other[d - 1], d) for d in range(1, group)]
    sends_mlp = scatter_step(terms_mlp, 0, sends_mlp, token)
    first = (first.astype(full) + zero(sends_mlp[0]) + zero(sends_mlp[1])).astype(low)
    backs = to_heads(combine(heads, terms, [first, second]))
    sends_mlp = scatter_step(terms_mlp, 1, sends_mlp, nothing)
    h1_later = (h1.astype(full) + (zero(sends_mlp[0]) + zero(sends_mlp[1]))[:, :1]).astype(low)

    lows, d_b_qkv, keep, early_att, send_att, after = weight_grads(
        heads, early, slot_ids.astype(jnp.int32), backs, h1_later, cotangent
    )
    both, sums1 = back_projections(lows, part, w_out, w_qkv, xhat, back2)
    theirs = across(both)
    output, d_hidden, finish_token = finish(
        hidden, cotangent, xhat, inv_std, gains, biases, both, theirs
    )
    halves = [other_core(array) for array in (early_att, send_att)]
    terms_att = terms_of(keep, [half[i] for half in halves for i in range(half.shape[0])])

    small = jnp.concatenate(
        [sums1.reshape(1, -1), sums2.reshape(1, -1), d_bias, d_b_up, d_b_qkv.reshape(1, -1)], axis=1
    )

    def unpack_some(name, route, cases, unit, shapes, found, old):
        parts, ids = zip(*found)
        *old, token = unpack(name, route, cases, unit, shapes, jnp.stack(ids), parts, old)
        return old, token

    unit_mlp = min(chunk, local_width)
    unit_att = min(keep.shape[1], local_width)
    unpack_mlp = functools.partial(
        unpack_some,
        "unpack_feed_forward",
        functools.partial(to_mlp, width),
        1 + unit_mlp // LANES,
        unit_mlp,
        ((width, hidden_units), (hidden_units, width)),
    )
    unpack_att = functools.partial(
        unpack_some,
        "unpack_attention",
        functools.partial(to_attention, width, local_width),
        2,
        unit_att,
        ((3, width, local_width), (local_width, width)),
    )

    steps_mlp, steps_round = iter(range(2, far)), iter(range(far))
    own_mlp, round_mlp, waiting, grads_mlp = None, None, [], None

    def advance_mlp(token, gate=None):
        nonlocal sends_mlp, own_mlp, round_mlp, waiting
        t = next(steps_mlp, None)
        if t is not None:
            sends_mlp = scatter_step(terms_mlp, t, sends_mlp, token)
            if t < far - 1:
                return zero(sends_mlp[0])
            own_mlp, round_mlp = sends_mlp, (sends_mlp, sends_mlp)
            waiting += gather_start(own_mlp)
            return zero(own_mlp)
        t = next(steps_round, None)
        if t is None:
            return nothing
        round_mlp, found = gather_step(t, round_mlp, gate)
        waiting += found
        return zero(round_mlp[0])

    sends_att = scatter_start(terms_att, nothing)
    for t in range(far):
        sends_att = scatter_step(terms_att, t, sends_att, advance_mlp(nothing))
    round_att, waiting_att, grads_att = (sends_att, sends_att), gather_start(sends_att), None
    small = small + zero(sends_att)[:, :1]
    distance = 1
    for t in range(far):
        ready, waiting = waiting, []
        advance_mlp(nothing, zero(round_att[0]))
        round_att, found = gather_step(t, round_att, None)
        waiting_att += found
        if distance < owners:
            small = small + lax.ppermute(small, "ctx", [(c, c ^ distance) for c in range(owners)])
            distance *= 2
        if ready:
            grads_mlp, more = unpack_mlp(ready, grads_mlp)
            small = small + more[:, :1]
        if t == far - 2:
            small = small + finish_token[:, :1]
            grads_att, more = unpack_att(waiting_att[:-4], None)
            waiting_att = waiting_att[-4:]
            small = small + more[:, :1]
    while distance < owners:
        small = small + lax.ppermute(small, "ctx", [(c, c ^ distance) for c in range(owners)])
        distance *= 2
    if waiting:
        grads_mlp, _ = unpack_mlp(waiting, grads_mlp)
    grads_att, _ = unpack_att(waiting_att, grads_att)

    norm_sums = small[:, : 4 * width]
    norm_sums = (norm_sums + across(norm_sums)).reshape(4, width)
    at = 4 * width
    d_bias = small[0, at : at + width]
    d_b_up = small[0, at + width : at + width + hidden_units]
    d_b_qkv = small[0, at + width + hidden_units :].reshape(3, local_width)
    d_w_up, d_w_down = grads_mlp
    d_w_qkv, d_w_out = grads_att
    return (
        output,
        d_hidden,
        norm_sums[0],
        norm_sums[1],
        norm_sums[2],
        norm_sums[3],
        d_w_qkv,
        d_b_qkv,
        d_w_out,
        d_bias,
        d_w_up,
        d_b_up,
        d_w_down,
        d_bias,
    )


def solution(mesh):
    placed = (
        P("ctx", None),
        P(),
        P(),
        P(),
        P(),
        P(),
        P(None, None, "tp"),
        P(None, "tp"),
        P("tp", None),
        P(),
        P(None, "tp"),
        P("tp"),
        P("tp", None),
        P(),
        P("ctx", None),
    )
    return jax.shard_map(
        local,
        mesh=mesh,
        in_specs=placed,
        out_specs=(
            P("ctx", None),
            P("ctx", None),
            P(),
            P(),
            P(),
            P(),
            P(None, None, "tp"),
            P(None, "tp"),
            P("tp", None),
            P(),
            P(None, "tp"),
            P("tp"),
            P("tp", None),
            P(),
        ),
        check_vma=False,
    )
```

```python
import functools

import jax
import jax.numpy as jnp
import numpy as np
from jax import lax
from jax.experimental import pallas as pl
from jax.experimental.pallas import tpu as pltpu
from jax.sharding import PartitionSpec as P

HEAD_DIM = 64
ROT = 16
HALF = ROT // 2
BLOCK = 128
LANES = 128
KEYS = 512
MIB = 1 << 20

norm_eps = 1e-05
masked_score = -1e30
score_scale = HEAD_DIM ** (-0.5)
low = jnp.bfloat16
full = jnp.float32


def mm(left, right):
    return lax.dot_general(left, right, (((1,), (0,)), ((), ())), preferred_element_type=full)


def mm_nt(left, right):
    return lax.dot_general(left, right, (((1,), (1,)), ((), ())), preferred_element_type=full)


def turn(tensor):
    return tensor.astype(full).T.astype(low)


def lane_ids(shape):
    return lax.broadcasted_iota(jnp.int32, shape, len(shape) - 1)


def row_ids(shape):
    return lax.broadcasted_iota(jnp.int32, shape, len(shape) - 2)


def rotary_partner(tensor):
    lanes = lane_ids(tensor.shape)
    ahead = pltpu.roll(tensor, LANES - HALF, 1)
    behind = pltpu.roll(tensor, HALF, 1)
    return jnp.where(lanes % ROT < HALF, ahead, behind)


def spec_vmem():
    return pl.BlockSpec(memory_space=pltpu.VMEM)


def spec_smem():
    return pl.BlockSpec(memory_space=pltpu.SMEM)


def spec_hbm():
    return pl.BlockSpec(memory_space=pltpu.HBM)


def params(mib):
    return pltpu.CompilerParams(vmem_limit_bytes=mib * MIB)


def shape_of(shape, kind):
    return jax.ShapeDtypeStruct(shape, kind)


def block_tables(inverse, blocks):
    row = row_ids((BLOCK, LANES)).astype(full)
    start = blocks.astype(full) * float(BLOCK)
    return jnp.cos(row * inverse), jnp.sin(row * inverse), jnp.cos(start * inverse), jnp.sin(start * inverse)


def project_kernel(heads, pair_ref, inv_ref, *rest):
    given, rest = rest[:12], rest[12:]
    h1_ref, h2_ref, xhat_ref, std_ref, d_bias_ref, gains_ref, bias_ref, b_up_out_ref, packed = rest[:9]
    held, sems = rest[9:-1], rest[-1]
    copies = [pltpu.make_async_copy(src, dst, sems.at[i]) for i, (src, dst) in enumerate(zip(given, held))]
    for copy in copies:
        copy.start()
    (
        hidden_ref,
        g1_ref,
        c1_ref,
        g2_ref,
        c2_ref,
        cot_ref,
        w_out_ref,
        w_qkv_ref,
        b_qkv_ref,
        b_up_ref,
        b_out_ref,
        b_down_ref,
    ) = held
    rows = hidden_ref.shape[0]
    me = lax.axis_index("ctx")
    pair = pair_ref[me]
    total_blocks = 2 * pair_ref.shape[0]

    first = jnp.where(row_ids((8, LANES)) == 0, pair, total_blocks - 1 - pair)
    inverse = inv_ref[...]
    cos_row, sin_row, cos_block, sin_block = block_tables(inverse, first)
    in_head = lane_ids((BLOCK, LANES)) % HEAD_DIM
    tables = []
    for half in range(2):
        cos_at, sin_at = cos_block[half : half + 1], sin_block[half : half + 1]
        cosine = cos_row * cos_at - sin_row * sin_at
        sine = sin_row * cos_at + cos_row * sin_at
        cosine = jnp.where(in_head < ROT, cosine, 1.0)
        sine = jnp.where(in_head < HALF, -sine, jnp.where(in_head < ROT, sine, 0.0))
        tables.append((cosine, sine))
    cosine = jnp.concatenate([tables[0][0], tables[1][0]], axis=0)
    sine = jnp.concatenate([tables[0][1], tables[1][1]], axis=0)

    for copy in copies[:5]:
        copy.wait()
    x = hidden_ref[...].astype(full)
    centred = x - jnp.mean(x, axis=-1, keepdims=True)
    spread = jnp.mean(centred * centred, axis=-1, keepdims=True)
    inv_std = lax.rsqrt(spread + norm_eps)
    xhat = centred * inv_std
    xhat_ref[...] = xhat
    std_ref[...] = jnp.broadcast_to(inv_std, std_ref.shape)

    def as_row(ref):
        return ref[...].astype(full)[None, :]

    gain1, gain2 = as_row(g1_ref), as_row(g2_ref)
    h1 = (xhat * gain1 + as_row(c1_ref)).astype(low)
    h1_ref[...] = h1
    h2_ref[...] = (xhat * gain2 + as_row(c2_ref)).astype(low)
    gains_ref[0:1] = gain1
    gains_ref[1:2] = gain2
    for copy in copies[5:]:
        copy.wait()
    b_up_out_ref[...] = as_row(b_up_ref)
    bias_ref[0:1] = as_row(b_out_ref)
    bias_ref[1:2] = as_row(b_down_ref)
    d_bias_ref[...] = jnp.sum(cot_ref[...].astype(full), axis=0, keepdims=True)

    lane = lane_ids((rows, LANES))

    def projected(s):
        return mm(h1, w_qkv_ref[s]) + b_qkv_ref[s : s + 1].astype(full)

    def turned(tile):
        return tile * cosine + rotary_partner(tile) * sine

    queries, keys, values = projected(0), projected(1), projected(2)
    grads = mm_nt(cot_ref[...], w_out_ref[...])
    left = lane < HEAD_DIM
    for i in range(heads // 2):
        cut = slice(i * LANES, (i + 1) * LANES)
        q = turned(queries[:, cut]).astype(low).astype(full) * score_scale
        k = turned(keys[:, cut])
        v = values[:, cut]
        g = grads[:, cut]
        packed[2 * i, :, :LANES] = jnp.where(left, g, pltpu.roll(q, HEAD_DIM, 1)).astype(low)
        packed[2 * i, :, LANES:] = jnp.where(left, v, pltpu.roll(k, HEAD_DIM, 1)).astype(low)
        packed[2 * i + 1, :, :LANES] = jnp.where(left, pltpu.roll(g, HEAD_DIM, 1), q).astype(low)
        packed[2 * i + 1, :, LANES:] = jnp.where(left, pltpu.roll(v, HEAD_DIM, 1), k).astype(low)


def project(heads, pair_of, inverse, given):
    hidden, w_out, b_up = given[0], given[6], given[9]
    rows, width = hidden.shape
    outs = [
        shape_of((rows, width), low),
        shape_of((rows, width), low),
        shape_of((rows, width), full),
        shape_of((rows, LANES), full),
        shape_of((1, width), full),
        shape_of((2, width), full),
        shape_of((2, width), full),
        shape_of((1, b_up.shape[0]), full),
        shape_of((heads, rows, 2 * LANES), low),
    ]
    return pl.pallas_call(
        functools.partial(project_kernel, heads),
        out_shape=outs,
        in_specs=[spec_smem(), spec_vmem()] + [spec_hbm()] * len(given),
        out_specs=[spec_vmem()] * len(outs),
        scratch_shapes=[pltpu.VMEM(array.shape, array.dtype) for array in given]
        + [pltpu.SemaphoreType.DMA((len(given),))],
        compiler_params=params(60),
        cost_estimate=pl.CostEstimate(
            flops=2 * rows * width * 4 * w_out.shape[0], bytes_accessed=8 * MIB, transcendentals=0
        ),
        name="project",
    )(pair_of, inverse, *given)


def mlp_kernel(early, ids_ref, *rest):
    given, rest = rest[:6], rest[6:]
    part_ref, back_ref, sums_ref, d_b_up_ref, keep_ref, early_ref, send_ref = rest[:7]
    h2_turned, part_acc, back_acc = rest[7:10]
    held, sems = rest[10:-1], rest[-1]
    copies = [pltpu.make_async_copy(src, dst, sems.at[i]) for i, (src, dst) in enumerate(zip(given, held))]
    h2_held, w_up_ref, b_up, cot_ref, w_down_ref, xhat_ref = held
    step = pl.program_id(0)
    steps = pl.num_programs(0)

    @pl.when(step == 0)
    def _():
        for copy in copies:
            copy.start()
        part_acc[...] = jnp.zeros_like(part_acc)
        back_acc[...] = jnp.zeros_like(back_acc)
        copies[0].wait()
        h2_turned[...] = turn(h2_held[...])
        for copy in copies[1:3]:
            copy.wait()

    at = [pl.multiple_of(ids_ref[b * steps + step] * LANES, LANES) for b in range(2)]
    w_up = jnp.concatenate([w_up_ref[:, pl.ds(i, LANES)] for i in at], axis=1)
    u = mm(h2_held[...], w_up) + jnp.concatenate([b_up[:, pl.ds(i, LANES)] for i in at], axis=1)

    @pl.when(step == 0)
    def _():
        for copy in copies[3:5]:
            copy.wait()

    cot = cot_ref[...]
    w_down = jnp.concatenate([w_down_ref[pl.ds(i, LANES), :] for i in at], axis=0)
    cdf = 0.5 * (1.0 + lax.erf(u * np.float32(np.sqrt(0.5))))
    active = u * cdf
    active_low = active.astype(low)
    slope = cdf + u * jnp.exp(-0.5 * u * u) * np.float32(1.0 / np.sqrt(2.0 * np.pi))
    du = (mm_nt(cot, w_down) * slope).astype(low)
    part_acc[...] += mm(active_low, w_down)
    back_acc[...] += mm_nt(du, w_up)
    d_b_up = jnp.sum(du.astype(full), axis=0, keepdims=True)
    up = mm(h2_turned[...], du).astype(low)
    down = mm(active.T.astype(low), cot).astype(low)
    depth = up.shape[0]

    def put(b, grad_ref):
        grad_ref[:depth] = up[:, b * LANES : (b + 1) * LANES]
        for t in range(down.shape[1] // LANES):
            grad_ref[depth + t * LANES : depth + (t + 1) * LANES] = down[
                b * LANES : (b + 1) * LANES, t * LANES : (t + 1) * LANES
            ]

    for b in range(2):
        d_b_up_ref[:, pl.ds(at[b], LANES)] = d_b_up[:, b * LANES : (b + 1) * LANES]
    put(0, keep_ref)

    @pl.when(step < early)
    def _():
        put(1, early_ref)

    @pl.when(step >= early)
    def _():
        put(1, send_ref)

    @pl.when(step == steps - 1)
    def _():
        copies[5].wait()
        part_ref[...] = part_acc[...]
        back = back_acc[...]
        back_ref[...] = back.astype(low)
        sums_ref[0:1] = jnp.sum(back * xhat_ref[...], axis=0, keepdims=True)
        sums_ref[1:2] = jnp.sum(back, axis=0, keepdims=True)


def mlp(ids, early, *given):
    rows, width = given[0].shape
    hidden_units = given[1].shape[1]
    steps = hidden_units // LANES // 2
    whole = lambda shape: pl.BlockSpec(shape, lambda f, c: (0,) * len(shape))
    grads = lambda at: pl.BlockSpec((2 * width, LANES), lambda f, c: (at(f), 0))
    outs = [
        shape_of((rows, width), full),
        shape_of((rows, width), low),
        shape_of((2, width), full),
        shape_of((1, hidden_units), full),
        shape_of((steps * 2 * width, LANES), low),
        shape_of((early * 2 * width, LANES), low),
        shape_of(((steps - early) * 2 * width, LANES), low),
    ]
    return pl.pallas_call(
        functools.partial(mlp_kernel, early),
        grid_spec=pltpu.PrefetchScalarGridSpec(
            num_scalar_prefetch=1,
            grid=(steps,),
            in_specs=[spec_hbm()] * len(given),
            out_specs=[whole(array.shape) for array in outs[:4]]
            + [
                grads(lambda f: f),
                grads(lambda f: jnp.minimum(f, early - 1)),
                grads(lambda f: jnp.maximum(f - early, 0)),
            ],
            scratch_shapes=[
                pltpu.VMEM((width, rows), low),
                pltpu.VMEM((rows, width), full),
                pltpu.VMEM((rows, width), full),
            ]
            + [pltpu.VMEM(array.shape, array.dtype) for array in given]
            + [pltpu.SemaphoreType.DMA((len(given),))],
        ),
        out_shape=outs,
        compiler_params=params(60),
        cost_estimate=pl.CostEstimate(
            flops=12 * rows * width * hidden_units, bytes_accessed=20 * MIB, transcendentals=0
        ),
        name="feed_forward",
    )(ids, *given)


def attention_kernel(heads, group, places, is_first, is_last, pair_ref, inv_ref, token_ref, *rest):
    del token_ref
    if is_first:
        got_ref, rest = rest[0], rest[1:]
        if group > 1:
            other_ref, rest = rest[0], rest[1:]
    else:
        rest = rest[4:]
    out_ref, rest = rest[0], rest[1:]
    if is_last:
        d_own_ref, rest = rest[0], rest[1:]
        if group > 1:
            d_other_ref, rest = rest[0], rest[1:]
    (values_keys, turned_keys, sums, queries), rest = rest[:4], rest[4:]
    token_out, rest = rest[0], rest[1:]
    weights_in, weights_out, stored, peaks, totals, weighted, finals, block_cos, block_sin = rest
    token_out[...] = jnp.zeros_like(token_out)

    rows = queries.shape[1]
    owners = pair_ref.shape[0]
    total_blocks = 2 * owners
    per_chunk = KEYS // BLOCK
    tasks = (total_blocks + 1 + per_chunk - 1) // per_chunk
    me = lax.axis_index("ctx")
    own_sub = lax.rem(me, group)

    def blocks_of(r, d):
        owner = r * group + lax.rem(own_sub + d, group)
        pair = pair_ref[owner]
        return pair, total_blocks - 1 - pair

    def place(tile, block):
        at = pl.multiple_of(block * BLOCK, BLOCK)
        values_keys[pl.ds(at, BLOCK), :] = tile
        turned_keys[:, pl.ds(at, BLOCK)] = turn(tile)

    if is_first:
        for r in range(heads):
            queries[r] = got_ref[r, :, :LANES]
            for half, block in enumerate(blocks_of(r, 0)):
                place(got_ref[r, half * BLOCK : (half + 1) * BLOCK, LANES:], block)
            for d in range(1, group):
                for half, block in enumerate(blocks_of(r, d)):
                    at = r * rows + half * BLOCK
                    place(other_ref[d - 1, at : at + BLOCK, :], block)
        sums[...] = jnp.zeros_like(sums)

    lane = lane_ids((BLOCK, LANES))
    left = lane < HEAD_DIM
    in_key = lane - HEAD_DIM
    moving = (in_key >= 0) & (in_key < ROT)
    forward = (in_key >= 0) & (in_key < HALF)
    cos_row, sin_row, block_cos[...], block_sin[...] = block_tables(inv_ref[...], row_ids(block_cos.shape))

    def rotated_back(tile, block):
        cos_at, sin_at = block_cos[pl.ds(block, 1), :], block_sin[pl.ds(block, 1), :]
        cosine = jnp.where(moving, cos_row * cos_at - sin_row * sin_at, 1.0)
        sine = sin_row * cos_at + cos_row * sin_at
        sine = jnp.where(moving, jnp.where(forward, sine, -sine), 0.0)
        return tile * cosine + rotary_partner(tile) * sine

    offset = row_ids((BLOCK, BLOCK)) - lane_ids((BLOCK, BLOCK))

    def one_pair(i, carry):
        blocks = blocks_of(places[0] + i, 0)
        first = blocks[0] // per_chunk + 1
        for half in range(2):
            both = queries[places[0] + i, half * BLOCK : (half + 1) * BLOCK, :]
            both_turned = turn(both)
            upper = row_ids((LANES, BLOCK)) < HEAD_DIM
            zero = jnp.zeros_like(both_turned)
            weights_in[half, :, :BLOCK] = jnp.where(upper, both_turned, zero)
            weights_in[half, :, BLOCK:] = jnp.where(upper, zero, both_turned)
            weights_out[half, :BLOCK, :] = jnp.where(left, both, zero)
            weights_out[half, BLOCK:, :] = jnp.where(left, zero, both)
        finals[...] = jnp.zeros_like(finals)

        def task(t):
            is_low = t < first
            chunk = jnp.where(is_low, first - 1 - t, t - first)
            return is_low, chunk

        runs = KEYS // BLOCK
        for t in range(tasks):
            is_low, chunk = task(t)
            weights = weights_in[jnp.where(is_low, 0, 1)]
            for u in range(runs):
                at = pl.multiple_of(chunk * KEYS + u * BLOCK, BLOCK)
                sub = slice(u * BLOCK, (u + 1) * BLOCK)
                both = mm(values_keys[pl.ds(at, BLOCK), :], weights)
                grads = both[:, :BLOCK]
                scores = both[:, BLOCK:]
                if t in (0, tasks - 1):
                    query_at = blocks[0 if t == 0 else 1] * BLOCK
                    scores = jnp.where(offset <= query_at - at, scores, masked_score)
                peak = jnp.max(scores, axis=0, keepdims=True)
                raised = jnp.exp(scores - peak)
                stored[t, sub, :BLOCK] = raised
                stored[t, sub, BLOCK:] = grads
                line = t * runs + u
                peaks[line : line + 1] = peak
                totals[line : line + 1] = jnp.sum(raised, axis=0, keepdims=True)
                weighted[line : line + 1] = jnp.sum(raised * grads, axis=0, keepdims=True)

        in_low = row_ids((tasks * runs, BLOCK)) < first * runs

        def finish(mine):
            top = jnp.max(jnp.where(mine, peaks[...], masked_score), axis=0, keepdims=True)
            factor = jnp.where(mine, jnp.exp(peaks[...] - top), 0.0)
            inverse = 1.0 / jnp.sum(totals[...] * factor, axis=0, keepdims=True)
            return factor * inverse, jnp.sum(weighted[...] * factor, axis=0, keepdims=True) * inverse

        (low_factor, low_delta), (high_factor, high_delta) = finish(in_low), finish(jnp.logical_not(in_low))
        peaks[...] = low_factor + high_factor

        for t in range(tasks):
            is_low, chunk = task(t)
            half = jnp.where(is_low, 0, 1)
            weights = weights_out[half]
            delta = jnp.where(is_low, low_delta, high_delta)
            parts = []
            for u in range(runs):
                sub = slice(u * BLOCK, (u + 1) * BLOCK)
                probs = stored[t, sub, :BLOCK] * peaks[t * runs + u : t * runs + u + 1]
                d_scores = probs * (stored[t, sub, BLOCK:] - delta)
                both = jnp.concatenate([probs, d_scores], axis=1).astype(low)
                at = pl.multiple_of(chunk * KEYS + u * BLOCK, BLOCK)
                sums[pl.ds(at, BLOCK), :] += mm(both, weights)
                parts.append(both)
            at = pl.multiple_of(chunk * KEYS, KEYS)
            finals[half] += mm(turned_keys[:, pl.ds(at, KEYS)], jnp.concatenate(parts, axis=0))

        for half in range(2):
            both = jnp.concatenate(
                [finals[half, :HEAD_DIM, :BLOCK], finals[half, HEAD_DIM:, BLOCK:] * score_scale], axis=0
            ).T
            out_ref[i, half * BLOCK : (half + 1) * BLOCK, :] = rotated_back(both, blocks[half]).astype(low)
        return carry

    lax.fori_loop(0, len(places), one_pair, 0)

    if is_last:
        for r in range(heads):
            for d in range(group):
                for half, block in enumerate(blocks_of(r, d)):
                    at = r * rows + half * BLOCK
                    tile = rotated_back(sums[pl.ds(pl.multiple_of(block * BLOCK, BLOCK), BLOCK), :], block)
                    if d == 0:
                        d_own_ref[at : at + BLOCK, :] = tile
                    else:
                        d_other_ref[d - 1, at : at + BLOCK, :] = tile


def attention(heads, group, places, pair_of, inverse, token, got, other, state):
    is_first, is_last = state is None, places[-1] == heads - 1
    rows = got.shape[1]
    owners = pair_of.shape[0]
    total_keys = owners * rows
    tasks = (2 * owners + KEYS // BLOCK) // (KEYS // BLOCK)
    operands = [pair_of, inverse, token]
    outs = [shape_of((len(places), rows, LANES), low)]
    if is_first:
        operands += [got] if other is None else [got, other]
    else:
        operands += list(state)
    if is_last:
        outs.append(shape_of((heads * rows, LANES), full))
        if group > 1:
            outs.append(shape_of((group - 1, heads * rows, LANES), full))
    kept = [
        shape_of((total_keys, LANES), low),
        shape_of((LANES, total_keys), low),
        shape_of((total_keys, LANES), full),
        shape_of((heads, rows, LANES), low),
    ]
    aliases = {} if is_first else {len(operands) - 4 + i: len(outs) + i for i in range(4)}
    found = pl.pallas_call(
        functools.partial(attention_kernel, heads, group, places, is_first, is_last),
        out_shape=outs + kept + [shape_of((1, LANES), full)],
        in_specs=[spec_smem()] + [spec_vmem()] * (len(operands) - 1),
        out_specs=[spec_vmem()] * (len(outs) + 5),
        input_output_aliases=aliases,
        scratch_shapes=[
            pltpu.VMEM((2, LANES, 2 * BLOCK), low),
            pltpu.VMEM((2, 2 * BLOCK, LANES), low),
            pltpu.VMEM((tasks, KEYS, 2 * BLOCK), full),
            pltpu.VMEM((tasks * KEYS // BLOCK, BLOCK), full),
            pltpu.VMEM((tasks * KEYS // BLOCK, BLOCK), full),
            pltpu.VMEM((tasks * KEYS // BLOCK, BLOCK), full),
            pltpu.VMEM((2, LANES, 2 * BLOCK), full),
            pltpu.VMEM((2 * owners, LANES), full),
            pltpu.VMEM((2 * owners, LANES), full),
        ],
        compiler_params=params(6 + total_keys * 5 * 256 // MIB),
        cost_estimate=pl.CostEstimate(
            flops=2_500_000_000 * len(places), bytes_accessed=2 * MIB, transcendentals=0
        ),
        name="attention",
    )(*operands)
    return found[0], found[1 : len(outs)], found[len(outs) : len(outs) + 4], found[-1]


def combine_kernel(heads, terms, *refs):
    out_ref = refs[-1]
    rows = out_ref.shape[1]
    for r in range(heads):
        cut = slice(r * rows, (r + 1) * rows)
        total = refs[0][cut, :]
        for term in refs[1:terms]:
            total = total + term[cut, :]
        out_ref[r, :, LANES:] = total.astype(low)
    at = 0
    for first_ref in refs[terms:-1]:
        out_ref[at : at + first_ref.shape[0], :, :LANES] = first_ref[...]
        at += first_ref.shape[0]


def combine(heads, terms, firsts):
    rows = firsts[0].shape[1]
    return pl.pallas_call(
        functools.partial(combine_kernel, heads, len(terms)),
        out_shape=shape_of((heads, rows, 2 * LANES), low),
        in_specs=[spec_vmem()] * (len(firsts) + len(terms)),
        out_specs=spec_vmem(),
        compiler_params=params(24),
        cost_estimate=pl.CostEstimate(flops=10**7, bytes_accessed=3 * MIB, transcendentals=0),
        name="combine",
    )(*terms, *firsts)


def weight_grads_kernel(
    heads, early, ids_ref, got_ref, h1_ref, cot_ref, ready_ref, low_ref, d_b_ref, keep_ref, early_ref, send_ref, token_ref, grads
):
    del ready_ref
    chips, chunk_rows = keep_ref.shape[:2]

    def put(at, tile):
        step = min(chunk_rows, tile.shape[0])
        for off in range(0, tile.shape[0], step):
            chunk, inside = divmod(at + off, chunk_rows)
            grads[chunk, inside : inside + step] = tile[off : off + step]

    rows = h1_ref.shape[0]
    left = lane_ids((rows, LANES)) < HEAD_DIM
    for i in range(heads // 2):
        cut = slice(i * LANES, (i + 1) * LANES)
        for first, second, half in ((0, 1, slice(0, LANES)), (3, 2, slice(LANES, 2 * LANES))):
            a, b = got_ref[2 * i, :, half].astype(full), got_ref[2 * i + 1, :, half].astype(full)
            low_ref[first, :, cut] = jnp.where(left, a, pltpu.roll(b, HEAD_DIM, 1)).astype(low)
            low_ref[second, :, cut] = jnp.where(left, pltpu.roll(a, HEAD_DIM, 1), b).astype(low)
    h1_turned = turn(h1_ref[...])
    depth, tiles = h1_turned.shape[0], heads // 2
    for s in range(3):
        d_proj = low_ref[1 + s]
        d_b_ref[s : s + 1] = jnp.sum(d_proj.astype(full), axis=0, keepdims=True)
        grad = mm(h1_turned, d_proj).astype(low)
        for t in range(tiles):
            put((s * tiles + t) * depth, grad[:, t * LANES : (t + 1) * LANES])
    grad = mm(turn(low_ref[0]), cot_ref[...]).astype(low)
    height = grad.shape[0]
    for t in range(depth // LANES):
        put(3 * tiles * depth + t * height, grad[:, t * LANES : (t + 1) * LANES])
    for t in range(chips):
        target = early_ref.at[t] if t < early else send_ref.at[t - early]
        target[...] = grads[ids_ref[chips + t]]
        keep_ref[t] = grads[ids_ref[t]]
    token_ref[...] = jnp.zeros_like(token_ref)


def weight_grads(heads, early, ids, got, h1, cot, ready):
    rows, width = h1.shape
    local_width = heads * HEAD_DIM
    chips = ids.shape[0] // 2
    chunk_rows = 4 * width * local_width // LANES // (2 * chips)
    outs = [
        shape_of((4, rows, local_width), low),
        shape_of((3, local_width), full),
        shape_of((chips, chunk_rows, LANES), low),
        shape_of((early, chunk_rows, LANES), low),
        shape_of((chips - early, chunk_rows, LANES), low),
        shape_of((1, LANES), full),
    ]
    return pl.pallas_call(
        functools.partial(weight_grads_kernel, heads, early),
        out_shape=outs,
        in_specs=[spec_smem()] + [spec_vmem()] * 4,
        out_specs=[spec_vmem()] * len(outs),
        scratch_shapes=[pltpu.VMEM((2 * chips, chunk_rows, LANES), low)],
        compiler_params=params(20),
        cost_estimate=pl.CostEstimate(
            flops=8 * rows * width * local_width, bytes_accessed=8 * MIB, transcendentals=0
        ),
        name="weight_grads",
    )(ids, got, h1, cot, ready)


def return_kernel(low_ref, part_ref, w_out_ref, w_qkv_ref, xhat_ref, both_ref, sums_ref):
    rows = xhat_ref.shape[0]
    both_ref[:rows] = (part_ref[...] + mm(low_ref[0], w_out_ref[...])).astype(low)
    back = mm_nt(low_ref[1], w_qkv_ref[0]) + mm_nt(low_ref[2], w_qkv_ref[1]) + mm_nt(low_ref[3], w_qkv_ref[2])
    both_ref[rows:] = back.astype(low)
    sums_ref[0:1] = jnp.sum(back * xhat_ref[...], axis=0, keepdims=True)
    sums_ref[1:2] = jnp.sum(back, axis=0, keepdims=True)


def back_projections(*given):
    rows, width = given[1].shape
    return pl.pallas_call(
        return_kernel,
        out_shape=[shape_of((2 * rows, width), low), shape_of((2, width), full)],
        in_specs=[spec_vmem()] * len(given),
        out_specs=[spec_vmem()] * 2,
        compiler_params=params(16),
        cost_estimate=pl.CostEstimate(
            flops=8 * rows * width * given[2].shape[0], bytes_accessed=8 * MIB, transcendentals=0
        ),
        name="back_projections",
    )(*given)


def finish_kernel(
    hidden_ref, cot_ref, xhat_ref, std_ref, gains_ref, bias_ref, ours_ref, theirs_ref, e2_ours_ref, e2_theirs_ref, out_ref, grad_ref, token_ref
):
    rows = hidden_ref.shape[0]
    gains = gains_ref[...]
    biases = bias_ref[...]
    summed = ours_ref[:rows].astype(full) + theirs_ref[:rows].astype(full)
    out_ref[...] = (hidden_ref[...].astype(full) + summed + biases[0:1] + biases[1:2]).astype(low)
    e1 = ours_ref[rows:].astype(full) + theirs_ref[rows:].astype(full)
    e2 = e2_ours_ref[...].astype(full) + e2_theirs_ref[...].astype(full)
    f = e1 * gains[0:1] + e2 * gains[1:2]
    xhat = xhat_ref[...]
    inv_std = std_ref[:, 0:1]
    grad_ref[...] = cot_ref[...].astype(full) + inv_std * (
        f - jnp.mean(f, axis=-1, keepdims=True) - xhat * jnp.mean(f * xhat, axis=-1, keepdims=True)
    )
    token_ref[...] = jnp.zeros_like(token_ref)


def finish(*operands):
    rows, width = operands[0].shape
    return pl.pallas_call(
        finish_kernel,
        out_shape=[shape_of((rows, width), low), shape_of((rows, width), full), shape_of((1, LANES), full)],
        in_specs=[spec_vmem()] * len(operands),
        out_specs=[spec_vmem()] * 3,
        compiler_params=params(24),
        cost_estimate=pl.CostEstimate(flops=10**7, bytes_accessed=8 * MIB, transcendentals=0),
        name="finish",
    )(*operands)


def to_attention(width, local_width, source, refs, base, unit):
    qkv_ref, out_ref = refs
    tiles = local_width // LANES
    split = 3 * tiles * width
    tile = base // width
    row = pl.multiple_of(lax.rem(base, width), unit)
    column = pl.multiple_of(lax.rem(tile, tiles) * LANES, LANES)
    yield base < split, source, qkv_ref.at[jnp.minimum(tile // tiles, 2), pl.ds(row, unit), pl.ds(column, LANES)]
    after = jnp.maximum(base - split, 0)
    row = pl.multiple_of(lax.rem(after, local_width), unit)
    column = pl.multiple_of(after // local_width * LANES, LANES)
    yield base >= split, source, out_ref.at[pl.ds(row, unit), pl.ds(column, LANES)]


def to_mlp(width, source, refs, base, unit):
    up_ref, down_ref = refs
    block, inside = base // (2 * width), lax.rem(base, 2 * width)
    block_at = pl.multiple_of(block * LANES, LANES)
    row = pl.multiple_of(jnp.minimum(inside, width - unit), unit)
    yield inside < width, source, up_ref.at[pl.ds(row, unit), pl.ds(block_at, LANES)]
    for t in range(unit // LANES):
        column = pl.multiple_of(jnp.maximum(inside - width, 0) + t * LANES, LANES)
        cut = source.at[pl.ds(t * LANES, LANES), :]
        yield inside >= width, cut, down_ref.at[pl.ds(block_at, LANES), pl.ds(column, LANES)]


def unpack_kernel(route, count, unit, has_old, ids_ref, *rest):
    parts, rest = rest[:count], rest[count:]
    rest = rest[2:] if has_old else rest
    targets, (token_ref, held, sems) = rest[:2], rest[2:]
    token_ref[...] = jnp.zeros_like(token_ref)
    chunk_rows = parts[0].shape[0]
    units = chunk_rows // unit
    per_unit = sems.shape[0] // (count * units)

    def moves():
        for i in range(count):
            for j in range(units):
                source = held.at[i, pl.ds(j * unit, unit), :]
                base = ids_ref[i] * chunk_rows + j * unit
                for n, (applies, piece, target) in enumerate(route(source, targets, base, unit)):
                    sem = sems.at[(i * units + j) * per_unit + n]
                    yield i, applies, pltpu.make_async_copy(piece, target, sem)

    done = -1
    for i, applies, copy in moves():
        if i != done:
            held[i] = parts[i][...].astype(full)
            done = i
        pl.when(applies)(copy.start)
    for i, applies, copy in moves():
        pl.when(applies)(copy.wait)


def unpack(name, route, cases, unit, shapes, ids, parts, old):
    count = len(parts)
    chunk_rows = parts[0].shape[0]
    operands = [ids, *parts, *(old or ())]
    return pl.pallas_call(
        functools.partial(unpack_kernel, route, count, unit, old is not None),
        out_shape=[shape_of(shape, full) for shape in shapes] + [shape_of((1, LANES), full)],
        in_specs=[spec_smem()] + [spec_vmem()] * count + [spec_hbm()] * (len(operands) - 1 - count),
        out_specs=[spec_hbm()] * 2 + [spec_vmem()],
        input_output_aliases={} if old is None else {1 + count: 0, 2 + count: 1},
        scratch_shapes=[
            pltpu.VMEM((count, chunk_rows, LANES), full),
            pltpu.SemaphoreType.DMA((count * (chunk_rows // unit) * cases,)),
        ],
        compiler_params=params(8 + count * chunk_rows * 3 * LANES * 2 // MIB),
        cost_estimate=pl.CostEstimate(
            flops=10**6, bytes_accessed=count * chunk_rows * LANES * 6, transcendentals=0
        ),
        name=name,
    )(*operands)


def local(
    hidden,
    pair_of,
    ln1_gain,
    ln1_bias,
    ln2_gain,
    ln2_bias,
    w_qkv,
    b_qkv,
    w_out,
    b_out,
    w_up,
    b_up,
    w_down,
    b_down,
    cotangent,
):
    owners = lax.axis_size("ctx")
    sides = lax.axis_size("tp")
    rows, width = hidden.shape
    local_width = w_qkv.shape[2]
    hidden_units = w_up.shape[1]
    heads = local_width // HEAD_DIM
    group = owners // heads

    exponent = np.arange(0, ROT, 2, dtype=np.float32) / np.float32(ROT)
    inverse = jnp.asarray(np.tile(np.float32(10000.0) ** (-exponent), LANES // HALF)[None, :], full)
    order = (0, 2, 4, 6, 7, 5, 3, 1) if owners == 16 else tuple(range(owners // 2))
    chips = len(order)

    def to_heads(array):
        groups = [[h * group + g for h in range(heads)] for g in range(group)]
        return lax.all_to_all(array, "ctx", 0, 0, axis_index_groups=groups, tiled=True)

    def group_shift(array, d):
        pairs = [(c, c // group * group + (c % group + d) % group) for c in range(owners)]
        return lax.ppermute(array, "ctx", pairs)

    me = lax.axis_index("ctx")
    chip, core = me // 2, lax.rem(me, 2)
    place = sum(jnp.where(chip == c, i, 0) for i, c in enumerate(order))
    way = 1 - 2 * core
    far, near = chips // 2, chips - 1 - chips // 2

    def ring(array, forward):
        pairs = []
        for i, c in enumerate(order):
            for k in range(2):
                step = 1 if (k == 0) == forward else -1
                pairs.append((2 * c + k, 2 * order[(i + step) % chips] + k))
        return lax.ppermute(array, "ctx", pairs)

    def other_core(array):
        return lax.ppermute(array, "ctx", [(c, c ^ 1) for c in range(owners)])

    def across(array):
        return lax.ppermute(array, "tp", [(t, (t + 1) % sides) for t in range(sides)])

    def target(distance):
        return lax.rem(place + way * distance + chips, chips)

    def zero(array):
        return array[:1].astype(full) * 0.0

    slots = [far, -near]
    for t in range(1, far):
        slots += [far - t] if t >= near else [far - t, t - near]
    slots.append(0)
    early = 2
    slot_ids = jnp.stack(
        [core * chips + target(d) for d in slots] + [(1 - core) * chips + target(-d) for d in slots]
    )

    def terms_of(keep, came):
        def term(i):
            return keep[i].astype(full) + came[i].astype(full)

        return {d: term(i) for i, d in enumerate(slots)}

    def scatter_start(terms, token):
        return (terms[far] + token).astype(low), (terms[-near] + token).astype(low)

    def scatter_step(terms, t, sends, token):
        long_send, short_send = sends
        long_got = ring(long_send, True).astype(full) + token
        last = t == far - 1
        long_next = long_got if last else (long_got + terms[far - 1 - t]).astype(low)
        short_next = short_send
        if t < near:
            short_got = ring(short_send, False).astype(full) + token
            short_next = short_got if t == near - 1 else (short_got + terms[t + 1 - near]).astype(low)
        if last:
            return (terms[0] + long_next + short_next).astype(low)
        return long_next, short_next

    base, other_base = core * chips, (1 - core) * chips

    def gather_start(own):
        return [(own, base + place), (other_core(own), other_base + place)]

    def gather_step(t, sends, token):
        long_send, short_send = sends
        if token is not None:
            long_send = (long_send.astype(full) + token).astype(low)
        long_got = ring(long_send, True)
        found = [(long_got, base + target(-t - 1)), (other_core(long_got), other_base + target(t + 1))]
        short_got = short_send
        if t < near:
            short_got = ring(short_send, False)
            found += [(short_got, base + target(t + 1)), (other_core(short_got), other_base + target(-t - 1))]
        return (long_got, short_got), found

    blocks = hidden_units // LANES // 2
    in_slots = blocks == chips
    mlp_ids = slot_ids if in_slots else jnp.concatenate(
        [core * blocks + jnp.arange(blocks), (1 - core) * blocks + jnp.arange(blocks)]
    )
    h1, h2, xhat, inv_std, d_bias, gains, biases, b_up_row, packed = project(
        heads,
        pair_of,
        inverse,
        (hidden, ln1_gain, ln1_bias, ln2_gain, ln2_bias, cotangent, w_out, w_qkv, b_qkv, b_up, b_out, b_down),
    )
    got = to_heads(packed)
    part, back2, sums2, d_b_up, keep_mlp, early_mlp, send_mlp = mlp(
        mlp_ids.astype(jnp.int32), early, h2, w_up, b_up_row, cotangent, w_down, xhat
    )
    chunk = keep_mlp.shape[0] // chips
    came_mlp = jnp.concatenate([other_core(early_mlp), other_core(send_mlp)]) if not in_slots else None
    if in_slots:
        halves = [other_core(array).reshape(-1, chunk, LANES) for array in (early_mlp, send_mlp)]
        came_mlp = [half[i] for half in halves for i in range(half.shape[0])]
        terms_mlp = terms_of(keep_mlp.reshape(chips, chunk, LANES), came_mlp)
    else:
        summed = (keep_mlp.astype(full) + came_mlp.astype(full)).reshape(chips, chunk, LANES)
        terms_mlp = {d: lax.dynamic_index_in_dim(summed, target(d), 0, keepdims=False) for d in slots}
    nothing = jnp.zeros((1, LANES), full)

    other = None
    if group > 1:
        mine = got[:, :, LANES:].reshape(heads * rows, LANES)
        other = jnp.stack([group_shift(mine, group - d) for d in range(1, group)])

    middle = heads // 4
    first, _, state, token = attention(
        heads, group, tuple(range(middle)), pair_of, inverse, sums2, got, other, None
    )
    sends_mlp = scatter_start(terms_mlp, token)
    token = zero(sends_mlp[0]) + zero(sends_mlp[1])
    second, ends, _, token = attention(
        heads, group, tuple(range(middle, heads)), pair_of, inverse, token, got, other, state
    )
    d_own, d_other = ends[0], (ends[1] if group > 1 else None)
    terms = [d_own] + [group_shift(d_other[d - 1], d) for d in range(1, group)]
    sends_mlp = scatter_step(terms_mlp, 0, sends_mlp, token)
    first = (first.astype(full) + zero(sends_mlp[0]) + zero(sends_mlp[1])).astype(low)
    combined = combine(heads, terms, [first, second])
    backs = to_heads(combined)
    theirs2 = across((back2.astype(full) + zero(combined[0])[:, :1]).astype(low))
    sends_mlp = scatter_step(terms_mlp, 1, sends_mlp, nothing)
    ready = zero(sends_mlp[0]) + zero(sends_mlp[1]) + zero(theirs2)[:, :LANES]

    lows, d_b_qkv, keep, early_att, send_att, after = weight_grads(
        heads, early, slot_ids.astype(jnp.int32), backs, h1, cotangent, ready
    )
    both, sums1 = back_projections(lows, part, w_out, w_qkv, xhat)
    theirs = across(both)
    output, d_hidden, finish_token = finish(
        hidden, cotangent, xhat, inv_std, gains, biases, both, theirs, back2, theirs2
    )
    halves = [other_core(array) for array in (early_att, send_att)]
    terms_att = terms_of(keep, [half[i] for half in halves for i in range(half.shape[0])])

    small = jnp.concatenate(
        [sums1.reshape(1, -1), sums2.reshape(1, -1), d_bias, d_b_up, d_b_qkv.reshape(1, -1)], axis=1
    )

    def unpack_some(name, route, cases, unit, shapes, found, old):
        parts, ids = zip(*found)
        *old, token = unpack(name, route, cases, unit, shapes, jnp.stack(ids), parts, old)
        return old, token

    unit_mlp = min(chunk, local_width)
    unit_att = min(keep.shape[1], local_width)
    unpack_mlp = functools.partial(
        unpack_some,
        "unpack_feed_forward",
        functools.partial(to_mlp, width),
        1 + unit_mlp // LANES,
        unit_mlp,
        ((width, hidden_units), (hidden_units, width)),
    )
    unpack_att = functools.partial(
        unpack_some,
        "unpack_attention",
        functools.partial(to_attention, width, local_width),
        2,
        unit_att,
        ((3, width, local_width), (local_width, width)),
    )

    steps_mlp, steps_round = iter(range(2, far)), iter(range(far))
    own_mlp, round_mlp, waiting, grads_mlp = None, None, [], None

    def advance_mlp(token, gate=None):
        nonlocal sends_mlp, own_mlp, round_mlp, waiting
        t = next(steps_mlp, None)
        if t is not None:
            sends_mlp = scatter_step(terms_mlp, t, sends_mlp, token)
            if t < far - 1:
                return zero(sends_mlp[0])
            own_mlp, round_mlp = sends_mlp, (sends_mlp, sends_mlp)
            waiting += gather_start(own_mlp)
            return zero(own_mlp)
        t = next(steps_round, None)
        if t is None:
            return nothing
        round_mlp, found = gather_step(t, round_mlp, gate)
        waiting += found
        return zero(round_mlp[0])

    sends_att = scatter_start(terms_att, nothing)
    for t in range(far):
        sends_att = scatter_step(terms_att, t, sends_att, advance_mlp(nothing))
    round_att, waiting_att, grads_att = (sends_att, sends_att), gather_start(sends_att), None
    small = small + zero(sends_att)[:, :1]
    distance = 1
    for t in range(far):
        ready, waiting = waiting, []
        advance_mlp(nothing, zero(round_att[0]))
        round_att, found = gather_step(t, round_att, None)
        waiting_att += found
        if distance < owners:
            small = small + lax.ppermute(small, "ctx", [(c, c ^ distance) for c in range(owners)])
            distance *= 2
        if ready:
            grads_mlp, more = unpack_mlp(ready, grads_mlp)
            small = small + more[:, :1]
        if t == far - 2:
            small = small + finish_token[:, :1]
            grads_att, more = unpack_att(waiting_att[:-4], None)
            waiting_att = waiting_att[-4:]
            small = small + more[:, :1]
    while distance < owners:
        small = small + lax.ppermute(small, "ctx", [(c, c ^ distance) for c in range(owners)])
        distance *= 2
    if waiting:
        grads_mlp, _ = unpack_mlp(waiting, grads_mlp)
    grads_att, _ = unpack_att(waiting_att, grads_att)

    norm_sums = small[:, : 4 * width]
    norm_sums = (norm_sums + across(norm_sums)).reshape(4, width)
    at = 4 * width
    d_bias = small[0, at : at + width]
    d_b_up = small[0, at + width : at + width + hidden_units]
    d_b_qkv = small[0, at + width + hidden_units :].reshape(3, local_width)
    d_w_up, d_w_down = grads_mlp
    d_w_qkv, d_w_out = grads_att
    return (
        output,
        d_hidden,
        norm_sums[0],
        norm_sums[1],
        norm_sums[2],
        norm_sums[3],
        d_w_qkv,
        d_b_qkv,
        d_w_out,
        d_bias,
        d_w_up,
        d_b_up,
        d_w_down,
        d_bias,
    )


def solution(mesh):
    placed = (
        P("ctx", None),
        P(),
        P(),
        P(),
        P(),
        P(),
        P(None, None, "tp"),
        P(None, "tp"),
        P("tp", None),
        P(),
        P(None, "tp"),
        P("tp"),
        P("tp", None),
        P(),
        P("ctx", None),
    )
    return jax.shard_map(
        local,
        mesh=mesh,
        in_specs=placed,
        out_specs=(
            P("ctx", None),
            P("ctx", None),
            P(),
            P(),
            P(),
            P(),
            P(None, None, "tp"),
            P(None, "tp"),
            P("tp", None),
            P(),
            P(None, "tp"),
            P("tp"),
            P("tp", None),
            P(),
        ),
        check_vma=False,
    )
```

```python
import functools

import jax
import jax.numpy as jnp
import numpy as np
from jax import lax
from jax.experimental import pallas as pl
from jax.experimental.pallas import tpu as pltpu
from jax.sharding import PartitionSpec as P

HEAD_DIM = 64
ROT = 16
HALF = ROT // 2
BLOCK = 128
LANES = 128
KEYS = 512
MIB = 1 << 20

norm_eps = 1e-05
masked_score = -1e30
score_scale = HEAD_DIM ** (-0.5)
low = jnp.bfloat16
full = jnp.float32


def mm(left, right):
    return lax.dot_general(left, right, (((1,), (0,)), ((), ())), preferred_element_type=full)


def mm_nt(left, right):
    return lax.dot_general(left, right, (((1,), (1,)), ((), ())), preferred_element_type=full)


def turn(tensor):
    return tensor.astype(full).T.astype(low)


def lane_ids(shape):
    return lax.broadcasted_iota(jnp.int32, shape, len(shape) - 1)


def row_ids(shape):
    return lax.broadcasted_iota(jnp.int32, shape, len(shape) - 2)


def rotary_partner(tensor):
    lanes = lane_ids(tensor.shape)
    ahead = pltpu.roll(tensor, LANES - HALF, 1)
    behind = pltpu.roll(tensor, HALF, 1)
    return jnp.where(lanes % ROT < HALF, ahead, behind)


def spec_vmem():
    return pl.BlockSpec(memory_space=pltpu.VMEM)


def spec_smem():
    return pl.BlockSpec(memory_space=pltpu.SMEM)


def spec_hbm():
    return pl.BlockSpec(memory_space=pltpu.HBM)


def params(mib):
    return pltpu.CompilerParams(vmem_limit_bytes=mib * MIB)


def shape_of(shape, kind):
    return jax.ShapeDtypeStruct(shape, kind)


def block_tables(inverse, blocks):
    row = row_ids((BLOCK, LANES)).astype(full)
    start = blocks.astype(full) * float(BLOCK)
    return jnp.cos(row * inverse), jnp.sin(row * inverse), jnp.cos(start * inverse), jnp.sin(start * inverse)


def project_kernel(heads, pair_ref, inv_ref, *rest):
    given, rest = rest[:12], rest[12:]
    h1_ref, h2_ref, xhat_ref, std_ref, d_bias_ref, gains_ref, bias_ref, b_up_out_ref, packed = rest[:9]
    held, sems = rest[9:-1], rest[-1]
    copies = [pltpu.make_async_copy(src, dst, sems.at[i]) for i, (src, dst) in enumerate(zip(given, held))]
    for copy in copies:
        copy.start()
    (
        hidden_ref,
        g1_ref,
        c1_ref,
        g2_ref,
        c2_ref,
        cot_ref,
        w_out_ref,
        w_qkv_ref,
        b_qkv_ref,
        b_up_ref,
        b_out_ref,
        b_down_ref,
    ) = held
    rows = hidden_ref.shape[0]
    me = lax.axis_index("ctx")
    pair = pair_ref[me]
    total_blocks = 2 * pair_ref.shape[0]

    first = jnp.where(row_ids((8, LANES)) == 0, pair, total_blocks - 1 - pair)
    inverse = inv_ref[...]
    cos_row, sin_row, cos_block, sin_block = block_tables(inverse, first)
    in_head = lane_ids((BLOCK, LANES)) % HEAD_DIM
    tables = []
    for half in range(2):
        cos_at, sin_at = cos_block[half : half + 1], sin_block[half : half + 1]
        cosine = cos_row * cos_at - sin_row * sin_at
        sine = sin_row * cos_at + cos_row * sin_at
        cosine = jnp.where(in_head < ROT, cosine, 1.0)
        sine = jnp.where(in_head < HALF, -sine, jnp.where(in_head < ROT, sine, 0.0))
        tables.append((cosine, sine))
    cosine = jnp.concatenate([tables[0][0], tables[1][0]], axis=0)
    sine = jnp.concatenate([tables[0][1], tables[1][1]], axis=0)

    for copy in copies[:5]:
        copy.wait()
    x = hidden_ref[...].astype(full)
    centred = x - jnp.mean(x, axis=-1, keepdims=True)
    spread = jnp.mean(centred * centred, axis=-1, keepdims=True)
    inv_std = lax.rsqrt(spread + norm_eps)
    xhat = centred * inv_std
    xhat_ref[...] = xhat
    std_ref[...] = jnp.broadcast_to(inv_std, std_ref.shape)

    def as_row(ref):
        return ref[...].astype(full)[None, :]

    gain1, gain2 = as_row(g1_ref), as_row(g2_ref)
    h1 = (xhat * gain1 + as_row(c1_ref)).astype(low)
    h1_ref[...] = h1
    h2_ref[...] = (xhat * gain2 + as_row(c2_ref)).astype(low)
    gains_ref[0:1] = gain1
    gains_ref[1:2] = gain2
    for copy in copies[5:]:
        copy.wait()
    b_up_out_ref[...] = as_row(b_up_ref)
    bias_ref[0:1] = as_row(b_out_ref)
    bias_ref[1:2] = as_row(b_down_ref)
    d_bias_ref[...] = jnp.sum(cot_ref[...].astype(full), axis=0, keepdims=True)

    lane = lane_ids((rows, LANES))

    def projected(s):
        return mm(h1, w_qkv_ref[s]) + b_qkv_ref[s : s + 1].astype(full)

    def turned(tile):
        return tile * cosine + rotary_partner(tile) * sine

    queries, keys, values = projected(0), projected(1), projected(2)
    grads = mm_nt(cot_ref[...], w_out_ref[...])
    left = lane < HEAD_DIM
    for i in range(heads // 2):
        cut = slice(i * LANES, (i + 1) * LANES)
        q = turned(queries[:, cut]).astype(low).astype(full) * score_scale
        k = turned(keys[:, cut])
        v = values[:, cut]
        g = grads[:, cut]
        packed[2 * i, :, :LANES] = jnp.where(left, g, pltpu.roll(q, HEAD_DIM, 1)).astype(low)
        packed[2 * i, :, LANES:] = jnp.where(left, v, pltpu.roll(k, HEAD_DIM, 1)).astype(low)
        packed[2 * i + 1, :, :LANES] = jnp.where(left, pltpu.roll(g, HEAD_DIM, 1), q).astype(low)
        packed[2 * i + 1, :, LANES:] = jnp.where(left, pltpu.roll(v, HEAD_DIM, 1), k).astype(low)


def project(heads, pair_of, inverse, given):
    hidden, w_out, b_up = given[0], given[6], given[9]
    rows, width = hidden.shape
    outs = [
        shape_of((rows, width), low),
        shape_of((rows, width), low),
        shape_of((rows, width), full),
        shape_of((rows, LANES), full),
        shape_of((1, width), full),
        shape_of((2, width), full),
        shape_of((2, width), full),
        shape_of((1, b_up.shape[0]), full),
        shape_of((heads, rows, 2 * LANES), low),
    ]
    return pl.pallas_call(
        functools.partial(project_kernel, heads),
        out_shape=outs,
        in_specs=[spec_smem(), spec_vmem()] + [spec_hbm()] * len(given),
        out_specs=[spec_vmem()] * len(outs),
        scratch_shapes=[pltpu.VMEM(array.shape, array.dtype) for array in given]
        + [pltpu.SemaphoreType.DMA((len(given),))],
        compiler_params=params(60),
        cost_estimate=pl.CostEstimate(
            flops=2 * rows * width * 4 * w_out.shape[0], bytes_accessed=8 * MIB, transcendentals=0
        ),
        name="project",
    )(pair_of, inverse, *given)


def mlp_kernel(early, ids_ref, *rest):
    given, rest = rest[:6], rest[6:]
    part_ref, back_ref, sums_ref, d_b_up_ref, keep_ref, early_ref, send_ref = rest[:7]
    h2_turned, part_acc, back_acc = rest[7:10]
    held, sems = rest[10:-1], rest[-1]
    copies = [pltpu.make_async_copy(src, dst, sems.at[i]) for i, (src, dst) in enumerate(zip(given, held))]
    h2_held, w_up_ref, b_up, cot_ref, w_down_ref, xhat_ref = held
    step = pl.program_id(0)
    steps = pl.num_programs(0)

    @pl.when(step == 0)
    def _():
        for copy in copies:
            copy.start()
        part_acc[...] = jnp.zeros_like(part_acc)
        back_acc[...] = jnp.zeros_like(back_acc)
        copies[0].wait()
        h2_turned[...] = turn(h2_held[...])
        for copy in copies[1:3]:
            copy.wait()

    at = [pl.multiple_of(ids_ref[b * steps + step] * LANES, LANES) for b in range(2)]
    w_up = jnp.concatenate([w_up_ref[:, pl.ds(i, LANES)] for i in at], axis=1)
    u = mm(h2_held[...], w_up) + jnp.concatenate([b_up[:, pl.ds(i, LANES)] for i in at], axis=1)

    @pl.when(step == 0)
    def _():
        for copy in copies[3:5]:
            copy.wait()

    cot = cot_ref[...]
    w_down = jnp.concatenate([w_down_ref[pl.ds(i, LANES), :] for i in at], axis=0)
    cdf = 0.5 * (1.0 + lax.erf(u * np.float32(np.sqrt(0.5))))
    active = u * cdf
    active_low = active.astype(low)
    slope = cdf + u * jnp.exp(-0.5 * u * u) * np.float32(1.0 / np.sqrt(2.0 * np.pi))
    du = (mm_nt(cot, w_down) * slope).astype(low)
    part_acc[...] += mm(active_low, w_down)
    back_acc[...] += mm_nt(du, w_up)
    d_b_up = jnp.sum(du.astype(full), axis=0, keepdims=True)
    up = mm(h2_turned[...], du).astype(low)
    down = mm(active.T.astype(low), cot).astype(low)
    depth = up.shape[0]

    def put(b, grad_ref):
        grad_ref[:depth] = up[:, b * LANES : (b + 1) * LANES]
        for t in range(down.shape[1] // LANES):
            grad_ref[depth + t * LANES : depth + (t + 1) * LANES] = down[
                b * LANES : (b + 1) * LANES, t * LANES : (t + 1) * LANES
            ]

    for b in range(2):
        d_b_up_ref[:, pl.ds(at[b], LANES)] = d_b_up[:, b * LANES : (b + 1) * LANES]
    put(0, keep_ref)

    @pl.when(step < early)
    def _():
        put(1, early_ref)

    @pl.when(step >= early)
    def _():
        put(1, send_ref)

    @pl.when(step == steps - 1)
    def _():
        copies[5].wait()
        part_ref[...] = part_acc[...]
        back = back_acc[...]
        back_ref[...] = back.astype(low)
        sums_ref[0:1] = jnp.sum(back * xhat_ref[...], axis=0, keepdims=True)
        sums_ref[1:2] = jnp.sum(back, axis=0, keepdims=True)


def mlp(ids, early, *given):
    rows, width = given[0].shape
    hidden_units = given[1].shape[1]
    steps = hidden_units // LANES // 2
    whole = lambda shape: pl.BlockSpec(shape, lambda f, c: (0,) * len(shape))
    grads = lambda at: pl.BlockSpec((2 * width, LANES), lambda f, c: (at(f), 0))
    outs = [
        shape_of((rows, width), full),
        shape_of((rows, width), low),
        shape_of((2, width), full),
        shape_of((1, hidden_units), full),
        shape_of((steps * 2 * width, LANES), low),
        shape_of((early * 2 * width, LANES), low),
        shape_of(((steps - early) * 2 * width, LANES), low),
    ]
    return pl.pallas_call(
        functools.partial(mlp_kernel, early),
        grid_spec=pltpu.PrefetchScalarGridSpec(
            num_scalar_prefetch=1,
            grid=(steps,),
            in_specs=[spec_hbm()] * len(given),
            out_specs=[whole(array.shape) for array in outs[:4]]
            + [
                grads(lambda f: f),
                grads(lambda f: jnp.minimum(f, early - 1)),
                grads(lambda f: jnp.maximum(f - early, 0)),
            ],
            scratch_shapes=[
                pltpu.VMEM((width, rows), low),
                pltpu.VMEM((rows, width), full),
                pltpu.VMEM((rows, width), full),
            ]
            + [pltpu.VMEM(array.shape, array.dtype) for array in given]
            + [pltpu.SemaphoreType.DMA((len(given),))],
        ),
        out_shape=outs,
        compiler_params=params(60),
        cost_estimate=pl.CostEstimate(
            flops=12 * rows * width * hidden_units, bytes_accessed=20 * MIB, transcendentals=0
        ),
        name="feed_forward",
    )(ids, *given)


def attention_kernel(heads, group, places, is_first, is_last, pair_ref, inv_ref, token_ref, *rest):
    del token_ref
    if is_first:
        got_ref, rest = rest[0], rest[1:]
        if group > 1:
            other_ref, rest = rest[0], rest[1:]
    else:
        rest = rest[4:]
    out_ref, rest = rest[0], rest[1:]
    if is_last:
        d_own_ref, rest = rest[0], rest[1:]
        if group > 1:
            d_other_ref, rest = rest[0], rest[1:]
    (values_keys, turned_keys, sums, queries), rest = rest[:4], rest[4:]
    token_out, rest = rest[0], rest[1:]
    weights_in, weights_out, stored, peaks, totals, weighted, finals, block_cos, block_sin = rest
    token_out[...] = jnp.zeros_like(token_out)

    rows = queries.shape[1]
    owners = pair_ref.shape[0]
    total_blocks = 2 * owners
    per_chunk = KEYS // BLOCK
    tasks = (total_blocks + 1 + per_chunk - 1) // per_chunk
    me = lax.axis_index("ctx")
    own_sub = lax.rem(me, group)

    def blocks_of(r, d):
        owner = r * group + lax.rem(own_sub + d, group)
        pair = pair_ref[owner]
        return pair, total_blocks - 1 - pair

    def place(tile, block):
        at = pl.multiple_of(block * BLOCK, BLOCK)
        values_keys[pl.ds(at, BLOCK), :] = tile
        turned_keys[:, pl.ds(at, BLOCK)] = turn(tile)

    if is_first:
        for r in range(heads):
            queries[r] = got_ref[r, :, :LANES]
            for half, block in enumerate(blocks_of(r, 0)):
                place(got_ref[r, half * BLOCK : (half + 1) * BLOCK, LANES:], block)
            for d in range(1, group):
                for half, block in enumerate(blocks_of(r, d)):
                    at = r * rows + half * BLOCK
                    place(other_ref[d - 1, at : at + BLOCK, :], block)
        sums[...] = jnp.zeros_like(sums)

    lane = lane_ids((BLOCK, LANES))
    left = lane < HEAD_DIM
    in_key = lane - HEAD_DIM
    moving = (in_key >= 0) & (in_key < ROT)
    forward = (in_key >= 0) & (in_key < HALF)
    cos_row, sin_row, block_cos[...], block_sin[...] = block_tables(inv_ref[...], row_ids(block_cos.shape))

    def rotated_back(tile, block):
        cos_at, sin_at = block_cos[pl.ds(block, 1), :], block_sin[pl.ds(block, 1), :]
        cosine = jnp.where(moving, cos_row * cos_at - sin_row * sin_at, 1.0)
        sine = sin_row * cos_at + cos_row * sin_at
        sine = jnp.where(moving, jnp.where(forward, sine, -sine), 0.0)
        return tile * cosine + rotary_partner(tile) * sine

    offset = row_ids((BLOCK, BLOCK)) - lane_ids((BLOCK, BLOCK))

    def one_pair(i, carry):
        blocks = blocks_of(places[0] + i, 0)
        first = blocks[0] // per_chunk + 1
        for half in range(2):
            both = queries[places[0] + i, half * BLOCK : (half + 1) * BLOCK, :]
            both_turned = turn(both)
            upper = row_ids((LANES, BLOCK)) < HEAD_DIM
            zero = jnp.zeros_like(both_turned)
            weights_in[half, :, :BLOCK] = jnp.where(upper, both_turned, zero)
            weights_in[half, :, BLOCK:] = jnp.where(upper, zero, both_turned)
            weights_out[half, :BLOCK, :] = jnp.where(left, both, zero)
            weights_out[half, BLOCK:, :] = jnp.where(left, zero, both)
        finals[...] = jnp.zeros_like(finals)

        def task(t):
            is_low = t < first
            chunk = jnp.where(is_low, first - 1 - t, t - first)
            return is_low, chunk

        runs = KEYS // BLOCK
        for t in range(tasks):
            is_low, chunk = task(t)
            weights = weights_in[jnp.where(is_low, 0, 1)]
            for u in range(runs):
                at = pl.multiple_of(chunk * KEYS + u * BLOCK, BLOCK)
                sub = slice(u * BLOCK, (u + 1) * BLOCK)
                both = mm(values_keys[pl.ds(at, BLOCK), :], weights)
                grads = both[:, :BLOCK]
                scores = both[:, BLOCK:]
                if t in (0, tasks - 1):
                    query_at = blocks[0 if t == 0 else 1] * BLOCK
                    scores = jnp.where(offset <= query_at - at, scores, masked_score)
                peak = jnp.max(scores, axis=0, keepdims=True)
                raised = jnp.exp(scores - peak)
                stored[t, sub, :BLOCK] = raised
                stored[t, sub, BLOCK:] = grads
                line = t * runs + u
                peaks[line : line + 1] = peak
                totals[line : line + 1] = jnp.sum(raised, axis=0, keepdims=True)
                weighted[line : line + 1] = jnp.sum(raised * grads, axis=0, keepdims=True)

        in_low = row_ids((tasks * runs, BLOCK)) < first * runs

        def finish(mine):
            top = jnp.max(jnp.where(mine, peaks[...], masked_score), axis=0, keepdims=True)
            factor = jnp.where(mine, jnp.exp(peaks[...] - top), 0.0)
            inverse = 1.0 / jnp.sum(totals[...] * factor, axis=0, keepdims=True)
            return factor * inverse, jnp.sum(weighted[...] * factor, axis=0, keepdims=True) * inverse

        (low_factor, low_delta), (high_factor, high_delta) = finish(in_low), finish(jnp.logical_not(in_low))
        peaks[...] = low_factor + high_factor

        for t in range(tasks):
            is_low, chunk = task(t)
            half = jnp.where(is_low, 0, 1)
            weights = weights_out[half]
            delta = jnp.where(is_low, low_delta, high_delta)
            parts = []
            for u in range(runs):
                sub = slice(u * BLOCK, (u + 1) * BLOCK)
                probs = stored[t, sub, :BLOCK] * peaks[t * runs + u : t * runs + u + 1]
                d_scores = probs * (stored[t, sub, BLOCK:] - delta)
                both = jnp.concatenate([probs, d_scores], axis=1).astype(low)
                at = pl.multiple_of(chunk * KEYS + u * BLOCK, BLOCK)
                sums[pl.ds(at, BLOCK), :] += mm(both, weights)
                parts.append(both)
            at = pl.multiple_of(chunk * KEYS, KEYS)
            finals[half] += mm(turned_keys[:, pl.ds(at, KEYS)], jnp.concatenate(parts, axis=0))

        for half in range(2):
            both = jnp.concatenate(
                [finals[half, :HEAD_DIM, :BLOCK], finals[half, HEAD_DIM:, BLOCK:] * score_scale], axis=0
            ).T
            out_ref[i, half * BLOCK : (half + 1) * BLOCK, :] = rotated_back(both, blocks[half]).astype(low)
        return carry

    lax.fori_loop(0, len(places), one_pair, 0)

    if is_last:
        for r in range(heads):
            for d in range(group):
                for half, block in enumerate(blocks_of(r, d)):
                    at = r * rows + half * BLOCK
                    tile = rotated_back(sums[pl.ds(pl.multiple_of(block * BLOCK, BLOCK), BLOCK), :], block)
                    if d == 0:
                        d_own_ref[at : at + BLOCK, :] = tile
                    else:
                        d_other_ref[d - 1, at : at + BLOCK, :] = tile


def attention(heads, group, places, pair_of, inverse, token, got, other, state):
    is_first, is_last = state is None, places[-1] == heads - 1
    rows = got.shape[1]
    owners = pair_of.shape[0]
    total_keys = owners * rows
    tasks = (2 * owners + KEYS // BLOCK) // (KEYS // BLOCK)
    operands = [pair_of, inverse, token]
    outs = [shape_of((len(places), rows, LANES), low)]
    if is_first:
        operands += [got] if other is None else [got, other]
    else:
        operands += list(state)
    if is_last:
        outs.append(shape_of((heads * rows, LANES), full))
        if group > 1:
            outs.append(shape_of((group - 1, heads * rows, LANES), full))
    kept = [
        shape_of((total_keys, LANES), low),
        shape_of((LANES, total_keys), low),
        shape_of((total_keys, LANES), full),
        shape_of((heads, rows, LANES), low),
    ]
    aliases = {} if is_first else {len(operands) - 4 + i: len(outs) + i for i in range(4)}
    found = pl.pallas_call(
        functools.partial(attention_kernel, heads, group, places, is_first, is_last),
        out_shape=outs + kept + [shape_of((1, LANES), full)],
        in_specs=[spec_smem()] + [spec_vmem()] * (len(operands) - 1),
        out_specs=[spec_vmem()] * (len(outs) + 5),
        input_output_aliases=aliases,
        scratch_shapes=[
            pltpu.VMEM((2, LANES, 2 * BLOCK), low),
            pltpu.VMEM((2, 2 * BLOCK, LANES), low),
            pltpu.VMEM((tasks, KEYS, 2 * BLOCK), full),
            pltpu.VMEM((tasks * KEYS // BLOCK, BLOCK), full),
            pltpu.VMEM((tasks * KEYS // BLOCK, BLOCK), full),
            pltpu.VMEM((tasks * KEYS // BLOCK, BLOCK), full),
            pltpu.VMEM((2, LANES, 2 * BLOCK), full),
            pltpu.VMEM((2 * owners, LANES), full),
            pltpu.VMEM((2 * owners, LANES), full),
        ],
        compiler_params=params(6 + total_keys * 5 * 256 // MIB),
        cost_estimate=pl.CostEstimate(
            flops=2_500_000_000 * len(places), bytes_accessed=2 * MIB, transcendentals=0
        ),
        name="attention",
    )(*operands)
    return found[0], found[1 : len(outs)], found[len(outs) : len(outs) + 4], found[-1]


def combine_kernel(heads, terms, *refs):
    out_ref = refs[-1]
    rows = out_ref.shape[1]
    for r in range(heads):
        cut = slice(r * rows, (r + 1) * rows)
        total = refs[0][cut, :]
        for term in refs[1:terms]:
            total = total + term[cut, :]
        out_ref[r, :, LANES:] = total.astype(low)
    at = 0
    for first_ref in refs[terms:-1]:
        out_ref[at : at + first_ref.shape[0], :, :LANES] = first_ref[...]
        at += first_ref.shape[0]


def combine(heads, terms, firsts):
    rows = firsts[0].shape[1]
    return pl.pallas_call(
        functools.partial(combine_kernel, heads, len(terms)),
        out_shape=shape_of((heads, rows, 2 * LANES), low),
        in_specs=[spec_vmem()] * (len(firsts) + len(terms)),
        out_specs=spec_vmem(),
        compiler_params=params(24),
        cost_estimate=pl.CostEstimate(flops=10**7, bytes_accessed=3 * MIB, transcendentals=0),
        name="combine",
    )(*terms, *firsts)


def weight_grads_kernel(
    heads, early, ids_ref, got_ref, h1_ref, cot_ref, ready_ref, low_ref, d_b_ref, keep_ref, early_ref, send_ref, token_ref, grads
):
    del ready_ref
    chips, chunk_rows = keep_ref.shape[:2]

    def put(at, tile):
        step = min(chunk_rows, tile.shape[0])
        for off in range(0, tile.shape[0], step):
            chunk, inside = divmod(at + off, chunk_rows)
            grads[chunk, inside : inside + step] = tile[off : off + step]

    rows = h1_ref.shape[0]
    left = lane_ids((rows, LANES)) < HEAD_DIM
    for i in range(heads // 2):
        cut = slice(i * LANES, (i + 1) * LANES)
        for first, second, half in ((0, 1, slice(0, LANES)), (3, 2, slice(LANES, 2 * LANES))):
            a, b = got_ref[2 * i, :, half].astype(full), got_ref[2 * i + 1, :, half].astype(full)
            low_ref[first, :, cut] = jnp.where(left, a, pltpu.roll(b, HEAD_DIM, 1)).astype(low)
            low_ref[second, :, cut] = jnp.where(left, pltpu.roll(a, HEAD_DIM, 1), b).astype(low)
    h1_turned = turn(h1_ref[...])
    depth, tiles = h1_turned.shape[0], heads // 2
    for s in range(3):
        d_proj = low_ref[1 + s]
        d_b_ref[s : s + 1] = jnp.sum(d_proj.astype(full), axis=0, keepdims=True)
        grad = mm(h1_turned, d_proj).astype(low)
        for t in range(tiles):
            put((s * tiles + t) * depth, grad[:, t * LANES : (t + 1) * LANES])
    grad = mm(turn(low_ref[0]), cot_ref[...]).astype(low)
    height = grad.shape[0]
    for t in range(depth // LANES):
        put(3 * tiles * depth + t * height, grad[:, t * LANES : (t + 1) * LANES])
    for t in range(chips):
        target = early_ref.at[t] if t < early else send_ref.at[t - early]
        target[...] = grads[ids_ref[chips + t]]
        keep_ref[t] = grads[ids_ref[t]]
    token_ref[...] = jnp.zeros_like(token_ref)


def weight_grads(heads, early, ids, got, h1, cot, ready):
    rows, width = h1.shape
    local_width = heads * HEAD_DIM
    chips = ids.shape[0] // 2
    chunk_rows = 4 * width * local_width // LANES // (2 * chips)
    outs = [
        shape_of((4, rows, local_width), low),
        shape_of((3, local_width), full),
        shape_of((chips, chunk_rows, LANES), low),
        shape_of((early, chunk_rows, LANES), low),
        shape_of((chips - early, chunk_rows, LANES), low),
        shape_of((1, LANES), full),
    ]
    return pl.pallas_call(
        functools.partial(weight_grads_kernel, heads, early),
        out_shape=outs,
        in_specs=[spec_smem()] + [spec_vmem()] * 4,
        out_specs=[spec_vmem()] * len(outs),
        scratch_shapes=[pltpu.VMEM((2 * chips, chunk_rows, LANES), low)],
        compiler_params=params(20),
        cost_estimate=pl.CostEstimate(
            flops=8 * rows * width * local_width, bytes_accessed=8 * MIB, transcendentals=0
        ),
        name="weight_grads",
    )(ids, got, h1, cot, ready)


def return_kernel(low_ref, part_ref, w_out_ref, w_qkv_ref, xhat_ref, both_ref, sums_ref):
    rows = xhat_ref.shape[0]
    both_ref[:rows] = (part_ref[...] + mm(low_ref[0], w_out_ref[...])).astype(low)
    back = mm_nt(low_ref[1], w_qkv_ref[0]) + mm_nt(low_ref[2], w_qkv_ref[1]) + mm_nt(low_ref[3], w_qkv_ref[2])
    both_ref[rows:] = back.astype(low)
    sums_ref[0:1] = jnp.sum(back * xhat_ref[...], axis=0, keepdims=True)
    sums_ref[1:2] = jnp.sum(back, axis=0, keepdims=True)


def back_projections(*given):
    rows, width = given[1].shape
    return pl.pallas_call(
        return_kernel,
        out_shape=[shape_of((2 * rows, width), low), shape_of((2, width), full)],
        in_specs=[spec_vmem()] * len(given),
        out_specs=[spec_vmem()] * 2,
        compiler_params=params(16),
        cost_estimate=pl.CostEstimate(
            flops=8 * rows * width * given[2].shape[0], bytes_accessed=8 * MIB, transcendentals=0
        ),
        name="back_projections",
    )(*given)


def finish_kernel(
    hidden_ref, cot_ref, xhat_ref, std_ref, gains_ref, bias_ref, ours_ref, theirs_ref, e2_ours_ref, e2_theirs_ref, out_ref, grad_ref, token_ref
):
    rows = hidden_ref.shape[0]
    gains = gains_ref[...]
    biases = bias_ref[...]
    summed = ours_ref[:rows].astype(full) + theirs_ref[:rows].astype(full)
    out_ref[...] = (hidden_ref[...].astype(full) + summed + biases[0:1] + biases[1:2]).astype(low)
    e1 = ours_ref[rows:].astype(full) + theirs_ref[rows:].astype(full)
    e2 = e2_ours_ref[...].astype(full) + e2_theirs_ref[...].astype(full)
    f = e1 * gains[0:1] + e2 * gains[1:2]
    xhat = xhat_ref[...]
    inv_std = std_ref[:, 0:1]
    grad_ref[...] = cot_ref[...].astype(full) + inv_std * (
        f - jnp.mean(f, axis=-1, keepdims=True) - xhat * jnp.mean(f * xhat, axis=-1, keepdims=True)
    )
    token_ref[...] = jnp.zeros_like(token_ref)


def finish(*operands):
    rows, width = operands[0].shape
    return pl.pallas_call(
        finish_kernel,
        out_shape=[shape_of((rows, width), low), shape_of((rows, width), full), shape_of((1, LANES), full)],
        in_specs=[spec_vmem()] * len(operands),
        out_specs=[spec_vmem()] * 3,
        compiler_params=params(24),
        cost_estimate=pl.CostEstimate(flops=10**7, bytes_accessed=8 * MIB, transcendentals=0),
        name="finish",
    )(*operands)


def to_attention(width, local_width, source, refs, base, unit):
    qkv_ref, out_ref = refs
    tiles = local_width // LANES
    split = 3 * tiles * width
    tile = base // width
    row = pl.multiple_of(lax.rem(base, width), unit)
    column = pl.multiple_of(lax.rem(tile, tiles) * LANES, LANES)
    yield base < split, source, qkv_ref.at[jnp.minimum(tile // tiles, 2), pl.ds(row, unit), pl.ds(column, LANES)]
    after = jnp.maximum(base - split, 0)
    row = pl.multiple_of(lax.rem(after, local_width), unit)
    column = pl.multiple_of(after // local_width * LANES, LANES)
    yield base >= split, source, out_ref.at[pl.ds(row, unit), pl.ds(column, LANES)]


def to_mlp(width, source, refs, base, unit):
    up_ref, down_ref = refs
    block, inside = base // (2 * width), lax.rem(base, 2 * width)
    block_at = pl.multiple_of(block * LANES, LANES)
    row = pl.multiple_of(jnp.minimum(inside, width - unit), unit)
    yield inside < width, source, up_ref.at[pl.ds(row, unit), pl.ds(block_at, LANES)]
    for t in range(unit // LANES):
        column = pl.multiple_of(jnp.maximum(inside - width, 0) + t * LANES, LANES)
        cut = source.at[pl.ds(t * LANES, LANES), :]
        yield inside >= width, cut, down_ref.at[pl.ds(block_at, LANES), pl.ds(column, LANES)]


def unpack_kernel(route, count, unit, has_old, ids_ref, *rest):
    parts, rest = rest[:count], rest[count:]
    rest = rest[2:] if has_old else rest
    targets, (token_ref, held, sems) = rest[:2], rest[2:]
    token_ref[...] = jnp.zeros_like(token_ref)
    chunk_rows = parts[0].shape[0]
    units = chunk_rows // unit
    per_unit = sems.shape[0] // (count * units)

    def moves():
        for i in range(count):
            for j in range(units):
                source = held.at[i, pl.ds(j * unit, unit), :]
                base = ids_ref[i] * chunk_rows + j * unit
                for n, (applies, piece, target) in enumerate(route(source, targets, base, unit)):
                    sem = sems.at[(i * units + j) * per_unit + n]
                    yield i, applies, pltpu.make_async_copy(piece, target, sem)

    done = -1
    for i, applies, copy in moves():
        if i != done:
            held[i] = parts[i][...].astype(full)
            done = i
        pl.when(applies)(copy.start)
    for i, applies, copy in moves():
        pl.when(applies)(copy.wait)


def unpack(name, route, cases, unit, shapes, ids, parts, old):
    count = len(parts)
    chunk_rows = parts[0].shape[0]
    operands = [ids, *parts, *(old or ())]
    return pl.pallas_call(
        functools.partial(unpack_kernel, route, count, unit, old is not None),
        out_shape=[shape_of(shape, full) for shape in shapes] + [shape_of((1, LANES), full)],
        in_specs=[spec_smem()] + [spec_vmem()] * count + [spec_hbm()] * (len(operands) - 1 - count),
        out_specs=[spec_hbm()] * 2 + [spec_vmem()],
        input_output_aliases={} if old is None else {1 + count: 0, 2 + count: 1},
        scratch_shapes=[
            pltpu.VMEM((count, chunk_rows, LANES), full),
            pltpu.SemaphoreType.DMA((count * (chunk_rows // unit) * cases,)),
        ],
        compiler_params=params(8 + count * chunk_rows * 3 * LANES * 2 // MIB),
        cost_estimate=pl.CostEstimate(
            flops=10**6, bytes_accessed=count * chunk_rows * LANES * 6, transcendentals=0
        ),
        name=name,
    )(*operands)


def local(
    hidden,
    pair_of,
    ln1_gain,
    ln1_bias,
    ln2_gain,
    ln2_bias,
    w_qkv,
    b_qkv,
    w_out,
    b_out,
    w_up,
    b_up,
    w_down,
    b_down,
    cotangent,
):
    owners = lax.axis_size("ctx")
    sides = lax.axis_size("tp")
    rows, width = hidden.shape
    local_width = w_qkv.shape[2]
    hidden_units = w_up.shape[1]
    heads = local_width // HEAD_DIM
    group = owners // heads

    exponent = np.arange(0, ROT, 2, dtype=np.float32) / np.float32(ROT)
    inverse = jnp.asarray(np.tile(np.float32(10000.0) ** (-exponent), LANES // HALF)[None, :], full)
    order = (0, 2, 4, 6, 7, 5, 3, 1) if owners == 16 else tuple(range(owners // 2))
    chips = len(order)

    def to_heads(array):
        groups = [[h * group + g for h in range(heads)] for g in range(group)]
        return lax.all_to_all(array, "ctx", 0, 0, axis_index_groups=groups, tiled=True)

    def group_shift(array, d):
        pairs = [(c, c // group * group + (c % group + d) % group) for c in range(owners)]
        return lax.ppermute(array, "ctx", pairs)

    me = lax.axis_index("ctx")
    chip, core = me // 2, lax.rem(me, 2)
    place = sum(jnp.where(chip == c, i, 0) for i, c in enumerate(order))
    way = 1 - 2 * core
    far, near = chips // 2, chips - 1 - chips // 2

    def ring(array, forward):
        pairs = []
        for i, c in enumerate(order):
            for k in range(2):
                step = 1 if (k == 0) == forward else -1
                pairs.append((2 * c + k, 2 * order[(i + step) % chips] + k))
        return lax.ppermute(array, "ctx", pairs)

    def other_core(array):
        return lax.ppermute(array, "ctx", [(c, c ^ 1) for c in range(owners)])

    def across(array):
        return lax.ppermute(array, "tp", [(t, (t + 1) % sides) for t in range(sides)])

    def target(distance):
        return lax.rem(place + way * distance + chips, chips)

    def zero(array):
        return array[:1].astype(full) * 0.0

    slots = [far, -near]
    for t in range(1, far):
        slots += [far - t] if t >= near else [far - t, t - near]
    slots.append(0)
    early = 2
    slot_ids = jnp.stack(
        [core * chips + target(d) for d in slots] + [(1 - core) * chips + target(-d) for d in slots]
    )

    def terms_of(keep, came):
        def term(i):
            return keep[i].astype(full) + came[i].astype(full)

        return {d: term(i) for i, d in enumerate(slots)}

    def scatter_start(terms, token):
        return (terms[far] + token).astype(low), (terms[-near] + token).astype(low)

    def scatter_step(terms, t, sends, token):
        long_send, short_send = sends
        long_got = ring(long_send, True).astype(full) + token
        last = t == far - 1
        long_next = long_got if last else (long_got + terms[far - 1 - t]).astype(low)
        short_next = short_send
        if t < near:
            short_got = ring(short_send, False).astype(full) + token
            short_next = short_got if t == near - 1 else (short_got + terms[t + 1 - near]).astype(low)
        if last:
            return (terms[0] + long_next + short_next).astype(low)
        return long_next, short_next

    base, other_base = core * chips, (1 - core) * chips

    def gather_start(own):
        return [(own, base + place), (other_core(own), other_base + place)]

    def gather_step(t, sends, token):
        long_send, short_send = sends
        if token is not None:
            long_send = (long_send.astype(full) + token).astype(low)
        long_got = ring(long_send, True)
        found = [(long_got, base + target(-t - 1)), (other_core(long_got), other_base + target(t + 1))]
        short_got = short_send
        if t < near:
            short_got = ring(short_send, False)
            found += [(short_got, base + target(t + 1)), (other_core(short_got), other_base + target(-t - 1))]
        return (long_got, short_got), found

    blocks = hidden_units // LANES // 2
    in_slots = blocks == chips
    mlp_ids = slot_ids if in_slots else jnp.concatenate(
        [core * blocks + jnp.arange(blocks), (1 - core) * blocks + jnp.arange(blocks)]
    )
    h1, h2, xhat, inv_std, d_bias, gains, biases, b_up_row, packed = project(
        heads,
        pair_of,
        inverse,
        (hidden, ln1_gain, ln1_bias, ln2_gain, ln2_bias, cotangent, w_out, w_qkv, b_qkv, b_up, b_out, b_down),
    )
    got = to_heads(packed)
    part, back2, sums2, d_b_up, keep_mlp, early_mlp, send_mlp = mlp(
        mlp_ids.astype(jnp.int32), early, h2, w_up, b_up_row, cotangent, w_down, xhat
    )
    chunk = keep_mlp.shape[0] // chips
    came_mlp = jnp.concatenate([other_core(early_mlp), other_core(send_mlp)]) if not in_slots else None
    if in_slots:
        halves = [other_core(array).reshape(-1, chunk, LANES) for array in (early_mlp, send_mlp)]
        came_mlp = [half[i] for half in halves for i in range(half.shape[0])]
        terms_mlp = terms_of(keep_mlp.reshape(chips, chunk, LANES), came_mlp)
    else:
        summed = (keep_mlp.astype(full) + came_mlp.astype(full)).reshape(chips, chunk, LANES)
        terms_mlp = {d: lax.dynamic_index_in_dim(summed, target(d), 0, keepdims=False) for d in slots}
    nothing = jnp.zeros((1, LANES), full)

    other = None
    if group > 1:
        mine = got[:, :, LANES:].reshape(heads * rows, LANES)
        other = jnp.stack([group_shift(mine, group - d) for d in range(1, group)])

    middle = heads // 4
    first, _, state, token = attention(
        heads, group, tuple(range(middle)), pair_of, inverse, sums2, got, other, None
    )
    sends_mlp = scatter_start(terms_mlp, token)
    token = zero(sends_mlp[0]) + zero(sends_mlp[1])
    second, ends, _, token = attention(
        heads, group, tuple(range(middle, heads)), pair_of, inverse, token, got, other, state
    )
    d_own, d_other = ends[0], (ends[1] if group > 1 else None)
    terms = [d_own] + [group_shift(d_other[d - 1], d) for d in range(1, group)]
    sends_mlp = scatter_step(terms_mlp, 0, sends_mlp, token)
    first = (first.astype(full) + zero(sends_mlp[0]) + zero(sends_mlp[1])).astype(low)
    combined = combine(heads, terms, [first, second])
    backs = to_heads(combined)
    theirs2 = across((back2.astype(full) + zero(combined[0])[:, :1]).astype(low))
    sends_mlp = scatter_step(terms_mlp, 1, sends_mlp, nothing)
    ready = zero(sends_mlp[0]) + zero(sends_mlp[1]) + zero(theirs2)[:, :LANES]

    lows, d_b_qkv, keep, early_att, send_att, after = weight_grads(
        heads, early, slot_ids.astype(jnp.int32), backs, h1, cotangent, ready
    )
    both, sums1 = back_projections(lows, part, w_out, w_qkv, xhat)
    theirs = across(both)
    output, d_hidden, finish_token = finish(
        hidden, cotangent, xhat, inv_std, gains, biases, both, theirs, back2, theirs2
    )
    halves = [other_core(array) for array in (early_att, send_att)]
    terms_att = terms_of(keep, [half[i] for half in halves for i in range(half.shape[0])])

    small = jnp.concatenate(
        [sums1.reshape(1, -1), sums2.reshape(1, -1), d_bias, d_b_up, d_b_qkv.reshape(1, -1)], axis=1
    )

    def unpack_some(name, route, cases, unit, shapes, found, old, wait=None):
        parts, ids = zip(*found)
        ids = jnp.stack(ids)
        if wait is not None:
            ids = ids + (wait[0, 0].astype(full) * 0.0).astype(jnp.int32)
        *old, token = unpack(name, route, cases, unit, shapes, ids, parts, old)
        return old, token

    unit_mlp = min(chunk, local_width)
    unit_att = min(keep.shape[1], local_width)
    unpack_mlp = functools.partial(
        unpack_some,
        "unpack_feed_forward",
        functools.partial(to_mlp, width),
        1 + unit_mlp // LANES,
        unit_mlp,
        ((width, hidden_units), (hidden_units, width)),
    )
    unpack_att = functools.partial(
        unpack_some,
        "unpack_attention",
        functools.partial(to_attention, width, local_width),
        2,
        unit_att,
        ((3, width, local_width), (local_width, width)),
    )

    steps_mlp, steps_round = iter(range(2, far)), iter(range(far))
    own_mlp, round_mlp, waiting, grads_mlp = None, None, [], None

    def advance_mlp(token, gate=None):
        nonlocal sends_mlp, own_mlp, round_mlp, waiting
        t = next(steps_mlp, None)
        if t is not None:
            sends_mlp = scatter_step(terms_mlp, t, sends_mlp, token)
            if t < far - 1:
                return zero(sends_mlp[0])
            own_mlp, round_mlp = sends_mlp, (sends_mlp, sends_mlp)
            waiting += gather_start(own_mlp)
            return zero(own_mlp)
        t = next(steps_round, None)
        if t is None:
            return nothing
        round_mlp, found = gather_step(t, round_mlp, gate)
        waiting += found
        return zero(round_mlp[0])

    sends_att = scatter_start(terms_att, nothing)
    for t in range(far):
        sends_att = scatter_step(terms_att, t, sends_att, advance_mlp(nothing))
    round_att, waiting_att, grads_att = (sends_att, sends_att), gather_start(sends_att), None
    norm_sums = small[:, : 4 * width]
    small = jnp.concatenate([norm_sums + across(norm_sums), small[:, 4 * width :]], axis=1)
    small = small + zero(sends_att)[:, :1]
    distance = 1
    for t in range(far):
        ready, waiting = waiting, []
        advance_mlp(nothing, zero(round_att[0]))
        round_att, found = gather_step(t, round_att, None)
        waiting_att += found
        if distance < owners:
            small = small + lax.ppermute(small, "ctx", [(c, c ^ distance) for c in range(owners)])
            distance *= 2
        if ready:
            grads_mlp, more = unpack_mlp(ready, grads_mlp, sends_att if t == 0 else None)
            small = small + more[:, :1]
        if t == far - 2:
            small = small + finish_token[:, :1]
            grads_att, more = unpack_att(waiting_att[:-4], None)
            waiting_att = waiting_att[-4:]
            small = small + more[:, :1]
    while distance < owners:
        small = small + lax.ppermute(small, "ctx", [(c, c ^ distance) for c in range(owners)])
        distance *= 2
    if waiting:
        grads_mlp, _ = unpack_mlp(waiting, grads_mlp)
    grads_att, _ = unpack_att(waiting_att, grads_att)

    norm_sums = small[:, : 4 * width].reshape(4, width)
    at = 4 * width
    d_bias = small[0, at : at + width]
    d_b_up = small[0, at + width : at + width + hidden_units]
    d_b_qkv = small[0, at + width + hidden_units :].reshape(3, local_width)
    d_w_up, d_w_down = grads_mlp
    d_w_qkv, d_w_out = grads_att
    return (
        output,
        d_hidden,
        norm_sums[0],
        norm_sums[1],
        norm_sums[2],
        norm_sums[3],
        d_w_qkv,
        d_b_qkv,
        d_w_out,
        d_bias,
        d_w_up,
        d_b_up,
        d_w_down,
        d_bias,
    )


def solution(mesh):
    placed = (
        P("ctx", None),
        P(),
        P(),
        P(),
        P(),
        P(),
        P(None, None, "tp"),
        P(None, "tp"),
        P("tp", None),
        P(),
        P(None, "tp"),
        P("tp"),
        P("tp", None),
        P(),
        P("ctx", None),
    )
    return jax.shard_map(
        local,
        mesh=mesh,
        in_specs=placed,
        out_specs=(
            P("ctx", None),
            P("ctx", None),
            P(),
            P(),
            P(),
            P(),
            P(None, None, "tp"),
            P(None, "tp"),
            P("tp", None),
            P(),
            P(None, "tp"),
            P("tp"),
            P("tp", None),
            P(),
        ),
        check_vma=False,
    )
```

```python
import functools

import jax
import jax.numpy as jnp
import numpy as np
from jax import lax
from jax.experimental import pallas as pl
from jax.experimental.pallas import tpu as pltpu
from jax.sharding import PartitionSpec as P

HEAD_DIM = 64
ROT = 16
HALF = ROT // 2
BLOCK = 128
LANES = 128
KEYS = 512
MIB = 1 << 20

norm_eps = 1e-05
masked_score = -1e30
score_scale = HEAD_DIM ** (-0.5)
low = jnp.bfloat16
full = jnp.float32


def mm(left, right):
    return lax.dot_general(left, right, (((1,), (0,)), ((), ())), preferred_element_type=full)


def mm_nt(left, right):
    return lax.dot_general(left, right, (((1,), (1,)), ((), ())), preferred_element_type=full)


def turn(tensor):
    return tensor.astype(full).T.astype(low)


def lane_ids(shape):
    return lax.broadcasted_iota(jnp.int32, shape, len(shape) - 1)


def row_ids(shape):
    return lax.broadcasted_iota(jnp.int32, shape, len(shape) - 2)


def rotary_partner(tensor):
    lanes = lane_ids(tensor.shape)
    ahead = pltpu.roll(tensor, LANES - HALF, 1)
    behind = pltpu.roll(tensor, HALF, 1)
    return jnp.where(lanes % ROT < HALF, ahead, behind)


def spec_vmem():
    return pl.BlockSpec(memory_space=pltpu.VMEM)


def spec_smem():
    return pl.BlockSpec(memory_space=pltpu.SMEM)


def spec_hbm():
    return pl.BlockSpec(memory_space=pltpu.HBM)


def params(mib):
    return pltpu.CompilerParams(vmem_limit_bytes=mib * MIB)


def shape_of(shape, kind):
    return jax.ShapeDtypeStruct(shape, kind)


def block_tables(inverse, blocks):
    row = row_ids((BLOCK, LANES)).astype(full)
    start = blocks.astype(full) * float(BLOCK)
    return jnp.cos(row * inverse), jnp.sin(row * inverse), jnp.cos(start * inverse), jnp.sin(start * inverse)


def project_kernel(heads, pair_ref, inv_ref, *rest):
    given, rest = rest[:12], rest[12:]
    h1_ref, h2_ref, xhat_ref, std_ref, d_bias_ref, gains_ref, bias_ref, b_up_out_ref, packed = rest[:9]
    held, sems = rest[9:-1], rest[-1]
    copies = [pltpu.make_async_copy(src, dst, sems.at[i]) for i, (src, dst) in enumerate(zip(given, held))]
    for copy in copies:
        copy.start()
    (
        hidden_ref,
        g1_ref,
        c1_ref,
        g2_ref,
        c2_ref,
        cot_ref,
        w_out_ref,
        w_qkv_ref,
        b_qkv_ref,
        b_up_ref,
        b_out_ref,
        b_down_ref,
    ) = held
    rows = hidden_ref.shape[0]
    me = lax.axis_index("ctx")
    pair = pair_ref[me]
    total_blocks = 2 * pair_ref.shape[0]

    first = jnp.where(row_ids((8, LANES)) == 0, pair, total_blocks - 1 - pair)
    inverse = inv_ref[...]
    cos_row, sin_row, cos_block, sin_block = block_tables(inverse, first)
    in_head = lane_ids((BLOCK, LANES)) % HEAD_DIM
    tables = []
    for half in range(2):
        cos_at, sin_at = cos_block[half : half + 1], sin_block[half : half + 1]
        cosine = cos_row * cos_at - sin_row * sin_at
        sine = sin_row * cos_at + cos_row * sin_at
        cosine = jnp.where(in_head < ROT, cosine, 1.0)
        sine = jnp.where(in_head < HALF, -sine, jnp.where(in_head < ROT, sine, 0.0))
        tables.append((cosine, sine))
    cosine = jnp.concatenate([tables[0][0], tables[1][0]], axis=0)
    sine = jnp.concatenate([tables[0][1], tables[1][1]], axis=0)

    for copy in copies[:5]:
        copy.wait()
    x = hidden_ref[...].astype(full)
    centred = x - jnp.mean(x, axis=-1, keepdims=True)
    spread = jnp.mean(centred * centred, axis=-1, keepdims=True)
    inv_std = lax.rsqrt(spread + norm_eps)
    xhat = centred * inv_std
    xhat_ref[...] = xhat
    std_ref[...] = jnp.broadcast_to(inv_std, std_ref.shape)

    def as_row(ref):
        return ref[...].astype(full)[None, :]

    gain1, gain2 = as_row(g1_ref), as_row(g2_ref)
    h1 = (xhat * gain1 + as_row(c1_ref)).astype(low)
    h1_ref[...] = h1
    h2_ref[...] = (xhat * gain2 + as_row(c2_ref)).astype(low)
    gains_ref[0:1] = gain1
    gains_ref[1:2] = gain2
    for copy in copies[5:]:
        copy.wait()
    b_up_out_ref[...] = as_row(b_up_ref)
    bias_ref[0:1] = as_row(b_out_ref)
    bias_ref[1:2] = as_row(b_down_ref)
    d_bias_ref[...] = jnp.sum(cot_ref[...].astype(full), axis=0, keepdims=True)

    lane = lane_ids((rows, LANES))

    def projected(s):
        return mm(h1, w_qkv_ref[s]) + b_qkv_ref[s : s + 1].astype(full)

    def turned(tile):
        return tile * cosine + rotary_partner(tile) * sine

    queries, keys, values = projected(0), projected(1), projected(2)
    grads = mm_nt(cot_ref[...], w_out_ref[...])
    left = lane < HEAD_DIM
    for i in range(heads // 2):
        cut = slice(i * LANES, (i + 1) * LANES)
        q = turned(queries[:, cut]).astype(low).astype(full) * score_scale
        k = turned(keys[:, cut])
        v = values[:, cut]
        g = grads[:, cut]
        packed[2 * i, :, :LANES] = jnp.where(left, g, pltpu.roll(q, HEAD_DIM, 1)).astype(low)
        packed[2 * i, :, LANES:] = jnp.where(left, v, pltpu.roll(k, HEAD_DIM, 1)).astype(low)
        packed[2 * i + 1, :, :LANES] = jnp.where(left, pltpu.roll(g, HEAD_DIM, 1), q).astype(low)
        packed[2 * i + 1, :, LANES:] = jnp.where(left, pltpu.roll(v, HEAD_DIM, 1), k).astype(low)


def project(heads, pair_of, inverse, given):
    hidden, w_out, b_up = given[0], given[6], given[9]
    rows, width = hidden.shape
    outs = [
        shape_of((rows, width), low),
        shape_of((rows, width), low),
        shape_of((rows, width), full),
        shape_of((rows, LANES), full),
        shape_of((1, width), full),
        shape_of((2, width), full),
        shape_of((2, width), full),
        shape_of((1, b_up.shape[0]), full),
        shape_of((heads, rows, 2 * LANES), low),
    ]
    return pl.pallas_call(
        functools.partial(project_kernel, heads),
        out_shape=outs,
        in_specs=[spec_smem(), spec_vmem()] + [spec_hbm()] * len(given),
        out_specs=[spec_vmem()] * len(outs),
        scratch_shapes=[pltpu.VMEM(array.shape, array.dtype) for array in given]
        + [pltpu.SemaphoreType.DMA((len(given),))],
        compiler_params=params(60),
        cost_estimate=pl.CostEstimate(
            flops=2 * rows * width * 4 * w_out.shape[0], bytes_accessed=8 * MIB, transcendentals=0
        ),
        name="project",
    )(pair_of, inverse, *given)


def mlp_kernel(early, ids_ref, *rest):
    given, rest = rest[:6], rest[6:]
    part_ref, back_ref, sums_ref, d_b_up_ref, keep_ref, early_ref, send_ref = rest[:7]
    h2_turned, part_acc, back_acc = rest[7:10]
    held, sems = rest[10:-1], rest[-1]
    copies = [pltpu.make_async_copy(src, dst, sems.at[i]) for i, (src, dst) in enumerate(zip(given, held))]
    h2_held, w_up_ref, b_up, cot_ref, w_down_ref, xhat_ref = held
    step = pl.program_id(0)
    steps = pl.num_programs(0)

    @pl.when(step == 0)
    def _():
        for copy in copies:
            copy.start()
        part_acc[...] = jnp.zeros_like(part_acc)
        back_acc[...] = jnp.zeros_like(back_acc)
        copies[0].wait()
        h2_turned[...] = turn(h2_held[...])
        for copy in copies[1:3]:
            copy.wait()

    at = [pl.multiple_of(ids_ref[b * steps + step] * LANES, LANES) for b in range(2)]
    w_up = jnp.concatenate([w_up_ref[:, pl.ds(i, LANES)] for i in at], axis=1)
    u = mm(h2_held[...], w_up) + jnp.concatenate([b_up[:, pl.ds(i, LANES)] for i in at], axis=1)

    @pl.when(step == 0)
    def _():
        for copy in copies[3:5]:
            copy.wait()

    cot = cot_ref[...]
    w_down = jnp.concatenate([w_down_ref[pl.ds(i, LANES), :] for i in at], axis=0)
    cdf = 0.5 * (1.0 + lax.erf(u * np.float32(np.sqrt(0.5))))
    active = u * cdf
    active_low = active.astype(low)
    slope = cdf + u * jnp.exp(-0.5 * u * u) * np.float32(1.0 / np.sqrt(2.0 * np.pi))
    du = (mm_nt(cot, w_down) * slope).astype(low)
    part_acc[...] += mm(active_low, w_down)
    back_acc[...] += mm_nt(du, w_up)
    d_b_up = jnp.sum(du.astype(full), axis=0, keepdims=True)
    up = mm(h2_turned[...], du).astype(low)
    down = mm(active.T.astype(low), cot).astype(low)
    depth = up.shape[0]

    def put(b, grad_ref):
        grad_ref[:depth] = up[:, b * LANES : (b + 1) * LANES]
        for t in range(down.shape[1] // LANES):
            grad_ref[depth + t * LANES : depth + (t + 1) * LANES] = down[
                b * LANES : (b + 1) * LANES, t * LANES : (t + 1) * LANES
            ]

    for b in range(2):
        d_b_up_ref[:, pl.ds(at[b], LANES)] = d_b_up[:, b * LANES : (b + 1) * LANES]
    put(0, keep_ref)

    @pl.when(step < early)
    def _():
        put(1, early_ref)

    @pl.when(step >= early)
    def _():
        put(1, send_ref)

    @pl.when(step == steps - 1)
    def _():
        copies[5].wait()
        part_ref[...] = part_acc[...]
        back = back_acc[...]
        back_ref[...] = back.astype(low)
        sums_ref[0:1] = jnp.sum(back * xhat_ref[...], axis=0, keepdims=True)
        sums_ref[1:2] = jnp.sum(back, axis=0, keepdims=True)


def mlp(ids, early, *given):
    rows, width = given[0].shape
    hidden_units = given[1].shape[1]
    steps = hidden_units // LANES // 2
    whole = lambda shape: pl.BlockSpec(shape, lambda f, c: (0,) * len(shape))
    grads = lambda at: pl.BlockSpec((2 * width, LANES), lambda f, c: (at(f), 0))
    outs = [
        shape_of((rows, width), full),
        shape_of((rows, width), low),
        shape_of((2, width), full),
        shape_of((1, hidden_units), full),
        shape_of((steps * 2 * width, LANES), low),
        shape_of((early * 2 * width, LANES), low),
        shape_of(((steps - early) * 2 * width, LANES), low),
    ]
    return pl.pallas_call(
        functools.partial(mlp_kernel, early),
        grid_spec=pltpu.PrefetchScalarGridSpec(
            num_scalar_prefetch=1,
            grid=(steps,),
            in_specs=[spec_hbm()] * len(given),
            out_specs=[whole(array.shape) for array in outs[:4]]
            + [
                grads(lambda f: f),
                grads(lambda f: jnp.minimum(f, early - 1)),
                grads(lambda f: jnp.maximum(f - early, 0)),
            ],
            scratch_shapes=[
                pltpu.VMEM((width, rows), low),
                pltpu.VMEM((rows, width), full),
                pltpu.VMEM((rows, width), full),
            ]
            + [pltpu.VMEM(array.shape, array.dtype) for array in given]
            + [pltpu.SemaphoreType.DMA((len(given),))],
        ),
        out_shape=outs,
        compiler_params=params(60),
        cost_estimate=pl.CostEstimate(
            flops=12 * rows * width * hidden_units, bytes_accessed=20 * MIB, transcendentals=0
        ),
        name="feed_forward",
    )(ids, *given)


def attention_kernel(heads, group, places, is_first, is_last, pair_ref, inv_ref, token_ref, *rest):
    del token_ref
    if is_first:
        got_ref, rest = rest[0], rest[1:]
        if group > 1:
            other_ref, rest = rest[0], rest[1:]
    else:
        rest = rest[4:]
    out_ref, rest = rest[0], rest[1:]
    if is_last:
        d_own_ref, rest = rest[0], rest[1:]
        if group > 1:
            d_other_ref, rest = rest[0], rest[1:]
    (values_keys, turned_keys, sums, queries), rest = rest[:4], rest[4:]
    token_out, rest = rest[0], rest[1:]
    weights_in, weights_out, stored, peaks, totals, weighted, finals, block_cos, block_sin = rest
    token_out[...] = jnp.zeros_like(token_out)

    rows = queries.shape[1]
    owners = pair_ref.shape[0]
    total_blocks = 2 * owners
    per_chunk = KEYS // BLOCK
    tasks = (total_blocks + 1 + per_chunk - 1) // per_chunk
    me = lax.axis_index("ctx")
    own_sub = lax.rem(me, group)

    def blocks_of(r, d):
        owner = r * group + lax.rem(own_sub + d, group)
        pair = pair_ref[owner]
        return pair, total_blocks - 1 - pair

    def place(tile, block):
        at = pl.multiple_of(block * BLOCK, BLOCK)
        values_keys[pl.ds(at, BLOCK), :] = tile
        turned_keys[:, pl.ds(at, BLOCK)] = turn(tile)

    if is_first:
        for r in range(heads):
            queries[r] = got_ref[r, :, :LANES]
            for half, block in enumerate(blocks_of(r, 0)):
                place(got_ref[r, half * BLOCK : (half + 1) * BLOCK, LANES:], block)
            for d in range(1, group):
                for half, block in enumerate(blocks_of(r, d)):
                    at = r * rows + half * BLOCK
                    place(other_ref[d - 1, at : at + BLOCK, :], block)
        sums[...] = jnp.zeros_like(sums)

    lane = lane_ids((BLOCK, LANES))
    left = lane < HEAD_DIM
    in_key = lane - HEAD_DIM
    moving = (in_key >= 0) & (in_key < ROT)
    forward = (in_key >= 0) & (in_key < HALF)
    cos_row, sin_row, block_cos[...], block_sin[...] = block_tables(inv_ref[...], row_ids(block_cos.shape))

    def rotated_back(tile, block):
        cos_at, sin_at = block_cos[pl.ds(block, 1), :], block_sin[pl.ds(block, 1), :]
        cosine = jnp.where(moving, cos_row * cos_at - sin_row * sin_at, 1.0)
        sine = sin_row * cos_at + cos_row * sin_at
        sine = jnp.where(moving, jnp.where(forward, sine, -sine), 0.0)
        return tile * cosine + rotary_partner(tile) * sine

    offset = row_ids((BLOCK, BLOCK)) - lane_ids((BLOCK, BLOCK))

    def one_pair(i, carry):
        blocks = blocks_of(places[0] + i, 0)
        first = blocks[0] // per_chunk + 1
        for half in range(2):
            both = queries[places[0] + i, half * BLOCK : (half + 1) * BLOCK, :]
            both_turned = turn(both)
            upper = row_ids((LANES, BLOCK)) < HEAD_DIM
            zero = jnp.zeros_like(both_turned)
            weights_in[half, :, :BLOCK] = jnp.where(upper, both_turned, zero)
            weights_in[half, :, BLOCK:] = jnp.where(upper, zero, both_turned)
            weights_out[half, :BLOCK, :] = jnp.where(left, both, zero)
            weights_out[half, BLOCK:, :] = jnp.where(left, zero, both)
        finals[...] = jnp.zeros_like(finals)

        def task(t):
            is_low = t < first
            chunk = jnp.where(is_low, first - 1 - t, t - first)
            return is_low, chunk

        runs = KEYS // BLOCK
        for t in range(tasks):
            is_low, chunk = task(t)
            weights = weights_in[jnp.where(is_low, 0, 1)]
            for u in range(runs):
                at = pl.multiple_of(chunk * KEYS + u * BLOCK, BLOCK)
                sub = slice(u * BLOCK, (u + 1) * BLOCK)
                both = mm(values_keys[pl.ds(at, BLOCK), :], weights)
                grads = both[:, :BLOCK]
                scores = both[:, BLOCK:]
                if t in (0, tasks - 1):
                    query_at = blocks[0 if t == 0 else 1] * BLOCK
                    scores = jnp.where(offset <= query_at - at, scores, masked_score)
                peak = jnp.max(scores, axis=0, keepdims=True)
                raised = jnp.exp(scores - peak)
                stored[t, sub, :BLOCK] = raised
                stored[t, sub, BLOCK:] = grads
                line = t * runs + u
                peaks[line : line + 1] = peak
                totals[line : line + 1] = jnp.sum(raised, axis=0, keepdims=True)
                weighted[line : line + 1] = jnp.sum(raised * grads, axis=0, keepdims=True)

        in_low = row_ids((tasks * runs, BLOCK)) < first * runs

        def finish(mine):
            top = jnp.max(jnp.where(mine, peaks[...], masked_score), axis=0, keepdims=True)
            factor = jnp.where(mine, jnp.exp(peaks[...] - top), 0.0)
            inverse = 1.0 / jnp.sum(totals[...] * factor, axis=0, keepdims=True)
            return factor * inverse, jnp.sum(weighted[...] * factor, axis=0, keepdims=True) * inverse

        (low_factor, low_delta), (high_factor, high_delta) = finish(in_low), finish(jnp.logical_not(in_low))
        peaks[...] = low_factor + high_factor

        for t in range(tasks):
            is_low, chunk = task(t)
            half = jnp.where(is_low, 0, 1)
            weights = weights_out[half]
            delta = jnp.where(is_low, low_delta, high_delta)
            parts = []
            for u in range(runs):
                sub = slice(u * BLOCK, (u + 1) * BLOCK)
                probs = stored[t, sub, :BLOCK] * peaks[t * runs + u : t * runs + u + 1]
                d_scores = probs * (stored[t, sub, BLOCK:] - delta)
                both = jnp.concatenate([probs, d_scores], axis=1).astype(low)
                at = pl.multiple_of(chunk * KEYS + u * BLOCK, BLOCK)
                sums[pl.ds(at, BLOCK), :] += mm(both, weights)
                parts.append(both)
            at = pl.multiple_of(chunk * KEYS, KEYS)
            finals[half] += mm(turned_keys[:, pl.ds(at, KEYS)], jnp.concatenate(parts, axis=0))

        for half in range(2):
            both = jnp.concatenate(
                [finals[half, :HEAD_DIM, :BLOCK], finals[half, HEAD_DIM:, BLOCK:] * score_scale], axis=0
            ).T
            out_ref[i, half * BLOCK : (half + 1) * BLOCK, :] = rotated_back(both, blocks[half]).astype(low)
        return carry

    lax.fori_loop(0, len(places), one_pair, 0)

    if is_last:
        for r in range(heads):
            for d in range(group):
                for half, block in enumerate(blocks_of(r, d)):
                    at = r * rows + half * BLOCK
                    tile = rotated_back(sums[pl.ds(pl.multiple_of(block * BLOCK, BLOCK), BLOCK), :], block)
                    if d == 0:
                        d_own_ref[at : at + BLOCK, :] = tile
                    else:
                        d_other_ref[d - 1, at : at + BLOCK, :] = tile


def attention(heads, group, places, pair_of, inverse, token, got, other, state):
    is_first, is_last = state is None, places[-1] == heads - 1
    rows = got.shape[1]
    owners = pair_of.shape[0]
    total_keys = owners * rows
    tasks = (2 * owners + KEYS // BLOCK) // (KEYS // BLOCK)
    operands = [pair_of, inverse, token]
    outs = [shape_of((len(places), rows, LANES), low)]
    if is_first:
        operands += [got] if other is None else [got, other]
    else:
        operands += list(state)
    if is_last:
        outs.append(shape_of((heads * rows, LANES), full))
        if group > 1:
            outs.append(shape_of((group - 1, heads * rows, LANES), full))
    kept = [
        shape_of((total_keys, LANES), low),
        shape_of((LANES, total_keys), low),
        shape_of((total_keys, LANES), full),
        shape_of((heads, rows, LANES), low),
    ]
    aliases = {} if is_first else {len(operands) - 4 + i: len(outs) + i for i in range(4)}
    found = pl.pallas_call(
        functools.partial(attention_kernel, heads, group, places, is_first, is_last),
        out_shape=outs + kept + [shape_of((1, LANES), full)],
        in_specs=[spec_smem()] + [spec_vmem()] * (len(operands) - 1),
        out_specs=[spec_vmem()] * (len(outs) + 5),
        input_output_aliases=aliases,
        scratch_shapes=[
            pltpu.VMEM((2, LANES, 2 * BLOCK), low),
            pltpu.VMEM((2, 2 * BLOCK, LANES), low),
            pltpu.VMEM((tasks, KEYS, 2 * BLOCK), full),
            pltpu.VMEM((tasks * KEYS // BLOCK, BLOCK), full),
            pltpu.VMEM((tasks * KEYS // BLOCK, BLOCK), full),
            pltpu.VMEM((tasks * KEYS // BLOCK, BLOCK), full),
            pltpu.VMEM((2, LANES, 2 * BLOCK), full),
            pltpu.VMEM((2 * owners, LANES), full),
            pltpu.VMEM((2 * owners, LANES), full),
        ],
        compiler_params=params(6 + total_keys * 5 * 256 // MIB),
        cost_estimate=pl.CostEstimate(
            flops=2_500_000_000 * len(places), bytes_accessed=2 * MIB, transcendentals=0
        ),
        name="attention",
    )(*operands)
    return found[0], found[1 : len(outs)], found[len(outs) : len(outs) + 4], found[-1]


def combine_kernel(heads, terms, *refs):
    out_ref = refs[-1]
    rows = out_ref.shape[1]
    for r in range(heads):
        cut = slice(r * rows, (r + 1) * rows)
        total = refs[0][cut, :]
        for term in refs[1:terms]:
            total = total + term[cut, :]
        out_ref[r, :, LANES:] = total.astype(low)
    at = 0
    for first_ref in refs[terms:-1]:
        out_ref[at : at + first_ref.shape[0], :, :LANES] = first_ref[...]
        at += first_ref.shape[0]


def combine(heads, terms, firsts):
    rows = firsts[0].shape[1]
    return pl.pallas_call(
        functools.partial(combine_kernel, heads, len(terms)),
        out_shape=shape_of((heads, rows, 2 * LANES), low),
        in_specs=[spec_vmem()] * (len(firsts) + len(terms)),
        out_specs=spec_vmem(),
        compiler_params=params(24),
        cost_estimate=pl.CostEstimate(flops=10**7, bytes_accessed=3 * MIB, transcendentals=0),
        name="combine",
    )(*terms, *firsts)


def weight_grads_kernel(
    heads, early, ids_ref, got_ref, h1_ref, cot_ref, ready_ref, low_ref, d_b_ref, keep_ref, early_ref, send_ref, token_ref, grads
):
    del ready_ref
    chips, chunk_rows = keep_ref.shape[:2]

    def put(at, tile):
        step = min(chunk_rows, tile.shape[0])
        for off in range(0, tile.shape[0], step):
            chunk, inside = divmod(at + off, chunk_rows)
            grads[chunk, inside : inside + step] = tile[off : off + step]

    rows = h1_ref.shape[0]
    left = lane_ids((rows, LANES)) < HEAD_DIM
    for i in range(heads // 2):
        cut = slice(i * LANES, (i + 1) * LANES)
        for first, second, half in ((0, 1, slice(0, LANES)), (3, 2, slice(LANES, 2 * LANES))):
            a, b = got_ref[2 * i, :, half].astype(full), got_ref[2 * i + 1, :, half].astype(full)
            low_ref[first, :, cut] = jnp.where(left, a, pltpu.roll(b, HEAD_DIM, 1)).astype(low)
            low_ref[second, :, cut] = jnp.where(left, pltpu.roll(a, HEAD_DIM, 1), b).astype(low)
    h1_turned = turn(h1_ref[...])
    depth, tiles = h1_turned.shape[0], heads // 2
    for s in range(3):
        d_proj = low_ref[1 + s]
        d_b_ref[s : s + 1] = jnp.sum(d_proj.astype(full), axis=0, keepdims=True)
        grad = mm(h1_turned, d_proj).astype(low)
        for t in range(tiles):
            put((s * tiles + t) * depth, grad[:, t * LANES : (t + 1) * LANES])
    grad = mm(turn(low_ref[0]), cot_ref[...]).astype(low)
    height = grad.shape[0]
    for t in range(depth // LANES):
        put(3 * tiles * depth + t * height, grad[:, t * LANES : (t + 1) * LANES])
    for t in range(chips):
        target = early_ref.at[t] if t < early else send_ref.at[t - early]
        target[...] = grads[ids_ref[chips + t]]
        keep_ref[t] = grads[ids_ref[t]]
    token_ref[...] = jnp.zeros_like(token_ref)


def weight_grads(heads, early, ids, got, h1, cot, ready):
    rows, width = h1.shape
    local_width = heads * HEAD_DIM
    chips = ids.shape[0] // 2
    chunk_rows = 4 * width * local_width // LANES // (2 * chips)
    outs = [
        shape_of((4, rows, local_width), low),
        shape_of((3, local_width), full),
        shape_of((chips, chunk_rows, LANES), low),
        shape_of((early, chunk_rows, LANES), low),
        shape_of((chips - early, chunk_rows, LANES), low),
        shape_of((1, LANES), full),
    ]
    return pl.pallas_call(
        functools.partial(weight_grads_kernel, heads, early),
        out_shape=outs,
        in_specs=[spec_smem()] + [spec_vmem()] * 4,
        out_specs=[spec_vmem()] * len(outs),
        scratch_shapes=[pltpu.VMEM((2 * chips, chunk_rows, LANES), low)],
        compiler_params=params(20),
        cost_estimate=pl.CostEstimate(
            flops=8 * rows * width * local_width, bytes_accessed=8 * MIB, transcendentals=0
        ),
        name="weight_grads",
    )(ids, got, h1, cot, ready)


def return_kernel(low_ref, part_ref, w_out_ref, w_qkv_ref, xhat_ref, both_ref, sums_ref):
    rows = xhat_ref.shape[0]
    both_ref[:rows] = (part_ref[...] + mm(low_ref[0], w_out_ref[...])).astype(low)
    back = mm_nt(low_ref[1], w_qkv_ref[0]) + mm_nt(low_ref[2], w_qkv_ref[1]) + mm_nt(low_ref[3], w_qkv_ref[2])
    both_ref[rows:] = back.astype(low)
    sums_ref[0:1] = jnp.sum(back * xhat_ref[...], axis=0, keepdims=True)
    sums_ref[1:2] = jnp.sum(back, axis=0, keepdims=True)


def back_projections(*given):
    rows, width = given[1].shape
    return pl.pallas_call(
        return_kernel,
        out_shape=[shape_of((2 * rows, width), low), shape_of((2, width), full)],
        in_specs=[spec_vmem()] * len(given),
        out_specs=[spec_vmem()] * 2,
        compiler_params=params(16),
        cost_estimate=pl.CostEstimate(
            flops=8 * rows * width * given[2].shape[0], bytes_accessed=8 * MIB, transcendentals=0
        ),
        name="back_projections",
    )(*given)


def finish_kernel(
    hidden_ref, cot_ref, xhat_ref, std_ref, gains_ref, bias_ref, ours_ref, theirs_ref, e2_ours_ref, e2_theirs_ref, out_ref, grad_ref, token_ref
):
    rows = hidden_ref.shape[0]
    gains = gains_ref[...]
    biases = bias_ref[...]
    summed = ours_ref[:rows].astype(full) + theirs_ref[:rows].astype(full)
    out_ref[...] = (hidden_ref[...].astype(full) + summed + biases[0:1] + biases[1:2]).astype(low)
    e1 = ours_ref[rows:].astype(full) + theirs_ref[rows:].astype(full)
    e2 = e2_ours_ref[...].astype(full) + e2_theirs_ref[...].astype(full)
    f = e1 * gains[0:1] + e2 * gains[1:2]
    xhat = xhat_ref[...]
    inv_std = std_ref[:, 0:1]
    grad_ref[...] = cot_ref[...].astype(full) + inv_std * (
        f - jnp.mean(f, axis=-1, keepdims=True) - xhat * jnp.mean(f * xhat, axis=-1, keepdims=True)
    )
    token_ref[...] = jnp.zeros_like(token_ref)


def finish(*operands):
    rows, width = operands[0].shape
    return pl.pallas_call(
        finish_kernel,
        out_shape=[shape_of((rows, width), low), shape_of((rows, width), full), shape_of((1, LANES), full)],
        in_specs=[spec_vmem()] * len(operands),
        out_specs=[spec_vmem()] * 3,
        compiler_params=params(24),
        cost_estimate=pl.CostEstimate(flops=10**7, bytes_accessed=8 * MIB, transcendentals=0),
        name="finish",
    )(*operands)


def to_attention(width, local_width, source, refs, base, unit):
    qkv_ref, out_ref = refs
    tiles = local_width // LANES
    split = 3 * tiles * width
    tile = base // width
    row = pl.multiple_of(lax.rem(base, width), unit)
    column = pl.multiple_of(lax.rem(tile, tiles) * LANES, LANES)
    yield base < split, source, qkv_ref.at[jnp.minimum(tile // tiles, 2), pl.ds(row, unit), pl.ds(column, LANES)]
    after = jnp.maximum(base - split, 0)
    row = pl.multiple_of(lax.rem(after, local_width), unit)
    column = pl.multiple_of(after // local_width * LANES, LANES)
    yield base >= split, source, out_ref.at[pl.ds(row, unit), pl.ds(column, LANES)]


def to_mlp(width, source, refs, base, unit):
    up_ref, down_ref = refs
    block, inside = base // (2 * width), lax.rem(base, 2 * width)
    block_at = pl.multiple_of(block * LANES, LANES)
    row = pl.multiple_of(jnp.minimum(inside, width - unit), unit)
    yield inside < width, source, up_ref.at[pl.ds(row, unit), pl.ds(block_at, LANES)]
    for t in range(unit // LANES):
        column = pl.multiple_of(jnp.maximum(inside - width, 0) + t * LANES, LANES)
        cut = source.at[pl.ds(t * LANES, LANES), :]
        yield inside >= width, cut, down_ref.at[pl.ds(block_at, LANES), pl.ds(column, LANES)]


def unpack_kernel(route, count, unit, has_old, ids_ref, *rest):
    parts, rest = rest[:count], rest[count:]
    rest = rest[2:] if has_old else rest
    targets, (token_ref, held, sems) = rest[:2], rest[2:]
    token_ref[...] = jnp.zeros_like(token_ref)
    chunk_rows = parts[0].shape[0]
    units = chunk_rows // unit
    per_unit = sems.shape[0] // (count * units)

    def moves():
        for i in range(count):
            for j in range(units):
                source = held.at[i, pl.ds(j * unit, unit), :]
                base = ids_ref[i] * chunk_rows + j * unit
                for n, (applies, piece, target) in enumerate(route(source, targets, base, unit)):
                    sem = sems.at[(i * units + j) * per_unit + n]
                    yield i, applies, pltpu.make_async_copy(piece, target, sem)

    done = -1
    for i, applies, copy in moves():
        if i != done:
            held[i] = parts[i][...].astype(full)
            done = i
        pl.when(applies)(copy.start)
    for i, applies, copy in moves():
        pl.when(applies)(copy.wait)


def unpack(name, route, cases, unit, shapes, ids, parts, old):
    count = len(parts)
    chunk_rows = parts[0].shape[0]
    operands = [ids, *parts, *(old or ())]
    return pl.pallas_call(
        functools.partial(unpack_kernel, route, count, unit, old is not None),
        out_shape=[shape_of(shape, full) for shape in shapes] + [shape_of((1, LANES), full)],
        in_specs=[spec_smem()] + [spec_vmem()] * count + [spec_hbm()] * (len(operands) - 1 - count),
        out_specs=[spec_hbm()] * 2 + [spec_vmem()],
        input_output_aliases={} if old is None else {1 + count: 0, 2 + count: 1},
        scratch_shapes=[
            pltpu.VMEM((count, chunk_rows, LANES), full),
            pltpu.SemaphoreType.DMA((count * (chunk_rows // unit) * cases,)),
        ],
        compiler_params=params(8 + count * chunk_rows * 3 * LANES * 2 // MIB),
        cost_estimate=pl.CostEstimate(
            flops=10**6, bytes_accessed=count * chunk_rows * LANES * 6, transcendentals=0
        ),
        name=name,
    )(*operands)


def local(
    hidden,
    pair_of,
    ln1_gain,
    ln1_bias,
    ln2_gain,
    ln2_bias,
    w_qkv,
    b_qkv,
    w_out,
    b_out,
    w_up,
    b_up,
    w_down,
    b_down,
    cotangent,
):
    owners = lax.axis_size("ctx")
    sides = lax.axis_size("tp")
    rows, width = hidden.shape
    local_width = w_qkv.shape[2]
    hidden_units = w_up.shape[1]
    heads = local_width // HEAD_DIM
    group = owners // heads

    exponent = np.arange(0, ROT, 2, dtype=np.float32) / np.float32(ROT)
    inverse = jnp.asarray(np.tile(np.float32(10000.0) ** (-exponent), LANES // HALF)[None, :], full)
    order = (0, 2, 4, 6, 7, 5, 3, 1) if owners == 16 else tuple(range(owners // 2))
    chips = len(order)

    def to_heads(array):
        groups = [[h * group + g for h in range(heads)] for g in range(group)]
        return lax.all_to_all(array, "ctx", 0, 0, axis_index_groups=groups, tiled=True)

    def group_shift(array, d):
        pairs = [(c, c // group * group + (c % group + d) % group) for c in range(owners)]
        return lax.ppermute(array, "ctx", pairs)

    me = lax.axis_index("ctx")
    chip, core = me // 2, lax.rem(me, 2)
    place = sum(jnp.where(chip == c, i, 0) for i, c in enumerate(order))
    way = 1 - 2 * core
    far, near = chips // 2, chips - 1 - chips // 2

    def ring(array, forward):
        pairs = []
        for i, c in enumerate(order):
            for k in range(2):
                step = 1 if (k == 0) == forward else -1
                pairs.append((2 * c + k, 2 * order[(i + step) % chips] + k))
        return lax.ppermute(array, "ctx", pairs)

    def other_core(array):
        return lax.ppermute(array, "ctx", [(c, c ^ 1) for c in range(owners)])

    def across(array):
        return lax.ppermute(array, "tp", [(t, (t + 1) % sides) for t in range(sides)])

    def target(distance):
        return lax.rem(place + way * distance + chips, chips)

    def zero(array):
        return array[:1].astype(full) * 0.0

    slots = [far, -near]
    for t in range(1, far):
        slots += [far - t] if t >= near else [far - t, t - near]
    slots.append(0)
    early = 2
    slot_ids = jnp.stack(
        [core * chips + target(d) for d in slots] + [(1 - core) * chips + target(-d) for d in slots]
    )

    def terms_of(keep, came):
        def term(i):
            return keep[i].astype(full) + came[i].astype(full)

        return {d: term(i) for i, d in enumerate(slots)}

    def scatter_start(terms, token):
        return (terms[far] + token).astype(low), (terms[-near] + token).astype(low)

    def scatter_step(terms, t, sends, token):
        long_send, short_send = sends
        long_got = ring(long_send, True).astype(full) + token
        last = t == far - 1
        long_next = long_got if last else (long_got + terms[far - 1 - t]).astype(low)
        short_next = short_send
        if t < near:
            short_got = ring(short_send, False).astype(full) + token
            short_next = short_got if t == near - 1 else (short_got + terms[t + 1 - near]).astype(low)
        if last:
            return (terms[0] + long_next + short_next).astype(low)
        return long_next, short_next

    base, other_base = core * chips, (1 - core) * chips

    def gather_start(own):
        return [(own, base + place), (other_core(own), other_base + place)]

    def gather_step(t, sends, token):
        long_send, short_send = sends
        if token is not None:
            long_send = (long_send.astype(full) + token).astype(low)
        long_got = ring(long_send, True)
        found = [(long_got, base + target(-t - 1)), (other_core(long_got), other_base + target(t + 1))]
        short_got = short_send
        if t < near:
            short_got = ring(short_send, False)
            found += [(short_got, base + target(t + 1)), (other_core(short_got), other_base + target(-t - 1))]
        return (long_got, short_got), found

    blocks = hidden_units // LANES // 2
    in_slots = blocks == chips
    mlp_ids = slot_ids if in_slots else jnp.concatenate(
        [core * blocks + jnp.arange(blocks), (1 - core) * blocks + jnp.arange(blocks)]
    )
    h1, h2, xhat, inv_std, d_bias, gains, biases, b_up_row, packed = project(
        heads,
        pair_of,
        inverse,
        (hidden, ln1_gain, ln1_bias, ln2_gain, ln2_bias, cotangent, w_out, w_qkv, b_qkv, b_up, b_out, b_down),
    )
    got = to_heads(packed)
    part, back2, sums2, d_b_up, keep_mlp, early_mlp, send_mlp = mlp(
        mlp_ids.astype(jnp.int32), early, h2, w_up, b_up_row, cotangent, w_down, xhat
    )
    chunk = keep_mlp.shape[0] // chips
    came_mlp = jnp.concatenate([other_core(early_mlp), other_core(send_mlp)]) if not in_slots else None
    if in_slots:
        halves = [other_core(array).reshape(-1, chunk, LANES) for array in (early_mlp, send_mlp)]
        came_mlp = [half[i] for half in halves for i in range(half.shape[0])]
        terms_mlp = terms_of(keep_mlp.reshape(chips, chunk, LANES), came_mlp)
    else:
        summed = (keep_mlp.astype(full) + came_mlp.astype(full)).reshape(chips, chunk, LANES)
        terms_mlp = {d: lax.dynamic_index_in_dim(summed, target(d), 0, keepdims=False) for d in slots}
    nothing = jnp.zeros((1, LANES), full)

    other = None
    if group > 1:
        mine = got[:, :, LANES:].reshape(heads * rows, LANES)
        other = jnp.stack([group_shift(mine, group - d) for d in range(1, group)])

    middle = 3 * heads // 8
    sends_mlp = scatter_start(terms_mlp, nothing)
    token = zero(sends_mlp[0]) + zero(sends_mlp[1])
    first, _, state, token = attention(
        heads, group, tuple(range(middle)), pair_of, inverse, token, got, other, None
    )
    sends_mlp = scatter_step(terms_mlp, 0, sends_mlp, token)
    token = zero(sends_mlp[0]) + zero(sends_mlp[1])
    second, ends, _, token = attention(
        heads, group, tuple(range(middle, heads)), pair_of, inverse, token, got, other, state
    )
    d_own, d_other = ends[0], (ends[1] if group > 1 else None)
    terms = [d_own] + [group_shift(d_other[d - 1], d) for d in range(1, group)]
    sends_mlp = scatter_step(terms_mlp, 1, sends_mlp, token)
    first = (first.astype(full) + zero(sends_mlp[0]) + zero(sends_mlp[1])).astype(low)
    combined = combine(heads, terms, [first, second])
    backs = to_heads(combined)
    theirs2 = across((back2.astype(full) + zero(combined[0])[:, :1]).astype(low))
    sends_mlp = scatter_step(terms_mlp, 2, sends_mlp, nothing)
    ready = zero(sends_mlp[0]) + zero(sends_mlp[1]) + zero(theirs2)[:, :LANES]

    lows, d_b_qkv, keep, early_att, send_att, after = weight_grads(
        heads, early, slot_ids.astype(jnp.int32), backs, h1, cotangent, ready
    )
    both, sums1 = back_projections(lows, part, w_out, w_qkv, xhat)
    theirs = across(both)
    output, d_hidden, finish_token = finish(
        hidden, cotangent, xhat, inv_std, gains, biases, both, theirs, back2, theirs2
    )
    halves = [other_core(array) for array in (early_att, send_att)]
    terms_att = terms_of(keep, [half[i] for half in halves for i in range(half.shape[0])])

    small = jnp.concatenate(
        [sums1.reshape(1, -1), sums2.reshape(1, -1), d_bias, d_b_up, d_b_qkv.reshape(1, -1)], axis=1
    )

    def unpack_some(name, route, cases, unit, shapes, found, old, wait=None):
        parts, ids = zip(*found)
        ids = jnp.stack(ids)
        if wait is not None:
            ids = ids + (wait[0, 0].astype(full) * 0.0).astype(jnp.int32)
        *old, token = unpack(name, route, cases, unit, shapes, ids, parts, old)
        return old, token

    unit_mlp = min(chunk, local_width)
    unit_att = min(keep.shape[1], local_width)
    unpack_mlp = functools.partial(
        unpack_some,
        "unpack_feed_forward",
        functools.partial(to_mlp, width),
        1 + unit_mlp // LANES,
        unit_mlp,
        ((width, hidden_units), (hidden_units, width)),
    )
    unpack_att = functools.partial(
        unpack_some,
        "unpack_attention",
        functools.partial(to_attention, width, local_width),
        2,
        unit_att,
        ((3, width, local_width), (local_width, width)),
    )

    steps_mlp, steps_round = iter(range(3, far)), iter(range(far))
    own_mlp, round_mlp, waiting, grads_mlp = None, None, [], None

    def advance_mlp(token, gate=None):
        nonlocal sends_mlp, own_mlp, round_mlp, waiting
        t = next(steps_mlp, None)
        if t is not None:
            sends_mlp = scatter_step(terms_mlp, t, sends_mlp, token)
            if t < far - 1:
                return zero(sends_mlp[0])
            own_mlp, round_mlp = sends_mlp, (sends_mlp, sends_mlp)
            waiting += gather_start(own_mlp)
            return zero(own_mlp)
        t = next(steps_round, None)
        if t is None:
            return nothing
        round_mlp, found = gather_step(t, round_mlp, gate)
        waiting += found
        return zero(round_mlp[0])

    sends_att = scatter_start(terms_att, nothing)
    for t in range(far):
        sends_att = scatter_step(terms_att, t, sends_att, advance_mlp(nothing))
    round_att, waiting_att, grads_att = (sends_att, sends_att), gather_start(sends_att), None
    norm_sums = small[:, : 4 * width]
    small = jnp.concatenate([norm_sums + across(norm_sums), small[:, 4 * width :]], axis=1)
    small = small + zero(sends_att)[:, :1]
    distance = 1
    for t in range(far):
        ready, waiting = waiting, []
        advance_mlp(nothing, zero(round_att[0]))
        round_att, found = gather_step(t, round_att, None)
        waiting_att += found
        if distance < owners:
            small = small + lax.ppermute(small, "ctx", [(c, c ^ distance) for c in range(owners)])
            distance *= 2
        if ready:
            grads_mlp, more = unpack_mlp(ready, grads_mlp, sends_att if t == 0 else None)
            small = small + more[:, :1]
        if t == far - 2:
            small = small + finish_token[:, :1]
            grads_att, more = unpack_att(waiting_att[:-4], None)
            waiting_att = waiting_att[-4:]
            small = small + more[:, :1]
    while distance < owners:
        small = small + lax.ppermute(small, "ctx", [(c, c ^ distance) for c in range(owners)])
        distance *= 2
    if waiting:
        grads_mlp, _ = unpack_mlp(waiting, grads_mlp)
    grads_att, _ = unpack_att(waiting_att, grads_att)

    norm_sums = small[:, : 4 * width].reshape(4, width)
    at = 4 * width
    d_bias = small[0, at : at + width]
    d_b_up = small[0, at + width : at + width + hidden_units]
    d_b_qkv = small[0, at + width + hidden_units :].reshape(3, local_width)
    d_w_up, d_w_down = grads_mlp
    d_w_qkv, d_w_out = grads_att
    return (
        output,
        d_hidden,
        norm_sums[0],
        norm_sums[1],
        norm_sums[2],
        norm_sums[3],
        d_w_qkv,
        d_b_qkv,
        d_w_out,
        d_bias,
        d_w_up,
        d_b_up,
        d_w_down,
        d_bias,
    )


def solution(mesh):
    placed = (
        P("ctx", None),
        P(),
        P(),
        P(),
        P(),
        P(),
        P(None, None, "tp"),
        P(None, "tp"),
        P("tp", None),
        P(),
        P(None, "tp"),
        P("tp"),
        P("tp", None),
        P(),
        P("ctx", None),
    )
    return jax.shard_map(
        local,
        mesh=mesh,
        in_specs=placed,
        out_specs=(
            P("ctx", None),
            P("ctx", None),
            P(),
            P(),
            P(),
            P(),
            P(None, None, "tp"),
            P(None, "tp"),
            P("tp", None),
            P(),
            P(None, "tp"),
            P("tp"),
            P("tp", None),
            P(),
        ),
        check_vma=False,
    )
```

```python
import functools

import jax
import jax.numpy as jnp
import numpy as np
from jax import lax
from jax.experimental import pallas as pl
from jax.experimental.pallas import tpu as pltpu
from jax.sharding import PartitionSpec as P

HEAD_DIM = 64
ROT = 16
HALF = ROT // 2
BLOCK = 128
LANES = 128
KEYS = 512
MIB = 1 << 20

norm_eps = 1e-05
masked_score = -1e30
score_scale = HEAD_DIM ** (-0.5)
low = jnp.bfloat16
full = jnp.float32


def mm(left, right):
    return lax.dot_general(left, right, (((1,), (0,)), ((), ())), preferred_element_type=full)


def mm_nt(left, right):
    return lax.dot_general(left, right, (((1,), (1,)), ((), ())), preferred_element_type=full)


def turn(tensor):
    return tensor.astype(full).T.astype(low)


def lane_ids(shape):
    return lax.broadcasted_iota(jnp.int32, shape, len(shape) - 1)


def row_ids(shape):
    return lax.broadcasted_iota(jnp.int32, shape, len(shape) - 2)


def rotary_partner(tensor):
    lanes = lane_ids(tensor.shape)
    ahead = pltpu.roll(tensor, LANES - HALF, 1)
    behind = pltpu.roll(tensor, HALF, 1)
    return jnp.where(lanes % ROT < HALF, ahead, behind)


def spec_vmem():
    return pl.BlockSpec(memory_space=pltpu.VMEM)


def spec_smem():
    return pl.BlockSpec(memory_space=pltpu.SMEM)


def spec_hbm():
    return pl.BlockSpec(memory_space=pltpu.HBM)


def params(mib):
    return pltpu.CompilerParams(vmem_limit_bytes=mib * MIB)


def shape_of(shape, kind):
    return jax.ShapeDtypeStruct(shape, kind)


def block_tables(inverse, blocks):
    row = row_ids((BLOCK, LANES)).astype(full)
    start = blocks.astype(full) * float(BLOCK)
    return jnp.cos(row * inverse), jnp.sin(row * inverse), jnp.cos(start * inverse), jnp.sin(start * inverse)


def project_kernel(heads, pair_ref, inv_ref, *rest):
    given, rest = rest[:12], rest[12:]
    h1_ref, h2_ref, xhat_ref, std_ref, d_bias_ref, gains_ref, bias_ref, b_up_out_ref, packed = rest[:9]
    held, sems = rest[9:-1], rest[-1]
    copies = [pltpu.make_async_copy(src, dst, sems.at[i]) for i, (src, dst) in enumerate(zip(given, held))]
    for copy in copies:
        copy.start()
    (
        hidden_ref,
        g1_ref,
        c1_ref,
        g2_ref,
        c2_ref,
        cot_ref,
        w_out_ref,
        w_qkv_ref,
        b_qkv_ref,
        b_up_ref,
        b_out_ref,
        b_down_ref,
    ) = held
    rows = hidden_ref.shape[0]
    me = lax.axis_index("ctx")
    pair = pair_ref[me]
    total_blocks = 2 * pair_ref.shape[0]

    first = jnp.where(row_ids((8, LANES)) == 0, pair, total_blocks - 1 - pair)
    inverse = inv_ref[...]
    cos_row, sin_row, cos_block, sin_block = block_tables(inverse, first)
    in_head = lane_ids((BLOCK, LANES)) % HEAD_DIM
    tables = []
    for half in range(2):
        cos_at, sin_at = cos_block[half : half + 1], sin_block[half : half + 1]
        cosine = cos_row * cos_at - sin_row * sin_at
        sine = sin_row * cos_at + cos_row * sin_at
        cosine = jnp.where(in_head < ROT, cosine, 1.0)
        sine = jnp.where(in_head < HALF, -sine, jnp.where(in_head < ROT, sine, 0.0))
        tables.append((cosine, sine))
    cosine = jnp.concatenate([tables[0][0], tables[1][0]], axis=0)
    sine = jnp.concatenate([tables[0][1], tables[1][1]], axis=0)

    for copy in copies[:5]:
        copy.wait()
    x = hidden_ref[...].astype(full)
    centred = x - jnp.mean(x, axis=-1, keepdims=True)
    spread = jnp.mean(centred * centred, axis=-1, keepdims=True)
    inv_std = lax.rsqrt(spread + norm_eps)
    xhat = centred * inv_std
    xhat_ref[...] = xhat
    std_ref[...] = jnp.broadcast_to(inv_std, std_ref.shape)

    def as_row(ref):
        return ref[...].astype(full)[None, :]

    gain1, gain2 = as_row(g1_ref), as_row(g2_ref)
    h1 = (xhat * gain1 + as_row(c1_ref)).astype(low)
    h1_ref[...] = h1
    h2_ref[...] = (xhat * gain2 + as_row(c2_ref)).astype(low)
    gains_ref[0:1] = gain1
    gains_ref[1:2] = gain2
    for copy in copies[5:]:
        copy.wait()
    b_up_out_ref[...] = as_row(b_up_ref)
    bias_ref[0:1] = as_row(b_out_ref)
    bias_ref[1:2] = as_row(b_down_ref)
    d_bias_ref[...] = jnp.sum(cot_ref[...].astype(full), axis=0, keepdims=True)

    lane = lane_ids((rows, LANES))

    def projected(s):
        return mm(h1, w_qkv_ref[s]) + b_qkv_ref[s : s + 1].astype(full)

    def turned(tile):
        return tile * cosine + rotary_partner(tile) * sine

    queries, keys, values = projected(0), projected(1), projected(2)
    grads = mm_nt(cot_ref[...], w_out_ref[...])
    left = lane < HEAD_DIM
    for i in range(heads // 2):
        cut = slice(i * LANES, (i + 1) * LANES)
        q = turned(queries[:, cut]).astype(low).astype(full) * score_scale
        k = turned(keys[:, cut])
        v = values[:, cut]
        g = grads[:, cut]
        packed[2 * i, :, :LANES] = jnp.where(left, g, pltpu.roll(q, HEAD_DIM, 1)).astype(low)
        packed[2 * i, :, LANES:] = jnp.where(left, v, pltpu.roll(k, HEAD_DIM, 1)).astype(low)
        packed[2 * i + 1, :, :LANES] = jnp.where(left, pltpu.roll(g, HEAD_DIM, 1), q).astype(low)
        packed[2 * i + 1, :, LANES:] = jnp.where(left, pltpu.roll(v, HEAD_DIM, 1), k).astype(low)


def project(heads, pair_of, inverse, given):
    hidden, w_out, b_up = given[0], given[6], given[9]
    rows, width = hidden.shape
    outs = [
        shape_of((rows, width), low),
        shape_of((rows, width), low),
        shape_of((rows, width), full),
        shape_of((rows, LANES), full),
        shape_of((1, width), full),
        shape_of((2, width), full),
        shape_of((2, width), full),
        shape_of((1, b_up.shape[0]), full),
        shape_of((heads, rows, 2 * LANES), low),
    ]
    return pl.pallas_call(
        functools.partial(project_kernel, heads),
        out_shape=outs,
        in_specs=[spec_smem(), spec_vmem()] + [spec_hbm()] * len(given),
        out_specs=[spec_vmem()] * len(outs),
        scratch_shapes=[pltpu.VMEM(array.shape, array.dtype) for array in given]
        + [pltpu.SemaphoreType.DMA((len(given),))],
        compiler_params=params(60),
        cost_estimate=pl.CostEstimate(
            flops=2 * rows * width * 4 * w_out.shape[0], bytes_accessed=8 * MIB, transcendentals=0
        ),
        name="project",
    )(pair_of, inverse, *given)


def mlp_kernel(early, ids_ref, *rest):
    given, rest = rest[:6], rest[6:]
    part_ref, back_ref, sums_ref, d_b_up_ref, keep_ref, early_ref, send_ref = rest[:7]
    h2_turned, part_acc, back_acc = rest[7:10]
    held, sems = rest[10:-1], rest[-1]
    copies = [pltpu.make_async_copy(src, dst, sems.at[i]) for i, (src, dst) in enumerate(zip(given, held))]
    h2_held, w_up_ref, b_up, cot_ref, w_down_ref, xhat_ref = held
    step = pl.program_id(0)
    steps = pl.num_programs(0)

    @pl.when(step == 0)
    def _():
        for copy in copies:
            copy.start()
        part_acc[...] = jnp.zeros_like(part_acc)
        back_acc[...] = jnp.zeros_like(back_acc)
        copies[0].wait()
        h2_turned[...] = turn(h2_held[...])
        for copy in copies[1:3]:
            copy.wait()

    at = [pl.multiple_of(ids_ref[b * steps + step] * LANES, LANES) for b in range(2)]
    w_up = jnp.concatenate([w_up_ref[:, pl.ds(i, LANES)] for i in at], axis=1)
    u = mm(h2_held[...], w_up) + jnp.concatenate([b_up[:, pl.ds(i, LANES)] for i in at], axis=1)

    @pl.when(step == 0)
    def _():
        for copy in copies[3:5]:
            copy.wait()

    cot = cot_ref[...]
    w_down = jnp.concatenate([w_down_ref[pl.ds(i, LANES), :] for i in at], axis=0)
    cdf = 0.5 * (1.0 + lax.erf(u * np.float32(np.sqrt(0.5))))
    active = u * cdf
    active_low = active.astype(low)
    slope = cdf + u * jnp.exp(-0.5 * u * u) * np.float32(1.0 / np.sqrt(2.0 * np.pi))
    du = (mm_nt(cot, w_down) * slope).astype(low)
    part_acc[...] += mm(active_low, w_down)
    back_acc[...] += mm_nt(du, w_up)
    d_b_up = jnp.sum(du.astype(full), axis=0, keepdims=True)
    up = mm(h2_turned[...], du).astype(low)
    down = mm(active.T.astype(low), cot).astype(low)
    depth = up.shape[0]

    def put(b, grad_ref):
        grad_ref[:depth] = up[:, b * LANES : (b + 1) * LANES]
        for t in range(down.shape[1] // LANES):
            grad_ref[depth + t * LANES : depth + (t + 1) * LANES] = down[
                b * LANES : (b + 1) * LANES, t * LANES : (t + 1) * LANES
            ]

    for b in range(2):
        d_b_up_ref[:, pl.ds(at[b], LANES)] = d_b_up[:, b * LANES : (b + 1) * LANES]
    put(0, keep_ref)

    @pl.when(step < early)
    def _():
        put(1, early_ref)

    @pl.when(step >= early)
    def _():
        put(1, send_ref)

    @pl.when(step == steps - 1)
    def _():
        copies[5].wait()
        part_ref[...] = part_acc[...]
        back = back_acc[...]
        back_ref[...] = back.astype(low)
        sums_ref[0:1] = jnp.sum(back * xhat_ref[...], axis=0, keepdims=True)
        sums_ref[1:2] = jnp.sum(back, axis=0, keepdims=True)


def mlp(ids, early, *given):
    rows, width = given[0].shape
    hidden_units = given[1].shape[1]
    steps = hidden_units // LANES // 2
    whole = lambda shape: pl.BlockSpec(shape, lambda f, c: (0,) * len(shape))
    grads = lambda at: pl.BlockSpec((2 * width, LANES), lambda f, c: (at(f), 0))
    outs = [
        shape_of((rows, width), full),
        shape_of((rows, width), low),
        shape_of((2, width), full),
        shape_of((1, hidden_units), full),
        shape_of((steps * 2 * width, LANES), low),
        shape_of((early * 2 * width, LANES), low),
        shape_of(((steps - early) * 2 * width, LANES), low),
    ]
    return pl.pallas_call(
        functools.partial(mlp_kernel, early),
        grid_spec=pltpu.PrefetchScalarGridSpec(
            num_scalar_prefetch=1,
            grid=(steps,),
            in_specs=[spec_hbm()] * len(given),
            out_specs=[whole(array.shape) for array in outs[:4]]
            + [
                grads(lambda f: f),
                grads(lambda f: jnp.minimum(f, early - 1)),
                grads(lambda f: jnp.maximum(f - early, 0)),
            ],
            scratch_shapes=[
                pltpu.VMEM((width, rows), low),
                pltpu.VMEM((rows, width), full),
                pltpu.VMEM((rows, width), full),
            ]
            + [pltpu.VMEM(array.shape, array.dtype) for array in given]
            + [pltpu.SemaphoreType.DMA((len(given),))],
        ),
        out_shape=outs,
        compiler_params=params(60),
        cost_estimate=pl.CostEstimate(
            flops=12 * rows * width * hidden_units, bytes_accessed=20 * MIB, transcendentals=0
        ),
        name="feed_forward",
    )(ids, *given)


def attention_kernel(heads, group, places, is_first, is_last, pair_ref, inv_ref, token_ref, *rest):
    del token_ref
    if is_first:
        got_ref, rest = rest[0], rest[1:]
        if group > 1:
            other_ref, rest = rest[0], rest[1:]
    else:
        rest = rest[4:]
    out_ref, rest = rest[0], rest[1:]
    if is_last:
        d_own_ref, rest = rest[0], rest[1:]
        if group > 1:
            d_other_ref, rest = rest[0], rest[1:]
    (values_keys, turned_keys, sums, queries), rest = rest[:4], rest[4:]
    token_out, rest = rest[0], rest[1:]
    weights_in, weights_out, stored, peaks, totals, weighted, finals, block_cos, block_sin = rest
    token_out[...] = jnp.zeros_like(token_out)

    rows = queries.shape[1]
    owners = pair_ref.shape[0]
    total_blocks = 2 * owners
    per_chunk = KEYS // BLOCK
    tasks = (total_blocks + 1 + per_chunk - 1) // per_chunk
    me = lax.axis_index("ctx")
    own_sub = lax.rem(me, group)

    def blocks_of(r, d):
        owner = r * group + lax.rem(own_sub + d, group)
        pair = pair_ref[owner]
        return pair, total_blocks - 1 - pair

    def place(tile, block):
        at = pl.multiple_of(block * BLOCK, BLOCK)
        values_keys[pl.ds(at, BLOCK), :] = tile
        turned_keys[:, pl.ds(at, BLOCK)] = turn(tile)

    if is_first:
        for r in range(heads):
            queries[r] = got_ref[r, :, :LANES]
            for half, block in enumerate(blocks_of(r, 0)):
                place(got_ref[r, half * BLOCK : (half + 1) * BLOCK, LANES:], block)
            for d in range(1, group):
                for half, block in enumerate(blocks_of(r, d)):
                    at = r * rows + half * BLOCK
                    place(other_ref[d - 1, at : at + BLOCK, :], block)
        sums[...] = jnp.zeros_like(sums)

    lane = lane_ids((BLOCK, LANES))
    left = lane < HEAD_DIM
    in_key = lane - HEAD_DIM
    moving = (in_key >= 0) & (in_key < ROT)
    forward = (in_key >= 0) & (in_key < HALF)
    cos_row, sin_row, block_cos[...], block_sin[...] = block_tables(inv_ref[...], row_ids(block_cos.shape))

    def rotated_back(tile, block):
        cos_at, sin_at = block_cos[pl.ds(block, 1), :], block_sin[pl.ds(block, 1), :]
        cosine = jnp.where(moving, cos_row * cos_at - sin_row * sin_at, 1.0)
        sine = sin_row * cos_at + cos_row * sin_at
        sine = jnp.where(moving, jnp.where(forward, sine, -sine), 0.0)
        return tile * cosine + rotary_partner(tile) * sine

    offset = row_ids((BLOCK, BLOCK)) - lane_ids((BLOCK, BLOCK))

    def one_pair(i, carry):
        blocks = blocks_of(places[0] + i, 0)
        first = blocks[0] // per_chunk + 1
        for half in range(2):
            both = queries[places[0] + i, half * BLOCK : (half + 1) * BLOCK, :]
            both_turned = turn(both)
            upper = row_ids((LANES, BLOCK)) < HEAD_DIM
            zero = jnp.zeros_like(both_turned)
            weights_in[half, :, :BLOCK] = jnp.where(upper, both_turned, zero)
            weights_in[half, :, BLOCK:] = jnp.where(upper, zero, both_turned)
            weights_out[half, :BLOCK, :] = jnp.where(left, both, zero)
            weights_out[half, BLOCK:, :] = jnp.where(left, zero, both)
        finals[...] = jnp.zeros_like(finals)

        def task(t):
            is_low = t < first
            chunk = jnp.where(is_low, first - 1 - t, t - first)
            return is_low, chunk

        runs = KEYS // BLOCK
        for t in range(tasks):
            is_low, chunk = task(t)
            weights = weights_in[jnp.where(is_low, 0, 1)]
            for u in range(runs):
                at = pl.multiple_of(chunk * KEYS + u * BLOCK, BLOCK)
                sub = slice(u * BLOCK, (u + 1) * BLOCK)
                both = mm(values_keys[pl.ds(at, BLOCK), :], weights)
                grads = both[:, :BLOCK]
                scores = both[:, BLOCK:]
                if t in (0, tasks - 1):
                    query_at = blocks[0 if t == 0 else 1] * BLOCK
                    scores = jnp.where(offset <= query_at - at, scores, masked_score)
                peak = jnp.max(scores, axis=0, keepdims=True)
                raised = jnp.exp(scores - peak)
                stored[t, sub, :BLOCK] = raised
                stored[t, sub, BLOCK:] = grads
                line = t * runs + u
                peaks[line : line + 1] = peak
                totals[line : line + 1] = jnp.sum(raised, axis=0, keepdims=True)
                weighted[line : line + 1] = jnp.sum(raised * grads, axis=0, keepdims=True)

        in_low = row_ids((tasks * runs, BLOCK)) < first * runs

        def finish(mine):
            top = jnp.max(jnp.where(mine, peaks[...], masked_score), axis=0, keepdims=True)
            factor = jnp.where(mine, jnp.exp(peaks[...] - top), 0.0)
            inverse = 1.0 / jnp.sum(totals[...] * factor, axis=0, keepdims=True)
            return factor * inverse, jnp.sum(weighted[...] * factor, axis=0, keepdims=True) * inverse

        (low_factor, low_delta), (high_factor, high_delta) = finish(in_low), finish(jnp.logical_not(in_low))
        peaks[...] = low_factor + high_factor

        for t in range(tasks):
            is_low, chunk = task(t)
            half = jnp.where(is_low, 0, 1)
            weights = weights_out[half]
            delta = jnp.where(is_low, low_delta, high_delta)
            parts = []
            for u in range(runs):
                sub = slice(u * BLOCK, (u + 1) * BLOCK)
                probs = stored[t, sub, :BLOCK] * peaks[t * runs + u : t * runs + u + 1]
                d_scores = probs * (stored[t, sub, BLOCK:] - delta)
                both = jnp.concatenate([probs, d_scores], axis=1).astype(low)
                at = pl.multiple_of(chunk * KEYS + u * BLOCK, BLOCK)
                sums[pl.ds(at, BLOCK), :] += mm(both, weights)
                parts.append(both)
            at = pl.multiple_of(chunk * KEYS, KEYS)
            finals[half] += mm(turned_keys[:, pl.ds(at, KEYS)], jnp.concatenate(parts, axis=0))

        for half in range(2):
            both = jnp.concatenate(
                [finals[half, :HEAD_DIM, :BLOCK], finals[half, HEAD_DIM:, BLOCK:] * score_scale], axis=0
            ).T
            out_ref[i, half * BLOCK : (half + 1) * BLOCK, :] = rotated_back(both, blocks[half]).astype(low)
        return carry

    lax.fori_loop(0, len(places), one_pair, 0)

    if is_last:
        for r in range(heads):
            for d in range(group):
                for half, block in enumerate(blocks_of(r, d)):
                    at = r * rows + half * BLOCK
                    tile = rotated_back(sums[pl.ds(pl.multiple_of(block * BLOCK, BLOCK), BLOCK), :], block)
                    if d == 0:
                        d_own_ref[at : at + BLOCK, :] = tile
                    else:
                        d_other_ref[d - 1, at : at + BLOCK, :] = tile


def attention(heads, group, places, pair_of, inverse, token, got, other, state):
    is_first, is_last = state is None, places[-1] == heads - 1
    rows = got.shape[1]
    owners = pair_of.shape[0]
    total_keys = owners * rows
    tasks = (2 * owners + KEYS // BLOCK) // (KEYS // BLOCK)
    operands = [pair_of, inverse, token]
    outs = [shape_of((len(places), rows, LANES), low)]
    if is_first:
        operands += [got] if other is None else [got, other]
    else:
        operands += list(state)
    if is_last:
        outs.append(shape_of((heads * rows, LANES), full))
        if group > 1:
            outs.append(shape_of((group - 1, heads * rows, LANES), full))
    kept = [
        shape_of((total_keys, LANES), low),
        shape_of((LANES, total_keys), low),
        shape_of((total_keys, LANES), full),
        shape_of((heads, rows, LANES), low),
    ]
    aliases = {} if is_first else {len(operands) - 4 + i: len(outs) + i for i in range(4)}
    found = pl.pallas_call(
        functools.partial(attention_kernel, heads, group, places, is_first, is_last),
        out_shape=outs + kept + [shape_of((1, LANES), full)],
        in_specs=[spec_smem()] + [spec_vmem()] * (len(operands) - 1),
        out_specs=[spec_vmem()] * (len(outs) + 5),
        input_output_aliases=aliases,
        scratch_shapes=[
            pltpu.VMEM((2, LANES, 2 * BLOCK), low),
            pltpu.VMEM((2, 2 * BLOCK, LANES), low),
            pltpu.VMEM((tasks, KEYS, 2 * BLOCK), full),
            pltpu.VMEM((tasks * KEYS // BLOCK, BLOCK), full),
            pltpu.VMEM((tasks * KEYS // BLOCK, BLOCK), full),
            pltpu.VMEM((tasks * KEYS // BLOCK, BLOCK), full),
            pltpu.VMEM((2, LANES, 2 * BLOCK), full),
            pltpu.VMEM((2 * owners, LANES), full),
            pltpu.VMEM((2 * owners, LANES), full),
        ],
        compiler_params=params(6 + total_keys * 5 * 256 // MIB),
        cost_estimate=pl.CostEstimate(
            flops=2_500_000_000 * len(places), bytes_accessed=2 * MIB, transcendentals=0
        ),
        name="attention",
    )(*operands)
    return found[0], found[1 : len(outs)], found[len(outs) : len(outs) + 4], found[-1]


def combine_kernel(heads, terms, *refs):
    out_ref = refs[-1]
    rows = out_ref.shape[1]
    for r in range(heads):
        cut = slice(r * rows, (r + 1) * rows)
        total = refs[0][cut, :]
        for term in refs[1:terms]:
            total = total + term[cut, :]
        out_ref[r, :, LANES:] = total.astype(low)
    at = 0
    for first_ref in refs[terms:-1]:
        out_ref[at : at + first_ref.shape[0], :, :LANES] = first_ref[...]
        at += first_ref.shape[0]


def combine(heads, terms, firsts):
    rows = firsts[0].shape[1]
    return pl.pallas_call(
        functools.partial(combine_kernel, heads, len(terms)),
        out_shape=shape_of((heads, rows, 2 * LANES), low),
        in_specs=[spec_vmem()] * (len(firsts) + len(terms)),
        out_specs=spec_vmem(),
        compiler_params=params(24),
        cost_estimate=pl.CostEstimate(flops=10**7, bytes_accessed=3 * MIB, transcendentals=0),
        name="combine",
    )(*terms, *firsts)


def weight_grads_kernel(
    heads, early, ids_ref, got_ref, h1_ref, cot_ref, ready_ref, low_ref, d_b_ref, keep_ref, early_ref, send_ref, token_ref, grads
):
    del ready_ref
    chips, chunk_rows = keep_ref.shape[:2]

    def put(at, tile):
        step = min(chunk_rows, tile.shape[0])
        for off in range(0, tile.shape[0], step):
            chunk, inside = divmod(at + off, chunk_rows)
            grads[chunk, inside : inside + step] = tile[off : off + step]

    rows = h1_ref.shape[0]
    left = lane_ids((rows, LANES)) < HEAD_DIM
    for i in range(heads // 2):
        cut = slice(i * LANES, (i + 1) * LANES)
        for first, second, half in ((0, 1, slice(0, LANES)), (3, 2, slice(LANES, 2 * LANES))):
            a, b = got_ref[2 * i, :, half].astype(full), got_ref[2 * i + 1, :, half].astype(full)
            low_ref[first, :, cut] = jnp.where(left, a, pltpu.roll(b, HEAD_DIM, 1)).astype(low)
            low_ref[second, :, cut] = jnp.where(left, pltpu.roll(a, HEAD_DIM, 1), b).astype(low)
    h1_turned = turn(h1_ref[...])
    depth, tiles = h1_turned.shape[0], heads // 2
    for s in range(3):
        d_proj = low_ref[1 + s]
        d_b_ref[s : s + 1] = jnp.sum(d_proj.astype(full), axis=0, keepdims=True)
        grad = mm(h1_turned, d_proj).astype(low)
        for t in range(tiles):
            put((s * tiles + t) * depth, grad[:, t * LANES : (t + 1) * LANES])
    grad = mm(turn(low_ref[0]), cot_ref[...]).astype(low)
    height = grad.shape[0]
    for t in range(depth // LANES):
        put(3 * tiles * depth + t * height, grad[:, t * LANES : (t + 1) * LANES])
    for t in range(chips):
        target = early_ref.at[t] if t < early else send_ref.at[t - early]
        target[...] = grads[ids_ref[chips + t]]
        keep_ref[t] = grads[ids_ref[t]]
    token_ref[...] = jnp.zeros_like(token_ref)


def weight_grads(heads, early, ids, got, h1, cot, ready):
    rows, width = h1.shape
    local_width = heads * HEAD_DIM
    chips = ids.shape[0] // 2
    chunk_rows = 4 * width * local_width // LANES // (2 * chips)
    outs = [
        shape_of((4, rows, local_width), low),
        shape_of((3, local_width), full),
        shape_of((chips, chunk_rows, LANES), low),
        shape_of((early, chunk_rows, LANES), low),
        shape_of((chips - early, chunk_rows, LANES), low),
        shape_of((1, LANES), full),
    ]
    return pl.pallas_call(
        functools.partial(weight_grads_kernel, heads, early),
        out_shape=outs,
        in_specs=[spec_smem()] + [spec_vmem()] * 4,
        out_specs=[spec_vmem()] * len(outs),
        scratch_shapes=[pltpu.VMEM((2 * chips, chunk_rows, LANES), low)],
        compiler_params=params(20),
        cost_estimate=pl.CostEstimate(
            flops=8 * rows * width * local_width, bytes_accessed=8 * MIB, transcendentals=0
        ),
        name="weight_grads",
    )(ids, got, h1, cot, ready)


def return_kernel(low_ref, part_ref, w_out_ref, w_qkv_ref, xhat_ref, both_ref, sums_ref):
    rows = xhat_ref.shape[0]
    both_ref[:rows] = (part_ref[...] + mm(low_ref[0], w_out_ref[...])).astype(low)
    back = mm_nt(low_ref[1], w_qkv_ref[0]) + mm_nt(low_ref[2], w_qkv_ref[1]) + mm_nt(low_ref[3], w_qkv_ref[2])
    both_ref[rows:] = back.astype(low)
    sums_ref[0:1] = jnp.sum(back * xhat_ref[...], axis=0, keepdims=True)
    sums_ref[1:2] = jnp.sum(back, axis=0, keepdims=True)


def back_projections(*given):
    rows, width = given[1].shape
    return pl.pallas_call(
        return_kernel,
        out_shape=[shape_of((2 * rows, width), low), shape_of((2, width), full)],
        in_specs=[spec_vmem()] * len(given),
        out_specs=[spec_vmem()] * 2,
        compiler_params=params(16),
        cost_estimate=pl.CostEstimate(
            flops=8 * rows * width * given[2].shape[0], bytes_accessed=8 * MIB, transcendentals=0
        ),
        name="back_projections",
    )(*given)


def finish_kernel(
    hidden_ref, cot_ref, xhat_ref, std_ref, gains_ref, bias_ref, ours_ref, theirs_ref, e2_ours_ref, e2_theirs_ref, out_ref, grad_ref, token_ref
):
    rows = hidden_ref.shape[0]
    gains = gains_ref[...]
    biases = bias_ref[...]
    summed = ours_ref[:rows].astype(full) + theirs_ref[:rows].astype(full)
    out_ref[...] = (hidden_ref[...].astype(full) + summed + biases[0:1] + biases[1:2]).astype(low)
    e1 = ours_ref[rows:].astype(full) + theirs_ref[rows:].astype(full)
    e2 = e2_ours_ref[...].astype(full) + e2_theirs_ref[...].astype(full)
    f = e1 * gains[0:1] + e2 * gains[1:2]
    xhat = xhat_ref[...]
    inv_std = std_ref[:, 0:1]
    grad_ref[...] = cot_ref[...].astype(full) + inv_std * (
        f - jnp.mean(f, axis=-1, keepdims=True) - xhat * jnp.mean(f * xhat, axis=-1, keepdims=True)
    )
    token_ref[...] = jnp.zeros_like(token_ref)


def finish(*operands):
    rows, width = operands[0].shape
    return pl.pallas_call(
        finish_kernel,
        out_shape=[shape_of((rows, width), low), shape_of((rows, width), full), shape_of((1, LANES), full)],
        in_specs=[spec_vmem()] * len(operands),
        out_specs=[spec_vmem()] * 3,
        compiler_params=params(24),
        cost_estimate=pl.CostEstimate(flops=10**7, bytes_accessed=8 * MIB, transcendentals=0),
        name="finish",
    )(*operands)


def to_attention(width, local_width, source, refs, base, unit):
    qkv_ref, out_ref = refs
    tiles = local_width // LANES
    split = 3 * tiles * width
    tile = base // width
    row = pl.multiple_of(lax.rem(base, width), unit)
    column = pl.multiple_of(lax.rem(tile, tiles) * LANES, LANES)
    yield base < split, source, qkv_ref.at[jnp.minimum(tile // tiles, 2), pl.ds(row, unit), pl.ds(column, LANES)]
    after = jnp.maximum(base - split, 0)
    row = pl.multiple_of(lax.rem(after, local_width), unit)
    column = pl.multiple_of(after // local_width * LANES, LANES)
    yield base >= split, source, out_ref.at[pl.ds(row, unit), pl.ds(column, LANES)]


def to_mlp(width, source, refs, base, unit):
    up_ref, down_ref = refs
    block, inside = base // (2 * width), lax.rem(base, 2 * width)
    block_at = pl.multiple_of(block * LANES, LANES)
    row = pl.multiple_of(jnp.minimum(inside, width - unit), unit)
    yield inside < width, source, up_ref.at[pl.ds(row, unit), pl.ds(block_at, LANES)]
    for t in range(unit // LANES):
        column = pl.multiple_of(jnp.maximum(inside - width, 0) + t * LANES, LANES)
        cut = source.at[pl.ds(t * LANES, LANES), :]
        yield inside >= width, cut, down_ref.at[pl.ds(block_at, LANES), pl.ds(column, LANES)]


def unpack_kernel(route, count, unit, has_old, ids_ref, *rest):
    parts, rest = rest[:count], rest[count:]
    rest = rest[2:] if has_old else rest
    targets, (token_ref, held, sems) = rest[:2], rest[2:]
    token_ref[...] = jnp.zeros_like(token_ref)
    chunk_rows = parts[0].shape[0]
    units = chunk_rows // unit
    per_unit = sems.shape[0] // (count * units)

    def moves():
        for i in range(count):
            for j in range(units):
                source = held.at[i, pl.ds(j * unit, unit), :]
                base = ids_ref[i] * chunk_rows + j * unit
                for n, (applies, piece, target) in enumerate(route(source, targets, base, unit)):
                    sem = sems.at[(i * units + j) * per_unit + n]
                    yield i, applies, pltpu.make_async_copy(piece, target, sem)

    done = -1
    for i, applies, copy in moves():
        if i != done:
            held[i] = parts[i][...].astype(full)
            done = i
        pl.when(applies)(copy.start)
    for i, applies, copy in moves():
        pl.when(applies)(copy.wait)


def unpack(name, route, cases, unit, shapes, ids, parts, old):
    count = len(parts)
    chunk_rows = parts[0].shape[0]
    operands = [ids, *parts, *(old or ())]
    return pl.pallas_call(
        functools.partial(unpack_kernel, route, count, unit, old is not None),
        out_shape=[shape_of(shape, full) for shape in shapes] + [shape_of((1, LANES), full)],
        in_specs=[spec_smem()] + [spec_vmem()] * count + [spec_hbm()] * (len(operands) - 1 - count),
        out_specs=[spec_hbm()] * 2 + [spec_vmem()],
        input_output_aliases={} if old is None else {1 + count: 0, 2 + count: 1},
        scratch_shapes=[
            pltpu.VMEM((count, chunk_rows, LANES), full),
            pltpu.SemaphoreType.DMA((count * (chunk_rows // unit) * cases,)),
        ],
        compiler_params=params(8 + count * chunk_rows * 3 * LANES * 2 // MIB),
        cost_estimate=pl.CostEstimate(
            flops=10**6, bytes_accessed=count * chunk_rows * LANES * 6, transcendentals=0
        ),
        name=name,
    )(*operands)


def local(
    hidden,
    pair_of,
    ln1_gain,
    ln1_bias,
    ln2_gain,
    ln2_bias,
    w_qkv,
    b_qkv,
    w_out,
    b_out,
    w_up,
    b_up,
    w_down,
    b_down,
    cotangent,
):
    owners = lax.axis_size("ctx")
    sides = lax.axis_size("tp")
    rows, width = hidden.shape
    local_width = w_qkv.shape[2]
    hidden_units = w_up.shape[1]
    heads = local_width // HEAD_DIM
    group = owners // heads

    exponent = np.arange(0, ROT, 2, dtype=np.float32) / np.float32(ROT)
    inverse = jnp.asarray(np.tile(np.float32(10000.0) ** (-exponent), LANES // HALF)[None, :], full)
    order = (0, 2, 4, 6, 7, 5, 3, 1) if owners == 16 else tuple(range(owners // 2))
    chips = len(order)

    def to_heads(array):
        groups = [[h * group + g for h in range(heads)] for g in range(group)]
        return lax.all_to_all(array, "ctx", 0, 0, axis_index_groups=groups, tiled=True)

    def group_shift(array, d):
        pairs = [(c, c // group * group + (c % group + d) % group) for c in range(owners)]
        return lax.ppermute(array, "ctx", pairs)

    me = lax.axis_index("ctx")
    chip, core = me // 2, lax.rem(me, 2)
    place = sum(jnp.where(chip == c, i, 0) for i, c in enumerate(order))
    way = 1 - 2 * core
    far, near = chips // 2, chips - 1 - chips // 2

    def ring(array, forward):
        pairs = []
        for i, c in enumerate(order):
            for k in range(2):
                step = 1 if (k == 0) == forward else -1
                pairs.append((2 * c + k, 2 * order[(i + step) % chips] + k))
        return lax.ppermute(array, "ctx", pairs)

    def other_core(array):
        return lax.ppermute(array, "ctx", [(c, c ^ 1) for c in range(owners)])

    def across(array):
        return lax.ppermute(array, "tp", [(t, (t + 1) % sides) for t in range(sides)])

    def target(distance):
        return lax.rem(place + way * distance + chips, chips)

    def zero(array):
        return array[:1].astype(full) * 0.0

    slots = [far, -near]
    for t in range(1, far):
        slots += [far - t] if t >= near else [far - t, t - near]
    slots.append(0)
    early = 2
    slot_ids = jnp.stack(
        [core * chips + target(d) for d in slots] + [(1 - core) * chips + target(-d) for d in slots]
    )

    def terms_of(keep, came):
        def term(i):
            return keep[i].astype(full) + came[i].astype(full)

        return {d: term(i) for i, d in enumerate(slots)}

    def scatter_start(terms, token):
        return (terms[far] + token).astype(low), (terms[-near] + token).astype(low)

    def scatter_step(terms, t, sends, token):
        long_send, short_send = sends
        long_got = ring(long_send, True).astype(full) + token
        last = t == far - 1
        long_next = long_got if last else (long_got + terms[far - 1 - t]).astype(low)
        short_next = short_send
        if t < near:
            short_got = ring(short_send, False).astype(full) + token
            short_next = short_got if t == near - 1 else (short_got + terms[t + 1 - near]).astype(low)
        if last:
            return (terms[0] + long_next + short_next).astype(low)
        return long_next, short_next

    base, other_base = core * chips, (1 - core) * chips

    def gather_start(own):
        return [(own, base + place), (other_core(own), other_base + place)]

    def gather_step(t, sends, token):
        long_send, short_send = sends
        if token is not None:
            long_send = (long_send.astype(full) + token).astype(low)
        long_got = ring(long_send, True)
        found = [(long_got, base + target(-t - 1)), (other_core(long_got), other_base + target(t + 1))]
        short_got = short_send
        if t < near:
            short_got = ring(short_send, False)
            found += [(short_got, base + target(t + 1)), (other_core(short_got), other_base + target(-t - 1))]
        return (long_got, short_got), found

    blocks = hidden_units // LANES // 2
    in_slots = blocks == chips
    mlp_ids = slot_ids if in_slots else jnp.concatenate(
        [core * blocks + jnp.arange(blocks), (1 - core) * blocks + jnp.arange(blocks)]
    )
    h1, h2, xhat, inv_std, d_bias, gains, biases, b_up_row, packed = project(
        heads,
        pair_of,
        inverse,
        (hidden, ln1_gain, ln1_bias, ln2_gain, ln2_bias, cotangent, w_out, w_qkv, b_qkv, b_up, b_out, b_down),
    )
    got = to_heads(packed)
    part, back2, sums2, d_b_up, keep_mlp, early_mlp, send_mlp = mlp(
        mlp_ids.astype(jnp.int32), early, h2, w_up, b_up_row, cotangent, w_down, xhat
    )
    chunk = keep_mlp.shape[0] // chips
    came_mlp = jnp.concatenate([other_core(early_mlp), other_core(send_mlp)]) if not in_slots else None
    if in_slots:
        halves = [other_core(array).reshape(-1, chunk, LANES) for array in (early_mlp, send_mlp)]
        came_mlp = [half[i] for half in halves for i in range(half.shape[0])]
        terms_mlp = terms_of(keep_mlp.reshape(chips, chunk, LANES), came_mlp)
    else:
        summed = (keep_mlp.astype(full) + came_mlp.astype(full)).reshape(chips, chunk, LANES)
        terms_mlp = {d: lax.dynamic_index_in_dim(summed, target(d), 0, keepdims=False) for d in slots}
    nothing = jnp.zeros((1, LANES), full)

    other = None
    if group > 1:
        mine = got[:, :, LANES:].reshape(heads * rows, LANES)
        other = jnp.stack([group_shift(mine, group - d) for d in range(1, group)])

    middle = 3 * heads // 8
    sends_mlp = scatter_start(terms_mlp, nothing)
    token = zero(sends_mlp[0]) + zero(sends_mlp[1])
    first, _, state, token = attention(
        heads, group, tuple(range(middle)), pair_of, inverse, token, got, other, None
    )
    sends_mlp = scatter_step(terms_mlp, 0, sends_mlp, token)
    token = zero(sends_mlp[0]) + zero(sends_mlp[1])
    second, ends, _, token = attention(
        heads, group, tuple(range(middle, heads)), pair_of, inverse, token, got, other, state
    )
    d_own, d_other = ends[0], (ends[1] if group > 1 else None)
    terms = [d_own] + [group_shift(d_other[d - 1], d) for d in range(1, group)]
    sends_mlp = scatter_step(terms_mlp, 1, sends_mlp, token)
    first = (first.astype(full) + zero(sends_mlp[0]) + zero(sends_mlp[1])).astype(low)
    combined = combine(heads, terms, [first, second])
    backs = to_heads(combined)
    theirs2 = across((back2.astype(full) + zero(combined[0])[:, :1]).astype(low))
    sends_mlp = scatter_step(terms_mlp, 2, sends_mlp, nothing)
    ready = zero(sends_mlp[0]) + zero(sends_mlp[1]) + zero(theirs2)[:, :LANES]

    lows, d_b_qkv, keep, early_att, send_att, after = weight_grads(
        heads, early, slot_ids.astype(jnp.int32), backs, h1, cotangent, ready
    )
    both, sums1 = back_projections(lows, part, w_out, w_qkv, xhat)
    theirs = across(both)
    output, d_hidden, finish_token = finish(
        hidden, cotangent, xhat, inv_std, gains, biases, both, theirs, back2, theirs2
    )
    halves = [other_core(array) for array in (early_att, send_att)]
    terms_att = terms_of(keep, [half[i] for half in halves for i in range(half.shape[0])])

    small = jnp.concatenate(
        [sums1.reshape(1, -1), sums2.reshape(1, -1), d_bias, d_b_up, d_b_qkv.reshape(1, -1)], axis=1
    )

    def unpack_some(name, route, cases, unit, shapes, found, old, wait=None):
        parts, ids = zip(*found)
        ids = jnp.stack(ids)
        if wait is not None:
            ids = ids + (wait[0, 0].astype(full) * 0.0).astype(jnp.int32)
        *old, token = unpack(name, route, cases, unit, shapes, ids, parts, old)
        return old, token

    unit_mlp = min(chunk, local_width)
    unit_att = min(keep.shape[1], local_width)
    unpack_mlp = functools.partial(
        unpack_some,
        "unpack_feed_forward",
        functools.partial(to_mlp, width),
        1 + unit_mlp // LANES,
        unit_mlp,
        ((width, hidden_units), (hidden_units, width)),
    )
    unpack_att = functools.partial(
        unpack_some,
        "unpack_attention",
        functools.partial(to_attention, width, local_width),
        2,
        unit_att,
        ((3, width, local_width), (local_width, width)),
    )

    steps_mlp, steps_round = iter(range(3, far)), iter(range(far))
    own_mlp, round_mlp, waiting, grads_mlp = None, None, [], None

    def advance_mlp(token, gate=None):
        nonlocal sends_mlp, own_mlp, round_mlp, waiting
        t = next(steps_mlp, None)
        if t is not None:
            sends_mlp = scatter_step(terms_mlp, t, sends_mlp, token)
            if t < far - 1:
                return zero(sends_mlp[0])
            own_mlp, round_mlp = sends_mlp, (sends_mlp, sends_mlp)
            waiting += gather_start(own_mlp)
            return zero(own_mlp)
        t = next(steps_round, None)
        if t is None:
            return nothing
        round_mlp, found = gather_step(t, round_mlp, gate)
        waiting += found
        return zero(round_mlp[0])

    sends_att = scatter_start(terms_att, nothing)
    before = nothing
    for t in range(far):
        later = advance_mlp(after if t == 0 else zero(sends_att[0]))
        sends_att = scatter_step(terms_att, t, sends_att, before)
        before = later
    round_att, waiting_att, grads_att = (sends_att, sends_att), gather_start(sends_att), None
    norm_sums = small[:, : 4 * width]
    small = jnp.concatenate([norm_sums + across(norm_sums), small[:, 4 * width :]], axis=1)
    small = small + zero(sends_att)[:, :1]
    distance = 1
    for t in range(far):
        ready, waiting = waiting, []
        advance_mlp(nothing, zero(round_att[0]))
        round_att, found = gather_step(t, round_att, None)
        waiting_att += found
        if distance < owners:
            small = small + lax.ppermute(small, "ctx", [(c, c ^ distance) for c in range(owners)])
            distance *= 2
        if ready:
            grads_mlp, more = unpack_mlp(ready, grads_mlp, sends_att if t == 0 else None)
            small = small + more[:, :1]
        if t == far - 2:
            small = small + finish_token[:, :1]
            grads_att, more = unpack_att(waiting_att[:-4], None)
            waiting_att = waiting_att[-4:]
            small = small + more[:, :1]
    while distance < owners:
        small = small + lax.ppermute(small, "ctx", [(c, c ^ distance) for c in range(owners)])
        distance *= 2
    if waiting:
        grads_mlp, _ = unpack_mlp(waiting, grads_mlp)
    grads_att, _ = unpack_att(waiting_att, grads_att)

    norm_sums = small[:, : 4 * width].reshape(4, width)
    at = 4 * width
    d_bias = small[0, at : at + width]
    d_b_up = small[0, at + width : at + width + hidden_units]
    d_b_qkv = small[0, at + width + hidden_units :].reshape(3, local_width)
    d_w_up, d_w_down = grads_mlp
    d_w_qkv, d_w_out = grads_att
    return (
        output,
        d_hidden,
        norm_sums[0],
        norm_sums[1],
        norm_sums[2],
        norm_sums[3],
        d_w_qkv,
        d_b_qkv,
        d_w_out,
        d_bias,
        d_w_up,
        d_b_up,
        d_w_down,
        d_bias,
    )


def solution(mesh):
    placed = (
        P("ctx", None),
        P(),
        P(),
        P(),
        P(),
        P(),
        P(None, None, "tp"),
        P(None, "tp"),
        P("tp", None),
        P(),
        P(None, "tp"),
        P("tp"),
        P("tp", None),
        P(),
        P("ctx", None),
    )
    return jax.shard_map(
        local,
        mesh=mesh,
        in_specs=placed,
        out_specs=(
            P("ctx", None),
            P("ctx", None),
            P(),
            P(),
            P(),
            P(),
            P(None, None, "tp"),
            P(None, "tp"),
            P("tp", None),
            P(),
            P(None, "tp"),
            P("tp"),
            P("tp", None),
            P(),
        ),
        check_vma=False,
    )
```
